32 devices in a mesh: rep: 4 (over x, core), shard: 8 (over z, y).
Axes of the slice: x: 2, y: 2, z: 4, core: 2. Of those that a mesh axis runs over, the one named last changes fastest.
Arguments:
- tokens: bfloat16 [4096, 1024], P(('rep', 'shard')), may hold values from -6 to 6
- encoder: bfloat16 [2048, 1024], P(('rep', 'shard')), may hold values from -6 to 6
- seq_len: int32 [4], P('rep'), may hold values from 256 to 1024, as said below
- enc_len: int32 [4], P('rep'), may hold values from 128 to 512, as said below
- d_mixed: bfloat16 [4096, 1024], P(('rep', 'shard')), may hold values from -6 to 6
- self_qkv: bfloat16 [1024, 3072], P('shard'), may hold values from -0.1875 to 0.1875
- self_out: bfloat16 [1024, 1024], P('shard'), may hold values from -0.75 to 0.75
- cross_qkv: bfloat16 [1024, 3072], P('shard'), may hold values from -0.1875 to 0.1875
- cross_out: bfloat16 [1024, 1024], P('shard'), may hold values from -0.75 to 0.75
- fc1_weight: bfloat16 [1024, 4096], P('shard'), may hold values from -0.1875 to 0.1875
- fc2_weight: bfloat16 [4096, 1024], P('shard'), may hold values from -0.09375 to 0.09375
- self_bias: float32 [3, 1024], replicated, may hold values from -3 to 3
- cross_bias: float32 [3, 1024], replicated, may hold values from -3 to 3
- norm_gain: float32 [3, 1024], replicated, may hold values from 0.5 to 1.5
- norm_bias: float32 [3, 1024], replicated, may hold values from -2 to 2
- fc1_bias: float32 [4096], replicated, may hold values from -2 to 2
- fc2_bias: float32 [1024], replicated, may hold values from -2 to 2
Outputs:
- mixed: bfloat16 [4096, 1024], P(('rep', 'shard'))
- d_tokens: float32 [4096, 1024], P(('rep', 'shard'))
- d_encoder: float32 [2048, 1024], P(('rep', 'shard'))
- d_self_qkv: float32 [1024, 3072], P('shard')
- d_self_out: float32 [1024, 1024], P('shard')
- d_cross_qkv: float32 [1024, 3072], P('shard')
- d_cross_out: float32 [1024, 1024], P('shard')
- d_fc1_weight: float32 [1024, 4096], P('shard')
- d_fc2_weight: float32 [4096, 1024], P('shard')
- d_self_bias: float32 [3, 1024], replicated
- d_cross_bias: float32 [3, 1024], replicated
- d_norm_gain: float32 [3, 1024], replicated
- d_norm_bias: float32 [3, 1024], replicated
- d_fc1_bias: float32 [4096], replicated
- d_fc2_bias: float32 [1024], replicated
The draws below stay inside these ranges and needn't reach their ends.
Inputs may be any that keep to these rules, and one draw needn't show every extreme that they name: `seq_len`: some sequence has all 1024 tokens valid. `enc_len`: some sequence has all 512 encoder states valid.
All inputs are finite; a program needn't handle non-finite values.
Results may differ from the reference program's by a relative error of at most 0.023.
Values may be sent and summed in bfloat16 or wider, within the bound.
A program may use at most 320 MiB of HBM per device.

```python
import math
import jax
import jax.numpy as jnp
from jax import lax

D = 1024
HEADS = 16
HEAD = 64
FF = 4096
GROUPS = 4
GROUP_TOK = 1024
ENC_GRP = 512
TOKENS = 4096
ENC_ROWS = 2048


def draw_seq_len(key, part):
    key = jax.random.fold_in(key, 11)
    first_key, second_key = jax.random.split(key)
    lengths = jax.random.randint(first_key, (GROUPS,), GROUP_TOK // 4, GROUP_TOK + 1)
    chosen = jax.random.randint(second_key, (), 0, GROUPS)
    return jnp.where(jnp.arange(GROUPS) == chosen, GROUP_TOK, lengths).astype(jnp.int32)


def draw_enc_len(key, part):
    key = jax.random.fold_in(key, 23)
    first_key, second_key = jax.random.split(key)
    lengths = jax.random.randint(first_key, (GROUPS,), ENC_GRP // 4, ENC_GRP + 1)
    chosen = jax.random.randint(second_key, (), 0, GROUPS)
    return jnp.where(jnp.arange(GROUPS) == chosen, ENC_GRP, lengths).astype(jnp.int32)


def block_scale(rng, dims, pieces, low, top_value):
    level = 1.0
    for dim, shards_of in pieces:
        steps = jax.random.uniform(jax.random.fold_in(jax.random.fold_in(rng, 6), dim), (shards_of,), jnp.float32, low / len(pieces), top_value / len(pieces))
        level = level * jnp.repeat(jnp.exp(steps), dims[dim] // shards_of).reshape((-1,) + (1,) * (len(dims) - 1 - dim))
    return level


def gaussian(rng, extent, deviation, bound, cuts=(), dtype=jnp.bfloat16):
    result = jax.random.normal(rng, extent, jnp.float32) * deviation
    if len(cuts) > 0:
        result = block_scale(rng, extent, cuts, -0.22, 0.18) * result
    return jnp.clip(result, min=-bound, max=bound).astype(dtype)


def setup_inputs(seed: int = 0) -> dict:
    key_of = jax.random.split(jax.random.key(seed), 18)
    return {
        "tokens": gaussian(key_of[0], (TOKENS, D), 1.0, 6.0, ((0, 32),)),
        "encoder": gaussian(key_of[1], (ENC_ROWS, D), 1.0, 6.0, ((0, 32),)),
        "seq_len": draw_seq_len(jax.random.fold_in(key_of[17], 71), 0),
        "enc_len": draw_enc_len(jax.random.fold_in(key_of[17], 71), 0),
        "d_mixed": gaussian(key_of[4], (TOKENS, D), 1.0, 6.0, ((0, 32),)),
        "self_qkv": gaussian(key_of[5], (D, 3 * D), D ** -0.5, 0.1875, ((0, 8),)),
        "self_out": gaussian(key_of[6], (D, D), (D // 16) ** -0.5, 0.75, ((0, 8),)),
        "cross_qkv": gaussian(key_of[7], (D, 3 * D), D ** -0.5, 0.1875, ((0, 8),)),
        "cross_out": gaussian(key_of[8], (D, D), (D // 16) ** -0.5, 0.75, ((0, 8),)),
        "fc1_weight": gaussian(key_of[9], (D, FF), D ** -0.5, 0.1875, ((0, 8),)),
        "fc2_weight": gaussian(key_of[10], (FF, D), FF ** -0.5, 0.09375, ((0, 8),)),
        "self_bias": gaussian(key_of[11], (3, D), 0.5, 3.0, (), jnp.float32),
        "cross_bias": gaussian(key_of[12], (3, D), 0.5, 3.0, (), jnp.float32),
        "norm_gain": jnp.clip(1.0 + 0.1 * jax.random.normal(key_of[13], (3, D), jnp.float32), 0.5, 1.5),
        "norm_bias": gaussian(key_of[14], (3, D), 0.3, 2.0, (), jnp.float32),
        "fc1_bias": gaussian(key_of[15], (FF,), 0.3, 2.0, (), jnp.float32),
        "fc2_bias": gaussian(key_of[16], (D,), 0.3, 2.0, (), jnp.float32),
    }


@jax.custom_vjp
def low(v):
    return lax.optimization_barrier(v.astype(jnp.bfloat16)).astype(jnp.float32)

@jax.custom_vjp
def low_back(v):
    return v

def low_keep(v):
    return (low(v), None)

def low_pass(kept, grad):
    return (grad,)

def back_keep(v):
    return (v, None)

def back_low(kept, grad):
    return (low(grad),)
low.defvjp(low_keep, low_pass)
low_back.defvjp(back_keep, back_low)

def both_round(values):
    return low_back(low(values))

def dense(left, right):
    return jnp.dot(left, right, precision=lax.Precision.HIGHEST)

def layer_norm(hidden, gain_row, shift_row):
    centre = hidden - lax.optimization_barrier(jnp.mean(hidden, -1, keepdims=True))
    spread = lax.optimization_barrier(jnp.mean(centre * centre, -1, keepdims=True))
    return centre * lax.rsqrt(spread + 1e-05) * gain_row + shift_row

def attention(query_all, key_all, value_all, allowed_fn):
    total_rows = query_all.shape[0]
    block_rows = math.gcd(total_rows, 512)
    key_heads = key_all.reshape(key_all.shape[0], HEADS, HEAD)
    value_heads = value_all.reshape(value_all.shape[0], HEADS, HEAD)

    def one_block(packed):
        query_block, first_row = packed
        scores = jnp.einsum('qhd,khd->hqk', query_block.reshape(block_rows, HEADS, HEAD), key_heads, precision=lax.Precision.HIGHEST)
        scores = low_back(scores)
        allowed = allowed_fn(first_row + jnp.arange(block_rows).astype(jnp.int32))
        scores = jnp.where(allowed[None], scores, -1e+30)
        highest = lax.optimization_barrier(jnp.max(scores, -1, keepdims=True))
        log_total = highest + jnp.log(lax.optimization_barrier(jnp.sum(jnp.exp(scores - highest), -1, keepdims=True)))
        weights_low = low(jnp.exp(scores - log_total))
        head_out = jnp.einsum('hqk,khd->qhd', weights_low, value_heads, precision=lax.Precision.HIGHEST)
        return head_out.reshape(block_rows, HEADS * HEAD)
    firsts = (jnp.arange(total_rows // block_rows) * block_rows).astype(jnp.int32)
    blocks = lax.map(jax.checkpoint(one_block), (query_all.reshape(-1, block_rows, HEADS * HEAD), firsts))
    return blocks.reshape(total_rows, HEADS * HEAD)

def reference(tokens, encoder, seq_len, enc_len, d_mixed, self_qkv, self_out, cross_qkv, cross_out, fc1_weight, fc2_weight, self_bias, cross_bias, norm_gain, norm_bias, fc1_bias, fc2_bias):
    key_index = jnp.arange(GROUP_TOK).astype(jnp.int32)
    enc_index = jnp.arange(ENC_GRP).astype(jnp.int32)

    def layer(x_all, e_all, w_sq, w_so, w_cq, w_co, w_up, w_down, s_bias, c_bias, n_gain, n_shift, up_bias, down_bias):
        results = []
        for group in range(GROUPS):
            x_rows = x_all[group * GROUP_TOK:(group + 1) * GROUP_TOK]
            e_rows = e_all[group * ENC_GRP:(group + 1) * ENC_GRP]
            joined = dense(x_rows, w_sq)
            query_s = both_round((joined[:, :D] + s_bias[0]) * 0.125)
            key_s = both_round(joined[:, D:2 * D])
            value_s = both_round(joined[:, 2 * D:] + s_bias[1])

            def causal(rows_at):
                return key_index[None, :] <= rows_at[:, None]
            attended = both_round(attention(query_s, key_s, value_s, causal))
            branch = low_back(dense(attended, w_so) + s_bias[2])
            first_norm = layer_norm(x_rows + branch, n_gain[0], n_shift[0])
            query_c = both_round((dense(low(first_norm), w_cq[:, :D]) + c_bias[0]) * 0.125)
            enc_proj = dense(e_rows, w_cq[:, D:])
            key_c = both_round(enc_proj[:, :D])
            value_c = both_round(enc_proj[:, D:] + c_bias[1])
            enc_limit = enc_len[group]

            def visible(rows_at, enc_limit=enc_limit):
                return jnp.broadcast_to((enc_index < enc_limit)[None, :], (rows_at.shape[0], ENC_GRP))
            cross_att = both_round(attention(query_c, key_c, value_c, visible))
            branch_c = low_back(dense(cross_att, w_co) + c_bias[2])
            second_norm = layer_norm(first_norm + branch_c, n_gain[1], n_shift[1])
            upward = low_back(dense(low(second_norm), w_up) + up_bias)
            activated = both_round(jax.nn.gelu(upward, approximate=False))
            branch_m = low_back(dense(activated, w_down) + down_bias)
            results.append(layer_norm(second_norm + branch_m, n_gain[2], n_shift[2]))
        return jnp.concatenate(results, 0)
    output, pull = jax.vjp(layer, tokens.astype(jnp.float32), encoder.astype(jnp.float32), self_qkv.astype(jnp.float32), self_out.astype(jnp.float32), cross_qkv.astype(jnp.float32), cross_out.astype(jnp.float32), fc1_weight.astype(jnp.float32), fc2_weight.astype(jnp.float32), self_bias, cross_bias, norm_gain, norm_bias, fc1_bias, fc2_bias)
    places = (jnp.arange(TOKENS) % GROUP_TOK).astype(jnp.int32)
    valid = (places < jnp.repeat(seq_len, GROUP_TOK)).astype(jnp.float32)
    g_tok, g_enc, g_sq, g_so, g_cq, g_co, g_up, g_down, g_sb, g_cb, g_gain, g_shift, g_upb, g_downb = pull(d_mixed.astype(jnp.float32) * valid[:, None])
    return (output.astype(jnp.bfloat16), g_tok, g_enc, g_sq, g_so, g_cq, g_co, g_up, g_down, g_sb, g_cb, g_gain, g_shift, g_upb, g_downb)
```

```python
from functools import partial

import jax
import jax.numpy as jnp
from jax import lax
from jax.experimental import pallas as pl
from jax.experimental.pallas import tpu as pltpu
from jax.sharding import PartitionSpec as P

HEADS = 16
HEAD = 64


def for_sending(array):
    return jax.tree.map(lambda a: a.astype(jnp.bfloat16) if a.dtype == jnp.float32 else a, array)


def layer_norm(hidden, gain_row, shift_row):
    centre = hidden - jnp.mean(hidden, -1, keepdims=True)
    spread = jnp.mean(centre * centre, -1, keepdims=True)
    return centre * lax.rsqrt(spread + 1e-05) * gain_row + shift_row


def exact_gelu(values):
    return jax.nn.gelu(values, approximate=False)


def contract_rows(left, right):
    return lax.dot_general(
        left, right, (((0,), (0,)), ((), ())), preferred_element_type=jnp.float32
    )


def back_dot(grad_rows, weight):
    return lax.dot_general(
        grad_rows, weight, (((1,), (1,)), ((), ())), preferred_element_type=jnp.float32
    )


def causal_mask(query_pos, key_pos):
    return key_pos[None, :] <= query_pos[:, None]


def enc_visible(query_pos, key_pos, enc_limit):
    return jnp.broadcast_to((key_pos < enc_limit)[None, :], (query_pos.shape[0], key_pos.shape[0]))


def only_live(step_fn, live_fn):

    def wrapped(totals, block_in, offset):
        return lax.cond(
            live_fn(block_in, offset), lambda: step_fn(totals, block_in, offset), lambda: totals
        )

    return wrapped


def self_fold(key_pair, step_fn, start_state, store):
    return step_fn(
        start_state,
        jax.tree.map(
            lambda a: lax.all_gather(a, "shard", axis=0, tiled=True), for_sending(key_pair)
        ),
        jnp.int32(0),
    )


def cross_fold(key_pair, step_fn, start_state, store):
    return step_fn(
        start_state,
        jax.tree.map(
            lambda a: lax.all_gather(a, "shard", axis=0, tiled=True), for_sending(key_pair)
        ),
        jnp.int32(0),
    )


def keys_live(query_pos, allowed_fn):

    def live_fn(block_in, offset):
        key_pos = jnp.arange(block_in[0].shape[0], dtype=jnp.int32)
        return jnp.any(allowed_fn(query_pos, key_pos))

    return live_fn


def head_scores(query_heads, query_pos, key_block, allowed_fn):
    key_count = key_block.shape[0]
    key_pos = jnp.arange(key_count, dtype=jnp.int32)
    scores = jnp.einsum(
        "qhd,khd->hqk",
        query_heads,
        key_block.reshape(key_count, HEADS, HEAD),
        preferred_element_type=jnp.float32,
    )
    return (scores, allowed_fn(query_pos, key_pos)[None])


def forward_pass(query_part, query_pos, key_pair, allowed_fn, folder):
    query_count = query_part.shape[0]
    query_heads = query_part.reshape(query_count, HEADS, HEAD)
    live_fn = keys_live(query_pos, allowed_fn)

    def stat_step(totals, block_in, offset):
        highest, mass = totals
        scores, allowed = head_scores(query_heads, query_pos, block_in[0], allowed_fn)
        masked = jnp.where(allowed, scores, -1e30)
        raised = jnp.maximum(highest, jnp.max(masked, -1))
        fresh = jnp.sum(jnp.where(allowed, jnp.exp(masked - raised[:, :, None]), 0.0), -1)
        return (raised, fresh)

    start_state = (
        jnp.full((HEADS, query_count), -1e30, jnp.float32),
        jnp.zeros((HEADS, query_count), jnp.float32),
    )
    highest, mass = folder(key_pair, only_live(stat_step, live_fn), start_state, None)
    log_total = highest + jnp.log(mass)

    def out_step(totals, block_in, offset):
        scores, allowed = head_scores(query_heads, query_pos, block_in[0], allowed_fn)
        weights_low = jnp.where(allowed, jnp.exp(scores - log_total[:, :, None]), 0.0).astype(
            jnp.bfloat16
        )
        value_heads = block_in[1].reshape(block_in[1].shape[0], HEADS, HEAD)
        return jnp.einsum(
            "hqk,khd->qhd", weights_low, value_heads, preferred_element_type=jnp.float32
        )

    summed = folder(
        key_pair,
        only_live(out_step, live_fn),
        jnp.zeros((query_count, HEADS, HEAD), jnp.float32),
        None,
    )
    return (log_total.T, summed)


def query_step(query_part, query_pos, allowed_fn, log_rows, delta_rows, d_out):
    query_count = query_part.shape[0]
    query_heads = query_part.reshape(query_count, HEADS, HEAD)
    grad_heads = d_out.reshape(query_count, HEADS, HEAD)
    log_total = log_rows.T
    correction = delta_rows.T

    def grad_step(totals, block_in, offset):
        key_block, value_block = block_in
        key_count = key_block.shape[0]
        scores, allowed = head_scores(query_heads, query_pos, key_block, allowed_fn)
        probs = jnp.where(allowed, jnp.exp(scores - log_total[:, :, None]), 0.0)
        d_probs = jnp.einsum(
            "qhd,khd->hqk",
            grad_heads,
            value_block.reshape(key_count, HEADS, HEAD),
            preferred_element_type=jnp.float32,
        )
        d_scores = (probs * (d_probs - correction[:, :, None])).astype(jnp.bfloat16)
        return jnp.einsum(
            "hqk,khd->qhd",
            d_scores,
            key_block.reshape(key_count, HEADS, HEAD),
            preferred_element_type=jnp.float32,
        )

    return only_live(grad_step, keys_live(query_pos, allowed_fn))


def query_grad(query_part, query_pos, key_pair, allowed_fn, folder, log_rows, delta_rows, d_out):
    query_count = query_part.shape[0]
    step_fn = query_step(query_part, query_pos, allowed_fn, log_rows, delta_rows, d_out)
    return folder(key_pair, step_fn, jnp.zeros((query_count, HEADS, HEAD), jnp.float32), None)


def key_step(own_keys, own_values, key_pos, allowed_fn, log_all, delta_all):
    key_count = own_keys.shape[0]
    key_heads = own_keys.reshape(key_count, HEADS, HEAD)
    value_heads = own_values.reshape(key_count, HEADS, HEAD)

    def step_fn(totals, block_in, offset):
        query_block, grad_block = block_in
        query_count = query_block.shape[0]
        query_pos = jnp.arange(query_count, dtype=jnp.int32)
        log_part = log_all.T
        delta_part = delta_all.T
        query_heads = query_block.reshape(query_count, HEADS, HEAD)
        grad_heads = grad_block.reshape(query_count, HEADS, HEAD)
        scores = jnp.einsum(
            "qhd,khd->hqk", query_heads, key_heads, preferred_element_type=jnp.float32
        )
        allowed = allowed_fn(query_pos, key_pos)[None]
        probs = jnp.where(allowed, jnp.exp(scores - log_part[:, :, None]), 0.0)
        d_values = jnp.einsum(
            "hqk,qhd->khd",
            probs.astype(jnp.bfloat16),
            grad_heads,
            preferred_element_type=jnp.float32,
        )
        d_probs = jnp.einsum(
            "qhd,khd->hqk", grad_heads, value_heads, preferred_element_type=jnp.float32
        )
        d_scores = (probs * (d_probs - delta_part[:, :, None])).astype(jnp.bfloat16)
        d_keys = jnp.einsum(
            "hqk,qhd->khd", d_scores, query_heads, preferred_element_type=jnp.float32
        )
        return (d_keys, d_values)

    def live_fn(block_in, offset):
        query_pos = jnp.arange(block_in[0].shape[0], dtype=jnp.int32)
        return jnp.any(allowed_fn(query_pos, key_pos))

    return only_live(step_fn, live_fn)


def column_sum(values):
    return jnp.sum(values.astype(jnp.float32), 0)


def local(
    tokens,
    encoder,
    seq_len,
    enc_len,
    d_mixed,
    self_qkv,
    self_out,
    cross_qkv,
    cross_out,
    fc1_weight,
    fc2_weight,
    self_bias,
    cross_bias,
    norm_gain,
    norm_bias,
    fc1_bias,
    fc2_bias,
):
    model_width = tokens.shape[1]
    tok_rows = tokens.shape[0]
    enc_rows = encoder.shape[0]
    device_at = lax.axis_index("shard")
    positions = device_at * tok_rows + jnp.arange(tok_rows, dtype=jnp.int32)
    enc_positions = device_at * enc_rows + jnp.arange(enc_rows, dtype=jnp.int32)
    seq_limit = seq_len[0]
    visible = partial(enc_visible, enc_limit=enc_len[0])
    w_sq, w_so = (
        lax.all_gather(self_qkv, "shard", axis=0, tiled=True),
        lax.all_gather(self_out, "shard", axis=0, tiled=True),
    )
    joined = jnp.dot(tokens, w_sq, preferred_element_type=jnp.float32)
    query_s = ((joined[:, :model_width] + self_bias[0]) * 0.125).astype(jnp.bfloat16)
    key_s = joined[:, model_width : 2 * model_width].astype(jnp.bfloat16)
    value_s = (joined[:, 2 * model_width :] + self_bias[1]).astype(jnp.bfloat16)
    self_lse, self_summed = forward_pass(
        query_s, positions, (key_s, value_s), causal_mask, self_fold
    )
    attended = self_summed.reshape(tok_rows, model_width).astype(jnp.bfloat16)
    branch = jnp.dot(attended, w_so, preferred_element_type=jnp.float32) + self_bias[2]
    first_norm, first_pull = jax.vjp(
        layer_norm, tokens.astype(jnp.float32) + branch, norm_gain[0], norm_bias[0]
    )
    w_cq, w_co = (
        lax.all_gather(cross_qkv, "shard", axis=0, tiled=True),
        lax.all_gather(cross_out, "shard", axis=0, tiled=True),
    )
    first_low = first_norm.astype(jnp.bfloat16)
    query_c = (
        (
            jnp.dot(first_low, w_cq[:, :model_width], preferred_element_type=jnp.float32)
            + cross_bias[0]
        )
        * 0.125
    ).astype(jnp.bfloat16)
    enc_proj = jnp.dot(encoder, w_cq[:, model_width:], preferred_element_type=jnp.float32)
    key_c = enc_proj[:, :model_width].astype(jnp.bfloat16)
    value_c = (enc_proj[:, model_width:] + cross_bias[1]).astype(jnp.bfloat16)
    cross_lse, cross_summed = forward_pass(
        query_c, positions, (key_c, value_c), visible, cross_fold
    )
    cross_att = cross_summed.reshape(tok_rows, model_width).astype(jnp.bfloat16)
    branch_c = jnp.dot(cross_att, w_co, preferred_element_type=jnp.float32) + cross_bias[2]
    second_norm, second_pull = jax.vjp(
        layer_norm, first_norm + branch_c, norm_gain[1], norm_bias[1]
    )
    w_up, w_down = (
        lax.all_gather(fc1_weight, "shard", axis=0, tiled=True),
        lax.all_gather(fc2_weight, "shard", axis=0, tiled=True),
    )
    second_low = second_norm.astype(jnp.bfloat16)
    upward = jnp.dot(second_low, w_up, preferred_element_type=jnp.float32) + fc1_bias
    activated, gelu_pull = jax.vjp(exact_gelu, upward)
    act_low = activated.astype(jnp.bfloat16)
    branch_m = jnp.dot(act_low, w_down, preferred_element_type=jnp.float32) + fc2_bias
    output, third_pull = jax.vjp(layer_norm, second_norm + branch_m, norm_gain[2], norm_bias[2])
    valid = (positions < seq_limit).astype(jnp.float32)[:, None]
    d_third, d_gain3, d_shift3 = third_pull(d_mixed.astype(jnp.float32) * valid)
    d_branch_m = d_third.astype(jnp.bfloat16)
    g_down = contract_rows(act_low, d_branch_m)
    d_act = back_dot(d_branch_m, w_down).astype(jnp.bfloat16)
    (d_up,) = gelu_pull(d_act.astype(jnp.float32))
    d_up_low = d_up.astype(jnp.bfloat16)
    g_up = contract_rows(second_low, d_up_low)
    d_second = d_third + back_dot(d_up_low, w_up)
    d_hidden2, d_gain2, d_shift2 = second_pull(d_second)
    d_branch_c = d_hidden2.astype(jnp.bfloat16)
    g_co = contract_rows(cross_att, d_branch_c)
    d_cross_att = back_dot(d_branch_c, w_co).astype(jnp.bfloat16)
    cross_delta = jnp.einsum(
        "qhd,qhd->qh", d_cross_att.reshape(tok_rows, HEADS, HEAD).astype(jnp.float32), cross_summed
    )
    d_query_c = query_grad(
        query_c,
        positions,
        (key_c, value_c),
        visible,
        cross_fold,
        cross_lse,
        cross_delta,
        d_cross_att,
    )
    d_query_cs = d_query_c.reshape(tok_rows, model_width).astype(jnp.bfloat16) * 0.125
    d_first = d_hidden2 + back_dot(d_query_cs, w_cq[:, :model_width])
    d_hidden1, d_gain1, d_shift1 = first_pull(d_first)
    d_branch = d_hidden1.astype(jnp.bfloat16)
    g_so = contract_rows(attended, d_branch)
    d_attended = back_dot(d_branch, w_so).astype(jnp.bfloat16)
    self_delta = jnp.einsum(
        "qhd,qhd->qh", d_attended.reshape(tok_rows, HEADS, HEAD).astype(jnp.float32), self_summed
    )
    stats = (
        lax.all_gather(self_lse, "shard", axis=0, tiled=True),
        lax.all_gather(self_delta, "shard", axis=0, tiled=True),
        lax.all_gather(cross_lse, "shard", axis=0, tiled=True),
        lax.all_gather(cross_delta, "shard", axis=0, tiled=True),
    )
    tok_zero = jnp.zeros((tok_rows, HEADS, HEAD), jnp.float32)
    query_side = query_step(query_s, positions, causal_mask, self_lse, self_delta, d_attended)
    key_side = key_step(key_s, value_s, positions, causal_mask, stats[0], stats[1])
    offset = jnp.int32(0)
    d_query_part = query_side(
        tok_zero,
        (
            lax.all_gather(key_s, "shard", axis=0, tiled=True),
            lax.all_gather(value_s, "shard", axis=0, tiled=True),
        ),
        offset,
    )
    d_key_part, d_value_part = key_side(
        (tok_zero, tok_zero),
        (
            lax.all_gather(query_s, "shard", axis=0, tiled=True),
            lax.all_gather(d_attended, "shard", axis=0, tiled=True),
        ),
        offset,
    )
    enc_zero = jnp.zeros((enc_rows, HEADS, HEAD), jnp.float32)
    d_key_c, d_value_c = key_step(key_c, value_c, enc_positions, visible, stats[2], stats[3])(
        (enc_zero, enc_zero),
        (
            lax.all_gather(query_c, "shard", axis=0, tiled=True),
            lax.all_gather(d_cross_att, "shard", axis=0, tiled=True),
        ),
        jnp.int32(0),
    )
    d_qs = d_query_part.reshape(tok_rows, model_width).astype(jnp.bfloat16) * 0.125
    d_ks = d_key_part.reshape(tok_rows, model_width).astype(jnp.bfloat16)
    d_vs = d_value_part.reshape(tok_rows, model_width).astype(jnp.bfloat16)
    d_joined = jnp.concatenate([d_qs, d_ks, d_vs], 1)
    g_sq = contract_rows(tokens, d_joined)
    d_tokens = d_hidden1 + back_dot(d_joined, w_sq)
    d_kc = d_key_c.reshape(enc_rows, model_width).astype(jnp.bfloat16)
    d_vc = d_value_c.reshape(enc_rows, model_width).astype(jnp.bfloat16)
    d_enc_proj = jnp.concatenate([d_kc, d_vc], 1)
    g_cq = jnp.concatenate(
        [contract_rows(first_low, d_query_cs), contract_rows(encoder, d_enc_proj)], 1
    )
    d_encoder = back_dot(d_enc_proj, w_cq[:, model_width:])
    d_self_bias = jnp.stack([column_sum(d_qs), column_sum(d_vs), column_sum(d_branch)])
    d_cross_bias = jnp.stack([column_sum(d_query_cs), column_sum(d_vc), column_sum(d_branch_c)])
    d_norm_gain = jnp.stack([d_gain1, d_gain2, d_gain3])
    d_norm_bias = jnp.stack([d_shift1, d_shift2, d_shift3])
    d_fc1_bias = column_sum(d_up_low)
    d_fc2_bias = column_sum(d_branch_m)
    row_grads = (
        lax.psum_scatter(g_sq, "shard", scatter_dimension=0, tiled=True),
        lax.psum_scatter(g_so, "shard", scatter_dimension=0, tiled=True),
        lax.psum_scatter(g_cq, "shard", scatter_dimension=0, tiled=True),
        lax.psum_scatter(g_co, "shard", scatter_dimension=0, tiled=True),
        lax.psum_scatter(g_up, "shard", scatter_dimension=0, tiled=True),
        lax.psum_scatter(g_down, "shard", scatter_dimension=0, tiled=True),
    )
    row_grads = lax.psum(
        (row_grads[0], row_grads[1], row_grads[2], row_grads[3], row_grads[4], row_grads[5]), "rep"
    )
    small_sums = lax.psum(
        (d_self_bias, d_cross_bias, d_norm_gain, d_norm_bias, d_fc1_bias, d_fc2_bias),
        ("rep", "shard"),
    )
    return (
        output.astype(jnp.bfloat16),
        d_tokens,
        d_encoder,
        row_grads[0],
        row_grads[1],
        row_grads[2],
        row_grads[3],
        row_grads[4],
        row_grads[5],
        small_sums[0],
        small_sums[1],
        small_sums[2],
        small_sums[3],
        small_sums[4],
        small_sums[5],
    )


MESH = pl.DeviceIdType.MESH
BF = jnp.bfloat16
F32 = jnp.float32
EPS = 1e-05


def dg(left, right, cl, cr):
    return lax.dot_general(
        left, right, (((cl,), (cr,)), ((), ())), preferred_element_type=F32
    )


class Names:
    pass


WIDTH = 1024
HIDDEN = 4096
ROWS = 128
ENC = 64
HALF = 64

SCRATCH = {
    "X": ((4, ROWS, WIDTH), BF),
    "E": ((4, ENC, WIDTH), BF),
    "DMX": ((ROWS, WIDTH), BF),
    "LSRC": ((8, 128), F32),
    "LENS": ((8, 128), F32),
    "WQKV": ((8, 128, 768), BF),
    "WSO": ((2, 128, WIDTH), BF),
    "WCQ": ((8, 128, 768), BF),
    "WCO": ((2, 128, WIDTH), BF),
    "WUP": ((8, 128, 1024), BF),
    "WDN": ((2, 512, WIDTH), BF),
    "QST": ((2, 3, 4, ROWS, 128), BF),
    "QKV": ((3, 8, ROWS, 128), BF),
    "P0": ((2, 256, 256), BF),
    "P1": ((2, 256, 512), BF),
    "P2": ((2, 256, 768), BF),
    "P3": ((2, 256, 1024), BF),
    "O": ((1024, 128), F32),
    "ATF": ((8, ROWS, 128), BF),
    "ATT": ((4, ROWS, 256), BF),
    "PB": ((4, ROWS, WIDTH), BF),
    "RB": ((3, ROWS, WIDTH), BF),
    "PBE": ((4, ENC, WIDTH), BF),
    "RBE": ((3, ENC, WIDTH), BF),
    "F": ((4, ROWS, WIDTH), BF),
    "S": ((4, ROWS, WIDTH), BF),
    "DM": ((4, ROWS, WIDTH), BF),
    "DC": ((4, ROWS, WIDTH), BF),
    "RES": ((ROWS, WIDTH), F32),
    "RES2": ((ROWS, WIDTH), F32),
    "XH": ((2, ROWS, WIDTH), F32),
    "RSTD": ((2, ROWS, 1), F32),
    "QC": ((4, ROWS, 256), BF),
    "KVC": ((8, ENC, 512), BF),
    "PC": ((4, 2, 256, 512), BF),
    "OC": ((2, 256, 256), F32),
    "CATT": ((4, ROWS, 256), BF),
    "ACT": ((4, ROWS, 1024), BF),
    "DGL": ((2, 256, 1024), BF),
    "DUP": ((4, ROWS, 1024), BF),
    "DQC": ((4, ROWS, 256), BF),
    "DKV": ((512, 512), F32),
    "DKS": ((4, ENC, 512), BF),
    "DKR": ((4, ENC, 512), BF),
    "DKL": ((4, ENC, 512), BF),
    "DATS": ((4, ROWS, 128), BF),
    "DO": ((8, ROWS, 128), BF),
    "DKVS": ((2, 1024, 128), F32),
    "DJN": ((3, 8, ROWS, 128), BF),
    "DJ": ((4, ROWS, 768), BF),
    "MXS": ((ROWS, WIDTH), BF),
    "DTS": ((ROWS, WIDTH), BF),
    "DES": ((ENC, WIDTH), BF),
    "SM": ((24, WIDTH), F32),
    "SMR": ((5, 24, WIDTH), F32),
}
for _name, _rows in (("SO", 128), ("CO", 128), ("DN", 512)):
    SCRATCH["GS_" + _name] = ((_rows, WIDTH), BF)
    SCRATCH["GR_" + _name] = ((_rows, WIDTH), BF)
    SCRATCH["GK_" + _name] = ((_rows, WIDTH), BF)
    SCRATCH["XS_" + _name] = ((_rows // 2, WIDTH), BF)
    SCRATCH["XR_" + _name] = ((_rows // 2, WIDTH), BF)
    SCRATCH["HS_" + _name] = ((_rows // 2, WIDTH), BF)
    SCRATCH["HR_" + _name] = ((_rows // 2, WIDTH), BF)
    SCRATCH["T_" + _name] = ((_rows, WIDTH), BF)
for _name, _cols in (("QKV", 384), ("CQ", 384), ("UP", 512)):
    SCRATCH["GS_" + _name] = ((8, 128, _cols), BF)
    SCRATCH["GR_" + _name] = ((8, 128, _cols), BF)
    SCRATCH["GK_" + _name] = ((8, 128, _cols), BF)
    SCRATCH["XS_" + _name] = ((8, HALF, _cols), BF)
    SCRATCH["XR_" + _name] = ((8, HALF, _cols), BF)
    SCRATCH["HS_" + _name] = ((4, HALF, _cols), BF)
    SCRATCH["HR_" + _name] = ((4, HALF, _cols), BF)
    SCRATCH["TS_" + _name] = ((4, HALF, _cols), BF)
    SCRATCH["T_" + _name] = ((8, 128, _cols), BF)

IN_NAMES = (
    "tokens", "encoder", "seq", "enc", "dmix", "w_sq", "w_so", "w_cq", "w_co", "w_up", "w_dn",
    "sb", "cb", "gain", "shift", "fb1", "fb2",
)
OUT_NAMES = (
    "o_mixed", "o_dtok", "o_denc", "o_sq", "o_so", "o_cq", "o_co", "o_up", "o_dn", "o_small",
)
VMEM_BYTES = 64 * 2**20 - 2**19
N_REMOTE = 400
N_LOCAL = 128


def layer_kernel(*refs):
    n_in, n_out = len(IN_NAMES), len(OUT_NAMES)
    r = Names()
    names = IN_NAMES + OUT_NAMES + tuple(SCRATCH)
    for name, ref in zip(names, refs):
        setattr(r, name, ref)
    send_sem, recv_sem, local_sem = refs[len(names) :]
    count = {"remote": 0, "local": 0}

    rep, shard = lax.axis_index("rep"), lax.axis_index("shard")
    x, c = rep // 2, rep % 2
    z, y = shard // 2, shard % 2
    h, l = z // 2, z % 2
    own = 2 * l + y
    t = 4 * c + own
    s_own = 4 * h + own

    def dev(xx, hh, ll, yy, cc):
        return (xx * 2 + cc, (2 * hh + ll) * 2 + yy)

    mate = dev(x, h, l, y, 1 - c)
    x_peer = dev(1 - x, h, l, y, c)
    h_peer = dev(x, 1 - h, l, y, c)
    swap_peer = dev(x, 1 - h, l, y, 1 - c)

    def peer_lc(j):
        return (l + j // 2) % 2, (y + j % 2) % 2

    def peer(j):
        ll, yy = peer_lc(j)
        return dev(x, h, ll, yy, c)

    def peer_block(j):
        ll, yy = peer_lc(j)
        return 2 * ll + yy

    def remote(src, dst, device):
        i = count["remote"]
        count["remote"] += 1
        return pltpu.make_async_remote_copy(
            src_ref=src,
            dst_ref=dst,
            send_sem=send_sem.at[i],
            recv_sem=recv_sem.at[i],
            device_id=device,
            device_id_type=MESH,
        )

    def local(src, dst):
        i = count["local"]
        count["local"] += 1
        return pltpu.make_async_copy(src, dst, local_sem.at[i])

    barrier = pltpu.get_barrier_semaphore()
    greet = [mate, x_peer, swap_peer]
    for m in range(1, 8):
        greet.append(dev(x, (h + m // 4) % 2, (l + (m // 2) % 2) % 2, (y + m % 2) % 2, c))
    for device in greet:
        pl.semaphore_signal(barrier, inc=1, device_id=device, device_id_type=MESH)
    r.LSRC[0:1, :] = jnp.full((1, 128), r.seq[0].astype(F32))
    r.LSRC[1:2, :] = jnp.full((1, 128), r.enc[0].astype(F32))
    r.SM[...] = jnp.zeros_like(r.SM)
    pl.semaphore_wait(barrier, len(greet))

    moved = [
        (r.tokens, r.X.at[own]),
        (r.encoder, r.E.at[own]),
        (r.LSRC, r.LENS),
        (r.dmix, r.DMX),
    ]
    swaps = [(remote(s, d, swap_peer), local(s, d)) for s, d in moved]
    stays = c == h

    def swap_start(i):
        @pl.when(stays)
        def _():
            swaps[i][1].start()

        @pl.when(jnp.logical_not(stays))
        def _():
            swaps[i][0].start()

    def swap_wait(i):
        @pl.when(stays)
        def _():
            swaps[i][1].wait()

        @pl.when(jnp.logical_not(stays))
        def _():
            swaps[i][0].wait()

    def column_sends(w_hbm, dst, parts, width):
        out = []
        for m in range(8):
            hh, ll, yy = (h + m // 4) % 2, (l + (m // 2) % 2) % 2, (y + m % 2) % 2
            tt = 4 * c + 2 * ll + yy
            for p in range(parts):
                col = pl.multiple_of(p * WIDTH + tt * width, 128)
                src = w_hbm.at[:, pl.ds(col, width)]
                at = dst.at[s_own, :, pl.ds(pl.multiple_of(p * 2 * width + c * width, 128), width)]
                if m == 0:
                    out.append(local(src, at))
                else:
                    out.append(remote(src, at, dev(x, hh, ll, yy, c)))
        return out

    def mate_sends(dst, parts, width):
        out = []
        for p in range(parts):
            at = dst.at[:, :, pl.ds(pl.multiple_of(p * 2 * width + c * width, 128), width)]
            out.append(remote(at, at, mate))
        return out

    def row_sends(w_hbm, dst, rows):
        k = rows // 2
        first = pl.ds(pl.multiple_of(c * k, 32), k)
        return [
            local(w_hbm, dst.at[h]),
            remote(w_hbm.at[first], dst.at[h, first], h_peer),
        ], remote(dst.at[1 - h, first], dst.at[1 - h, first], mate)

    def leave(src, out):
        cp = remote(src, out, swap_peer)

        @pl.when(stays)
        def _():
            out[...] = src[...]

        @pl.when(jnp.logical_not(stays))
        def _():
            cp.start()

        return cp

    def start(copies):
        for cp in copies:
            cp.start()

    def wait(copies):
        for cp in copies:
            cp.wait()

    def gather(buf, rows):
        return [remote(buf.at[own, rows], buf.at[own, rows], peer(j)) for j in (1, 2, 3)]

    swap_start(0)
    sq = column_sends(r.w_sq, r.WQKV, 3, 128)
    start(sq)
    swap_start(1)
    swap_start(2)
    swap_start(3)
    swap_wait(0)
    all_rows = pl.ds(0, ROWS)
    ag_x = gather(r.X, all_rows)
    start(ag_x)
    swap_wait(1)
    ag_e = gather(r.E, pl.ds(0, ENC))
    start(ag_e)
    so, so_mate = row_sends(r.w_so, r.WSO, 128)
    cq = column_sends(r.w_cq, r.WCQ, 3, 128)
    co, co_mate = row_sends(r.w_co, r.WCO, 128)
    up = column_sends(r.w_up, r.WUP, 1, 512)
    dn, dn_mate = row_sends(r.w_dn, r.WDN, 512)
    for group in (so, cq, co, up, dn):
        start(group)
    swap_wait(2)
    swap_wait(3)
    wait(sq)
    sq_mate = mate_sends(r.WQKV, 3, 128)
    start(sq_mate)
    wait(ag_x)

    lane = lax.broadcasted_iota(jnp.int32, (1, 128), 1)
    heads = [lane // 64 == 0, lane // 64 == 1]

    def head_of(v, hh):
        return jnp.where(heads[hh], v, jnp.zeros_like(v))

    def own_cols(ref, row, width):
        off = [pl.multiple_of((4 * k + own) * width, 128) for k in range(2)]
        return jnp.concatenate([ref[row : row + 1, pl.ds(o, width)] for o in off], 1)

    def blocks(ref, a, width):
        return ref[:, a * HALF : (a + 1) * HALF, :].reshape(4 * HALF, width)

    def shards(ref, rows, cols):
        return ref[rows.start // 128 : rows.stop // 128, :, cols].reshape(rows.stop - rows.start, -1)

    def add_small(row, col, width, value):
        at = slice(0, width) if isinstance(col, int) else pl.ds(pl.multiple_of(col, 128), width)
        r.SM[row : row + 1, at] += value

    def colsum(v):
        return jnp.sum(v, 0, keepdims=True)

    wait(sq_mate)
    bias_q = own_cols(r.sb, 0, 128)
    bias_v = own_cols(r.sb, 1, 128)
    for i in range(2):
        lhs = r.X[2 * i : 2 * i + 2].reshape(256, WIDTH)
        for p in range(3):
            out = dg(lhs, r.WQKV[:, :, p * 256 : (p + 1) * 256].reshape(WIDTH, 256), 1, 0)
            if p == 0:
                out = (out + bias_q) * 0.125
            if p == 2:
                out = out + bias_v
            out = out.astype(BF)
            for k in range(2):
                r.QST[k, p, 2 * i : 2 * i + 2] = out[:, k * 128 : (k + 1) * 128].reshape(2, ROWS, 128)
    mine = pl.ds(4 * c, 4)
    theirs = pl.ds(4 * (1 - c), 4)
    qkv_x = [remote(r.QST.at[1 - c], r.QKV.at[:, mine], mate)]
    start(qkv_x)
    r.QKV[:, mine] = r.QST[c]

    wait(ag_e)
    wait(cq)
    cq_mate = mate_sends(r.WCQ, 3, 128)
    start(cq_mate)
    wait(so)
    so_mate.start()
    wait(qkv_x)

    def keys(p, n):
        return r.QKV[p, 0 : n // ROWS].reshape(n, 128)

    probs = [r.P0, r.P1, r.P2, r.P3]
    for i in range(4):
        n = (i + 1) * 256
        q = r.QKV[0, 2 * i : 2 * i + 2].reshape(256, 128)
        outs = []
        for hh in range(2):
            s = dg(head_of(q, hh), keys(1, n), 1, 1)
            qpos = lax.broadcasted_iota(jnp.int32, (256, n), 0) + i * 256
            kpos = lax.broadcasted_iota(jnp.int32, (256, n), 1)
            s = jnp.where(kpos <= qpos, s, -1e30)
            e = jnp.exp(s - jnp.max(s, 1, keepdims=True))
            p = (e * (1.0 / jnp.sum(e, 1, keepdims=True))).astype(BF)
            probs[i][hh] = p
            outs.append(dg(p, keys(2, n), 1, 0))
        o = jnp.where(heads[0], outs[0], outs[1])
        r.O[i * 256 : (i + 1) * 256] = o
        r.ATF[2 * i : 2 * i + 2] = o.astype(BF).reshape(2, ROWS, 128)
    my_cols = pl.ds(pl.multiple_of(c * 128, 128), 128)
    att_x = remote(r.ATF.at[theirs], r.ATT.at[:, :, my_cols], mate)
    att_x.start()
    r.ATT[:, :, my_cols] = r.ATF[mine]

    wait(cq_mate)
    bias_cv = own_cols(r.cb, 1, 128)
    for k in range(2):
        out = dg(
            r.E[...].reshape(4 * ENC, WIDTH),
            r.WCQ[:, :, 256 + k * 256 : 512 + k * 256].reshape(WIDTH, 256),
            1,
            0,
        )
        if k == 1:
            out = out + bias_cv
        r.KVC[mine, :, k * 256 : (k + 1) * 256] = out.astype(BF).reshape(4, ENC, 256)
    kvc_x = remote(r.KVC.at[mine], r.KVC.at[mine], mate)
    kvc_x.start()
    so_mate.wait()
    att_x.wait()

    def scatter(a):
        rows = pl.ds(a * HALF, HALF)
        return [remote(r.PB.at[peer_block(j), rows], r.RB.at[j - 1, rows], peer(j)) for j in (1, 2, 3)]

    def summed(a):
        rows = slice(a * HALF, (a + 1) * HALF)
        total = r.PB[own, rows].astype(F32)
        for j in range(3):
            total = total + r.RB[j, rows].astype(F32)
        return total

    def partial(a, lhs, w, contract, chunk=512):
        for n in range(WIDTH // chunk):
            cols = slice(n * chunk, (n + 1) * chunk)
            out = dg(lhs, w(cols), 1, contract)
            r.PB[:, a * HALF : (a + 1) * HALF, cols] = out.astype(BF).reshape(4, HALF, chunk)
        sends = scatter(a)
        start(sends)
        return sends

    def norm(i, rows, hidden):
        centre = hidden - jnp.mean(hidden, -1, keepdims=True)
        rstd = lax.rsqrt(jnp.mean(centre * centre, -1, keepdims=True) + EPS)
        xhat = centre * rstd
        return xhat, rstd, xhat * r.gain[i : i + 1, :] + r.shift[i : i + 1, :]

    def norm_back(i, dy, xhat, rstd):
        add_small(6 + i, 0, WIDTH, colsum(dy * xhat))
        add_small(9 + i, 0, WIDTH, colsum(dy))
        d = dy * r.gain[i : i + 1, :]
        mean_d = jnp.mean(d, -1, keepdims=True)
        mean_dx = jnp.mean(d * xhat, -1, keepdims=True)
        return rstd * (d - mean_d - xhat * mean_dx)

    def half(a):
        return slice(a * HALF, (a + 1) * HALF)

    rs = [
        partial(a, blocks(r.ATT, a, 256), lambda cols: r.WSO[:, :, cols].reshape(256, -1), 0)
        for a in range(2)
    ]
    ag = []
    for a in range(2):
        wait(rs[a])
        hidden = r.X[own, half(a)].astype(F32) + summed(a) + r.sb[2:3, :]
        xhat, rstd, out = norm(0, half(a), hidden)
        r.XH[0, half(a)] = xhat
        r.RSTD[0, half(a)] = rstd
        r.RES[half(a)] = out
        r.F[own, half(a)] = out.astype(BF)
        g = gather(r.F, pl.ds(a * HALF, HALF))
        start(g)
        ag.append(g)

    wait(co)
    co_mate.start()
    wait(up)
    up_mate = mate_sends(r.WUP, 1, 512)
    start(up_mate)
    wait(dn)
    dn_mate.start()
    kvc_x.wait()
    co_mate.wait()
    bias_cq = own_cols(r.cb, 0, 128)
    limit = r.LENS[1:2, 0:1]
    visible = lax.broadcasted_iota(jnp.int32, (1, 512), 1).astype(F32) < limit

    def enc_keys(part, k):
        return r.KVC[:, :, part * 256 + k * 128 : part * 256 + (k + 1) * 128].reshape(512, 128)

    rs = []
    for a in range(2):
        wait(ag[a])
        q = dg(blocks(r.F, a, WIDTH), r.WCQ[:, :, 0:256].reshape(WIDTH, 256), 1, 0)
        q = ((q + bias_cq) * 0.125).astype(BF)
        r.QC[:, half(a)] = q.reshape(4, HALF, 256)
        for k in range(2):
            outs = []
            for hh in range(2):
                s = dg(head_of(q[:, k * 128 : (k + 1) * 128], hh), enc_keys(0, k), 1, 1)
                s = jnp.where(visible, s, -1e30)
                e = jnp.exp(s - jnp.max(s, 1, keepdims=True))
                p = (e * (1.0 / jnp.sum(e, 1, keepdims=True))).astype(BF)
                r.PC[2 * k + hh, a] = p
                outs.append(dg(p, enc_keys(1, k), 1, 0))
            o = jnp.where(heads[0], outs[0], outs[1])
            r.OC[a, :, k * 128 : (k + 1) * 128] = o
            r.CATT[:, half(a), k * 128 : (k + 1) * 128] = o.astype(BF).reshape(4, HALF, 128)
        rs.append(
            partial(a, blocks(r.CATT, a, 256), lambda cols: r.WCO[:, :, cols].reshape(256, -1), 0)
        )
    ag = []
    for a in range(2):
        wait(rs[a])
        hidden = r.RES[half(a)] + summed(a) + r.cb[2:3, :]
        xhat, rstd, out = norm(1, half(a), hidden)
        r.XH[1, half(a)] = xhat
        r.RSTD[1, half(a)] = rstd
        r.RES2[half(a)] = out
        r.S[own, half(a)] = out.astype(BF)
        g = gather(r.S, pl.ds(a * HALF, HALF))
        start(g)
        ag.append(g)

    wait(up_mate)
    dn_mate.wait()
    bias_up = [r.fb1[0:1, pl.ds(pl.multiple_of((4 * k + own) * 512, 128), 512)] for k in range(2)]
    rs = []
    for a in range(2):
        wait(ag[a])
        lhs = blocks(r.S, a, WIDTH)
        for k in range(2):
            cols = slice(k * 512, (k + 1) * 512)
            u = dg(lhs, r.WUP[:, :, cols].reshape(WIDTH, 512), 1, 0) + bias_up[k]
            cdf = 0.5 + 0.5 * lax.erf(u * 0.7071067811865476)
            r.ACT[:, half(a), cols] = (u * cdf).astype(BF).reshape(4, HALF, 512)
            slope = cdf + u * (jnp.exp(-0.5 * u * u) * 0.3989422804014327)
            r.DGL[a, :, cols] = slope.astype(BF)
        rs.append(
            partial(a, blocks(r.ACT, a, 1024), lambda cols: r.WDN[:, :, cols].reshape(1024, -1), 0)
        )
    ag = []
    seq_limit = r.LENS[0:1, 0:1]
    for a in range(2):
        wait(rs[a])
        hidden = r.RES2[half(a)] + summed(a) + r.fb2[0:1, :]
        xhat, rstd, out = norm(2, half(a), hidden)
        r.MXS[half(a)] = out.astype(BF)
        place = lax.broadcasted_iota(jnp.int32, (HALF, 1), 0) + (t * ROWS + a * HALF)
        dy = jnp.where(place.astype(F32) < seq_limit, r.DMX[half(a)].astype(F32), 0.0)
        d = norm_back(2, dy, xhat, rstd)
        r.RES[half(a)] = d
        low = d.astype(BF)
        r.DM[own, half(a)] = low
        add_small(16, 0, WIDTH, colsum(low.astype(F32)))
        g = gather(r.DM, pl.ds(a * HALF, HALF))
        start(g)
        ag.append(g)

    mx_out = leave(r.MXS, r.o_mixed)

    def both(v):
        return v.reshape(-1, v.shape[-1])

    class ColumnGrad:
        def __init__(self, name, out, parts):
            self.parts, self.out = parts, out
            for key in ("GS", "GR", "GK", "XS", "XR", "HS", "HR", "TS", "T"):
                setattr(self, key, getattr(r, key + "_" + name))

        def compute(self, left, right, col, width):
            for target, k in ((self.GS, 1 - c), (self.GK, c)):
                rhs = right(k)
                for i in range(4):
                    out = dg(left(slice(i * 256, (i + 1) * 256)), rhs, 0, 0)
                    target[2 * i : 2 * i + 2, :, col : col + width] = out.astype(BF).reshape(2, 128, width)

        def s0(self):
            self.core = remote(self.GS, self.GR, mate)
            self.core.start()

        def s1(self):
            self.core.wait()
            theirs_x = pl.ds(pl.multiple_of((1 - x) * HALF, HALF), HALF)
            self.XS[...] = (self.GK[:, theirs_x].astype(F32) + self.GR[:, theirs_x].astype(F32)).astype(BF)
            self.xc = remote(self.XS, self.XR, x_peer)
            self.xc.start()

        def total(self, shards):
            mine_x = pl.ds(pl.multiple_of(x * HALF, HALF), HALF)
            return (
                self.GK[shards, mine_x].astype(F32)
                + self.GR[shards, mine_x].astype(F32)
                + self.XR[shards].astype(F32)
            )

        def s2(self):
            self.xc.wait()
            self.HS[...] = self.total(pl.ds(4 * (1 - h), 4)).astype(BF)
            self.hc = remote(self.HS, self.HR, h_peer)
            self.hc.start()

        def s3(self):
            self.hc.wait()
            mine_x = pl.ds(pl.multiple_of(x * HALF, HALF), HALF)
            self.TS[...] = (self.total(pl.ds(4 * h, 4)) + self.HR[...].astype(F32)).astype(BF)
            self.lc = [
                remote(self.TS.at[peer_block(j)], self.T.at[t, mine_x], peer(j)) for j in (1, 2, 3)
            ]
            start(self.lc)
            self.T[t, mine_x] = self.TS[own]

        def s4(self):
            wait(self.lc)
            mine_x = pl.ds(pl.multiple_of(x * HALF, HALF), HALF)
            theirs_x = pl.ds(pl.multiple_of((1 - x) * HALF, HALF), HALF)
            part = self.T.at[pl.ds(4 * c, 4), mine_x]
            other = self.T.at[pl.ds(4 * c, 4), theirs_x]
            self.x2 = remote(part, part, x_peer)
            self.m1 = remote(part, part, mate)
            self.m2 = remote(other, other, mate)
            self.x2.start()
            self.m1.start()

        def s5(self):
            self.x2.wait()
            self.m2.start()

        def s6(self):
            self.m1.wait()
            self.m2.wait()
            width = self.T.shape[2] // self.parts
            self.outs = []
            for tt in range(8):
                for p in range(self.parts):
                    at = p * WIDTH + tt * width
                    self.outs.append(
                        local(
                            self.T.at[tt, :, p * width : (p + 1) * width],
                            self.out.at[:, at : at + width],
                        )
                    )
            start(self.outs)

        def s7(self):
            wait(self.outs)

    class RowGrad:
        def __init__(self, name, out):
            self.out = out
            for key in ("GS", "GR", "GK", "XS", "XR", "HS", "HR", "T"):
                setattr(self, key, getattr(r, key + "_" + name))
            self.n = self.GS.shape[0] // 2

        def compute(self, left, right):
            for target, k in ((self.GS, 1 - c), (self.GK, c)):
                lhs = left(k)
                for i in range(2):
                    cols = slice(i * 512, (i + 1) * 512)
                    target[:, cols] = dg(lhs, right(cols), 0, 0).astype(BF)

        def s0(self):
            self.core = remote(self.GS, self.GR, mate)
            self.core.start()

        def rows(self, k):
            return pl.ds(pl.multiple_of(k * self.n, HALF), self.n)

        def s1(self):
            self.core.wait()
            rows = self.rows(1 - x)
            self.XS[...] = (self.GK[rows].astype(F32) + self.GR[rows].astype(F32)).astype(BF)
            self.xc = remote(self.XS, self.XR, x_peer)
            self.xc.start()

        def total(self):
            rows = self.rows(x)
            return self.GK[rows].astype(F32) + self.GR[rows].astype(F32) + self.XR[...].astype(F32)

        def s2(self):
            self.xc.wait()
            self.hc = remote(self.HS, self.HR, h_peer)

            @pl.when(jnp.logical_not(stays))
            def _():
                self.HS[...] = self.total().astype(BF)
                self.hc.start()

        def s3(self):
            part, other = self.T.at[self.rows(x)], self.T.at[self.rows(1 - x)]
            self.x2 = remote(part, part, x_peer)
            self.m1 = remote(part, part, mate)
            self.m2 = remote(other, other, mate)

            @pl.when(jnp.logical_not(stays))
            def _():
                self.hc.wait_send()

            @pl.when(stays)
            def _():
                self.hc.wait_recv()
                self.T[self.rows(x)] = (self.total() + self.HR[...].astype(F32)).astype(BF)
                self.x2.start()
                self.m1.start()

        def s4(self):
            pass

        def s5(self):
            @pl.when(stays)
            def _():
                self.x2.wait()
                self.m2.start()

        def s6(self):
            @pl.when(stays)
            def _():
                self.m1.wait_send()
                self.m2.wait_send()

            @pl.when(jnp.logical_not(stays))
            def _():
                self.m1.wait_recv()
                self.m2.wait_recv()

            self.outs = [local(self.T, self.out)]
            start(self.outs)

        def s7(self):
            wait(self.outs)

    g_dn = RowGrad("DN", r.o_dn)
    g_up = ColumnGrad("UP", r.o_up, 1)
    g_co = RowGrad("CO", r.o_co)
    g_cq = ColumnGrad("CQ", r.o_cq, 3)
    g_so = RowGrad("SO", r.o_so)
    g_sq = ColumnGrad("QKV", r.o_sq, 3)

    def lanes(ref, k, width, base=0):
        return ref[:, :, pl.ds(pl.multiple_of(base + k * width, 128), width)].reshape(-1, width)

    rs = []
    for a in range(2):
        wait(ag[a])
        lhs = blocks(r.DM, a, WIDTH)
        for k in range(2):
            cols = slice(k * 512, (k + 1) * 512)
            d_act = dg(lhs, r.WDN[k], 1, 1).astype(BF).astype(F32)
            low = (d_act * r.DGL[a, :, cols].astype(F32)).astype(BF)
            r.DUP[:, half(a), cols] = low.reshape(4, HALF, 512)
            r.SM[pl.ds(12 + 2 * k + l, 1), pl.ds(pl.multiple_of(y * 512, 512), 512)] += colsum(low.astype(F32))
        rs.append(
            partial(a, blocks(r.DUP, a, 1024), lambda cols: shards(r.WUP, cols, slice(0, 1024)), 1)
        )
    g_dn.compute(lambda k: lanes(r.ACT, k, 512), lambda cols: r.DM[:, :, cols].reshape(512, -1))
    g_dn.s0()
    g_up.compute(lambda cols: r.S[:, :, cols].reshape(512, -1), lambda k: lanes(r.DUP, k, 512), 0, 512)
    g_up.s0()
    ag = []
    for a in range(2):
        wait(rs[a])
        d = norm_back(1, r.RES[half(a)] + summed(a), r.XH[1, half(a)], r.RSTD[1, half(a)])
        r.RES2[half(a)] = d
        low = d.astype(BF)
        r.DC[own, half(a)] = low
        add_small(5, 0, WIDTH, colsum(low.astype(F32)))
        g = gather(r.DC, pl.ds(a * HALF, HALF))
        start(g)
        ag.append(g)
    g_dn.s1()
    g_up.s1()

    rs = []
    for a in range(2):
        wait(ag[a])
        d_att = dg(blocks(r.DC, a, WIDTH), r.WCO[...].reshape(256, WIDTH), 1, 1).astype(BF)
        for k in range(2):
            cols = slice(k * 128, (k + 1) * 128)
            d_pair = d_att[:, cols]
            o_pair = r.OC[a, :, cols]
            q_pair = blocks(r.QC, a, 256)[:, cols]
            ds, kk, dk, dv = [], [], None, None
            for hh in range(2):
                d_head = head_of(d_pair, hh)
                delta = jnp.sum(d_head.astype(F32) * o_pair, 1, keepdims=True)
                p = r.PC[2 * k + hh, a]
                d_scores = (p.astype(F32) * (dg(d_head, enc_keys(1, k), 1, 1) - delta)).astype(BF)
                ds.append(dg(d_scores, enc_keys(0, k), 1, 0))
                new_dk = dg(d_scores, head_of(q_pair, hh), 0, 0)
                new_dv = dg(p, d_head, 0, 0)
                dk = new_dk if dk is None else dk + new_dk
                dv = new_dv if dv is None else dv + new_dv
            dq = jnp.where(heads[0], ds[0], ds[1]).astype(BF) * 0.125
            dq = dq.astype(BF)
            r.DQC[:, half(a), cols] = dq.reshape(4, HALF, 128)
            add_small(3, (4 * k + own) * 128, 128, colsum(dq.astype(F32)))
            if a == 0:
                r.DKV[:, cols] = dk
                r.DKV[:, 256 + k * 128 : 384 + k * 128] = dv
            else:
                r.DKV[:, cols] += dk
                r.DKV[:, 256 + k * 128 : 384 + k * 128] += dv
        rs.append(
            partial(a, blocks(r.DQC, a, 256), lambda cols: shards(r.WCQ, cols, slice(0, 256)), 1)
        )
    my_enc = pl.ds(pl.multiple_of(c * 256, 256), 256)
    their_enc = pl.ds(pl.multiple_of((1 - c) * 256, 256), 256)
    r.DKS[...] = r.DKV[their_enc].astype(BF).reshape(4, ENC, 512)
    dk_x = remote(r.DKS, r.DKR, mate)
    dk_x.start()
    g_dn.s2()
    g_up.s2()
    g_co.compute(lambda k: lanes(r.CATT, k, 128), lambda cols: r.DC[:, :, cols].reshape(512, -1))
    g_co.s0()
    ag = []
    for a in range(2):
        wait(rs[a])
        d = norm_back(0, r.RES2[half(a)] + summed(a), r.XH[0, half(a)], r.RSTD[0, half(a)])
        r.RES[half(a)] = d
        low = d.astype(BF)
        r.DM[own, half(a)] = low
        add_small(2, 0, WIDTH, colsum(low.astype(F32)))
        g = gather(r.DM, pl.ds(a * HALF, HALF))
        start(g)
        ag.append(g)
    dk_x.wait()
    low = (r.DKV[my_enc] + r.DKR[...].reshape(256, 512).astype(F32)).astype(BF)
    r.DKL[...] = low.reshape(4, ENC, 512)
    dv_sum = colsum(low[:, 256:512].astype(F32))
    for k in range(2):
        add_small(4, (4 * k + own) * 128, 128, dv_sum[:, k * 128 : (k + 1) * 128])
    for n in range(2):
        cols = slice(n * 512, (n + 1) * 512)
        out = dg(low, shards(r.WCQ, cols, slice(256, 768)), 1, 1)
        r.PBE[:, :, cols] = out.astype(BF).reshape(4, ENC, 512)
    rs_e = [remote(r.PBE.at[peer_block(j)], r.RBE.at[j - 1], peer(j)) for j in (1, 2, 3)]
    start(rs_e)
    g_dn.s3()
    g_up.s3()
    g_co.s1()
    g_cq.compute(lambda cols: r.F[:, :, cols].reshape(512, -1), lambda k: lanes(r.DQC, k, 128), 0, 128)
    for p in range(2):
        g_cq.compute(
            lambda cols: r.E[:, :, cols].reshape(256, -1),
            lambda k, p=p: lanes(r.DKL, k, 128, 256 * p),
            128 + 128 * p,
            128,
        )
    g_cq.s0()

    do_x = []
    for a in range(2):
        wait(ag[a])
        d_att = dg(blocks(r.DM, a, WIDTH), r.WSO[...].reshape(256, WIDTH), 1, 1).astype(BF)
        mine_d = jnp.where(c == 0, d_att[:, 0:128], d_att[:, 128:256])
        theirs_d = jnp.where(c == 0, d_att[:, 128:256], d_att[:, 0:128])
        r.DATS[:, half(a)] = theirs_d.reshape(4, HALF, 128)
        r.DO[mine, half(a)] = mine_d.reshape(4, HALF, 128)
        rows = pl.ds(a * HALF, HALF)
        do_x.append(remote(r.DATS.at[:, rows], r.DO.at[mine, rows], mate))
        do_x[a].start()
    g_dn.s4()
    g_up.s4()
    g_co.s2()
    g_cq.s1()
    g_so.compute(lambda k: lanes(r.ATT, k, 128), lambda cols: r.DM[:, :, cols].reshape(512, -1))
    g_so.s0()
    wait(rs_e)
    d_enc = r.PBE[own].astype(F32)
    for j in range(3):
        d_enc = d_enc + r.RBE[j].astype(F32)
    r.DES[...] = d_enc.astype(BF)
    de_out = leave(r.DES, r.o_denc)

    wait(do_x)
    r.DKVS[...] = jnp.zeros_like(r.DKVS)
    for i in range(4):
        n = (i + 1) * 256
        q = r.QKV[0, 2 * i : 2 * i + 2].reshape(256, 128)
        d_pair = r.DO[2 * i : 2 * i + 2].reshape(256, 128)
        o_pair = r.O[i * 256 : (i + 1) * 256]
        dqs, dk, dv = [], None, None
        for hh in range(2):
            d_head = head_of(d_pair, hh)
            delta = jnp.sum(d_head.astype(F32) * o_pair, 1, keepdims=True)
            p = probs[i][hh]
            d_scores = (p.astype(F32) * (dg(d_head, keys(2, n), 1, 1) - delta)).astype(BF)
            dqs.append(dg(d_scores, keys(1, n), 1, 0))
            new_dk = dg(d_scores, head_of(q, hh), 0, 0)
            new_dv = dg(p, d_head, 0, 0)
            dk = new_dk if dk is None else dk + new_dk
            dv = new_dv if dv is None else dv + new_dv
        dq = (jnp.where(heads[0], dqs[0], dqs[1]).astype(BF) * 0.125).astype(BF)
        r.DJN[0, 2 * i : 2 * i + 2] = dq.reshape(2, ROWS, 128)
        add_small(0, t * 128, 128, colsum(dq.astype(F32)))
        r.DKVS[0, 0:n] += dk
        r.DKVS[1, 0:n] += dv
    r.DJN[1] = r.DKVS[0].astype(BF).reshape(8, ROWS, 128)
    low = r.DKVS[1].astype(BF)
    r.DJN[2] = low.reshape(8, ROWS, 128)
    add_small(1, t * 128, 128, colsum(low.astype(F32)))
    dj_x = []
    for p in range(3):
        at = pl.ds(pl.multiple_of(p * 256 + c * 128, 128), 128)
        dj_x.append(remote(r.DJN.at[p, theirs], r.DJ.at[:, :, at], mate))
        dj_x[p].start()
        r.DJ[:, :, at] = r.DJN[p, mine]
    wait(dj_x)
    rs = [
        partial(a, blocks(r.DJ, a, 768), lambda cols: shards(r.WQKV, cols, slice(0, 768)), 1)
        for a in range(2)
    ]
    for p in range(3):
        g_sq.compute(
            lambda cols: r.X[:, :, cols].reshape(512, -1),
            lambda k, p=p: lanes(r.DJ, k, 128, 256 * p),
            128 * p,
            128,
        )
    g_sq.s0()
    g_dn.s5()
    g_up.s5()
    g_co.s3()
    g_cq.s2()
    g_so.s1()
    g_sq.s1()
    for a in range(2):
        wait(rs[a])
        r.DTS[half(a)] = (r.RES[half(a)] + summed(a)).astype(BF)
    dt_out = leave(r.DTS, r.o_dtok)

    y_peer, l_peer = peer(1), peer(2)

    def small_step(i, device):
        cp = remote(r.SM, r.SMR.at[i], device)
        cp.start()
        return cp

    def small_add(i, cp):
        cp.wait()
        r.SM[...] += r.SMR[i]

    small = small_step(0, mate)
    g_dn.s6()
    g_up.s6()
    g_co.s4()
    g_co.s5()
    g_cq.s3()
    g_so.s2()
    g_sq.s2()
    small_add(0, small)
    small = small_step(1, y_peer)
    g_co.s6()
    g_cq.s4()
    g_so.s3()
    g_sq.s3()
    small_add(1, small)
    small = small_step(2, l_peer)
    g_cq.s5()
    g_so.s4()
    g_so.s5()
    g_sq.s4()
    small_add(2, small)
    small = small_step(3, x_peer)
    g_cq.s6()
    g_so.s6()
    g_sq.s5()
    small_add(3, small)
    small = small_step(4, h_peer)
    g_sq.s6()
    small_add(4, small)
    r.o_small[...] = r.SM[...]

    @pl.when(jnp.logical_not(stays))
    def _():
        mx_out.wait()
        de_out.wait()
        dt_out.wait()

    for g in (g_dn, g_up, g_co, g_cq, g_so, g_sq):
        g.s7()


def on_chip(*args):
    (tokens, encoder, seq_len, enc_len, d_mixed, *rest) = args
    *mats, self_bias, cross_bias, norm_gain, norm_bias, fc1_bias, fc2_bias = rest
    anywhere = pl.BlockSpec(memory_space=pl.ANY)
    vmem = pl.BlockSpec(memory_space=pltpu.VMEM)
    smem = pl.BlockSpec(memory_space=pltpu.SMEM)
    shapes = [
        ((ROWS, WIDTH), BF),
        ((ROWS, WIDTH), BF),
        ((ENC, WIDTH), BF),
        ((128, 3 * WIDTH), BF),
        ((128, WIDTH), BF),
        ((128, 3 * WIDTH), BF),
        ((128, WIDTH), BF),
        ((128, HIDDEN), BF),
        ((512, WIDTH), BF),
        ((24, WIDTH), F32),
    ]
    outs = pl.pallas_call(
        layer_kernel,
        out_shape=[jax.ShapeDtypeStruct(s, d) for s, d in shapes],
        in_specs=[anywhere, anywhere, smem, smem, anywhere] + [anywhere] * 6 + [vmem] * 6,
        out_specs=[vmem] * 3 + [anywhere] * 6 + [vmem],
        scratch_shapes=[pltpu.VMEM(s, d) for s, d in SCRATCH.values()]
        + [
            pltpu.SemaphoreType.DMA((N_REMOTE,)),
            pltpu.SemaphoreType.DMA((N_REMOTE,)),
            pltpu.SemaphoreType.DMA((N_LOCAL,)),
        ],
        compiler_params=pltpu.CompilerParams(
            collective_id=0, has_side_effects=True, vmem_limit_bytes=VMEM_BYTES
        ),
        cost_estimate=pl.CostEstimate(
            flops=16 * 10**9, bytes_accessed=16 * 2**20, transcendentals=8 * 2**20
        ),
    )(
        tokens, encoder, seq_len, enc_len, d_mixed, *mats,
        self_bias, cross_bias, norm_gain, norm_bias,
        fc1_bias.reshape(1, -1), fc2_bias.reshape(1, -1),
    )
    mixed, d_tokens, d_encoder, *grads, small = outs
    return (
        mixed,
        d_tokens.astype(F32),
        d_encoder.astype(F32),
        *[g.astype(F32) for g in grads],
        small[0:3],
        small[3:6],
        small[6:9],
        small[9:12],
        small[12:16].reshape(-1),
        small[16],
    )


def fits(mesh, tokens, encoder, self_qkv, fc1_weight):
    return (
        (mesh.shape["rep"], mesh.shape["shard"]) == (4, 8)
        and tokens.shape == (32 * ROWS, WIDTH)
        and encoder.shape == (32 * ENC, WIDTH)
        and self_qkv.shape == (WIDTH, 3 * WIDTH)
        and fc1_weight.shape == (WIDTH, HIDDEN)
    )


def solution(mesh):
    def placed(body):
        return jax.shard_map(
            body,
            mesh=mesh,
            in_specs=(
                P(("rep", "shard"), None),
                P(("rep", "shard"), None),
                P("rep"),
                P("rep"),
                P(("rep", "shard"), None),
                P("shard", None),
                P("shard", None),
                P("shard", None),
                P("shard", None),
                P("shard", None),
                P("shard", None),
                P(),
                P(),
                P(),
                P(),
                P(),
                P(),
            ),
            out_specs=(
                P(("rep", "shard"), None),
                P(("rep", "shard"), None),
                P(("rep", "shard"), None),
                P("shard", None),
                P("shard", None),
                P("shard", None),
                P("shard", None),
                P("shard", None),
                P("shard", None),
                P(),
                P(),
                P(),
                P(),
                P(),
                P(),
            ),
            check_vma=False,
        )

    def run(*args):
        fast = fits(mesh, args[0], args[1], args[5], args[9])
        return placed(on_chip if fast else local)(*args)

    return run
```

```python
from functools import partial

import jax
import jax.numpy as jnp
from jax import lax
from jax.experimental import pallas as pl
from jax.experimental.pallas import tpu as pltpu
from jax.sharding import PartitionSpec as P

HEADS = 16
HEAD = 64


def for_sending(array):
    return jax.tree.map(lambda a: a.astype(jnp.bfloat16) if a.dtype == jnp.float32 else a, array)


def layer_norm(hidden, gain_row, shift_row):
    centre = hidden - jnp.mean(hidden, -1, keepdims=True)
    spread = jnp.mean(centre * centre, -1, keepdims=True)
    return centre * lax.rsqrt(spread + 1e-05) * gain_row + shift_row


def exact_gelu(values):
    return jax.nn.gelu(values, approximate=False)


def contract_rows(left, right):
    return lax.dot_general(
        left, right, (((0,), (0,)), ((), ())), preferred_element_type=jnp.float32
    )


def back_dot(grad_rows, weight):
    return lax.dot_general(
        grad_rows, weight, (((1,), (1,)), ((), ())), preferred_element_type=jnp.float32
    )


def causal_mask(query_pos, key_pos):
    return key_pos[None, :] <= query_pos[:, None]


def enc_visible(query_pos, key_pos, enc_limit):
    return jnp.broadcast_to((key_pos < enc_limit)[None, :], (query_pos.shape[0], key_pos.shape[0]))


def only_live(step_fn, live_fn):

    def wrapped(totals, block_in, offset):
        return lax.cond(
            live_fn(block_in, offset), lambda: step_fn(totals, block_in, offset), lambda: totals
        )

    return wrapped


def self_fold(key_pair, step_fn, start_state, store):
    return step_fn(
        start_state,
        jax.tree.map(
            lambda a: lax.all_gather(a, "shard", axis=0, tiled=True), for_sending(key_pair)
        ),
        jnp.int32(0),
    )


def cross_fold(key_pair, step_fn, start_state, store):
    return step_fn(
        start_state,
        jax.tree.map(
            lambda a: lax.all_gather(a, "shard", axis=0, tiled=True), for_sending(key_pair)
        ),
        jnp.int32(0),
    )


def keys_live(query_pos, allowed_fn):

    def live_fn(block_in, offset):
        key_pos = jnp.arange(block_in[0].shape[0], dtype=jnp.int32)
        return jnp.any(allowed_fn(query_pos, key_pos))

    return live_fn


def head_scores(query_heads, query_pos, key_block, allowed_fn):
    key_count = key_block.shape[0]
    key_pos = jnp.arange(key_count, dtype=jnp.int32)
    scores = jnp.einsum(
        "qhd,khd->hqk",
        query_heads,
        key_block.reshape(key_count, HEADS, HEAD),
        preferred_element_type=jnp.float32,
    )
    return (scores, allowed_fn(query_pos, key_pos)[None])


def forward_pass(query_part, query_pos, key_pair, allowed_fn, folder):
    query_count = query_part.shape[0]
    query_heads = query_part.reshape(query_count, HEADS, HEAD)
    live_fn = keys_live(query_pos, allowed_fn)

    def stat_step(totals, block_in, offset):
        highest, mass = totals
        scores, allowed = head_scores(query_heads, query_pos, block_in[0], allowed_fn)
        masked = jnp.where(allowed, scores, -1e30)
        raised = jnp.maximum(highest, jnp.max(masked, -1))
        fresh = jnp.sum(jnp.where(allowed, jnp.exp(masked - raised[:, :, None]), 0.0), -1)
        return (raised, fresh)

    start_state = (
        jnp.full((HEADS, query_count), -1e30, jnp.float32),
        jnp.zeros((HEADS, query_count), jnp.float32),
    )
    highest, mass = folder(key_pair, only_live(stat_step, live_fn), start_state, None)
    log_total = highest + jnp.log(mass)

    def out_step(totals, block_in, offset):
        scores, allowed = head_scores(query_heads, query_pos, block_in[0], allowed_fn)
        weights_low = jnp.where(allowed, jnp.exp(scores - log_total[:, :, None]), 0.0).astype(
            jnp.bfloat16
        )
        value_heads = block_in[1].reshape(block_in[1].shape[0], HEADS, HEAD)
        return jnp.einsum(
            "hqk,khd->qhd", weights_low, value_heads, preferred_element_type=jnp.float32
        )

    summed = folder(
        key_pair,
        only_live(out_step, live_fn),
        jnp.zeros((query_count, HEADS, HEAD), jnp.float32),
        None,
    )
    return (log_total.T, summed)


def query_step(query_part, query_pos, allowed_fn, log_rows, delta_rows, d_out):
    query_count = query_part.shape[0]
    query_heads = query_part.reshape(query_count, HEADS, HEAD)
    grad_heads = d_out.reshape(query_count, HEADS, HEAD)
    log_total = log_rows.T
    correction = delta_rows.T

    def grad_step(totals, block_in, offset):
        key_block, value_block = block_in
        key_count = key_block.shape[0]
        scores, allowed = head_scores(query_heads, query_pos, key_block, allowed_fn)
        probs = jnp.where(allowed, jnp.exp(scores - log_total[:, :, None]), 0.0)
        d_probs = jnp.einsum(
            "qhd,khd->hqk",
            grad_heads,
            value_block.reshape(key_count, HEADS, HEAD),
            preferred_element_type=jnp.float32,
        )
        d_scores = (probs * (d_probs - correction[:, :, None])).astype(jnp.bfloat16)
        return jnp.einsum(
            "hqk,khd->qhd",
            d_scores,
            key_block.reshape(key_count, HEADS, HEAD),
            preferred_element_type=jnp.float32,
        )

    return only_live(grad_step, keys_live(query_pos, allowed_fn))


def query_grad(query_part, query_pos, key_pair, allowed_fn, folder, log_rows, delta_rows, d_out):
    query_count = query_part.shape[0]
    step_fn = query_step(query_part, query_pos, allowed_fn, log_rows, delta_rows, d_out)
    return folder(key_pair, step_fn, jnp.zeros((query_count, HEADS, HEAD), jnp.float32), None)


def key_step(own_keys, own_values, key_pos, allowed_fn, log_all, delta_all):
    key_count = own_keys.shape[0]
    key_heads = own_keys.reshape(key_count, HEADS, HEAD)
    value_heads = own_values.reshape(key_count, HEADS, HEAD)

    def step_fn(totals, block_in, offset):
        query_block, grad_block = block_in
        query_count = query_block.shape[0]
        query_pos = jnp.arange(query_count, dtype=jnp.int32)
        log_part = log_all.T
        delta_part = delta_all.T
        query_heads = query_block.reshape(query_count, HEADS, HEAD)
        grad_heads = grad_block.reshape(query_count, HEADS, HEAD)
        scores = jnp.einsum(
            "qhd,khd->hqk", query_heads, key_heads, preferred_element_type=jnp.float32
        )
        allowed = allowed_fn(query_pos, key_pos)[None]
        probs = jnp.where(allowed, jnp.exp(scores - log_part[:, :, None]), 0.0)
        d_values = jnp.einsum(
            "hqk,qhd->khd",
            probs.astype(jnp.bfloat16),
            grad_heads,
            preferred_element_type=jnp.float32,
        )
        d_probs = jnp.einsum(
            "qhd,khd->hqk", grad_heads, value_heads, preferred_element_type=jnp.float32
        )
        d_scores = (probs * (d_probs - delta_part[:, :, None])).astype(jnp.bfloat16)
        d_keys = jnp.einsum(
            "hqk,qhd->khd", d_scores, query_heads, preferred_element_type=jnp.float32
        )
        return (d_keys, d_values)

    def live_fn(block_in, offset):
        query_pos = jnp.arange(block_in[0].shape[0], dtype=jnp.int32)
        return jnp.any(allowed_fn(query_pos, key_pos))

    return only_live(step_fn, live_fn)


def column_sum(values):
    return jnp.sum(values.astype(jnp.float32), 0)


def local(
    tokens,
    encoder,
    seq_len,
    enc_len,
    d_mixed,
    self_qkv,
    self_out,
    cross_qkv,
    cross_out,
    fc1_weight,
    fc2_weight,
    self_bias,
    cross_bias,
    norm_gain,
    norm_bias,
    fc1_bias,
    fc2_bias,
):
    model_width = tokens.shape[1]
    tok_rows = tokens.shape[0]
    enc_rows = encoder.shape[0]
    device_at = lax.axis_index("shard")
    positions = device_at * tok_rows + jnp.arange(tok_rows, dtype=jnp.int32)
    enc_positions = device_at * enc_rows + jnp.arange(enc_rows, dtype=jnp.int32)
    seq_limit = seq_len[0]
    visible = partial(enc_visible, enc_limit=enc_len[0])
    w_sq, w_so = (
        lax.all_gather(self_qkv, "shard", axis=0, tiled=True),
        lax.all_gather(self_out, "shard", axis=0, tiled=True),
    )
    joined = jnp.dot(tokens, w_sq, preferred_element_type=jnp.float32)
    query_s = ((joined[:, :model_width] + self_bias[0]) * 0.125).astype(jnp.bfloat16)
    key_s = joined[:, model_width : 2 * model_width].astype(jnp.bfloat16)
    value_s = (joined[:, 2 * model_width :] + self_bias[1]).astype(jnp.bfloat16)
    self_lse, self_summed = forward_pass(
        query_s, positions, (key_s, value_s), causal_mask, self_fold
    )
    attended = self_summed.reshape(tok_rows, model_width).astype(jnp.bfloat16)
    branch = jnp.dot(attended, w_so, preferred_element_type=jnp.float32) + self_bias[2]
    first_norm, first_pull = jax.vjp(
        layer_norm, tokens.astype(jnp.float32) + branch, norm_gain[0], norm_bias[0]
    )
    w_cq, w_co = (
        lax.all_gather(cross_qkv, "shard", axis=0, tiled=True),
        lax.all_gather(cross_out, "shard", axis=0, tiled=True),
    )
    first_low = first_norm.astype(jnp.bfloat16)
    query_c = (
        (
            jnp.dot(first_low, w_cq[:, :model_width], preferred_element_type=jnp.float32)
            + cross_bias[0]
        )
        * 0.125
    ).astype(jnp.bfloat16)
    enc_proj = jnp.dot(encoder, w_cq[:, model_width:], preferred_element_type=jnp.float32)
    key_c = enc_proj[:, :model_width].astype(jnp.bfloat16)
    value_c = (enc_proj[:, model_width:] + cross_bias[1]).astype(jnp.bfloat16)
    cross_lse, cross_summed = forward_pass(
        query_c, positions, (key_c, value_c), visible, cross_fold
    )
    cross_att = cross_summed.reshape(tok_rows, model_width).astype(jnp.bfloat16)
    branch_c = jnp.dot(cross_att, w_co, preferred_element_type=jnp.float32) + cross_bias[2]
    second_norm, second_pull = jax.vjp(
        layer_norm, first_norm + branch_c, norm_gain[1], norm_bias[1]
    )
    w_up, w_down = (
        lax.all_gather(fc1_weight, "shard", axis=0, tiled=True),
        lax.all_gather(fc2_weight, "shard", axis=0, tiled=True),
    )
    second_low = second_norm.astype(jnp.bfloat16)
    upward = jnp.dot(second_low, w_up, preferred_element_type=jnp.float32) + fc1_bias
    activated, gelu_pull = jax.vjp(exact_gelu, upward)
    act_low = activated.astype(jnp.bfloat16)
    branch_m = jnp.dot(act_low, w_down, preferred_element_type=jnp.float32) + fc2_bias
    output, third_pull = jax.vjp(layer_norm, second_norm + branch_m, norm_gain[2], norm_bias[2])
    valid = (positions < seq_limit).astype(jnp.float32)[:, None]
    d_third, d_gain3, d_shift3 = third_pull(d_mixed.astype(jnp.float32) * valid)
    d_branch_m = d_third.astype(jnp.bfloat16)
    g_down = contract_rows(act_low, d_branch_m)
    d_act = back_dot(d_branch_m, w_down).astype(jnp.bfloat16)
    (d_up,) = gelu_pull(d_act.astype(jnp.float32))
    d_up_low = d_up.astype(jnp.bfloat16)
    g_up = contract_rows(second_low, d_up_low)
    d_second = d_third + back_dot(d_up_low, w_up)
    d_hidden2, d_gain2, d_shift2 = second_pull(d_second)
    d_branch_c = d_hidden2.astype(jnp.bfloat16)
    g_co = contract_rows(cross_att, d_branch_c)
    d_cross_att = back_dot(d_branch_c, w_co).astype(jnp.bfloat16)
    cross_delta = jnp.einsum(
        "qhd,qhd->qh", d_cross_att.reshape(tok_rows, HEADS, HEAD).astype(jnp.float32), cross_summed
    )
    d_query_c = query_grad(
        query_c,
        positions,
        (key_c, value_c),
        visible,
        cross_fold,
        cross_lse,
        cross_delta,
        d_cross_att,
    )
    d_query_cs = d_query_c.reshape(tok_rows, model_width).astype(jnp.bfloat16) * 0.125
    d_first = d_hidden2 + back_dot(d_query_cs, w_cq[:, :model_width])
    d_hidden1, d_gain1, d_shift1 = first_pull(d_first)
    d_branch = d_hidden1.astype(jnp.bfloat16)
    g_so = contract_rows(attended, d_branch)
    d_attended = back_dot(d_branch, w_so).astype(jnp.bfloat16)
    self_delta = jnp.einsum(
        "qhd,qhd->qh", d_attended.reshape(tok_rows, HEADS, HEAD).astype(jnp.float32), self_summed
    )
    stats = (
        lax.all_gather(self_lse, "shard", axis=0, tiled=True),
        lax.all_gather(self_delta, "shard", axis=0, tiled=True),
        lax.all_gather(cross_lse, "shard", axis=0, tiled=True),
        lax.all_gather(cross_delta, "shard", axis=0, tiled=True),
    )
    tok_zero = jnp.zeros((tok_rows, HEADS, HEAD), jnp.float32)
    query_side = query_step(query_s, positions, causal_mask, self_lse, self_delta, d_attended)
    key_side = key_step(key_s, value_s, positions, causal_mask, stats[0], stats[1])
    offset = jnp.int32(0)
    d_query_part = query_side(
        tok_zero,
        (
            lax.all_gather(key_s, "shard", axis=0, tiled=True),
            lax.all_gather(value_s, "shard", axis=0, tiled=True),
        ),
        offset,
    )
    d_key_part, d_value_part = key_side(
        (tok_zero, tok_zero),
        (
            lax.all_gather(query_s, "shard", axis=0, tiled=True),
            lax.all_gather(d_attended, "shard", axis=0, tiled=True),
        ),
        offset,
    )
    enc_zero = jnp.zeros((enc_rows, HEADS, HEAD), jnp.float32)
    d_key_c, d_value_c = key_step(key_c, value_c, enc_positions, visible, stats[2], stats[3])(
        (enc_zero, enc_zero),
        (
            lax.all_gather(query_c, "shard", axis=0, tiled=True),
            lax.all_gather(d_cross_att, "shard", axis=0, tiled=True),
        ),
        jnp.int32(0),
    )
    d_qs = d_query_part.reshape(tok_rows, model_width).astype(jnp.bfloat16) * 0.125
    d_ks = d_key_part.reshape(tok_rows, model_width).astype(jnp.bfloat16)
    d_vs = d_value_part.reshape(tok_rows, model_width).astype(jnp.bfloat16)
    d_joined = jnp.concatenate([d_qs, d_ks, d_vs], 1)
    g_sq = contract_rows(tokens, d_joined)
    d_tokens = d_hidden1 + back_dot(d_joined, w_sq)
    d_kc = d_key_c.reshape(enc_rows, model_width).astype(jnp.bfloat16)
    d_vc = d_value_c.reshape(enc_rows, model_width).astype(jnp.bfloat16)
    d_enc_proj = jnp.concatenate([d_kc, d_vc], 1)
    g_cq = jnp.concatenate(
        [contract_rows(first_low, d_query_cs), contract_rows(encoder, d_enc_proj)], 1
    )
    d_encoder = back_dot(d_enc_proj, w_cq[:, model_width:])
    d_self_bias = jnp.stack([column_sum(d_qs), column_sum(d_vs), column_sum(d_branch)])
    d_cross_bias = jnp.stack([column_sum(d_query_cs), column_sum(d_vc), column_sum(d_branch_c)])
    d_norm_gain = jnp.stack([d_gain1, d_gain2, d_gain3])
    d_norm_bias = jnp.stack([d_shift1, d_shift2, d_shift3])
    d_fc1_bias = column_sum(d_up_low)
    d_fc2_bias = column_sum(d_branch_m)
    row_grads = (
        lax.psum_scatter(g_sq, "shard", scatter_dimension=0, tiled=True),
        lax.psum_scatter(g_so, "shard", scatter_dimension=0, tiled=True),
        lax.psum_scatter(g_cq, "shard", scatter_dimension=0, tiled=True),
        lax.psum_scatter(g_co, "shard", scatter_dimension=0, tiled=True),
        lax.psum_scatter(g_up, "shard", scatter_dimension=0, tiled=True),
        lax.psum_scatter(g_down, "shard", scatter_dimension=0, tiled=True),
    )
    row_grads = lax.psum(
        (row_grads[0], row_grads[1], row_grads[2], row_grads[3], row_grads[4], row_grads[5]), "rep"
    )
    small_sums = lax.psum(
        (d_self_bias, d_cross_bias, d_norm_gain, d_norm_bias, d_fc1_bias, d_fc2_bias),
        ("rep", "shard"),
    )
    return (
        output.astype(jnp.bfloat16),
        d_tokens,
        d_encoder,
        row_grads[0],
        row_grads[1],
        row_grads[2],
        row_grads[3],
        row_grads[4],
        row_grads[5],
        small_sums[0],
        small_sums[1],
        small_sums[2],
        small_sums[3],
        small_sums[4],
        small_sums[5],
    )


MESH = pl.DeviceIdType.MESH
BF = jnp.bfloat16
F32 = jnp.float32
EPS = 1e-05


def dg(left, right, cl, cr):
    return lax.dot_general(
        left, right, (((cl,), (cr,)), ((), ())), preferred_element_type=F32
    )


class Names:
    pass


WIDTH = 1024
HIDDEN = 4096
ROWS = 128
ENC = 64
HALF = 64

SCRATCH = {
    "X": ((8, ROWS, WIDTH), BF),
    "E": ((4, ENC, WIDTH), BF),
    "DMX": ((ROWS, WIDTH), BF),
    "LSRC": ((8, 128), F32),
    "LENS": ((8, 128), F32),
    "WQKV": ((8, 128, 768), BF),
    "WSO": ((2, 128, WIDTH), BF),
    "WCQ": ((8, 128, 768), BF),
    "WCO": ((2, 128, WIDTH), BF),
    "WUP": ((8, 128, 1024), BF),
    "WDN": ((2, 512, WIDTH), BF),
    "QST": ((2, 3, 4, ROWS, 128), BF),
    "QKV": ((3, 8, ROWS, 128), BF),
    "P0": ((2, 256, 256), BF),
    "P1": ((2, 256, 512), BF),
    "P2": ((2, 256, 768), BF),
    "P3": ((2, 256, 1024), BF),
    "O": ((1024, 128), F32),
    "ATF": ((8, ROWS, 128), BF),
    "ATT": ((4, ROWS, 256), BF),
    "PB": ((4, ROWS, WIDTH), BF),
    "RB": ((3, ROWS, WIDTH), BF),
    "PBE": ((4, ENC, WIDTH), BF),
    "RBE": ((3, ENC, WIDTH), BF),
    "F": ((4, ROWS, WIDTH), BF),
    "S": ((4, ROWS, WIDTH), BF),
    "DM": ((4, ROWS, WIDTH), BF),
    "DC": ((4, ROWS, WIDTH), BF),
    "RES": ((ROWS, WIDTH), F32),
    "RES2": ((ROWS, WIDTH), F32),
    "XH": ((2, ROWS, WIDTH), F32),
    "RSTD": ((2, ROWS, 1), F32),
    "QC": ((4, ROWS, 256), BF),
    "KVC": ((8, ENC, 512), BF),
    "PC": ((4, 2, 256, 512), BF),
    "OC": ((2, 256, 256), F32),
    "CATT": ((4, ROWS, 256), BF),
    "ACT": ((4, ROWS, 1024), BF),
    "DGL": ((2, 256, 1024), BF),
    "DUP": ((4, ROWS, 1024), BF),
    "DQC": ((4, ROWS, 256), BF),
    "DKV": ((512, 512), F32),
    "DKS": ((4, ENC, 512), BF),
    "DKR": ((4, ENC, 512), BF),
    "DKL": ((4, ENC, 512), BF),
    "DATS": ((4, ROWS, 128), BF),
    "DO": ((8, ROWS, 128), BF),
    "DKVS": ((2, 1024, 128), F32),
    "DJN": ((3, 8, ROWS, 128), BF),
    "DJ": ((4, ROWS, 768), BF),
    "MXS": ((ROWS, WIDTH), BF),
    "DTS": ((ROWS, WIDTH), BF),
    "DES": ((ENC, WIDTH), BF),
    "SM": ((24, WIDTH), F32),
    "SMR": ((5, 24, WIDTH), F32),
    "SB": ((8, WIDTH), F32),
    "SBR": ((5, 8, WIDTH), F32),
}
for _name, _rows in (("SO", 128), ("CO", 128), ("DN", 512)):
    SCRATCH["GS_" + _name] = ((_rows, WIDTH), BF)
    SCRATCH["GR_" + _name] = ((_rows, WIDTH), BF)
    SCRATCH["GK_" + _name] = ((_rows, WIDTH), BF)
    SCRATCH["XS_" + _name] = ((_rows // 2, WIDTH), BF)
    SCRATCH["XR_" + _name] = ((_rows // 2, WIDTH), BF)
    SCRATCH["HS_" + _name] = ((_rows // 2, WIDTH), BF)
    SCRATCH["HR_" + _name] = ((_rows // 2, WIDTH), BF)
    SCRATCH["T_" + _name] = ((_rows, WIDTH), BF)
for _name, _cols in (("SQ0", 128), ("SQ1", 128), ("SQ2", 128), ("CQ", 384), ("UP", 512)):
    if _cols > 128:
        SCRATCH["GS_" + _name] = ((8, 128, _cols), BF)
        SCRATCH["GR_" + _name] = ((8, 128, _cols), BF)
    SCRATCH["GK_" + _name] = ((8, 128, _cols), BF)
    SCRATCH["XS_" + _name] = ((8, HALF, _cols), BF)
    SCRATCH["XR_" + _name] = ((8, HALF, _cols), BF)
    SCRATCH["HS_" + _name] = ((4, HALF, _cols), BF)
    SCRATCH["HR_" + _name] = ((4, HALF, _cols), BF)
    SCRATCH["TS_" + _name] = ((4, HALF, _cols), BF)
    SCRATCH["T_" + _name] = ((8, 128, _cols), BF)

IN_NAMES = (
    "tokens", "encoder", "seq", "enc", "dmix", "w_sq", "w_so", "w_cq", "w_co", "w_up", "w_dn",
    "sb", "cb", "gain", "shift", "fb1", "fb2",
)
OUT_NAMES = (
    "o_mixed", "o_dtok", "o_denc", "o_sq", "o_so", "o_cq", "o_co", "o_up", "o_dn", "o_small",
)
VMEM_BYTES = 64 * 2**20 - 2**19
N_REMOTE = 400
N_LOCAL = 128


def layer_kernel(*refs):
    n_in, n_out = len(IN_NAMES), len(OUT_NAMES)
    r = Names()
    names = IN_NAMES + OUT_NAMES + tuple(SCRATCH)
    for name, ref in zip(names, refs):
        setattr(r, name, ref)
    send_sem, recv_sem, local_sem = refs[len(names) :]
    count = {"remote": 0, "local": 0}

    rep, shard = lax.axis_index("rep"), lax.axis_index("shard")
    x, c = rep // 2, rep % 2
    z, y = shard // 2, shard % 2
    h, l = z // 2, z % 2
    own = 2 * l + y
    t = 4 * c + own
    s_own = 4 * h + own

    def dev(xx, hh, ll, yy, cc):
        return (xx * 2 + cc, (2 * hh + ll) * 2 + yy)

    mate = dev(x, h, l, y, 1 - c)
    x_peer = dev(1 - x, h, l, y, c)
    h_peer = dev(x, 1 - h, l, y, c)
    swap_peer = dev(x, 1 - h, l, y, 1 - c)

    def peer_lc(j):
        return (l + j // 2) % 2, (y + j % 2) % 2

    def peer(j):
        ll, yy = peer_lc(j)
        return dev(x, h, ll, yy, c)

    def peer_block(j):
        ll, yy = peer_lc(j)
        return 2 * ll + yy

    def remote(src, dst, device):
        i = count["remote"]
        count["remote"] += 1
        return pltpu.make_async_remote_copy(
            src_ref=src,
            dst_ref=dst,
            send_sem=send_sem.at[i],
            recv_sem=recv_sem.at[i],
            device_id=device,
            device_id_type=MESH,
        )

    def local(src, dst):
        i = count["local"]
        count["local"] += 1
        return pltpu.make_async_copy(src, dst, local_sem.at[i])

    barrier = pltpu.get_barrier_semaphore()
    greet = [mate, x_peer, swap_peer]
    for m in range(1, 8):
        greet.append(dev(x, (h + m // 4) % 2, (l + (m // 2) % 2) % 2, (y + m % 2) % 2, c))
    for device in greet:
        pl.semaphore_signal(barrier, inc=1, device_id=device, device_id_type=MESH)
    r.LSRC[0:1, :] = jnp.full((1, 128), r.seq[0].astype(F32))
    r.LSRC[1:2, :] = jnp.full((1, 128), r.enc[0].astype(F32))
    r.SM[...] = jnp.zeros_like(r.SM)
    r.SB[...] = jnp.zeros_like(r.SB)
    pl.semaphore_wait(barrier, len(greet))

    moved = [
        (r.tokens, r.X.at[t]),
        (r.encoder, r.E.at[own]),
        (r.LSRC, r.LENS),
        (r.dmix, r.DMX),
    ]
    swaps = [(remote(s, d, swap_peer), local(s, d)) for s, d in moved]
    there = r.X.at[4 * (1 - c) + own]
    swaps[0] = (remote(r.tokens, there, swap_peer), swaps[0][1])
    stays = c == h

    def swap_start(i):
        @pl.when(stays)
        def _():
            swaps[i][1].start()

        @pl.when(jnp.logical_not(stays))
        def _():
            swaps[i][0].start()

    def swap_wait(i):
        @pl.when(stays)
        def _():
            swaps[i][1].wait()

        @pl.when(jnp.logical_not(stays))
        def _():
            swaps[i][0].wait()

    my_x = pl.ds(pl.multiple_of(x * HALF, HALF), HALF)
    other_x = pl.ds(pl.multiple_of((1 - x) * HALF, HALF), HALF)

    class ColumnWeight:
        def __init__(self, w_hbm, dst, parts, width):
            self.w, self.dst, self.parts, self.width = w_hbm, dst, parts, width

        def at(self, p, shards, rows):
            first = pl.multiple_of(p * 2 * self.width + c * self.width, 128)
            return self.dst.at[shards, rows, pl.ds(first, self.width)]

        def send(self):
            self.first = [[] for _ in range(self.parts)]
            for p in range(self.parts):
                for m in (4, 5, 6, 7, 1, 2, 3, 0):
                    hh, ll, yy = (h + m // 4) % 2, (l + (m // 2) % 2) % 2, (y + m % 2) % 2
                    col = pl.multiple_of(p * WIDTH + (4 * c + 2 * ll + yy) * self.width, 128)
                    src = self.w.at[my_x, pl.ds(col, self.width)]
                    at = self.at(p, s_own, my_x)
                    if m == 0:
                        self.first[p].append(local(src, at))
                    else:
                        self.first[p].append(remote(src, at, dev(x, hh, ll, yy, c)))
            for copies in self.first:
                start(copies)

        def cross(self):
            self.xc, self.m1 = [], []
            for p in range(self.parts):
                wait(self.first[p])
                at = self.at(p, slice(None), my_x)
                self.xc.append(remote(at, at, x_peer))
                self.m1.append(remote(at, at, mate))
                self.xc[p].start()
                self.m1[p].start()

        def share(self):
            self.m2 = []
            for p in range(self.parts):
                self.xc[p].wait()
                at = self.at(p, slice(None), other_x)
                self.m2.append(remote(at, at, mate))
                self.m2[p].start()

        def ready(self):
            wait(self.m1)
            wait(self.m2)

    class RowWeight:
        def __init__(self, w_hbm, dst, rows):
            self.w, self.dst, self.n = w_hbm, dst, rows // 4

        def rows(self, xx):
            return pl.ds(pl.multiple_of(c * 2 * self.n + xx * self.n, 32), self.n)

        def send(self):
            at = self.rows(x)
            self.first = [local(self.w, self.dst.at[h]), remote(self.w.at[at], self.dst.at[h, at], h_peer)]
            start(self.first)

        def cross(self):
            wait(self.first)
            at = self.dst.at[1 - h, self.rows(x)]
            self.xc, self.m1 = remote(at, at, x_peer), remote(at, at, mate)
            self.xc.start()
            self.m1.start()

        def share(self):
            self.xc.wait()
            at = self.dst.at[1 - h, self.rows(1 - x)]
            self.m2 = remote(at, at, mate)
            self.m2.start()

        def ready(self):
            self.m1.wait()
            self.m2.wait()

    def leave(src, out):
        cp = remote(src, out, swap_peer)

        @pl.when(stays)
        def _():
            out[...] = src[...]

        @pl.when(jnp.logical_not(stays))
        def _():
            cp.start()

        return cp

    def start(copies):
        for cp in copies:
            cp.start()

    def wait(copies):
        for cp in copies:
            cp.wait()

    def gather(buf, rows, at=own):
        return [remote(buf.at[at, rows], buf.at[at, rows], peer(j)) for j in (1, 2, 3)]

    mine = pl.ds(4 * c, 4)
    theirs = pl.ds(4 * (1 - c), 4)
    w_sq = ColumnWeight(r.w_sq, r.WQKV, 3, 128)
    w_so = RowWeight(r.w_so, r.WSO, 128)
    w_cq = ColumnWeight(r.w_cq, r.WCQ, 3, 128)
    w_co = RowWeight(r.w_co, r.WCO, 128)
    w_up = ColumnWeight(r.w_up, r.WUP, 1, 512)
    w_dn = RowWeight(r.w_dn, r.WDN, 512)
    swap_start(0)
    w_sq.send()
    swap_start(1)
    swap_start(2)
    swap_wait(0)
    ag_x = gather(r.X, pl.ds(0, ROWS), t)
    start(ag_x)
    w_sq.cross()
    w_so.send()
    swap_wait(1)
    ag_e = gather(r.E, pl.ds(0, ENC))
    start(ag_e)
    w_cq.send()
    w_co.send()
    w_sq.share()
    wait(ag_x)
    x_both = remote(r.X.at[mine], r.X.at[mine], mate)
    x_both.start()
    w_sq.ready()

    lane = lax.broadcasted_iota(jnp.int32, (1, 128), 1)
    heads = [lane // 64 == 0, lane // 64 == 1]

    def head_of(v, hh):
        return jnp.where(heads[hh], v, jnp.zeros_like(v))

    def own_cols(ref, row, width):
        off = [pl.multiple_of((4 * k + own) * width, 128) for k in range(2)]
        return jnp.concatenate([ref[row : row + 1, pl.ds(o, width)] for o in off], 1)

    def blocks(ref, a, width):
        return ref[:, a * HALF : (a + 1) * HALF, :].reshape(4 * HALF, width)

    def shards(ref, rows, cols):
        return ref[rows.start // 128 : rows.stop // 128, :, cols].reshape(rows.stop - rows.start, -1)

    def add_small(row, col, width, value):
        at = slice(0, width) if isinstance(col, int) else pl.ds(pl.multiple_of(col, 128), width)
        r.SM[row : row + 1, at] += value

    def colsum(v):
        return jnp.sum(v, 0, keepdims=True)

    bias_q = own_cols(r.sb, 0, 128)
    bias_v = own_cols(r.sb, 1, 128)
    for i in range(2):
        lhs = r.X[pl.ds(4 * c + 2 * i, 2)].reshape(256, WIDTH)
        for p in range(3):
            out = dg(lhs, r.WQKV[:, :, p * 256 : (p + 1) * 256].reshape(WIDTH, 256), 1, 0)
            if p == 0:
                out = (out + bias_q) * 0.125
            if p == 2:
                out = out + bias_v
            out = out.astype(BF)
            for k in range(2):
                r.QST[k, p, 2 * i : 2 * i + 2] = out[:, k * 128 : (k + 1) * 128].reshape(2, ROWS, 128)
    qkv_x = [remote(r.QST.at[1 - c], r.QKV.at[:, mine], mate)]
    start(qkv_x)
    r.QKV[:, mine] = r.QST[c]

    w_up.send()
    w_dn.send()
    swap_start(3)
    w_so.cross()
    wait(qkv_x)

    def keys(p, n):
        return r.QKV[p, 0 : n // ROWS].reshape(n, 128)

    probs = [r.P0, r.P1, r.P2, r.P3]
    for i in range(4):
        n = (i + 1) * 256
        q = r.QKV[0, 2 * i : 2 * i + 2].reshape(256, 128)
        outs = []
        for hh in range(2):
            s = dg(head_of(q, hh), keys(1, n), 1, 1)
            qpos = lax.broadcasted_iota(jnp.int32, (256, n), 0) + i * 256
            kpos = lax.broadcasted_iota(jnp.int32, (256, n), 1)
            s = jnp.where(kpos <= qpos, s, -1e30)
            e = jnp.exp(s - jnp.max(s, 1, keepdims=True))
            p = (e * (1.0 / jnp.sum(e, 1, keepdims=True))).astype(BF)
            probs[i][hh] = p
            outs.append(dg(p, keys(2, n), 1, 0))
        o = jnp.where(heads[0], outs[0], outs[1])
        r.O[i * 256 : (i + 1) * 256] = o
        r.ATF[2 * i : 2 * i + 2] = o.astype(BF).reshape(2, ROWS, 128)
    my_cols = pl.ds(pl.multiple_of(c * 128, 128), 128)
    att_x = remote(r.ATF.at[theirs], r.ATT.at[:, :, my_cols], mate)
    att_x.start()
    r.ATT[:, :, my_cols] = r.ATF[mine]

    w_so.share()
    w_cq.cross()
    w_so.ready()
    att_x.wait()

    def scatter(a):
        rows = pl.ds(a * HALF, HALF)
        return [remote(r.PB.at[peer_block(j), rows], r.RB.at[j - 1, rows], peer(j)) for j in (1, 2, 3)]

    def summed(a):
        rows = slice(a * HALF, (a + 1) * HALF)
        total = r.PB[own, rows].astype(F32)
        for j in range(3):
            total = total + r.RB[j, rows].astype(F32)
        return total

    def partial(a, lhs, w, contract, chunk=512):
        for n in range(WIDTH // chunk):
            cols = slice(n * chunk, (n + 1) * chunk)
            out = dg(lhs, w(cols), 1, contract)
            r.PB[:, a * HALF : (a + 1) * HALF, cols] = out.astype(BF).reshape(4, HALF, chunk)
        sends = scatter(a)
        start(sends)
        return sends

    def norm(i, rows, hidden):
        centre = hidden - jnp.mean(hidden, -1, keepdims=True)
        rstd = lax.rsqrt(jnp.mean(centre * centre, -1, keepdims=True) + EPS)
        xhat = centre * rstd
        return xhat, rstd, xhat * r.gain[i : i + 1, :] + r.shift[i : i + 1, :]

    def norm_back(i, dy, xhat, rstd):
        add_small(6 + i, 0, WIDTH, colsum(dy * xhat))
        add_small(9 + i, 0, WIDTH, colsum(dy))
        d = dy * r.gain[i : i + 1, :]
        mean_d = jnp.mean(d, -1, keepdims=True)
        mean_dx = jnp.mean(d * xhat, -1, keepdims=True)
        return rstd * (d - mean_d - xhat * mean_dx)

    def half(a):
        return slice(a * HALF, (a + 1) * HALF)

    rs = [
        partial(a, blocks(r.ATT, a, 256), lambda cols: r.WSO[:, :, cols].reshape(256, -1), 0)
        for a in range(2)
    ]
    w_cq.share()
    w_co.cross()
    ag = []
    for a in range(2):
        wait(rs[a])
        hidden = r.X[t, half(a)].astype(F32) + summed(a) + r.sb[2:3, :]
        xhat, rstd, out = norm(0, half(a), hidden)
        r.XH[0, half(a)] = xhat
        r.RSTD[0, half(a)] = rstd
        r.RES[half(a)] = out
        r.F[own, half(a)] = out.astype(BF)
        g = gather(r.F, pl.ds(a * HALF, HALF))
        start(g)
        ag.append(g)

    w_cq.ready()
    wait(ag_e)
    bias_cv = own_cols(r.cb, 1, 128)
    for k in range(2):
        out = dg(
            r.E[...].reshape(4 * ENC, WIDTH),
            r.WCQ[:, :, 256 + k * 256 : 512 + k * 256].reshape(WIDTH, 256),
            1,
            0,
        )
        if k == 1:
            out = out + bias_cv
        r.KVC[mine, :, k * 256 : (k + 1) * 256] = out.astype(BF).reshape(4, ENC, 256)
    kvc_x = remote(r.KVC.at[mine], r.KVC.at[mine], mate)
    kvc_x.start()
    w_co.share()
    swap_wait(2)
    kvc_x.wait()
    w_co.ready()
    bias_cq = own_cols(r.cb, 0, 128)
    limit = r.LENS[1:2, 0:1]
    visible = lax.broadcasted_iota(jnp.int32, (1, 512), 1).astype(F32) < limit

    def enc_keys(part, k):
        return r.KVC[:, :, part * 256 + k * 128 : part * 256 + (k + 1) * 128].reshape(512, 128)

    rs = []
    for a in range(2):
        wait(ag[a])
        q = dg(blocks(r.F, a, WIDTH), r.WCQ[:, :, 0:256].reshape(WIDTH, 256), 1, 0)
        q = ((q + bias_cq) * 0.125).astype(BF)
        r.QC[:, half(a)] = q.reshape(4, HALF, 256)
        for k in range(2):
            outs = []
            for hh in range(2):
                s = dg(head_of(q[:, k * 128 : (k + 1) * 128], hh), enc_keys(0, k), 1, 1)
                s = jnp.where(visible, s, -1e30)
                e = jnp.exp(s - jnp.max(s, 1, keepdims=True))
                p = (e * (1.0 / jnp.sum(e, 1, keepdims=True))).astype(BF)
                r.PC[2 * k + hh, a] = p
                outs.append(dg(p, enc_keys(1, k), 1, 0))
            o = jnp.where(heads[0], outs[0], outs[1])
            r.OC[a, :, k * 128 : (k + 1) * 128] = o
            r.CATT[:, half(a), k * 128 : (k + 1) * 128] = o.astype(BF).reshape(4, HALF, 128)
        rs.append(
            partial(a, blocks(r.CATT, a, 256), lambda cols: r.WCO[:, :, cols].reshape(256, -1), 0)
        )
    w_up.cross()
    ag = []
    for a in range(2):
        wait(rs[a])
        hidden = r.RES[half(a)] + summed(a) + r.cb[2:3, :]
        xhat, rstd, out = norm(1, half(a), hidden)
        r.XH[1, half(a)] = xhat
        r.RSTD[1, half(a)] = rstd
        r.RES2[half(a)] = out
        r.S[own, half(a)] = out.astype(BF)
        g = gather(r.S, pl.ds(a * HALF, HALF))
        start(g)
        ag.append(g)

    w_up.share()
    w_dn.cross()
    w_up.ready()
    bias_up = [r.fb1[0:1, pl.ds(pl.multiple_of((4 * k + own) * 512, 128), 512)] for k in range(2)]
    rs = []
    for a in range(2):
        wait(ag[a])
        lhs = blocks(r.S, a, WIDTH)
        for k in range(2):
            cols = slice(k * 512, (k + 1) * 512)
            u = dg(lhs, r.WUP[:, :, cols].reshape(WIDTH, 512), 1, 0) + bias_up[k]
            cdf = 0.5 + 0.5 * lax.erf(u * 0.7071067811865476)
            r.ACT[:, half(a), cols] = (u * cdf).astype(BF).reshape(4, HALF, 512)
            slope = cdf + u * (jnp.exp(-0.5 * u * u) * 0.3989422804014327)
            r.DGL[a, :, cols] = slope.astype(BF)
        if a == 0:
            w_dn.share()
            w_dn.ready()
        rs.append(
            partial(a, blocks(r.ACT, a, 1024), lambda cols: r.WDN[:, :, cols].reshape(1024, -1), 0)
        )
    ag = []
    seq_limit = r.LENS[0:1, 0:1]
    swap_wait(3)
    x_both.wait()
    for a in range(2):
        wait(rs[a])
        hidden = r.RES2[half(a)] + summed(a) + r.fb2[0:1, :]
        xhat, rstd, out = norm(2, half(a), hidden)
        r.MXS[half(a)] = out.astype(BF)
        place = lax.broadcasted_iota(jnp.int32, (HALF, 1), 0) + (t * ROWS + a * HALF)
        dy = jnp.where(place.astype(F32) < seq_limit, r.DMX[half(a)].astype(F32), 0.0)
        d = norm_back(2, dy, xhat, rstd)
        r.RES[half(a)] = d
        low = d.astype(BF)
        r.DM[own, half(a)] = low
        add_small(16, 0, WIDTH, colsum(low.astype(F32)))
        g = gather(r.DM, pl.ds(a * HALF, HALF))
        start(g)
        ag.append(g)

    mx_out = leave(r.MXS, r.o_mixed)

    y_peer, l_peer = peer(1), peer(2)

    def small_step(i, device):
        cp = remote(r.SM, r.SMR.at[i], device)
        cp.start()
        return cp

    def small_add(i, cp):
        cp.wait()
        r.SM[...] += r.SMR[i]

    def bias_step(i, device):
        cp = remote(r.SB, r.SBR.at[i], device)
        cp.start()
        return cp

    def bias_add(i, cp):
        cp.wait()
        r.SB[...] += r.SBR[i]

    def both(v):
        return v.reshape(-1, v.shape[-1])

    class ColumnGrad:
        def __init__(self, name, out, parts, part=0):
            self.parts, self.out = parts, out
            for key in ("GS", "GR", "GK", "XS", "XR", "HS", "HR", "TS", "T"):
                setattr(self, key, getattr(r, key + "_" + name, None))
            self.part = part

        def compute(self, left, right, col, width):
            for target, k in ((self.GS, 1 - c), (self.GK, c)):
                rhs = right(k)
                for i in range(4):
                    out = dg(left(slice(i * 256, (i + 1) * 256)), rhs, 0, 0)
                    target[2 * i : 2 * i + 2, :, col : col + width] = out.astype(BF).reshape(2, 128, width)

        def compute_own(self, left, right):
            for i in range(4):
                out = dg(left(slice(i * 256, (i + 1) * 256)), right, 0, 0)
                self.GK[2 * i : 2 * i + 2] = out.astype(BF).reshape(2, 128, -1)

        def s0(self):
            self.core = remote(self.GS, self.GR, mate)
            self.core.start()

        def chip(self, shards, rows):
            if self.GR is None:
                return self.GK[shards, rows].astype(F32)
            return self.GK[shards, rows].astype(F32) + self.GR[shards, rows].astype(F32)

        def s1(self):
            if self.GR is not None:
                self.core.wait()
            self.XS[...] = self.chip(slice(None), other_x).astype(BF)
            self.xc = remote(self.XS, self.XR, x_peer)
            self.xc.start()

        def total(self, shards):
            return self.chip(shards, my_x) + self.XR[shards].astype(F32)

        def s2(self):
            self.xc.wait()
            self.HS[...] = self.total(pl.ds(4 * (1 - h), 4)).astype(BF)
            self.hc = remote(self.HS, self.HR, h_peer)
            self.hc.start()

        def s3(self):
            self.hc.wait()
            self.TS[...] = (self.total(pl.ds(4 * h, 4)) + self.HR[...].astype(F32)).astype(BF)
            self.lc = [
                remote(self.TS.at[peer_block(j)], self.T.at[t, my_x], peer(j)) for j in (1, 2, 3)
            ]
            start(self.lc)
            self.T[t, my_x] = self.TS[own]

        def s4(self):
            wait(self.lc)
            part = self.T.at[pl.ds(4 * c, 4), my_x]
            other = self.T.at[pl.ds(4 * c, 4), other_x]
            self.x2 = remote(part, part, x_peer)
            self.m1 = remote(part, part, mate)
            self.m2 = remote(other, other, mate)
            self.x2.start()
            self.m1.start()

        def s5(self):
            self.x2.wait()
            self.m2.start()

        def s6(self):
            self.m1.wait()
            self.m2.wait()
            width = self.T.shape[2] // self.parts
            self.outs = []
            for tt in range(8):
                for p in range(self.parts):
                    at = (p + self.part) * WIDTH + tt * width
                    self.outs.append(
                        local(
                            self.T.at[tt, :, p * width : (p + 1) * width],
                            self.out.at[:, at : at + width],
                        )
                    )
            start(self.outs)

        def s7(self):
            wait(self.outs)

    class RowGrad:
        def __init__(self, name, out):
            self.out = out
            for key in ("GS", "GR", "GK", "XS", "XR", "HS", "HR", "T"):
                setattr(self, key, getattr(r, key + "_" + name))
            self.n = self.GS.shape[0] // 2

        def compute(self, left, right):
            for target, k in ((self.GS, 1 - c), (self.GK, c)):
                lhs = left(k)
                for i in range(2):
                    cols = slice(i * 512, (i + 1) * 512)
                    target[:, cols] = dg(lhs, right(cols), 0, 0).astype(BF)

        def s0(self):
            self.core = remote(self.GS, self.GR, mate)
            self.core.start()

        def rows(self, k):
            return pl.ds(pl.multiple_of(k * self.n, HALF), self.n)

        def s1(self):
            self.core.wait()
            rows = self.rows(1 - x)
            self.XS[...] = (self.GK[rows].astype(F32) + self.GR[rows].astype(F32)).astype(BF)
            self.xc = remote(self.XS, self.XR, x_peer)
            self.xc.start()

        def total(self):
            rows = self.rows(x)
            return self.GK[rows].astype(F32) + self.GR[rows].astype(F32) + self.XR[...].astype(F32)

        def s2(self):
            self.xc.wait()
            self.hc = remote(self.HS, self.HR, h_peer)

            @pl.when(jnp.logical_not(stays))
            def _():
                self.HS[...] = self.total().astype(BF)
                self.hc.start()

        def s3(self):
            part, other = self.T.at[self.rows(x)], self.T.at[self.rows(1 - x)]
            self.x2 = remote(part, part, x_peer)
            self.m1 = remote(part, part, mate)
            self.m2 = remote(other, other, mate)

            @pl.when(jnp.logical_not(stays))
            def _():
                self.hc.wait_send()

            @pl.when(stays)
            def _():
                self.hc.wait_recv()
                self.T[self.rows(x)] = (self.total() + self.HR[...].astype(F32)).astype(BF)
                self.x2.start()
                self.m1.start()

        def s4(self):
            pass

        def s5(self):
            @pl.when(stays)
            def _():
                self.x2.wait()
                self.m2.start()

        def s6(self):
            @pl.when(stays)
            def _():
                self.m1.wait_send()
                self.m2.wait_send()

            @pl.when(jnp.logical_not(stays))
            def _():
                self.m1.wait_recv()
                self.m2.wait_recv()

            self.outs = [local(self.T, self.out)]
            start(self.outs)

        def s7(self):
            wait(self.outs)

    g_dn = RowGrad("DN", r.o_dn)
    g_up = ColumnGrad("UP", r.o_up, 1)
    g_co = RowGrad("CO", r.o_co)
    g_cq = ColumnGrad("CQ", r.o_cq, 3)
    g_so = RowGrad("SO", r.o_so)
    g_sq = [ColumnGrad("SQ%d" % p, r.o_sq, 1, p) for p in range(3)]

    def lanes(ref, k, width, base=0):
        return ref[:, :, pl.ds(pl.multiple_of(base + k * width, 128), width)].reshape(-1, width)

    rs = []
    for a in range(2):
        wait(ag[a])
        lhs = blocks(r.DM, a, WIDTH)
        for k in range(2):
            cols = slice(k * 512, (k + 1) * 512)
            d_act = dg(lhs, r.WDN[k], 1, 1).astype(BF).astype(F32)
            low = (d_act * r.DGL[a, :, cols].astype(F32)).astype(BF)
            r.DUP[:, half(a), cols] = low.reshape(4, HALF, 512)
            r.SM[pl.ds(12 + 2 * k + l, 1), pl.ds(pl.multiple_of(y * 512, 512), 512)] += colsum(low.astype(F32))
        rs.append(
            partial(a, blocks(r.DUP, a, 1024), lambda cols: shards(r.WUP, cols, slice(0, 1024)), 1)
        )
    g_dn.compute(lambda k: lanes(r.ACT, k, 512), lambda cols: r.DM[:, :, cols].reshape(512, -1))
    g_dn.s0()
    g_up.compute(lambda cols: r.S[:, :, cols].reshape(512, -1), lambda k: lanes(r.DUP, k, 512), 0, 512)
    g_up.s0()
    ag = []
    for a in range(2):
        wait(rs[a])
        d = norm_back(1, r.RES[half(a)] + summed(a), r.XH[1, half(a)], r.RSTD[1, half(a)])
        r.RES2[half(a)] = d
        low = d.astype(BF)
        r.DC[own, half(a)] = low
        add_small(5, 0, WIDTH, colsum(low.astype(F32)))
        g = gather(r.DC, pl.ds(a * HALF, HALF))
        start(g)
        ag.append(g)
    g_dn.s1()
    g_up.s1()

    rs = []
    for a in range(2):
        wait(ag[a])
        d_att = dg(blocks(r.DC, a, WIDTH), r.WCO[...].reshape(256, WIDTH), 1, 1).astype(BF)
        for k in range(2):
            cols = slice(k * 128, (k + 1) * 128)
            d_pair = d_att[:, cols]
            o_pair = r.OC[a, :, cols]
            q_pair = blocks(r.QC, a, 256)[:, cols]
            ds, kk, dk, dv = [], [], None, None
            for hh in range(2):
                d_head = head_of(d_pair, hh)
                delta = jnp.sum(d_head.astype(F32) * o_pair, 1, keepdims=True)
                p = r.PC[2 * k + hh, a]
                d_scores = (p.astype(F32) * (dg(d_head, enc_keys(1, k), 1, 1) - delta)).astype(BF)
                ds.append(dg(d_scores, enc_keys(0, k), 1, 0))
                new_dk = dg(d_scores, head_of(q_pair, hh), 0, 0)
                new_dv = dg(p, d_head, 0, 0)
                dk = new_dk if dk is None else dk + new_dk
                dv = new_dv if dv is None else dv + new_dv
            dq = jnp.where(heads[0], ds[0], ds[1]).astype(BF) * 0.125
            dq = dq.astype(BF)
            r.DQC[:, half(a), cols] = dq.reshape(4, HALF, 128)
            add_small(3, (4 * k + own) * 128, 128, colsum(dq.astype(F32)))
            if a == 0:
                r.DKV[:, cols] = dk
                r.DKV[:, 256 + k * 128 : 384 + k * 128] = dv
            else:
                r.DKV[:, cols] += dk
                r.DKV[:, 256 + k * 128 : 384 + k * 128] += dv
        rs.append(
            partial(a, blocks(r.DQC, a, 256), lambda cols: shards(r.WCQ, cols, slice(0, 256)), 1)
        )
    my_enc = pl.ds(pl.multiple_of(c * 256, 256), 256)
    their_enc = pl.ds(pl.multiple_of((1 - c) * 256, 256), 256)
    r.DKS[...] = r.DKV[their_enc].astype(BF).reshape(4, ENC, 512)
    dk_x = remote(r.DKS, r.DKR, mate)
    dk_x.start()
    g_co.compute(lambda k: lanes(r.CATT, k, 128), lambda cols: r.DC[:, :, cols].reshape(512, -1))
    g_co.s0()
    ag = []
    for a in range(2):
        wait(rs[a])
        d = norm_back(0, r.RES2[half(a)] + summed(a), r.XH[0, half(a)], r.RSTD[0, half(a)])
        r.RES[half(a)] = d
        low = d.astype(BF)
        r.DM[own, half(a)] = low
        add_small(2, 0, WIDTH, colsum(low.astype(F32)))
        g = gather(r.DM, pl.ds(a * HALF, HALF))
        start(g)
        ag.append(g)
    g_dn.s2()
    g_up.s2()
    dk_x.wait()
    low = (r.DKV[my_enc] + r.DKR[...].reshape(256, 512).astype(F32)).astype(BF)
    r.DKL[...] = low.reshape(4, ENC, 512)
    dv_sum = colsum(low[:, 256:512].astype(F32))
    for k in range(2):
        add_small(4, (4 * k + own) * 128, 128, dv_sum[:, k * 128 : (k + 1) * 128])
    for n in range(2):
        cols = slice(n * 512, (n + 1) * 512)
        out = dg(low, shards(r.WCQ, cols, slice(256, 768)), 1, 1)
        r.PBE[:, :, cols] = out.astype(BF).reshape(4, ENC, 512)
    rs_e = [remote(r.PBE.at[peer_block(j)], r.RBE.at[j - 1], peer(j)) for j in (1, 2, 3)]
    start(rs_e)
    g_co.s1()
    g_cq.compute(lambda cols: r.F[:, :, cols].reshape(512, -1), lambda k: lanes(r.DQC, k, 128), 0, 128)
    for p in range(2):
        g_cq.compute(
            lambda cols: r.E[:, :, cols].reshape(256, -1),
            lambda k, p=p: lanes(r.DKL, k, 128, 256 * p),
            128 + 128 * p,
            128,
        )
    g_cq.s0()

    do_x = []
    for a in range(2):
        wait(ag[a])
        d_att = dg(blocks(r.DM, a, WIDTH), r.WSO[...].reshape(256, WIDTH), 1, 1).astype(BF)
        mine_d = jnp.where(c == 0, d_att[:, 0:128], d_att[:, 128:256])
        theirs_d = jnp.where(c == 0, d_att[:, 128:256], d_att[:, 0:128])
        r.DATS[:, half(a)] = theirs_d.reshape(4, HALF, 128)
        r.DO[mine, half(a)] = mine_d.reshape(4, HALF, 128)
        rows = pl.ds(a * HALF, HALF)
        do_x.append(remote(r.DATS.at[:, rows], r.DO.at[mine, rows], mate))
        do_x[a].start()
    small = small_step(0, mate)
    g_so.compute(lambda k: lanes(r.ATT, k, 128), lambda cols: r.DM[:, :, cols].reshape(512, -1))
    g_so.s0()
    g_cq.s1()
    small_add(0, small)
    small = small_step(1, y_peer)
    g_dn.s3()
    g_up.s3()
    wait(rs_e)
    d_enc = r.PBE[own].astype(F32)
    for j in range(3):
        d_enc = d_enc + r.RBE[j].astype(F32)
    r.DES[...] = d_enc.astype(BF)
    de_out = leave(r.DES, r.o_denc)
    small_add(1, small)
    small = small_step(2, l_peer)

    wait(do_x)
    r.DKVS[...] = jnp.zeros_like(r.DKVS)
    for i in range(4):
        n = (i + 1) * 256
        q = r.QKV[0, 2 * i : 2 * i + 2].reshape(256, 128)
        d_pair = r.DO[2 * i : 2 * i + 2].reshape(256, 128)
        o_pair = r.O[i * 256 : (i + 1) * 256]
        dqs, dk, dv = [], None, None
        for hh in range(2):
            d_head = head_of(d_pair, hh)
            delta = jnp.sum(d_head.astype(F32) * o_pair, 1, keepdims=True)
            p = probs[i][hh]
            d_scores = (p.astype(F32) * (dg(d_head, keys(2, n), 1, 1) - delta)).astype(BF)
            dqs.append(dg(d_scores, keys(1, n), 1, 0))
            new_dk = dg(d_scores, head_of(q, hh), 0, 0)
            new_dv = dg(p, d_head, 0, 0)
            dk = new_dk if dk is None else dk + new_dk
            dv = new_dv if dv is None else dv + new_dv
        dq = (jnp.where(heads[0], dqs[0], dqs[1]).astype(BF) * 0.125).astype(BF)
        r.DJN[0, 2 * i : 2 * i + 2] = dq.reshape(2, ROWS, 128)
        r.SB[0:1, pl.ds(pl.multiple_of(t * 128, 128), 128)] += colsum(dq.astype(F32))
        r.DKVS[0, 0:n] += dk
        r.DKVS[1, 0:n] += dv
    r.DJN[1] = r.DKVS[0].astype(BF).reshape(8, ROWS, 128)
    low = r.DKVS[1].astype(BF)
    r.DJN[2] = low.reshape(8, ROWS, 128)
    r.SB[1:2, pl.ds(pl.multiple_of(t * 128, 128), 128)] = colsum(low.astype(F32))
    dj_x = []
    for p in range(3):
        at = pl.ds(pl.multiple_of(p * 256 + c * 128, 128), 128)
        dj_x.append(remote(r.DJN.at[p, theirs], r.DJ.at[:, :, at], mate))
        dj_x[p].start()
        r.DJ[:, :, at] = r.DJN[p, mine]
    for p in range(3):
        g_sq[p].compute_own(lambda cols: r.X[:, :, cols].reshape(1024, -1), r.DJN[p].reshape(1024, 128))
        g_sq[p].s1()
    wait(dj_x)
    rs = [
        partial(a, blocks(r.DJ, a, 768), lambda cols: shards(r.WQKV, cols, slice(0, 768)), 1)
        for a in range(2)
    ]
    bias = bias_step(0, mate)
    small_add(2, small)
    small = small_step(3, x_peer)
    g_dn.s4()
    g_up.s4()
    g_co.s2()
    g_cq.s2()
    g_so.s1()
    bias_add(0, bias)
    bias = bias_step(1, y_peer)
    for g in g_sq:
        g.s2()
    small_add(3, small)
    small = small_step(4, h_peer)
    for a in range(2):
        wait(rs[a])
        r.DTS[half(a)] = (r.RES[half(a)] + summed(a)).astype(BF)
    dt_out = leave(r.DTS, r.o_dtok)
    bias_add(1, bias)
    bias = bias_step(2, l_peer)
    g_so.s2()
    g_dn.s5()
    g_up.s5()
    g_co.s3()
    g_cq.s3()
    for g in g_sq:
        g.s3()
    bias_add(2, bias)
    bias = bias_step(3, x_peer)
    g_so.s3()
    g_co.s5()
    g_cq.s4()
    for g in g_sq:
        g.s4()
    small_add(4, small)
    g_dn.s6()
    g_up.s6()
    bias_add(3, bias)
    bias = bias_step(4, h_peer)
    g_so.s5()
    g_cq.s5()
    for g in g_sq:
        g.s5()
    g_co.s6()
    g_so.s6()
    g_cq.s6()
    bias_add(4, bias)
    for g in g_sq:
        g.s6()
    r.SM[0:2, :] = r.SB[0:2, :]
    r.o_small[...] = r.SM[...]

    @pl.when(jnp.logical_not(stays))
    def _():
        mx_out.wait()
        de_out.wait()
        dt_out.wait()

    for g in (g_dn, g_up, g_co, g_cq, g_so, *g_sq):
        g.s7()


def on_chip(*args):
    (tokens, encoder, seq_len, enc_len, d_mixed, *rest) = args
    *mats, self_bias, cross_bias, norm_gain, norm_bias, fc1_bias, fc2_bias = rest
    anywhere = pl.BlockSpec(memory_space=pl.ANY)
    vmem = pl.BlockSpec(memory_space=pltpu.VMEM)
    smem = pl.BlockSpec(memory_space=pltpu.SMEM)
    shapes = [
        ((ROWS, WIDTH), BF),
        ((ROWS, WIDTH), BF),
        ((ENC, WIDTH), BF),
        ((128, 3 * WIDTH), BF),
        ((128, WIDTH), BF),
        ((128, 3 * WIDTH), BF),
        ((128, WIDTH), BF),
        ((128, HIDDEN), BF),
        ((512, WIDTH), BF),
        ((24, WIDTH), F32),
    ]
    outs = pl.pallas_call(
        layer_kernel,
        out_shape=[jax.ShapeDtypeStruct(s, d) for s, d in shapes],
        in_specs=[anywhere, anywhere, smem, smem, anywhere] + [anywhere] * 6 + [vmem] * 6,
        out_specs=[vmem] * 3 + [anywhere] * 6 + [vmem],
        scratch_shapes=[pltpu.VMEM(s, d) for s, d in SCRATCH.values()]
        + [
            pltpu.SemaphoreType.DMA((N_REMOTE,)),
            pltpu.SemaphoreType.DMA((N_REMOTE,)),
            pltpu.SemaphoreType.DMA((N_LOCAL,)),
        ],
        compiler_params=pltpu.CompilerParams(
            collective_id=0, has_side_effects=True, vmem_limit_bytes=VMEM_BYTES
        ),
        cost_estimate=pl.CostEstimate(
            flops=16 * 10**9, bytes_accessed=16 * 2**20, transcendentals=8 * 2**20
        ),
    )(
        tokens, encoder, seq_len, enc_len, d_mixed, *mats,
        self_bias, cross_bias, norm_gain, norm_bias,
        fc1_bias.reshape(1, -1), fc2_bias.reshape(1, -1),
    )
    steps = 4

    def rows_of(shape):
        return pl.BlockSpec((shape[0] // steps, shape[1]), lambda i: (i, 0))

    def whole(shape):
        return pl.BlockSpec(shape, lambda i: (0, 0))

    wide = [(s, BF if k == 0 else F32) for k, (s, _) in enumerate(shapes[:-1])]
    flat = [((3, WIDTH), F32)] * 4 + [((1, HIDDEN), F32), ((1, WIDTH), F32)]
    *results, fc1_sum, fc2_sum = pl.pallas_call(
        widen_kernel,
        grid=(steps,),
        out_shape=[jax.ShapeDtypeStruct(s, d) for s, d in wide + flat],
        in_specs=[rows_of(s) for s, _ in shapes[:-1]] + [whole(shapes[-1][0])],
        out_specs=[rows_of(s) for s, _ in wide] + [whole(s) for s, _ in flat],
        compiler_params=pltpu.CompilerParams(vmem_limit_bytes=32 * 2**20),
    )(*outs)
    return (*results, fc1_sum.reshape(-1), fc2_sum.reshape(-1))


def widen_kernel(*refs):
    n = len(OUT_NAMES)
    small, flat = refs[n - 1], refs[2 * n - 1 :]
    for src, dst in zip(refs[: n - 1], refs[n:]):
        dst[...] = src[...].astype(dst.dtype)
    for k in range(4):
        flat[k][...] = small[3 * k : 3 * k + 3, :]
        flat[4][0:1, k * WIDTH : (k + 1) * WIDTH] = small[12 + k : 13 + k, :]
    flat[5][...] = small[16:17, :]


def fits(mesh, tokens, encoder, self_qkv, fc1_weight):
    return (
        (mesh.shape["rep"], mesh.shape["shard"]) == (4, 8)
        and tokens.shape == (32 * ROWS, WIDTH)
        and encoder.shape == (32 * ENC, WIDTH)
        and self_qkv.shape == (WIDTH, 3 * WIDTH)
        and fc1_weight.shape == (WIDTH, HIDDEN)
    )


def solution(mesh):
    def placed(body):
        return jax.shard_map(
            body,
            mesh=mesh,
            in_specs=(
                P(("rep", "shard"), None),
                P(("rep", "shard"), None),
                P("rep"),
                P("rep"),
                P(("rep", "shard"), None),
                P("shard", None),
                P("shard", None),
                P("shard", None),
                P("shard", None),
                P("shard", None),
                P("shard", None),
                P(),
                P(),
                P(),
                P(),
                P(),
                P(),
            ),
            out_specs=(
                P(("rep", "shard"), None),
                P(("rep", "shard"), None),
                P(("rep", "shard"), None),
                P("shard", None),
                P("shard", None),
                P("shard", None),
                P("shard", None),
                P("shard", None),
                P("shard", None),
                P(),
                P(),
                P(),
                P(),
                P(),
                P(),
            ),
            check_vma=False,
        )

    def run(*args):
        fast = fits(mesh, args[0], args[1], args[5], args[9])
        return placed(on_chip if fast else local)(*args)

    return run
```

```python
from functools import partial

import jax
import jax.numpy as jnp
from jax import lax
from jax.experimental import pallas as pl
from jax.experimental.pallas import tpu as pltpu
from jax.sharding import PartitionSpec as P

HEADS = 16
HEAD = 64


def for_sending(array):
    return jax.tree.map(lambda a: a.astype(jnp.bfloat16) if a.dtype == jnp.float32 else a, array)


def layer_norm(hidden, gain_row, shift_row):
    centre = hidden - jnp.mean(hidden, -1, keepdims=True)
    spread = jnp.mean(centre * centre, -1, keepdims=True)
    return centre * lax.rsqrt(spread + 1e-05) * gain_row + shift_row


def exact_gelu(values):
    return jax.nn.gelu(values, approximate=False)


def contract_rows(left, right):
    return lax.dot_general(
        left, right, (((0,), (0,)), ((), ())), preferred_element_type=jnp.float32
    )


def back_dot(grad_rows, weight):
    return lax.dot_general(
        grad_rows, weight, (((1,), (1,)), ((), ())), preferred_element_type=jnp.float32
    )


def causal_mask(query_pos, key_pos):
    return key_pos[None, :] <= query_pos[:, None]


def enc_visible(query_pos, key_pos, enc_limit):
    return jnp.broadcast_to((key_pos < enc_limit)[None, :], (query_pos.shape[0], key_pos.shape[0]))


def only_live(step_fn, live_fn):

    def wrapped(totals, block_in, offset):
        return lax.cond(
            live_fn(block_in, offset), lambda: step_fn(totals, block_in, offset), lambda: totals
        )

    return wrapped


def self_fold(key_pair, step_fn, start_state, store):
    return step_fn(
        start_state,
        jax.tree.map(
            lambda a: lax.all_gather(a, "shard", axis=0, tiled=True), for_sending(key_pair)
        ),
        jnp.int32(0),
    )


def cross_fold(key_pair, step_fn, start_state, store):
    return step_fn(
        start_state,
        jax.tree.map(
            lambda a: lax.all_gather(a, "shard", axis=0, tiled=True), for_sending(key_pair)
        ),
        jnp.int32(0),
    )


def keys_live(query_pos, allowed_fn):

    def live_fn(block_in, offset):
        key_pos = jnp.arange(block_in[0].shape[0], dtype=jnp.int32)
        return jnp.any(allowed_fn(query_pos, key_pos))

    return live_fn


def head_scores(query_heads, query_pos, key_block, allowed_fn):
    key_count = key_block.shape[0]
    key_pos = jnp.arange(key_count, dtype=jnp.int32)
    scores = jnp.einsum(
        "qhd,khd->hqk",
        query_heads,
        key_block.reshape(key_count, HEADS, HEAD),
        preferred_element_type=jnp.float32,
    )
    return (scores, allowed_fn(query_pos, key_pos)[None])


def forward_pass(query_part, query_pos, key_pair, allowed_fn, folder):
    query_count = query_part.shape[0]
    query_heads = query_part.reshape(query_count, HEADS, HEAD)
    live_fn = keys_live(query_pos, allowed_fn)

    def stat_step(totals, block_in, offset):
        highest, mass = totals
        scores, allowed = head_scores(query_heads, query_pos, block_in[0], allowed_fn)
        masked = jnp.where(allowed, scores, -1e30)
        raised = jnp.maximum(highest, jnp.max(masked, -1))
        fresh = jnp.sum(jnp.where(allowed, jnp.exp(masked - raised[:, :, None]), 0.0), -1)
        return (raised, fresh)

    start_state = (
        jnp.full((HEADS, query_count), -1e30, jnp.float32),
        jnp.zeros((HEADS, query_count), jnp.float32),
    )
    highest, mass = folder(key_pair, only_live(stat_step, live_fn), start_state, None)
    log_total = highest + jnp.log(mass)

    def out_step(totals, block_in, offset):
        scores, allowed = head_scores(query_heads, query_pos, block_in[0], allowed_fn)
        weights_low = jnp.where(allowed, jnp.exp(scores - log_total[:, :, None]), 0.0).astype(
            jnp.bfloat16
        )
        value_heads = block_in[1].reshape(block_in[1].shape[0], HEADS, HEAD)
        return jnp.einsum(
            "hqk,khd->qhd", weights_low, value_heads, preferred_element_type=jnp.float32
        )

    summed = folder(
        key_pair,
        only_live(out_step, live_fn),
        jnp.zeros((query_count, HEADS, HEAD), jnp.float32),
        None,
    )
    return (log_total.T, summed)


def query_step(query_part, query_pos, allowed_fn, log_rows, delta_rows, d_out):
    query_count = query_part.shape[0]
    query_heads = query_part.reshape(query_count, HEADS, HEAD)
    grad_heads = d_out.reshape(query_count, HEADS, HEAD)
    log_total = log_rows.T
    correction = delta_rows.T

    def grad_step(totals, block_in, offset):
        key_block, value_block = block_in
        key_count = key_block.shape[0]
        scores, allowed = head_scores(query_heads, query_pos, key_block, allowed_fn)
        probs = jnp.where(allowed, jnp.exp(scores - log_total[:, :, None]), 0.0)
        d_probs = jnp.einsum(
            "qhd,khd->hqk",
            grad_heads,
            value_block.reshape(key_count, HEADS, HEAD),
            preferred_element_type=jnp.float32,
        )
        d_scores = (probs * (d_probs - correction[:, :, None])).astype(jnp.bfloat16)
        return jnp.einsum(
            "hqk,khd->qhd",
            d_scores,
            key_block.reshape(key_count, HEADS, HEAD),
            preferred_element_type=jnp.float32,
        )

    return only_live(grad_step, keys_live(query_pos, allowed_fn))


def query_grad(query_part, query_pos, key_pair, allowed_fn, folder, log_rows, delta_rows, d_out):
    query_count = query_part.shape[0]
    step_fn = query_step(query_part, query_pos, allowed_fn, log_rows, delta_rows, d_out)
    return folder(key_pair, step_fn, jnp.zeros((query_count, HEADS, HEAD), jnp.float32), None)


def key_step(own_keys, own_values, key_pos, allowed_fn, log_all, delta_all):
    key_count = own_keys.shape[0]
    key_heads = own_keys.reshape(key_count, HEADS, HEAD)
    value_heads = own_values.reshape(key_count, HEADS, HEAD)

    def step_fn(totals, block_in, offset):
        query_block, grad_block = block_in
        query_count = query_block.shape[0]
        query_pos = jnp.arange(query_count, dtype=jnp.int32)
        log_part = log_all.T
        delta_part = delta_all.T
        query_heads = query_block.reshape(query_count, HEADS, HEAD)
        grad_heads = grad_block.reshape(query_count, HEADS, HEAD)
        scores = jnp.einsum(
            "qhd,khd->hqk", query_heads, key_heads, preferred_element_type=jnp.float32
        )
        allowed = allowed_fn(query_pos, key_pos)[None]
        probs = jnp.where(allowed, jnp.exp(scores - log_part[:, :, None]), 0.0)
        d_values = jnp.einsum(
            "hqk,qhd->khd",
            probs.astype(jnp.bfloat16),
            grad_heads,
            preferred_element_type=jnp.float32,
        )
        d_probs = jnp.einsum(
            "qhd,khd->hqk", grad_heads, value_heads, preferred_element_type=jnp.float32
        )
        d_scores = (probs * (d_probs - delta_part[:, :, None])).astype(jnp.bfloat16)
        d_keys = jnp.einsum(
            "hqk,qhd->khd", d_scores, query_heads, preferred_element_type=jnp.float32
        )
        return (d_keys, d_values)

    def live_fn(block_in, offset):
        query_pos = jnp.arange(block_in[0].shape[0], dtype=jnp.int32)
        return jnp.any(allowed_fn(query_pos, key_pos))

    return only_live(step_fn, live_fn)


def column_sum(values):
    return jnp.sum(values.astype(jnp.float32), 0)


def local(
    tokens,
    encoder,
    seq_len,
    enc_len,
    d_mixed,
    self_qkv,
    self_out,
    cross_qkv,
    cross_out,
    fc1_weight,
    fc2_weight,
    self_bias,
    cross_bias,
    norm_gain,
    norm_bias,
    fc1_bias,
    fc2_bias,
):
    model_width = tokens.shape[1]
    tok_rows = tokens.shape[0]
    enc_rows = encoder.shape[0]
    device_at = lax.axis_index("shard")
    positions = device_at * tok_rows + jnp.arange(tok_rows, dtype=jnp.int32)
    enc_positions = device_at * enc_rows + jnp.arange(enc_rows, dtype=jnp.int32)
    seq_limit = seq_len[0]
    visible = partial(enc_visible, enc_limit=enc_len[0])
    w_sq, w_so = (
        lax.all_gather(self_qkv, "shard", axis=0, tiled=True),
        lax.all_gather(self_out, "shard", axis=0, tiled=True),
    )
    joined = jnp.dot(tokens, w_sq, preferred_element_type=jnp.float32)
    query_s = ((joined[:, :model_width] + self_bias[0]) * 0.125).astype(jnp.bfloat16)
    key_s = joined[:, model_width : 2 * model_width].astype(jnp.bfloat16)
    value_s = (joined[:, 2 * model_width :] + self_bias[1]).astype(jnp.bfloat16)
    self_lse, self_summed = forward_pass(
        query_s, positions, (key_s, value_s), causal_mask, self_fold
    )
    attended = self_summed.reshape(tok_rows, model_width).astype(jnp.bfloat16)
    branch = jnp.dot(attended, w_so, preferred_element_type=jnp.float32) + self_bias[2]
    first_norm, first_pull = jax.vjp(
        layer_norm, tokens.astype(jnp.float32) + branch, norm_gain[0], norm_bias[0]
    )
    w_cq, w_co = (
        lax.all_gather(cross_qkv, "shard", axis=0, tiled=True),
        lax.all_gather(cross_out, "shard", axis=0, tiled=True),
    )
    first_low = first_norm.astype(jnp.bfloat16)
    query_c = (
        (
            jnp.dot(first_low, w_cq[:, :model_width], preferred_element_type=jnp.float32)
            + cross_bias[0]
        )
        * 0.125
    ).astype(jnp.bfloat16)
    enc_proj = jnp.dot(encoder, w_cq[:, model_width:], preferred_element_type=jnp.float32)
    key_c = enc_proj[:, :model_width].astype(jnp.bfloat16)
    value_c = (enc_proj[:, model_width:] + cross_bias[1]).astype(jnp.bfloat16)
    cross_lse, cross_summed = forward_pass(
        query_c, positions, (key_c, value_c), visible, cross_fold
    )
    cross_att = cross_summed.reshape(tok_rows, model_width).astype(jnp.bfloat16)
    branch_c = jnp.dot(cross_att, w_co, preferred_element_type=jnp.float32) + cross_bias[2]
    second_norm, second_pull = jax.vjp(
        layer_norm, first_norm + branch_c, norm_gain[1], norm_bias[1]
    )
    w_up, w_down = (
        lax.all_gather(fc1_weight, "shard", axis=0, tiled=True),
        lax.all_gather(fc2_weight, "shard", axis=0, tiled=True),
    )
    second_low = second_norm.astype(jnp.bfloat16)
    upward = jnp.dot(second_low, w_up, preferred_element_type=jnp.float32) + fc1_bias
    activated, gelu_pull = jax.vjp(exact_gelu, upward)
    act_low = activated.astype(jnp.bfloat16)
    branch_m = jnp.dot(act_low, w_down, preferred_element_type=jnp.float32) + fc2_bias
    output, third_pull = jax.vjp(layer_norm, second_norm + branch_m, norm_gain[2], norm_bias[2])
    valid = (positions < seq_limit).astype(jnp.float32)[:, None]
    d_third, d_gain3, d_shift3 = third_pull(d_mixed.astype(jnp.float32) * valid)
    d_branch_m = d_third.astype(jnp.bfloat16)
    g_down = contract_rows(act_low, d_branch_m)
    d_act = back_dot(d_branch_m, w_down).astype(jnp.bfloat16)
    (d_up,) = gelu_pull(d_act.astype(jnp.float32))
    d_up_low = d_up.astype(jnp.bfloat16)
    g_up = contract_rows(second_low, d_up_low)
    d_second = d_third + back_dot(d_up_low, w_up)
    d_hidden2, d_gain2, d_shift2 = second_pull(d_second)
    d_branch_c = d_hidden2.astype(jnp.bfloat16)
    g_co = contract_rows(cross_att, d_branch_c)
    d_cross_att = back_dot(d_branch_c, w_co).astype(jnp.bfloat16)
    cross_delta = jnp.einsum(
        "qhd,qhd->qh", d_cross_att.reshape(tok_rows, HEADS, HEAD).astype(jnp.float32), cross_summed
    )
    d_query_c = query_grad(
        query_c,
        positions,
        (key_c, value_c),
        visible,
        cross_fold,
        cross_lse,
        cross_delta,
        d_cross_att,
    )
    d_query_cs = d_query_c.reshape(tok_rows, model_width).astype(jnp.bfloat16) * 0.125
    d_first = d_hidden2 + back_dot(d_query_cs, w_cq[:, :model_width])
    d_hidden1, d_gain1, d_shift1 = first_pull(d_first)
    d_branch = d_hidden1.astype(jnp.bfloat16)
    g_so = contract_rows(attended, d_branch)
    d_attended = back_dot(d_branch, w_so).astype(jnp.bfloat16)
    self_delta = jnp.einsum(
        "qhd,qhd->qh", d_attended.reshape(tok_rows, HEADS, HEAD).astype(jnp.float32), self_summed
    )
    stats = (
        lax.all_gather(self_lse, "shard", axis=0, tiled=True),
        lax.all_gather(self_delta, "shard", axis=0, tiled=True),
        lax.all_gather(cross_lse, "shard", axis=0, tiled=True),
        lax.all_gather(cross_delta, "shard", axis=0, tiled=True),
    )
    tok_zero = jnp.zeros((tok_rows, HEADS, HEAD), jnp.float32)
    query_side = query_step(query_s, positions, causal_mask, self_lse, self_delta, d_attended)
    key_side = key_step(key_s, value_s, positions, causal_mask, stats[0], stats[1])
    offset = jnp.int32(0)
    d_query_part = query_side(
        tok_zero,
        (
            lax.all_gather(key_s, "shard", axis=0, tiled=True),
            lax.all_gather(value_s, "shard", axis=0, tiled=True),
        ),
        offset,
    )
    d_key_part, d_value_part = key_side(
        (tok_zero, tok_zero),
        (
            lax.all_gather(query_s, "shard", axis=0, tiled=True),
            lax.all_gather(d_attended, "shard", axis=0, tiled=True),
        ),
        offset,
    )
    enc_zero = jnp.zeros((enc_rows, HEADS, HEAD), jnp.float32)
    d_key_c, d_value_c = key_step(key_c, value_c, enc_positions, visible, stats[2], stats[3])(
        (enc_zero, enc_zero),
        (
            lax.all_gather(query_c, "shard", axis=0, tiled=True),
            lax.all_gather(d_cross_att, "shard", axis=0, tiled=True),
        ),
        jnp.int32(0),
    )
    d_qs = d_query_part.reshape(tok_rows, model_width).astype(jnp.bfloat16) * 0.125
    d_ks = d_key_part.reshape(tok_rows, model_width).astype(jnp.bfloat16)
    d_vs = d_value_part.reshape(tok_rows, model_width).astype(jnp.bfloat16)
    d_joined = jnp.concatenate([d_qs, d_ks, d_vs], 1)
    g_sq = contract_rows(tokens, d_joined)
    d_tokens = d_hidden1 + back_dot(d_joined, w_sq)
    d_kc = d_key_c.reshape(enc_rows, model_width).astype(jnp.bfloat16)
    d_vc = d_value_c.reshape(enc_rows, model_width).astype(jnp.bfloat16)
    d_enc_proj = jnp.concatenate([d_kc, d_vc], 1)
    g_cq = jnp.concatenate(
        [contract_rows(first_low, d_query_cs), contract_rows(encoder, d_enc_proj)], 1
    )
    d_encoder = back_dot(d_enc_proj, w_cq[:, model_width:])
    d_self_bias = jnp.stack([column_sum(d_qs), column_sum(d_vs), column_sum(d_branch)])
    d_cross_bias = jnp.stack([column_sum(d_query_cs), column_sum(d_vc), column_sum(d_branch_c)])
    d_norm_gain = jnp.stack([d_gain1, d_gain2, d_gain3])
    d_norm_bias = jnp.stack([d_shift1, d_shift2, d_shift3])
    d_fc1_bias = column_sum(d_up_low)
    d_fc2_bias = column_sum(d_branch_m)
    row_grads = (
        lax.psum_scatter(g_sq, "shard", scatter_dimension=0, tiled=True),
        lax.psum_scatter(g_so, "shard", scatter_dimension=0, tiled=True),
        lax.psum_scatter(g_cq, "shard", scatter_dimension=0, tiled=True),
        lax.psum_scatter(g_co, "shard", scatter_dimension=0, tiled=True),
        lax.psum_scatter(g_up, "shard", scatter_dimension=0, tiled=True),
        lax.psum_scatter(g_down, "shard", scatter_dimension=0, tiled=True),
    )
    row_grads = lax.psum(
        (row_grads[0], row_grads[1], row_grads[2], row_grads[3], row_grads[4], row_grads[5]), "rep"
    )
    small_sums = lax.psum(
        (d_self_bias, d_cross_bias, d_norm_gain, d_norm_bias, d_fc1_bias, d_fc2_bias),
        ("rep", "shard"),
    )
    return (
        output.astype(jnp.bfloat16),
        d_tokens,
        d_encoder,
        row_grads[0],
        row_grads[1],
        row_grads[2],
        row_grads[3],
        row_grads[4],
        row_grads[5],
        small_sums[0],
        small_sums[1],
        small_sums[2],
        small_sums[3],
        small_sums[4],
        small_sums[5],
    )


MESH = pl.DeviceIdType.MESH
BF = jnp.bfloat16
F32 = jnp.float32
EPS = 1e-05


def dg(left, right, cl, cr):
    return lax.dot_general(
        left, right, (((cl,), (cr,)), ((), ())), preferred_element_type=F32
    )


class Names:
    pass


WIDTH = 1024
HIDDEN = 4096
ROWS = 128
ENC = 64
HALF = 64
NSUB = 4
SUB = ROWS // NSUB

SCRATCH = {
    "X": ((8, ROWS, WIDTH), BF),
    "E": ((4, ENC, WIDTH), BF),
    "DMX": ((ROWS, WIDTH), BF),
    "LSRC": ((8, 128), F32),
    "LENS": ((8, 128), F32),
    "WQKV": ((8, 128, 768), BF),
    "WSO": ((2, 128, WIDTH), BF),
    "WCQ": ((8, 128, 768), BF),
    "WCO": ((2, 128, WIDTH), BF),
    "WUP": ((8, 128, 1024), BF),
    "WDN": ((2, 512, WIDTH), BF),
    "QST": ((2, 3, 4, ROWS, 128), BF),
    "QKV": ((3, 8, ROWS, 128), BF),
    "P0": ((2, 256, 256), BF),
    "P1": ((2, 256, 512), BF),
    "P2": ((2, 256, 768), BF),
    "P3": ((2, 256, 1024), BF),
    "O": ((1024, 128), F32),
    "ATF": ((8, ROWS, 128), BF),
    "ATT": ((4, ROWS, 256), BF),
    "PB": ((4, ROWS, WIDTH), BF),
    "RB": ((3, ROWS, WIDTH), BF),
    "PBE": ((4, ENC, WIDTH), BF),
    "RBE": ((3, ENC, WIDTH), BF),
    "F": ((4, ROWS, WIDTH), BF),
    "S": ((4, ROWS, WIDTH), BF),
    "DM": ((4, ROWS, WIDTH), BF),
    "DC": ((4, ROWS, WIDTH), BF),
    "DB": ((4, ROWS, WIDTH), BF),
    "RES": ((ROWS, WIDTH), F32),
    "RES2": ((ROWS, WIDTH), F32),
    "XH": ((2, ROWS, WIDTH), F32),
    "RSTD": ((2, ROWS, 1), F32),
    "QC": ((4, ROWS, 256), BF),
    "KVC": ((8, ENC, 512), BF),
    "PC": ((4, NSUB, 4 * SUB, 512), BF),
    "OC": ((NSUB, 4 * SUB, 256), F32),
    "CATT": ((4, ROWS, 256), BF),
    "ACT": ((4, ROWS, 1024), BF),
    "DGL": ((NSUB, 4 * SUB, 1024), BF),
    "DUP": ((4, ROWS, 1024), BF),
    "DQC": ((4, ROWS, 256), BF),
    "DKV": ((512, 512), F32),
    "DKS": ((4, ENC, 512), BF),
    "DKR": ((4, ENC, 512), BF),
    "DKL": ((4, ENC, 512), BF),
    "DATS": ((4, ROWS, 128), BF),
    "DO": ((8, ROWS, 128), BF),
    "DKVS": ((2, 1024, 128), F32),
    "DJN": ((3, 8, ROWS, 128), BF),
    "DJ": ((4, ROWS, 768), BF),
    "MXS": ((ROWS, WIDTH), BF),
    "DTS": ((ROWS, WIDTH), BF),
    "DES": ((ENC, WIDTH), BF),
    "SM": ((24, WIDTH), F32),
    "SMR": ((5, 24, WIDTH), F32),
    "SB": ((8, WIDTH), F32),
    "SBR": ((5, 8, WIDTH), F32),
}
for _name, _rows in (("SO", 128), ("CO", 128), ("DN", 512)):
    SCRATCH["GS_" + _name] = ((_rows, WIDTH), BF)
    SCRATCH["GR_" + _name] = ((_rows, WIDTH), BF)
    SCRATCH["GK_" + _name] = ((_rows, WIDTH), BF)
    SCRATCH["XS_" + _name] = ((_rows // 2, WIDTH), BF)
    SCRATCH["XR_" + _name] = ((_rows // 2, WIDTH), BF)
    SCRATCH["HS_" + _name] = ((_rows // 2, WIDTH), BF)
    SCRATCH["HR_" + _name] = ((_rows // 2, WIDTH), BF)
    SCRATCH["T_" + _name] = ((_rows, WIDTH), BF)
for _name, _cols in (("SQ0", 128), ("SQ1", 128), ("SQ2", 128), ("CQ", 384), ("UP", 512)):
    if _cols > 128:
        SCRATCH["GS_" + _name] = ((8, 128, _cols), BF)
        SCRATCH["GR_" + _name] = ((8, 128, _cols), BF)
    SCRATCH["GK_" + _name] = ((8, 128, _cols), BF)
    SCRATCH["XS_" + _name] = ((8, HALF, _cols), BF)
    SCRATCH["XR_" + _name] = ((8, HALF, _cols), BF)
    SCRATCH["HS_" + _name] = ((4, HALF, _cols), BF)
    SCRATCH["HR_" + _name] = ((4, HALF, _cols), BF)
    SCRATCH["TS_" + _name] = ((4, HALF, _cols), BF)
    SCRATCH["T_" + _name] = ((8, 128, _cols), BF)

IN_NAMES = (
    "tokens", "encoder", "seq", "enc", "dmix", "w_sq", "w_so", "w_cq", "w_co", "w_up", "w_dn",
    "sb", "cb", "gain", "shift", "fb1", "fb2",
)
OUT_NAMES = (
    "o_mixed", "o_dtok", "o_denc", "o_sq", "o_so", "o_cq", "o_co", "o_up", "o_dn", "o_small",
)
VMEM_BYTES = 64 * 2**20 - 2**19
N_REMOTE = 400
N_LOCAL = 128


def layer_kernel(*refs):
    n_in, n_out = len(IN_NAMES), len(OUT_NAMES)
    r = Names()
    names = IN_NAMES + OUT_NAMES + tuple(SCRATCH)
    for name, ref in zip(names, refs):
        setattr(r, name, ref)
    send_sem, recv_sem, local_sem = refs[len(names) :]
    count = {"remote": 0, "local": 0}

    rep, shard = lax.axis_index("rep"), lax.axis_index("shard")
    x, c = rep // 2, rep % 2
    z, y = shard // 2, shard % 2
    h, l = z // 2, z % 2
    own = 2 * l + y
    t = 4 * c + own
    s_own = 4 * h + own

    def dev(xx, hh, ll, yy, cc):
        return (xx * 2 + cc, (2 * hh + ll) * 2 + yy)

    mate = dev(x, h, l, y, 1 - c)
    x_peer = dev(1 - x, h, l, y, c)
    h_peer = dev(x, 1 - h, l, y, c)
    swap_peer = dev(x, 1 - h, l, y, 1 - c)

    def peer_lc(j):
        return (l + j // 2) % 2, (y + j % 2) % 2

    def peer(j):
        ll, yy = peer_lc(j)
        return dev(x, h, ll, yy, c)

    def peer_block(j):
        ll, yy = peer_lc(j)
        return 2 * ll + yy

    def remote(src, dst, device):
        i = count["remote"]
        count["remote"] += 1
        return pltpu.make_async_remote_copy(
            src_ref=src,
            dst_ref=dst,
            send_sem=send_sem.at[i],
            recv_sem=recv_sem.at[i],
            device_id=device,
            device_id_type=MESH,
        )

    def local(src, dst):
        i = count["local"]
        count["local"] += 1
        return pltpu.make_async_copy(src, dst, local_sem.at[i])

    barrier = pltpu.get_barrier_semaphore()
    greet = [mate, x_peer, swap_peer]
    for m in range(1, 8):
        greet.append(dev(x, (h + m // 4) % 2, (l + (m // 2) % 2) % 2, (y + m % 2) % 2, c))
    for device in greet:
        pl.semaphore_signal(barrier, inc=1, device_id=device, device_id_type=MESH)
    r.LSRC[0:1, :] = jnp.full((1, 128), r.seq[0].astype(F32))
    r.LSRC[1:2, :] = jnp.full((1, 128), r.enc[0].astype(F32))
    r.SM[...] = jnp.zeros_like(r.SM)
    r.SB[...] = jnp.zeros_like(r.SB)
    pl.semaphore_wait(barrier, len(greet))

    moved = [
        (r.tokens, r.X.at[4 * (1 - c) + own], r.X.at[t]),
        (r.encoder, r.E.at[own], r.E.at[own]),
        (r.LSRC, r.LENS, r.LENS),
        (r.dmix, r.DMX, r.DMX),
    ]
    swaps = [(remote(s, there, swap_peer), local(s, here)) for s, there, here in moved]
    stays = c == h

    def swap_start(i):
        @pl.when(stays)
        def _():
            swaps[i][1].start()

        @pl.when(jnp.logical_not(stays))
        def _():
            swaps[i][0].start()

    def swap_wait(i):
        @pl.when(stays)
        def _():
            swaps[i][1].wait()

        @pl.when(jnp.logical_not(stays))
        def _():
            swaps[i][0].wait()

    my_x = pl.ds(pl.multiple_of(x * HALF, HALF), HALF)
    other_x = pl.ds(pl.multiple_of((1 - x) * HALF, HALF), HALF)
    inner = h != l

    class ColumnWeight:
        def __init__(self, w_hbm, dst, parts, width, full=False):
            self.w, self.dst, self.parts, self.width, self.full = w_hbm, dst, parts, width, full

        def at(self, p, shards, rows):
            first = pl.multiple_of(p * 2 * self.width + c * self.width, 128)
            return self.dst.at[shards, rows, pl.ds(first, self.width)]

        def rows(self, m):
            return slice(0, 128) if self.full and m < 4 else my_x

        def build(self):
            self.first, self.hop = [], []
            for p in range(self.parts):
                copies = []
                for m in range(8):
                    hh, ll, yy = (h + m // 4) % 2, (l + (m // 2) % 2) % 2, (y + m % 2) % 2
                    col = pl.multiple_of(p * WIDTH + (4 * c + 2 * ll + yy) * self.width, 128)
                    src = self.w.at[self.rows(m), pl.ds(col, self.width)]
                    at = self.at(p, s_own, self.rows(m))
                    copies.append(local(src, at) if m == 0 else remote(src, at, dev(x, hh, ll, yy, c)))
                self.first.append(copies)
                on = self.at(p, pl.ds(4 * h + 2 * (1 - l), 2), my_x)
                self.hop.append(remote(on, on, h_peer))

        def near(self):
            for copies in self.first:
                start(copies[1:4] + copies[0:1])

        def far(self):
            for copies in self.first:
                start(copies[4:6])

            @pl.when(inner)
            def _():
                for copies in self.first:
                    start(copies[6:8])

        def send(self):
            self.build()
            self.far()
            self.near()

        def relay(self):
            @pl.when(inner)
            def _():
                for copies, hop in zip(self.first, self.hop):
                    copies[2].wait_recv()
                    copies[3].wait_recv()
                    hop.start()

        def cross(self):
            self.xc, self.m1 = [], []
            for p in range(self.parts):
                copies, hop = self.first[p], self.hop[p]
                wait(copies[4:6])
                wait(copies[0:2])

                @pl.when(inner)
                def _():
                    wait(copies[6:8])
                    copies[2].wait_send()
                    copies[3].wait_send()
                    hop.wait_send()

                @pl.when(jnp.logical_not(inner))
                def _():
                    wait(copies[2:4])
                    hop.wait_recv()

                at = self.at(p, pl.ds(4 * (1 - h), 4) if self.full else slice(None), my_x)
                self.xc.append(remote(at, at, x_peer))
                self.xc[p].start()
                self.m1.append(remote(at, at, mate))
                if self.full:
                    at = self.at(p, pl.ds(4 * h, 4), slice(None))
                    self.m1.append(remote(at, at, mate))
                for cp in self.m1[-2 if self.full else -1 :]:
                    cp.start()

        def share(self):
            self.m2 = []
            for p in range(self.parts):
                self.xc[p].wait()
                at = self.at(p, pl.ds(4 * (1 - h), 4) if self.full else slice(None), other_x)
                self.m2.append(remote(at, at, mate))
                self.m2[p].start()

        def ready(self):
            wait(self.m1)
            wait(self.m2)

    class RowWeight:
        def __init__(self, w_hbm, dst, rows):
            self.w, self.dst, self.n = w_hbm, dst, rows // 4

        def rows(self, xx):
            return pl.ds(pl.multiple_of(c * 2 * self.n + xx * self.n, 32), self.n)

        def send(self):
            at = self.rows(x)
            self.first = [local(self.w, self.dst.at[h]), remote(self.w.at[at], self.dst.at[h, at], h_peer)]
            start(self.first)

        def cross(self):
            wait(self.first)
            at = self.dst.at[1 - h, self.rows(x)]
            self.xc, self.m1 = remote(at, at, x_peer), remote(at, at, mate)
            self.xc.start()
            self.m1.start()

        def share(self):
            self.xc.wait()
            at = self.dst.at[1 - h, self.rows(1 - x)]
            self.m2 = remote(at, at, mate)
            self.m2.start()

        def ready(self):
            self.m1.wait()
            self.m2.wait()

    def leave(src, out):
        cp = remote(src, out, swap_peer)

        @pl.when(stays)
        def _():
            out[...] = src[...]

        @pl.when(jnp.logical_not(stays))
        def _():
            cp.start()

        return cp

    def start(copies):
        for cp in copies:
            cp.start()

    def wait(copies):
        for cp in copies:
            cp.wait()

    NBR = (1, 2)

    class Gather:
        def __init__(self, buf, rows, first, base=0):
            self.first = first - 1
            blk = buf.at[base + own, rows]
            self.direct = [remote(blk, blk, peer(j)) for j in NBR]
            on = buf.at[base + peer_block(first), rows]
            self.hop = remote(on, on, peer(3 - first))

        def start(self):
            start(self.direct)

        def relay(self):
            self.direct[self.first].wait_recv()
            self.hop.start()

        def wait(self):
            self.direct[1 - self.first].wait_recv()
            self.hop.wait_recv()
            for cp in (*self.direct, self.hop):
                cp.wait_send()

    class Scatter:
        def __init__(self, buf, land, rows):
            self.buf, self.land, self.rows = buf, land, rows
            self.sends = [remote(buf.at[peer_block(j), rows], land.at[j - 1, rows], peer(j)) for j in (3, 1, 2)]

        def start(self):
            start(self.sends)

        def finish(self):
            wait(self.sends)
            total = self.buf[own, self.rows].astype(F32)
            for j in range(3):
                total = total + self.land[j, self.rows].astype(F32)
            return total

    def span(a):
        return pl.ds(a * SUB, SUB)

    def half(a):
        return slice(a * SUB, (a + 1) * SUB)

    def way(a):
        return 1 + a % 2

    mine = pl.ds(4 * c, 4)
    theirs = pl.ds(4 * (1 - c), 4)
    w_sq = ColumnWeight(r.w_sq, r.WQKV, 3, 128, True)
    w_so = RowWeight(r.w_so, r.WSO, 128)
    w_cq = ColumnWeight(r.w_cq, r.WCQ, 3, 128)
    w_co = RowWeight(r.w_co, r.WCO, 128)
    w_up = ColumnWeight(r.w_up, r.WUP, 1, 512)
    w_dn = RowWeight(r.w_dn, r.WDN, 512)
    ag_x = [Gather(r.X, pl.ds(k * HALF, HALF), 2, 4 * c) for k in range(2)]
    swap_start(0)
    w_sq.build()

    @pl.when(stays)
    def _():
        swaps[0][1].wait()
        for g in ag_x:
            g.direct[0].start()
        for g in ag_x:
            g.direct[0].wait_recv()
        for g in ag_x:
            g.direct[1].start()
        w_sq.near()
        w_sq.far()
        w_sq.relay()
        for g in ag_x:
            g.relay()

    @pl.when(jnp.logical_not(stays))
    def _():
        w_sq.far()
        w_sq.near()
        w_sq.relay()
        swaps[0][0].wait()
        start(ag_x)
        for g in ag_x:
            g.relay()
            g.direct[0].wait_recv()

    swap_start(1)
    swap_start(2)
    w_so.send()
    w_cq.send()
    w_sq.cross()
    w_cq.relay()
    w_co.send()
    swap_wait(1)
    ag_e = Gather(r.E, pl.ds(0, ENC), 2)
    ag_e.start()
    w_up.send()
    w_dn.send()
    for g in ag_x:
        g.hop.wait_recv()
        for cp in (*g.direct, g.hop):
            cp.wait_send()
    x_both = remote(r.X.at[mine], r.X.at[mine], mate)
    x_both.start()
    w_sq.share()
    w_sq.ready()

    lane = lax.broadcasted_iota(jnp.int32, (1, 128), 1)
    heads = [lane // 64 == 0, lane // 64 == 1]

    def head_of(v, hh):
        return jnp.where(heads[hh], v, jnp.zeros_like(v))

    def own_cols(ref, row, width):
        off = [pl.multiple_of((4 * k + own) * width, 128) for k in range(2)]
        return jnp.concatenate([ref[row : row + 1, pl.ds(o, width)] for o in off], 1)

    def blocks(ref, a, width):
        return ref[:, half(a), :].reshape(4 * SUB, width)

    def shards(ref, rows, cols):
        return ref[rows.start // 128 : rows.stop // 128, :, cols].reshape(rows.stop - rows.start, -1)

    def add_small(row, col, width, value):
        at = slice(0, width) if isinstance(col, int) else pl.ds(pl.multiple_of(col, 128), width)
        r.SM[row : row + 1, at] += value

    def colsum(v):
        return jnp.sum(v, 0, keepdims=True)

    bias_q = own_cols(r.sb, 0, 128)
    bias_v = own_cols(r.sb, 1, 128)
    for i in range(2):
        lhs = r.X[pl.ds(4 * c + 2 * i, 2)].reshape(256, WIDTH)
        for p in range(3):
            out = dg(lhs, r.WQKV[:, :, p * 256 : (p + 1) * 256].reshape(WIDTH, 256), 1, 0)
            if p == 0:
                out = (out + bias_q) * 0.125
            if p == 2:
                out = out + bias_v
            out = out.astype(BF)
            for k in range(2):
                r.QST[k, p, 2 * i : 2 * i + 2] = out[:, k * 128 : (k + 1) * 128].reshape(2, ROWS, 128)
    qkv_x = remote(r.QST.at[1 - c], r.QKV.at[:, mine], mate)
    qkv_x.start()
    r.QKV[:, mine] = r.QST[c]
    ag_e.relay()
    w_so.cross()
    qkv_x.wait()

    def keys(p, n):
        return r.QKV[p, 0 : n // ROWS].reshape(n, 128)

    probs = [r.P0, r.P1, r.P2, r.P3]
    for i in range(4):
        n = (i + 1) * 256
        q = r.QKV[0, 2 * i : 2 * i + 2].reshape(256, 128)
        outs = []
        for hh in range(2):
            s = dg(head_of(q, hh), keys(1, n), 1, 1)
            qpos = lax.broadcasted_iota(jnp.int32, (256, n), 0) + i * 256
            kpos = lax.broadcasted_iota(jnp.int32, (256, n), 1)
            s = jnp.where(kpos <= qpos, s, -1e30)
            e = jnp.exp(s - jnp.max(s, 1, keepdims=True))
            p = (e * (1.0 / jnp.sum(e, 1, keepdims=True))).astype(BF)
            probs[i][hh] = p
            outs.append(dg(p, keys(2, n), 1, 0))
        o = jnp.where(heads[0], outs[0], outs[1])
        r.O[i * 256 : (i + 1) * 256] = o
        r.ATF[2 * i : 2 * i + 2] = o.astype(BF).reshape(2, ROWS, 128)
    my_cols = pl.ds(pl.multiple_of(c * 128, 128), 128)
    att_x = remote(r.ATF.at[theirs], r.ATT.at[:, :, my_cols], mate)
    att_x.start()
    r.ATT[:, :, my_cols] = r.ATF[mine]
    w_so.share()
    w_so.ready()
    att_x.wait()

    def partial(a, lhs, w, contract, chunk=512):
        for n in range(WIDTH // chunk):
            cols = slice(n * chunk, (n + 1) * chunk)
            out = dg(lhs, w(cols), 1, contract)
            r.PB[:, half(a), cols] = out.astype(BF).reshape(4, SUB, chunk)
        return scattered(a)

    def scattered(a):
        sums = Scatter(r.PB, r.RB, span(a))
        sums.start()
        return sums

    def norm(i, rows, hidden):
        centre = hidden - jnp.mean(hidden, -1, keepdims=True)
        rstd = lax.rsqrt(jnp.mean(centre * centre, -1, keepdims=True) + EPS)
        xhat = centre * rstd
        return xhat, rstd, xhat * r.gain[i : i + 1, :] + r.shift[i : i + 1, :]

    def norm_back(i, dy, xhat, rstd):
        add_small(6 + i, 0, WIDTH, colsum(dy * xhat))
        add_small(9 + i, 0, WIDTH, colsum(dy))
        d = dy * r.gain[i : i + 1, :]
        mean_d = jnp.mean(d, -1, keepdims=True)
        mean_dx = jnp.mean(d * xhat, -1, keepdims=True)
        return rstd * (d - mean_d - xhat * mean_dx)

    def gathered(buf, a, value, first=None):
        buf[own, half(a)] = value
        g = Gather(buf, span(a), first or way(a))
        g.start()
        return g

    def comp1(a):
        return partial(a, blocks(r.ATT, a, 256), lambda cols: r.WSO[:, :, cols].reshape(256, -1), 0)

    def fin1(a, total):
        hidden = r.X[t, half(a)].astype(F32) + total + r.sb[2:3, :]
        xhat, rstd, out = norm(0, half(a), hidden)
        r.XH[0, half(a)] = xhat
        r.RSTD[0, half(a)] = rstd
        r.RES[half(a)] = out
        return gathered(r.F, a, out.astype(BF), 2)

    def encoder_kv():
        w_cq.ready()
        ag_e.wait()
        bias_cv = own_cols(r.cb, 1, 128)
        for k in range(2):
            out = dg(
                r.E[...].reshape(4 * ENC, WIDTH),
                r.WCQ[:, :, 256 + k * 256 : 512 + k * 256].reshape(WIDTH, 256),
                1,
                0,
            )
            if k == 1:
                out = out + bias_cv
            r.KVC[mine, :, k * 256 : (k + 1) * 256] = out.astype(BF).reshape(4, ENC, 256)
        kvc_x.start()

    kvc_x = remote(r.KVC.at[mine], r.KVC.at[mine], mate)

    def enc_keys(part, k):
        return r.KVC[:, :, part * 256 + k * 128 : part * 256 + (k + 1) * 128].reshape(512, 128)

    def comp2(a):
        bias_cq = own_cols(r.cb, 0, 128)
        visible = lax.broadcasted_iota(jnp.int32, (1, 512), 1).astype(F32) < r.LENS[1:2, 0:1]
        q = dg(blocks(r.F, a, WIDTH), r.WCQ[:, :, 0:256].reshape(WIDTH, 256), 1, 0)
        q = ((q + bias_cq) * 0.125).astype(BF)
        r.QC[:, half(a)] = q.reshape(4, SUB, 256)
        for k in range(2):
            outs = []
            for hh in range(2):
                s = dg(head_of(q[:, k * 128 : (k + 1) * 128], hh), enc_keys(0, k), 1, 1)
                s = jnp.where(visible, s, -1e30)
                e = jnp.exp(s - jnp.max(s, 1, keepdims=True))
                p = (e * (1.0 / jnp.sum(e, 1, keepdims=True))).astype(BF)
                r.PC[2 * k + hh, a] = p
                outs.append(dg(p, enc_keys(1, k), 1, 0))
            o = jnp.where(heads[0], outs[0], outs[1])
            r.OC[a, :, k * 128 : (k + 1) * 128] = o
            r.CATT[:, half(a), k * 128 : (k + 1) * 128] = o.astype(BF).reshape(4, SUB, 128)
        return partial(a, blocks(r.CATT, a, 256), lambda cols: r.WCO[:, :, cols].reshape(256, -1), 0)

    def fin2(a, total):
        hidden = r.RES[half(a)] + total + r.cb[2:3, :]
        xhat, rstd, out = norm(1, half(a), hidden)
        r.XH[1, half(a)] = xhat
        r.RSTD[1, half(a)] = rstd
        r.RES2[half(a)] = out
        return gathered(r.S, a, out.astype(BF), 2)

    def comp3(a):
        lhs = blocks(r.S, a, WIDTH)
        for k in range(2):
            cols = slice(k * 512, (k + 1) * 512)
            bias_up = r.fb1[0:1, pl.ds(pl.multiple_of((4 * k + own) * 512, 128), 512)]
            u = dg(lhs, r.WUP[:, :, cols].reshape(WIDTH, 512), 1, 0) + bias_up
            cdf = 0.5 + 0.5 * lax.erf(u * 0.7071067811865476)
            r.ACT[:, half(a), cols] = (u * cdf).astype(BF).reshape(4, SUB, 512)
            slope = cdf + u * (jnp.exp(-0.5 * u * u) * 0.3989422804014327)
            r.DGL[a, :, cols] = slope.astype(BF)
        return partial(a, blocks(r.ACT, a, 1024), lambda cols: r.WDN[:, :, cols].reshape(1024, -1), 0)

    def fin3(a, total):
        hidden = r.RES2[half(a)] + total + r.fb2[0:1, :]
        xhat, rstd, out = norm(2, half(a), hidden)
        r.MXS[half(a)] = out.astype(BF)
        place = lax.broadcasted_iota(jnp.int32, (SUB, 1), 0) + (t * ROWS + a * SUB)
        dy = jnp.where(place.astype(F32) < r.LENS[0:1, 0:1], r.DMX[half(a)].astype(F32), 0.0)
        d = norm_back(2, dy, xhat, rstd)
        r.RES[half(a)] = d
        low = d.astype(BF)
        add_small(16, 0, WIDTH, colsum(low.astype(F32)))
        return gathered(r.DM, a, low)

    def comp4(a):
        lhs = blocks(r.DM, a, WIDTH)
        for k in range(2):
            cols = slice(k * 512, (k + 1) * 512)
            d_act = dg(lhs, r.WDN[k], 1, 1).astype(BF).astype(F32)
            low = (d_act * r.DGL[a, :, cols].astype(F32)).astype(BF)
            r.DUP[:, half(a), cols] = low.reshape(4, SUB, 512)
            at = pl.ds(pl.multiple_of(y * 512, 512), 512)
            r.SM[pl.ds(12 + 2 * k + l, 1), at] += colsum(low.astype(F32))
        return partial(a, blocks(r.DUP, a, 1024), lambda cols: shards(r.WUP, cols, slice(0, 1024)), 1)

    def fin4(a, total):
        d = norm_back(1, r.RES[half(a)] + total, r.XH[1, half(a)], r.RSTD[1, half(a)])
        r.RES2[half(a)] = d
        low = d.astype(BF)
        add_small(5, 0, WIDTH, colsum(low.astype(F32)))
        return gathered(r.DC, a, low)

    def comp5(a):
        d_att = dg(blocks(r.DC, a, WIDTH), r.WCO[...].reshape(256, WIDTH), 1, 1).astype(BF)
        for k in range(2):
            cols = slice(k * 128, (k + 1) * 128)
            d_pair = d_att[:, cols]
            o_pair = r.OC[a, :, cols]
            q_pair = blocks(r.QC, a, 256)[:, cols]
            ds, dk, dv = [], None, None
            for hh in range(2):
                d_head = head_of(d_pair, hh)
                delta = jnp.sum(d_head.astype(F32) * o_pair, 1, keepdims=True)
                p = r.PC[2 * k + hh, a]
                d_scores = (p.astype(F32) * (dg(d_head, enc_keys(1, k), 1, 1) - delta)).astype(BF)
                ds.append(dg(d_scores, enc_keys(0, k), 1, 0))
                new_dk = dg(d_scores, head_of(q_pair, hh), 0, 0)
                new_dv = dg(p, d_head, 0, 0)
                dk = new_dk if dk is None else dk + new_dk
                dv = new_dv if dv is None else dv + new_dv
            dq = (jnp.where(heads[0], ds[0], ds[1]).astype(BF) * 0.125).astype(BF)
            r.DQC[:, half(a), cols] = dq.reshape(4, SUB, 128)
            add_small(3, (4 * k + own) * 128, 128, colsum(dq.astype(F32)))
            dv_cols = slice(256 + k * 128, 384 + k * 128)
            if a == 0:
                r.DKV[:, cols] = dk
                r.DKV[:, dv_cols] = dv
            else:
                r.DKV[:, cols] += dk
                r.DKV[:, dv_cols] += dv
        return partial(a, blocks(r.DQC, a, 256), lambda cols: shards(r.WCQ, cols, slice(0, 256)), 1)

    def fin5(a, total):
        d = norm_back(0, r.RES2[half(a)] + total, r.XH[0, half(a)], r.RSTD[0, half(a)])
        r.RES[half(a)] = d
        low = d.astype(BF)
        add_small(2, 0, WIDTH, colsum(low.astype(F32)))
        return gathered(r.DB, a, low)

    do_x = []

    def comp6(a):
        d_att = dg(blocks(r.DB, a, WIDTH), r.WSO[...].reshape(256, WIDTH), 1, 1).astype(BF)
        mine_d = jnp.where(c == 0, d_att[:, 0:128], d_att[:, 128:256])
        theirs_d = jnp.where(c == 0, d_att[:, 128:256], d_att[:, 0:128])
        r.DATS[:, half(a)] = theirs_d.reshape(4, SUB, 128)
        r.DO[mine, half(a)] = mine_d.reshape(4, SUB, 128)
        do_x.append(remote(r.DATS.at[:, span(a)], r.DO.at[mine, span(a)], mate))
        do_x[a].start()

    y_peer, l_peer = peer(1), peer(2)

    def small_step(i, device):
        cp = remote(r.SM, r.SMR.at[i], device)
        cp.start()
        return cp

    def small_add(i, cp):
        cp.wait()
        r.SM[...] += r.SMR[i]

    def bias_step(i, device):
        cp = remote(r.SB, r.SBR.at[i], device)
        cp.start()
        return cp

    def bias_add(i, cp):
        cp.wait()
        r.SB[...] += r.SBR[i]

    class ColumnGrad:
        def __init__(self, name, out, parts, part=0):
            self.parts, self.out = parts, out
            for key in ("GS", "GR", "GK", "XS", "XR", "HS", "HR", "TS", "T"):
                setattr(self, key, getattr(r, key + "_" + name, None))
            self.part = part

        def compute(self, left, right, col, width):
            for target, k in ((self.GS, 1 - c), (self.GK, c)):
                rhs = right(k)
                for i in range(4):
                    out = dg(left(slice(i * 256, (i + 1) * 256)), rhs, 0, 0)
                    target[2 * i : 2 * i + 2, :, col : col + width] = out.astype(BF).reshape(2, 128, width)

        def compute_own(self, left, right):
            for i in range(4):
                out = dg(left(slice(i * 256, (i + 1) * 256)), right, 0, 0)
                self.GK[2 * i : 2 * i + 2] = out.astype(BF).reshape(2, 128, -1)

        def s0(self):
            self.core = remote(self.GS, self.GR, mate)
            self.core.start()

        def chip(self, shards, rows):
            if self.GR is None:
                return self.GK[shards, rows].astype(F32)
            return self.GK[shards, rows].astype(F32) + self.GR[shards, rows].astype(F32)

        def s1(self):
            if self.GR is not None:
                self.core.wait()
            self.XS[...] = self.chip(slice(None), other_x).astype(BF)
            self.xc = remote(self.XS, self.XR, x_peer)
            self.xc.start()

        def total(self, shards):
            return self.chip(shards, my_x) + self.XR[shards].astype(F32)

        def s2(self):
            self.xc.wait()
            self.HS[...] = self.total(pl.ds(4 * (1 - h), 4)).astype(BF)
            self.hc = remote(self.HS, self.HR, h_peer)
            self.hc.start()

        def s3(self):
            self.hc.wait()
            self.TS[...] = (self.total(pl.ds(4 * h, 4)) + self.HR[...].astype(F32)).astype(BF)
            self.lc = [
                remote(self.TS.at[peer_block(j)], self.T.at[t, my_x], peer(j)) for j in (1, 2, 3)
            ]
            start(self.lc)
            self.T[t, my_x] = self.TS[own]

        def s4(self):
            wait(self.lc)
            part = self.T.at[pl.ds(4 * c, 4), my_x]
            other = self.T.at[pl.ds(4 * c, 4), other_x]
            self.x2 = remote(part, part, x_peer)
            self.m1 = remote(part, part, mate)
            self.m2 = remote(other, other, mate)
            self.x2.start()
            self.m1.start()

        def s5(self):
            self.x2.wait()
            self.m2.start()

        def s6(self):
            self.m1.wait()
            self.m2.wait()
            width = self.T.shape[2] // self.parts
            self.outs = []
            for tt in range(8):
                for p in range(self.parts):
                    at = (p + self.part) * WIDTH + tt * width
                    self.outs.append(
                        local(
                            self.T.at[tt, :, p * width : (p + 1) * width],
                            self.out.at[:, at : at + width],
                        )
                    )
            start(self.outs)

        def s7(self):
            wait(self.outs)

    class RowGrad:
        def __init__(self, name, out):
            self.out = out
            for key in ("GS", "GR", "GK", "XS", "XR", "HS", "HR", "T"):
                setattr(self, key, getattr(r, key + "_" + name))
            self.n = self.GS.shape[0] // 2

        def compute(self, left, right):
            for target, k in ((self.GS, 1 - c), (self.GK, c)):
                lhs = left(k)
                for i in range(2):
                    cols = slice(i * 512, (i + 1) * 512)
                    target[:, cols] = dg(lhs, right(cols), 0, 0).astype(BF)

        def s0(self):
            self.core = remote(self.GS, self.GR, mate)
            self.core.start()

        def rows(self, k):
            return pl.ds(pl.multiple_of(k * self.n, HALF), self.n)

        def s1(self):
            self.core.wait()
            rows = self.rows(1 - x)
            self.XS[...] = (self.GK[rows].astype(F32) + self.GR[rows].astype(F32)).astype(BF)
            self.xc = remote(self.XS, self.XR, x_peer)
            self.xc.start()

        def total(self):
            rows = self.rows(x)
            return self.GK[rows].astype(F32) + self.GR[rows].astype(F32) + self.XR[...].astype(F32)

        def s2(self):
            self.xc.wait()
            self.hc = remote(self.HS, self.HR, h_peer)

            @pl.when(jnp.logical_not(stays))
            def _():
                self.HS[...] = self.total().astype(BF)
                self.hc.start()

        def s3(self):
            part, other = self.T.at[self.rows(x)], self.T.at[self.rows(1 - x)]
            self.x2 = remote(part, part, x_peer)
            self.m1 = remote(part, part, mate)
            self.m2 = remote(other, other, mate)

            @pl.when(jnp.logical_not(stays))
            def _():
                self.hc.wait_send()

            @pl.when(stays)
            def _():
                self.hc.wait_recv()
                self.T[self.rows(x)] = (self.total() + self.HR[...].astype(F32)).astype(BF)
                self.x2.start()
                self.m1.start()

        def s4(self):
            pass

        def s5(self):
            @pl.when(stays)
            def _():
                self.x2.wait()
                self.m2.start()

        def s6(self):
            @pl.when(stays)
            def _():
                self.m1.wait_send()
                self.m2.wait_send()

            @pl.when(jnp.logical_not(stays))
            def _():
                self.m1.wait_recv()
                self.m2.wait_recv()

            self.outs = [local(self.T, self.out)]
            start(self.outs)

        def s7(self):
            wait(self.outs)

    g_dn = RowGrad("DN", r.o_dn)
    g_up = ColumnGrad("UP", r.o_up, 1)
    g_co = RowGrad("CO", r.o_co)
    g_cq = ColumnGrad("CQ", r.o_cq, 3)
    g_so = RowGrad("SO", r.o_so)
    g_sq = [ColumnGrad("SQ%d" % p, r.o_sq, 1, p) for p in range(3)]

    def lanes(ref, k, width, base=0):
        return ref[:, :, pl.ds(pl.multiple_of(base + k * width, 128), width)].reshape(-1, width)

    rs_e = Scatter(r.PBE, r.RBE, slice(0, ENC))
    dk_x = remote(r.DKS, r.DKR, mate)

    def encoder_swap():
        their_enc = pl.ds(pl.multiple_of((1 - c) * 256, 256), 256)
        r.DKS[...] = r.DKV[their_enc].astype(BF).reshape(4, ENC, 512)
        dk_x.start()

    def encoder_back():
        dk_x.wait()
        my_enc = pl.ds(pl.multiple_of(c * 256, 256), 256)
        low = (r.DKV[my_enc] + r.DKR[...].reshape(256, 512).astype(F32)).astype(BF)
        r.DKL[...] = low.reshape(4, ENC, 512)
        dv_sum = colsum(low[:, 256:512].astype(F32))
        for k in range(2):
            add_small(4, (4 * k + own) * 128, 128, dv_sum[:, k * 128 : (k + 1) * 128])
        for n in range(2):
            cols = slice(n * 512, (n + 1) * 512)
            out = dg(low, shards(r.WCQ, cols, slice(256, 768)), 1, 1)
            r.PBE[:, :, cols] = out.astype(BF).reshape(4, ENC, 512)
        rs_e.start()

    def encoder_out():
        r.DES[...] = rs_e.finish().astype(BF)
        outs["enc"] = leave(r.DES, r.o_denc)

    def mixed_out():
        outs["mixed"] = leave(r.MXS, r.o_mixed)

    def grad_dn():
        g_dn.compute(lambda k: lanes(r.ACT, k, 512), lambda cols: r.DM[:, :, cols].reshape(512, -1))
        g_dn.s0()

    def grad_up():
        g_up.compute(lambda cols: r.S[:, :, cols].reshape(512, -1), lambda k: lanes(r.DUP, k, 512), 0, 512)
        g_up.s0()

    def grad_co():
        g_co.compute(lambda k: lanes(r.CATT, k, 128), lambda cols: r.DC[:, :, cols].reshape(512, -1))
        g_co.s0()

    def grad_cq():
        g_cq.compute(lambda cols: r.F[:, :, cols].reshape(512, -1), lambda k: lanes(r.DQC, k, 128), 0, 128)
        for p in range(2):
            g_cq.compute(
                lambda cols: r.E[:, :, cols].reshape(256, -1),
                lambda k, p=p: lanes(r.DKL, k, 128, 256 * p),
                128 + 128 * p,
                128,
            )
        g_cq.s0()

    def grad_so():
        g_so.compute(lambda k: lanes(r.ATT, k, 128), lambda cols: r.DB[:, :, cols].reshape(512, -1))
        g_so.s0()

    outs, steps = {}, {}

    def small_first():
        steps["small"] = small_step(0, mate)

    def small_next(i):
        def move():
            small_add(i, steps["small"])
            if i < 4:
                steps["small"] = small_step(i + 1, (mate, y_peer, l_peer, x_peer, h_peer)[i + 1])

        return move

    beside = {
        0: [w_cq.cross, w_up.relay],
        1: [w_co.cross],
        2: [w_cq.share],
        3: [encoder_kv, w_co.share, lambda: swap_start(3), lambda: swap_wait(2), kvc_x.wait, w_co.ready, w_up.cross],
        4: [w_dn.cross],
        5: [w_up.share],
        6: [w_dn.share],
        7: [w_up.ready, w_dn.ready],
        8: [lambda: swap_wait(3), x_both.wait],
        13: [mixed_out],
        15: [grad_dn, grad_up],
        16: [g_dn.s1, g_up.s1],
        18: [g_dn.s2],
        19: [encoder_swap, grad_co],
        20: [encoder_back, grad_cq, g_co.s1],
        21: [g_cq.s1, g_up.s2, small_first],
        22: [small_next(0), g_dn.s3],
        23: [grad_so, g_co.s2, small_next(1), encoder_out, g_dn.s4, g_so.s1],
    }

    comps = [comp1, comp2, comp3, comp4, comp5]
    fins = [fin1, fin2, fin3, fin4, fin5]
    rs, ag = {}, {}
    for slot in range(6 * NSUB):
        p, a = divmod(slot, NSUB)
        if p > 0:
            ag[p - 1, a].wait()
        if p < 5:
            rs[p, a] = comps[p](a)
        else:
            comp6(a)
        p, a = divmod(slot - 1, NSUB)
        if 0 <= p < 5:
            ag[p, a] = fins[p](a, rs[p, a].finish())
        p, a = divmod(slot - 2, NSUB)
        if 0 <= p < 5:
            ag[p, a].relay()
        for job in beside.get(slot, ()):
            job()

    wait(do_x)
    r.DKVS[...] = jnp.zeros_like(r.DKVS)
    for i in range(4):
        n = (i + 1) * 256
        q = r.QKV[0, 2 * i : 2 * i + 2].reshape(256, 128)
        d_pair = r.DO[2 * i : 2 * i + 2].reshape(256, 128)
        o_pair = r.O[i * 256 : (i + 1) * 256]
        dqs, dk, dv = [], None, None
        for hh in range(2):
            d_head = head_of(d_pair, hh)
            delta = jnp.sum(d_head.astype(F32) * o_pair, 1, keepdims=True)
            p = probs[i][hh]
            d_scores = (p.astype(F32) * (dg(d_head, keys(2, n), 1, 1) - delta)).astype(BF)
            dqs.append(dg(d_scores, keys(1, n), 1, 0))
            new_dk = dg(d_scores, head_of(q, hh), 0, 0)
            new_dv = dg(p, d_head, 0, 0)
            dk = new_dk if dk is None else dk + new_dk
            dv = new_dv if dv is None else dv + new_dv
        dq = (jnp.where(heads[0], dqs[0], dqs[1]).astype(BF) * 0.125).astype(BF)
        r.DJN[0, 2 * i : 2 * i + 2] = dq.reshape(2, ROWS, 128)
        r.SB[0:1, pl.ds(pl.multiple_of(t * 128, 128), 128)] += colsum(dq.astype(F32))
        r.DKVS[0, 0:n] += dk
        r.DKVS[1, 0:n] += dv
    r.DJN[1] = r.DKVS[0].astype(BF).reshape(8, ROWS, 128)
    low = r.DKVS[1].astype(BF)
    r.DJN[2] = low.reshape(8, ROWS, 128)
    r.SB[1:2, pl.ds(pl.multiple_of(t * 128, 128), 128)] = colsum(low.astype(F32))
    dj_x = []
    for p in range(3):
        at = pl.ds(pl.multiple_of(p * 256 + c * 128, 128), 128)
        dj_x.append(remote(r.DJN.at[p, theirs], r.DJ.at[:, :, at], mate))
        dj_x[p].start()
        r.DJ[:, :, at] = r.DJN[p, mine]
    bias = bias_step(0, mate)
    for p in range(3):
        g_sq[p].compute_own(lambda cols: r.X[:, :, cols].reshape(1024, -1), r.DJN[p].reshape(1024, 128))
        g_sq[p].s1()
    g_so.s2()
    g_cq.s2()
    g_up.s3()
    wait(dj_x)
    rs6 = [
        partial(a, blocks(r.DJ, a, 768), lambda cols: shards(r.WQKV, cols, slice(0, 768)), 1)
        for a in range(NSUB)
    ]
    small_next(2)()
    bias_add(0, bias)
    bias = bias_step(1, y_peer)
    g_co.s3()
    g_sq[0].s2()
    g_sq[1].s2()
    g_sq[2].s2()
    bias_add(1, bias)
    bias = bias_step(2, l_peer)
    g_up.s4()
    for a in range(2):
        r.DTS[half(a)] = (r.RES[half(a)] + rs6[a].finish()).astype(BF)
    g_so.s3()
    g_cq.s3()
    g_sq[0].s3()
    for a in range(2, NSUB):
        r.DTS[half(a)] = (r.RES[half(a)] + rs6[a].finish()).astype(BF)
    outs["tokens"] = leave(r.DTS, r.o_dtok)
    g_sq[1].s3()
    small_next(3)()
    bias_add(2, bias)
    bias = bias_step(3, x_peer)
    g_dn.s5()
    g_co.s5()
    g_sq[2].s3()
    g_cq.s4()
    g_sq[0].s4()
    g_up.s5()
    g_sq[1].s4()
    g_dn.s6()
    g_so.s5()
    bias_add(3, bias)
    bias = bias_step(4, h_peer)
    g_sq[2].s4()
    small_next(4)()
    g_up.s6()
    g_co.s6()
    g_cq.s5()
    g_sq[0].s5()
    g_sq[1].s5()
    g_so.s6()
    g_cq.s6()
    bias_add(4, bias)
    g_sq[0].s6()
    g_sq[2].s5()
    g_sq[1].s6()
    g_sq[2].s6()
    r.SM[0:2, :] = r.SB[0:2, :]
    r.o_small[...] = r.SM[...]

    @pl.when(jnp.logical_not(stays))
    def _():
        for cp in outs.values():
            cp.wait()

    for g in (g_dn, g_up, g_co, g_cq, g_so, *g_sq):
        g.s7()


def on_chip(*args):
    (tokens, encoder, seq_len, enc_len, d_mixed, *rest) = args
    *mats, self_bias, cross_bias, norm_gain, norm_bias, fc1_bias, fc2_bias = rest
    anywhere = pl.BlockSpec(memory_space=pl.ANY)
    vmem = pl.BlockSpec(memory_space=pltpu.VMEM)
    smem = pl.BlockSpec(memory_space=pltpu.SMEM)
    shapes = [
        ((ROWS, WIDTH), BF),
        ((ROWS, WIDTH), BF),
        ((ENC, WIDTH), BF),
        ((128, 3 * WIDTH), BF),
        ((128, WIDTH), BF),
        ((128, 3 * WIDTH), BF),
        ((128, WIDTH), BF),
        ((128, HIDDEN), BF),
        ((512, WIDTH), BF),
        ((24, WIDTH), F32),
    ]
    outs = pl.pallas_call(
        layer_kernel,
        out_shape=[jax.ShapeDtypeStruct(s, d) for s, d in shapes],
        in_specs=[anywhere, anywhere, smem, smem, anywhere] + [anywhere] * 6 + [vmem] * 6,
        out_specs=[vmem] * 3 + [anywhere] * 6 + [vmem],
        scratch_shapes=[pltpu.VMEM(s, d) for s, d in SCRATCH.values()]
        + [
            pltpu.SemaphoreType.DMA((N_REMOTE,)),
            pltpu.SemaphoreType.DMA((N_REMOTE,)),
            pltpu.SemaphoreType.DMA((N_LOCAL,)),
        ],
        compiler_params=pltpu.CompilerParams(
            collective_id=0, has_side_effects=True, vmem_limit_bytes=VMEM_BYTES
        ),
        cost_estimate=pl.CostEstimate(
            flops=16 * 10**9, bytes_accessed=16 * 2**20, transcendentals=8 * 2**20
        ),
    )(
        tokens, encoder, seq_len, enc_len, d_mixed, *mats,
        self_bias, cross_bias, norm_gain, norm_bias,
        fc1_bias.reshape(1, -1), fc2_bias.reshape(1, -1),
    )
    steps = 4

    def rows_of(shape):
        return pl.BlockSpec((shape[0] // steps, shape[1]), lambda i: (i, 0))

    def whole(shape):
        return pl.BlockSpec(shape, lambda i: (0, 0))

    wide = [(s, BF if k == 0 else F32) for k, (s, _) in enumerate(shapes[:-1])]
    flat = [((3, WIDTH), F32)] * 4 + [((1, HIDDEN), F32), ((1, WIDTH), F32)]
    *results, fc1_sum, fc2_sum = pl.pallas_call(
        widen_kernel,
        grid=(steps,),
        out_shape=[jax.ShapeDtypeStruct(s, d) for s, d in wide + flat],
        in_specs=[rows_of(s) for s, _ in shapes[:-1]] + [whole(shapes[-1][0])],
        out_specs=[rows_of(s) for s, _ in wide] + [whole(s) for s, _ in flat],
        compiler_params=pltpu.CompilerParams(vmem_limit_bytes=VMEM_BYTES),
    )(*outs)
    return (*results, fc1_sum.reshape(-1), fc2_sum.reshape(-1))


def widen_kernel(*refs):
    n = len(OUT_NAMES)
    small, flat = refs[n - 1], refs[2 * n - 1 :]
    for src, dst in zip(refs[: n - 1], refs[n:]):
        dst[...] = src[...].astype(dst.dtype)
    for k in range(4):
        flat[k][...] = small[3 * k : 3 * k + 3, :]
        flat[4][0:1, k * WIDTH : (k + 1) * WIDTH] = small[12 + k : 13 + k, :]
    flat[5][...] = small[16:17, :]


def fits(mesh, tokens, encoder, self_qkv, fc1_weight):
    return (
        (mesh.shape["rep"], mesh.shape["shard"]) == (4, 8)
        and tokens.shape == (32 * ROWS, WIDTH)
        and encoder.shape == (32 * ENC, WIDTH)
        and self_qkv.shape == (WIDTH, 3 * WIDTH)
        and fc1_weight.shape == (WIDTH, HIDDEN)
    )


def solution(mesh):
    def placed(body):
        return jax.shard_map(
            body,
            mesh=mesh,
            in_specs=(
                P(("rep", "shard"), None),
                P(("rep", "shard"), None),
                P("rep"),
                P("rep"),
                P(("rep", "shard"), None),
                P("shard", None),
                P("shard", None),
                P("shard", None),
                P("shard", None),
                P("shard", None),
                P("shard", None),
                P(),
                P(),
                P(),
                P(),
                P(),
                P(),
            ),
            out_specs=(
                P(("rep", "shard"), None),
                P(("rep", "shard"), None),
                P(("rep", "shard"), None),
                P("shard", None),
                P("shard", None),
                P("shard", None),
                P("shard", None),
                P("shard", None),
                P("shard", None),
                P(),
                P(),
                P(),
                P(),
                P(),
                P(),
            ),
            check_vma=False,
        )

    def run(*args):
        fast = fits(mesh, args[0], args[1], args[5], args[9])
        return placed(on_chip if fast else local)(*args)

    return run
```

```python
from functools import partial

import jax
import jax.numpy as jnp
from jax import lax
from jax.experimental import pallas as pl
from jax.experimental.pallas import tpu as pltpu
from jax.sharding import PartitionSpec as P

HEADS = 16
HEAD = 64


def for_sending(array):
    return jax.tree.map(lambda a: a.astype(jnp.bfloat16) if a.dtype == jnp.float32 else a, array)


def layer_norm(hidden, gain_row, shift_row):
    centre = hidden - jnp.mean(hidden, -1, keepdims=True)
    spread = jnp.mean(centre * centre, -1, keepdims=True)
    return centre * lax.rsqrt(spread + 1e-05) * gain_row + shift_row


def exact_gelu(values):
    return jax.nn.gelu(values, approximate=False)


def contract_rows(left, right):
    return lax.dot_general(
        left, right, (((0,), (0,)), ((), ())), preferred_element_type=jnp.float32
    )


def back_dot(grad_rows, weight):
    return lax.dot_general(
        grad_rows, weight, (((1,), (1,)), ((), ())), preferred_element_type=jnp.float32
    )


def causal_mask(query_pos, key_pos):
    return key_pos[None, :] <= query_pos[:, None]


def enc_visible(query_pos, key_pos, enc_limit):
    return jnp.broadcast_to((key_pos < enc_limit)[None, :], (query_pos.shape[0], key_pos.shape[0]))


def only_live(step_fn, live_fn):

    def wrapped(totals, block_in, offset):
        return lax.cond(
            live_fn(block_in, offset), lambda: step_fn(totals, block_in, offset), lambda: totals
        )

    return wrapped


def self_fold(key_pair, step_fn, start_state, store):
    return step_fn(
        start_state,
        jax.tree.map(
            lambda a: lax.all_gather(a, "shard", axis=0, tiled=True), for_sending(key_pair)
        ),
        jnp.int32(0),
    )


def cross_fold(key_pair, step_fn, start_state, store):
    return step_fn(
        start_state,
        jax.tree.map(
            lambda a: lax.all_gather(a, "shard", axis=0, tiled=True), for_sending(key_pair)
        ),
        jnp.int32(0),
    )


def keys_live(query_pos, allowed_fn):

    def live_fn(block_in, offset):
        key_pos = jnp.arange(block_in[0].shape[0], dtype=jnp.int32)
        return jnp.any(allowed_fn(query_pos, key_pos))

    return live_fn


def head_scores(query_heads, query_pos, key_block, allowed_fn):
    key_count = key_block.shape[0]
    key_pos = jnp.arange(key_count, dtype=jnp.int32)
    scores = jnp.einsum(
        "qhd,khd->hqk",
        query_heads,
        key_block.reshape(key_count, HEADS, HEAD),
        preferred_element_type=jnp.float32,
    )
    return (scores, allowed_fn(query_pos, key_pos)[None])


def forward_pass(query_part, query_pos, key_pair, allowed_fn, folder):
    query_count = query_part.shape[0]
    query_heads = query_part.reshape(query_count, HEADS, HEAD)
    live_fn = keys_live(query_pos, allowed_fn)

    def stat_step(totals, block_in, offset):
        highest, mass = totals
        scores, allowed = head_scores(query_heads, query_pos, block_in[0], allowed_fn)
        masked = jnp.where(allowed, scores, -1e30)
        raised = jnp.maximum(highest, jnp.max(masked, -1))
        fresh = jnp.sum(jnp.where(allowed, jnp.exp(masked - raised[:, :, None]), 0.0), -1)
        return (raised, fresh)

    start_state = (
        jnp.full((HEADS, query_count), -1e30, jnp.float32),
        jnp.zeros((HEADS, query_count), jnp.float32),
    )
    highest, mass = folder(key_pair, only_live(stat_step, live_fn), start_state, None)
    log_total = highest + jnp.log(mass)

    def out_step(totals, block_in, offset):
        scores, allowed = head_scores(query_heads, query_pos, block_in[0], allowed_fn)
        weights_low = jnp.where(allowed, jnp.exp(scores - log_total[:, :, None]), 0.0).astype(
            jnp.bfloat16
        )
        value_heads = block_in[1].reshape(block_in[1].shape[0], HEADS, HEAD)
        return jnp.einsum(
            "hqk,khd->qhd", weights_low, value_heads, preferred_element_type=jnp.float32
        )

    summed = folder(
        key_pair,
        only_live(out_step, live_fn),
        jnp.zeros((query_count, HEADS, HEAD), jnp.float32),
        None,
    )
    return (log_total.T, summed)


def query_step(query_part, query_pos, allowed_fn, log_rows, delta_rows, d_out):
    query_count = query_part.shape[0]
    query_heads = query_part.reshape(query_count, HEADS, HEAD)
    grad_heads = d_out.reshape(query_count, HEADS, HEAD)
    log_total = log_rows.T
    correction = delta_rows.T

    def grad_step(totals, block_in, offset):
        key_block, value_block = block_in
        key_count = key_block.shape[0]
        scores, allowed = head_scores(query_heads, query_pos, key_block, allowed_fn)
        probs = jnp.where(allowed, jnp.exp(scores - log_total[:, :, None]), 0.0)
        d_probs = jnp.einsum(
            "qhd,khd->hqk",
            grad_heads,
            value_block.reshape(key_count, HEADS, HEAD),
            preferred_element_type=jnp.float32,
        )
        d_scores = (probs * (d_probs - correction[:, :, None])).astype(jnp.bfloat16)
        return jnp.einsum(
            "hqk,khd->qhd",
            d_scores,
            key_block.reshape(key_count, HEADS, HEAD),
            preferred_element_type=jnp.float32,
        )

    return only_live(grad_step, keys_live(query_pos, allowed_fn))


def query_grad(query_part, query_pos, key_pair, allowed_fn, folder, log_rows, delta_rows, d_out):
    query_count = query_part.shape[0]
    step_fn = query_step(query_part, query_pos, allowed_fn, log_rows, delta_rows, d_out)
    return folder(key_pair, step_fn, jnp.zeros((query_count, HEADS, HEAD), jnp.float32), None)


def key_step(own_keys, own_values, key_pos, allowed_fn, log_all, delta_all):
    key_count = own_keys.shape[0]
    key_heads = own_keys.reshape(key_count, HEADS, HEAD)
    value_heads = own_values.reshape(key_count, HEADS, HEAD)

    def step_fn(totals, block_in, offset):
        query_block, grad_block = block_in
        query_count = query_block.shape[0]
        query_pos = jnp.arange(query_count, dtype=jnp.int32)
        log_part = log_all.T
        delta_part = delta_all.T
        query_heads = query_block.reshape(query_count, HEADS, HEAD)
        grad_heads = grad_block.reshape(query_count, HEADS, HEAD)
        scores = jnp.einsum(
            "qhd,khd->hqk", query_heads, key_heads, preferred_element_type=jnp.float32
        )
        allowed = allowed_fn(query_pos, key_pos)[None]
        probs = jnp.where(allowed, jnp.exp(scores - log_part[:, :, None]), 0.0)
        d_values = jnp.einsum(
            "hqk,qhd->khd",
            probs.astype(jnp.bfloat16),
            grad_heads,
            preferred_element_type=jnp.float32,
        )
        d_probs = jnp.einsum(
            "qhd,khd->hqk", grad_heads, value_heads, preferred_element_type=jnp.float32
        )
        d_scores = (probs * (d_probs - delta_part[:, :, None])).astype(jnp.bfloat16)
        d_keys = jnp.einsum(
            "hqk,qhd->khd", d_scores, query_heads, preferred_element_type=jnp.float32
        )
        return (d_keys, d_values)

    def live_fn(block_in, offset):
        query_pos = jnp.arange(block_in[0].shape[0], dtype=jnp.int32)
        return jnp.any(allowed_fn(query_pos, key_pos))

    return only_live(step_fn, live_fn)


def column_sum(values):
    return jnp.sum(values.astype(jnp.float32), 0)


def local(
    tokens,
    encoder,
    seq_len,
    enc_len,
    d_mixed,
    self_qkv,
    self_out,
    cross_qkv,
    cross_out,
    fc1_weight,
    fc2_weight,
    self_bias,
    cross_bias,
    norm_gain,
    norm_bias,
    fc1_bias,
    fc2_bias,
):
    model_width = tokens.shape[1]
    tok_rows = tokens.shape[0]
    enc_rows = encoder.shape[0]
    device_at = lax.axis_index("shard")
    positions = device_at * tok_rows + jnp.arange(tok_rows, dtype=jnp.int32)
    enc_positions = device_at * enc_rows + jnp.arange(enc_rows, dtype=jnp.int32)
    seq_limit = seq_len[0]
    visible = partial(enc_visible, enc_limit=enc_len[0])
    w_sq, w_so = (
        lax.all_gather(self_qkv, "shard", axis=0, tiled=True),
        lax.all_gather(self_out, "shard", axis=0, tiled=True),
    )
    joined = jnp.dot(tokens, w_sq, preferred_element_type=jnp.float32)
    query_s = ((joined[:, :model_width] + self_bias[0]) * 0.125).astype(jnp.bfloat16)
    key_s = joined[:, model_width : 2 * model_width].astype(jnp.bfloat16)
    value_s = (joined[:, 2 * model_width :] + self_bias[1]).astype(jnp.bfloat16)
    self_lse, self_summed = forward_pass(
        query_s, positions, (key_s, value_s), causal_mask, self_fold
    )
    attended = self_summed.reshape(tok_rows, model_width).astype(jnp.bfloat16)
    branch = jnp.dot(attended, w_so, preferred_element_type=jnp.float32) + self_bias[2]
    first_norm, first_pull = jax.vjp(
        layer_norm, tokens.astype(jnp.float32) + branch, norm_gain[0], norm_bias[0]
    )
    w_cq, w_co = (
        lax.all_gather(cross_qkv, "shard", axis=0, tiled=True),
        lax.all_gather(cross_out, "shard", axis=0, tiled=True),
    )
    first_low = first_norm.astype(jnp.bfloat16)
    query_c = (
        (
            jnp.dot(first_low, w_cq[:, :model_width], preferred_element_type=jnp.float32)
            + cross_bias[0]
        )
        * 0.125
    ).astype(jnp.bfloat16)
    enc_proj = jnp.dot(encoder, w_cq[:, model_width:], preferred_element_type=jnp.float32)
    key_c = enc_proj[:, :model_width].astype(jnp.bfloat16)
    value_c = (enc_proj[:, model_width:] + cross_bias[1]).astype(jnp.bfloat16)
    cross_lse, cross_summed = forward_pass(
        query_c, positions, (key_c, value_c), visible, cross_fold
    )
    cross_att = cross_summed.reshape(tok_rows, model_width).astype(jnp.bfloat16)
    branch_c = jnp.dot(cross_att, w_co, preferred_element_type=jnp.float32) + cross_bias[2]
    second_norm, second_pull = jax.vjp(
        layer_norm, first_norm + branch_c, norm_gain[1], norm_bias[1]
    )
    w_up, w_down = (
        lax.all_gather(fc1_weight, "shard", axis=0, tiled=True),
        lax.all_gather(fc2_weight, "shard", axis=0, tiled=True),
    )
    second_low = second_norm.astype(jnp.bfloat16)
    upward = jnp.dot(second_low, w_up, preferred_element_type=jnp.float32) + fc1_bias
    activated, gelu_pull = jax.vjp(exact_gelu, upward)
    act_low = activated.astype(jnp.bfloat16)
    branch_m = jnp.dot(act_low, w_down, preferred_element_type=jnp.float32) + fc2_bias
    output, third_pull = jax.vjp(layer_norm, second_norm + branch_m, norm_gain[2], norm_bias[2])
    valid = (positions < seq_limit).astype(jnp.float32)[:, None]
    d_third, d_gain3, d_shift3 = third_pull(d_mixed.astype(jnp.float32) * valid)
    d_branch_m = d_third.astype(jnp.bfloat16)
    g_down = contract_rows(act_low, d_branch_m)
    d_act = back_dot(d_branch_m, w_down).astype(jnp.bfloat16)
    (d_up,) = gelu_pull(d_act.astype(jnp.float32))
    d_up_low = d_up.astype(jnp.bfloat16)
    g_up = contract_rows(second_low, d_up_low)
    d_second = d_third + back_dot(d_up_low, w_up)
    d_hidden2, d_gain2, d_shift2 = second_pull(d_second)
    d_branch_c = d_hidden2.astype(jnp.bfloat16)
    g_co = contract_rows(cross_att, d_branch_c)
    d_cross_att = back_dot(d_branch_c, w_co).astype(jnp.bfloat16)
    cross_delta = jnp.einsum(
        "qhd,qhd->qh", d_cross_att.reshape(tok_rows, HEADS, HEAD).astype(jnp.float32), cross_summed
    )
    d_query_c = query_grad(
        query_c,
        positions,
        (key_c, value_c),
        visible,
        cross_fold,
        cross_lse,
        cross_delta,
        d_cross_att,
    )
    d_query_cs = d_query_c.reshape(tok_rows, model_width).astype(jnp.bfloat16) * 0.125
    d_first = d_hidden2 + back_dot(d_query_cs, w_cq[:, :model_width])
    d_hidden1, d_gain1, d_shift1 = first_pull(d_first)
    d_branch = d_hidden1.astype(jnp.bfloat16)
    g_so = contract_rows(attended, d_branch)
    d_attended = back_dot(d_branch, w_so).astype(jnp.bfloat16)
    self_delta = jnp.einsum(
        "qhd,qhd->qh", d_attended.reshape(tok_rows, HEADS, HEAD).astype(jnp.float32), self_summed
    )
    stats = (
        lax.all_gather(self_lse, "shard", axis=0, tiled=True),
        lax.all_gather(self_delta, "shard", axis=0, tiled=True),
        lax.all_gather(cross_lse, "shard", axis=0, tiled=True),
        lax.all_gather(cross_delta, "shard", axis=0, tiled=True),
    )
    tok_zero = jnp.zeros((tok_rows, HEADS, HEAD), jnp.float32)
    query_side = query_step(query_s, positions, causal_mask, self_lse, self_delta, d_attended)
    key_side = key_step(key_s, value_s, positions, causal_mask, stats[0], stats[1])
    offset = jnp.int32(0)
    d_query_part = query_side(
        tok_zero,
        (
            lax.all_gather(key_s, "shard", axis=0, tiled=True),
            lax.all_gather(value_s, "shard", axis=0, tiled=True),
        ),
        offset,
    )
    d_key_part, d_value_part = key_side(
        (tok_zero, tok_zero),
        (
            lax.all_gather(query_s, "shard", axis=0, tiled=True),
            lax.all_gather(d_attended, "shard", axis=0, tiled=True),
        ),
        offset,
    )
    enc_zero = jnp.zeros((enc_rows, HEADS, HEAD), jnp.float32)
    d_key_c, d_value_c = key_step(key_c, value_c, enc_positions, visible, stats[2], stats[3])(
        (enc_zero, enc_zero),
        (
            lax.all_gather(query_c, "shard", axis=0, tiled=True),
            lax.all_gather(d_cross_att, "shard", axis=0, tiled=True),
        ),
        jnp.int32(0),
    )
    d_qs = d_query_part.reshape(tok_rows, model_width).astype(jnp.bfloat16) * 0.125
    d_ks = d_key_part.reshape(tok_rows, model_width).astype(jnp.bfloat16)
    d_vs = d_value_part.reshape(tok_rows, model_width).astype(jnp.bfloat16)
    d_joined = jnp.concatenate([d_qs, d_ks, d_vs], 1)
    g_sq = contract_rows(tokens, d_joined)
    d_tokens = d_hidden1 + back_dot(d_joined, w_sq)
    d_kc = d_key_c.reshape(enc_rows, model_width).astype(jnp.bfloat16)
    d_vc = d_value_c.reshape(enc_rows, model_width).astype(jnp.bfloat16)
    d_enc_proj = jnp.concatenate([d_kc, d_vc], 1)
    g_cq = jnp.concatenate(
        [contract_rows(first_low, d_query_cs), contract_rows(encoder, d_enc_proj)], 1
    )
    d_encoder = back_dot(d_enc_proj, w_cq[:, model_width:])
    d_self_bias = jnp.stack([column_sum(d_qs), column_sum(d_vs), column_sum(d_branch)])
    d_cross_bias = jnp.stack([column_sum(d_query_cs), column_sum(d_vc), column_sum(d_branch_c)])
    d_norm_gain = jnp.stack([d_gain1, d_gain2, d_gain3])
    d_norm_bias = jnp.stack([d_shift1, d_shift2, d_shift3])
    d_fc1_bias = column_sum(d_up_low)
    d_fc2_bias = column_sum(d_branch_m)
    row_grads = (
        lax.psum_scatter(g_sq, "shard", scatter_dimension=0, tiled=True),
        lax.psum_scatter(g_so, "shard", scatter_dimension=0, tiled=True),
        lax.psum_scatter(g_cq, "shard", scatter_dimension=0, tiled=True),
        lax.psum_scatter(g_co, "shard", scatter_dimension=0, tiled=True),
        lax.psum_scatter(g_up, "shard", scatter_dimension=0, tiled=True),
        lax.psum_scatter(g_down, "shard", scatter_dimension=0, tiled=True),
    )
    row_grads = lax.psum(
        (row_grads[0], row_grads[1], row_grads[2], row_grads[3], row_grads[4], row_grads[5]), "rep"
    )
    small_sums = lax.psum(
        (d_self_bias, d_cross_bias, d_norm_gain, d_norm_bias, d_fc1_bias, d_fc2_bias),
        ("rep", "shard"),
    )
    return (
        output.astype(jnp.bfloat16),
        d_tokens,
        d_encoder,
        row_grads[0],
        row_grads[1],
        row_grads[2],
        row_grads[3],
        row_grads[4],
        row_grads[5],
        small_sums[0],
        small_sums[1],
        small_sums[2],
        small_sums[3],
        small_sums[4],
        small_sums[5],
    )


MESH = pl.DeviceIdType.MESH
BF = jnp.bfloat16
F32 = jnp.float32
EPS = 1e-05


def dg(left, right, cl, cr):
    return lax.dot_general(
        left, right, (((cl,), (cr,)), ((), ())), preferred_element_type=F32
    )


class Names:
    pass


WIDTH = 1024
HIDDEN = 4096
ROWS = 128
ENC = 64
HALF = 64
NSUB = 4
SUB = ROWS // NSUB

SCRATCH = {
    "X": ((8, ROWS, WIDTH), BF),
    "E": ((4, ENC, WIDTH), BF),
    "DMX": ((ROWS, WIDTH), BF),
    "LSRC": ((8, 128), F32),
    "LENS": ((8, 128), F32),
    "WQKV": ((8, 128, 768), BF),
    "WSO": ((2, 128, WIDTH), BF),
    "WCQ": ((8, 128, 768), BF),
    "WCO": ((2, 128, WIDTH), BF),
    "WUP": ((8, 128, 1024), BF),
    "WDN": ((2, 512, WIDTH), BF),
    "QST": ((2, 3, 4, ROWS, 128), BF),
    "QKV": ((3, 8, ROWS, 128), BF),
    "P0": ((2, 256, 256), BF),
    "P1": ((2, 256, 512), BF),
    "P2": ((2, 256, 768), BF),
    "P3": ((2, 256, 1024), BF),
    "O": ((1024, 128), F32),
    "ATF": ((8, ROWS, 128), BF),
    "ATT": ((4, ROWS, 256), BF),
    "PB": ((4, ROWS, WIDTH), BF),
    "RB": ((3, ROWS, WIDTH), BF),
    "VIA": ((ROWS, WIDTH), BF),
    "VIAE": ((ENC, WIDTH), BF),
    "PBE": ((4, ENC, WIDTH), BF),
    "RBE": ((3, ENC, WIDTH), BF),
    "F": ((4, ROWS, WIDTH), BF),
    "S": ((4, ROWS, WIDTH), BF),
    "DM": ((4, ROWS, WIDTH), BF),
    "DC": ((4, ROWS, WIDTH), BF),
    "DB": ((4, ROWS, WIDTH), BF),
    "RES": ((ROWS, WIDTH), F32),
    "RES2": ((ROWS, WIDTH), F32),
    "XH": ((2, ROWS, WIDTH), F32),
    "RSTD": ((2, ROWS, 1), F32),
    "QC": ((4, ROWS, 256), BF),
    "KVC": ((8, ENC, 512), BF),
    "PC": ((4, NSUB, 4 * SUB, 512), BF),
    "OC": ((NSUB, 4 * SUB, 256), F32),
    "CATT": ((4, ROWS, 256), BF),
    "ACT": ((4, ROWS, 1024), BF),
    "DGL": ((NSUB, 4 * SUB, 1024), BF),
    "DUP": ((4, ROWS, 1024), BF),
    "DQC": ((4, ROWS, 256), BF),
    "DKV": ((512, 512), F32),
    "DKS": ((4, ENC, 512), BF),
    "DKR": ((4, ENC, 512), BF),
    "DKL": ((4, ENC, 512), BF),
    "DATS": ((4, ROWS, 128), BF),
    "DO": ((8, ROWS, 128), BF),
    "DKVS": ((2, 1024, 128), F32),
    "DJN": ((3, 8, ROWS, 128), BF),
    "DJ": ((4, ROWS, 768), BF),
    "MXS": ((ROWS, WIDTH), BF),
    "DTS": ((ROWS, WIDTH), BF),
    "DES": ((ENC, WIDTH), BF),
    "SM": ((16, WIDTH), F32),
    "SMR": ((16, WIDTH), F32),
    "SM4": ((4, 16, WIDTH), F32),
    "SB": ((8, WIDTH), F32),
    "SBR": ((8, WIDTH), F32),
    "SB4": ((4, 8, WIDTH), F32),
    "ALL": ((24, WIDTH), F32),
    "ALLR": ((2, 24, WIDTH), F32),
}
for _name, _rows in (("SO", 128), ("CO", 128), ("DN", 512)):
    SCRATCH["GS_" + _name] = ((_rows, WIDTH), BF)
    SCRATCH["GR_" + _name] = ((_rows, WIDTH), BF)
    SCRATCH["GK_" + _name] = ((_rows, WIDTH), BF)
    SCRATCH["XS_" + _name] = ((_rows // 2, WIDTH), BF)
    SCRATCH["XR_" + _name] = ((_rows // 2, WIDTH), BF)
    SCRATCH["HS_" + _name] = ((_rows // 2, WIDTH), BF)
    SCRATCH["HR_" + _name] = ((_rows // 2, WIDTH), BF)
    SCRATCH["T_" + _name] = ((_rows, WIDTH), BF)
for _name, _cols in (("SQ0", 128), ("SQ1", 128), ("SQ2", 128), ("CQ", 384), ("UP", 512)):
    if _cols > 128:
        SCRATCH["GS_" + _name] = ((8, 128, _cols), BF)
        SCRATCH["GR_" + _name] = ((8, 128, _cols), BF)
    SCRATCH["GK_" + _name] = ((8, 128, _cols), BF)
    SCRATCH["XS_" + _name] = ((8, HALF, _cols), BF)
    SCRATCH["XR_" + _name] = ((8, HALF, _cols), BF)
    SCRATCH["HS_" + _name] = ((4, HALF, _cols), BF)
    SCRATCH["HR_" + _name] = ((4, HALF, _cols), BF)
    SCRATCH["TS_" + _name] = ((4, HALF, _cols), BF)
    SCRATCH["T_" + _name] = ((8, 128, _cols), BF)

IN_NAMES = (
    "tokens", "encoder", "seq", "enc", "dmix", "w_sq", "w_so", "w_cq", "w_co", "w_up", "w_dn",
    "sb", "cb", "gain", "shift", "fb1", "fb2",
)
OUT_NAMES = (
    "o_mixed", "o_dtok", "o_denc", "o_sq", "o_so", "o_cq", "o_co", "o_up", "o_dn", "o_small",
)
VMEM_BYTES = 64 * 2**20 - 2**19
N_SEND, N_RECV, N_LOCAL = 133, 140, 20


def layer_kernel(*refs):
    n_in, n_out = len(IN_NAMES), len(OUT_NAMES)
    r = Names()
    names = IN_NAMES + OUT_NAMES + tuple(SCRATCH)
    for name, ref in zip(names, refs):
        setattr(r, name, ref)
    send_sem, recv_sem, local_sem = refs[len(names) :]
    count = {"send": 0, "recv": 0, "local": 0}

    def new(kind):
        count[kind] += 1
        return count[kind] - 1

    def pair():
        return new("send"), new("recv")

    rep, shard = lax.axis_index("rep"), lax.axis_index("shard")
    x, c = rep // 2, rep % 2
    z, y = shard // 2, shard % 2
    h, l = z // 2, z % 2
    own = 2 * l + y
    t = 4 * c + own
    s_own = 4 * h + own

    def dev(xx, hh, ll, yy, cc):
        return (xx * 2 + cc, (2 * hh + ll) * 2 + yy)

    mate = dev(x, h, l, y, 1 - c)
    x_peer = dev(1 - x, h, l, y, c)
    h_peer = dev(x, 1 - h, l, y, c)
    swap_peer = dev(x, 1 - h, l, y, 1 - c)

    def peer_lc(j):
        return (l + j // 2) % 2, (y + j % 2) % 2

    def peer(j):
        ll, yy = peer_lc(j)
        return dev(x, h, ll, yy, c)

    def peer_block(j):
        ll, yy = peer_lc(j)
        return 2 * ll + yy

    def remote(src, dst, device, sems=None):
        i, j = sems or pair()
        return pltpu.make_async_remote_copy(
            src_ref=src,
            dst_ref=dst,
            send_sem=send_sem.at[i],
            recv_sem=recv_sem.at[j],
            device_id=device,
            device_id_type=MESH,
        )

    def all_of(ref, sems):
        return remote(ref, ref, mate, sems)

    def local(src, dst, sem=None):
        return pltpu.make_async_copy(src, dst, local_sem.at[new("local") if sem is None else sem])

    barrier = pltpu.get_barrier_semaphore()
    greet = [mate, x_peer, swap_peer]
    for m in range(1, 8):
        greet.append(dev(x, (h + m // 4) % 2, (l + (m // 2) % 2) % 2, (y + m % 2) % 2, c))
    for device in greet:
        pl.semaphore_signal(barrier, inc=1, device_id=device, device_id_type=MESH)
    r.LSRC[0:1, :] = jnp.full((1, 128), r.seq[0].astype(F32))
    r.LSRC[1:2, :] = jnp.full((1, 128), r.enc[0].astype(F32))
    r.SM[...] = jnp.zeros_like(r.SM)
    r.SB[...] = jnp.zeros_like(r.SB)
    pl.semaphore_wait(barrier, len(greet))

    moved = [
        (r.tokens, r.X.at[4 * (1 - c) + own], r.X.at[t]),
        (r.encoder, r.E.at[own], r.E.at[own]),
        (r.LSRC, r.LENS, r.LENS),
        (r.dmix, r.DMX, r.DMX),
    ]
    swaps = [(remote(s, there, swap_peer), local(s, here)) for s, there, here in moved]
    stays = c == h

    def swap_start(i):
        @pl.when(stays)
        def _():
            swaps[i][1].start()

        @pl.when(jnp.logical_not(stays))
        def _():
            swaps[i][0].start()

    def swap_wait(i):
        @pl.when(stays)
        def _():
            swaps[i][1].wait()

        @pl.when(jnp.logical_not(stays))
        def _():
            swaps[i][0].wait()

    my_x = pl.ds(pl.multiple_of(x * HALF, HALF), HALF)
    other_x = pl.ds(pl.multiple_of((1 - x) * HALF, HALF), HALF)
    inner = h != l

    class ColumnWeight:
        def __init__(self, w_hbm, dst, groups, width, full=False):
            self.w, self.dst, self.width, self.full = w_hbm, dst, width, full
            self.groups = [(parts, [pair() for _ in range(6)], new("local")) for parts in groups]

        def at(self, p, shards, rows):
            first = pl.multiple_of(p * 2 * self.width + c * self.width, 128)
            return self.dst.at[shards, rows, pl.ds(first, self.width)]

        def rows(self, m):
            return slice(0, 128) if self.full and m < 4 else my_x

        def bytes(self, parts, blocks, rows):
            return self.dst.at[0:blocks, rows, 0 : len(parts) * self.width]

        def copy(self, p, m, sems, sem):
            hh, ll, yy = (h + m // 4) % 2, (l + (m // 2) % 2) % 2, (y + m % 2) % 2
            col = pl.multiple_of(p * WIDTH + (4 * c + 2 * ll + yy) * self.width, 128)
            src = self.w.at[self.rows(m), pl.ds(col, self.width)]
            at = self.at(p, s_own, self.rows(m))
            if m == 0:
                return local(src, at, sem)
            return remote(src, at, dev(x, hh, ll, yy, c), sems[m // 4])

        def near(self):
            for parts, sems, sem in self.groups:
                for p in parts:
                    start([self.copy(p, m, sems, sem) for m in (1, 2, 3, 0)])

        def far(self):
            for parts, sems, sem in self.groups:
                for p in parts:
                    start([self.copy(p, m, sems, sem) for m in (4, 5)])

            @pl.when(inner)
            def _():
                for parts, sems, sem in self.groups:
                    for p in parts:
                        start([self.copy(p, m, sems, sem) for m in (6, 7)])

        def send(self):
            self.far()
            self.near()

        def relay(self):
            @pl.when(inner)
            def _():
                for parts, sems, sem in self.groups:
                    all_of(self.bytes(parts, 3, self.rows(1)), sems[0]).wait_recv()
                    for p in parts:
                        on = self.at(p, pl.ds(4 * h + 2 * (1 - l), 2), my_x)
                        remote(on, on, h_peer, sems[2]).start()

        def cross(self):
            for parts, sems, sem in self.groups:
                near = all_of(self.bytes(parts, 3, self.rows(1)), sems[0])
                hop = all_of(self.bytes(parts, 2, my_x), sems[2])
                near.wait_send()
                here = self.dst.at[0, self.rows(0), 0 : len(parts) * self.width]
                local(here, here, sem).wait()

                @pl.when(inner)
                def _():
                    all_of(self.bytes(parts, 4, my_x), sems[1]).wait()
                    hop.wait_send()

                @pl.when(jnp.logical_not(inner))
                def _():
                    near.wait_recv()
                    all_of(self.bytes(parts, 2, my_x), sems[1]).wait()
                    hop.wait_recv()

                shards = pl.ds(4 * (1 - h), 4) if self.full else slice(None)
                for p in parts:
                    at = self.at(p, shards, my_x)
                    remote(at, at, x_peer, sems[3]).start()
                for p in parts:
                    at = self.at(p, shards, my_x)
                    remote(at, at, mate, sems[4]).start()
                    if self.full:
                        at = self.at(p, pl.ds(4 * h, 4), slice(None))
                        remote(at, at, mate, sems[4]).start()

        def share(self):
            for parts, sems, sem in self.groups:
                all_of(self.bytes(parts, 4 if self.full else 8, my_x), sems[3]).wait()
                shards = pl.ds(4 * (1 - h), 4) if self.full else slice(None)
                for p in parts:
                    at = self.at(p, shards, other_x)
                    remote(at, at, mate, sems[5]).start()

        def ready(self):
            for parts, sems, sem in self.groups:
                all_of(self.bytes(parts, 6 if self.full else 4, slice(None)), sems[4]).wait()
                all_of(self.bytes(parts, 4 if self.full else 8, my_x), sems[5]).wait()

    class RowWeight:
        def __init__(self, w_hbm, dst, rows):
            self.w, self.dst, self.n = w_hbm, dst, rows // 4

        def rows(self, xx):
            return pl.ds(pl.multiple_of(c * 2 * self.n + xx * self.n, 32), self.n)

        def send(self):
            at = self.rows(x)
            self.first = [local(self.w, self.dst.at[h]), remote(self.w.at[at], self.dst.at[h, at], h_peer)]
            start(self.first)

        def cross(self):
            wait(self.first)
            at = self.dst.at[1 - h, self.rows(x)]
            self.xc, self.m1 = remote(at, at, x_peer), remote(at, at, mate)
            self.xc.start()
            self.m1.start()

        def share(self):
            self.xc.wait()
            at = self.dst.at[1 - h, self.rows(1 - x)]
            self.m2 = remote(at, at, mate)
            self.m2.start()

        def ready(self):
            self.m1.wait()
            self.m2.wait()

    def leave(src, out):
        cp = remote(src, out, swap_peer)

        @pl.when(stays)
        def _():
            out[...] = src[...]

        @pl.when(jnp.logical_not(stays))
        def _():
            cp.start()

        return cp

    def start(copies):
        for cp in copies:
            cp.start()

    def wait(copies):
        for cp in copies:
            cp.wait()

    NBR = (1, 2)

    class Gather:
        def __init__(self, buf, rows, first, base=0, sems=None, apart=False):
            self.first = first - 1
            self.sems = sems or gather_sems()
            send, recv_first, recv_rest = self.sems
            blk = buf.at[base + own, rows]
            self.direct = [
                remote(blk, blk, peer(j), (send, recv_first if j == first else recv_rest)) for j in NBR
            ]
            on = buf.at[base + peer_block(first), rows]
            self.hop = remote(on, on, peer(3 - first), None if apart else (send, recv_rest))
            self.two, self.three = buf.at[0:2, rows], buf.at[0:3, rows]

        def start(self):
            start(self.direct)

        def relay(self):
            self.direct[self.first].wait_recv()
            self.hop.start()

        def wait(self):
            send, recv_first, recv_rest = self.sems
            all_of(self.two, (send, recv_rest)).wait_recv()
            all_of(self.three, (send, recv_rest)).wait_send()

    def gather_sems():
        return new("send"), new("recv"), new("recv")

    class Scatter:
        def __init__(self, buf, land, rows, sems=None):
            self.buf, self.land, self.rows, self.sems = buf, land, rows, sems or pair()
            self.sends = [
                remote(buf.at[peer_block(j), rows], land.at[j - 1, rows], peer(j), self.sems) for j in (3, 1, 2)
            ]

        def start(self):
            start(self.sends)

        def finish(self):
            all_of(self.land.at[:, self.rows], self.sems).wait()
            total = self.buf[own, self.rows].astype(F32)
            for j in range(3):
                total = total + self.land[j, self.rows].astype(F32)
            return total

    class RelayScatter:
        def __init__(self, buf, via, land, rows, sems):
            self.buf, self.via, self.land, self.rows = buf, via, land, rows
            self.second = peer_block(2)
            self.first, self.rest = sems
            self.sends = [
                remote(buf.at[peer_block(3), rows], via.at[rows], peer(1), self.first),
                remote(buf.at[peer_block(1), rows], land.at[0, rows], peer(1), self.rest),
            ]
            self.last = remote(buf.at[self.second, rows], land.at[1, rows], peer(2), self.rest)

        def start(self):
            start(self.sends)

        def relay(self):
            self.sends[0].wait()
            total = self.buf[self.second, self.rows].astype(F32) + self.via[self.rows].astype(F32)
            self.buf[self.second, self.rows] = total.astype(BF)
            self.last.start()

        def finish(self):
            all_of(self.land.at[0:2, self.rows], self.rest).wait()
            return (
                self.buf[own, self.rows].astype(F32)
                + self.land[0, self.rows].astype(F32)
                + self.land[1, self.rows].astype(F32)
            )

    gather_triples = [gather_sems() for _ in range(NSUB)]
    scatter_pairs = [pair() for _ in range(NSUB)]

    def span(a):
        return pl.ds(a * SUB, SUB)

    def half(a):
        return slice(a * SUB, (a + 1) * SUB)

    def way(a):
        return 1 + a % 2

    mine = pl.ds(4 * c, 4)
    theirs = pl.ds(4 * (1 - c), 4)
    w_sq = ColumnWeight(r.w_sq, r.WQKV, [[0], [1], [2]], 128, True)
    w_so = RowWeight(r.w_so, r.WSO, 128)
    w_cq = ColumnWeight(r.w_cq, r.WCQ, [[0, 1, 2]], 128)
    w_co = RowWeight(r.w_co, r.WCO, 128)
    w_up = ColumnWeight(r.w_up, r.WUP, [[0]], 512)
    w_dn = RowWeight(r.w_dn, r.WDN, 512)
    ag_x = [Gather(r.X, pl.ds(k * HALF, HALF), 2, 4 * c, apart=True) for k in range(2)]
    swap_start(0)

    @pl.when(stays)
    def _():
        swaps[0][1].wait()
        for g in ag_x:
            g.direct[0].start()
        w_sq.near()
        for g in ag_x:
            g.direct[0].wait_recv()
        w_sq.far()
        for g in ag_x:
            g.direct[1].start()
        swaps[1][1].start()
        swaps[2][1].start()
        w_sq.relay()
        for g in ag_x:
            g.relay()

    @pl.when(jnp.logical_not(stays))
    def _():
        w_sq.near()
        w_sq.far()
        w_sq.relay()
        swaps[1][0].start()
        swaps[2][0].start()
        swaps[0][0].wait()
        start(ag_x)
        for g in ag_x:
            g.relay()
            g.direct[0].wait_recv()

    w_so.send()
    w_cq.send()
    w_sq.cross()
    w_co.send()
    swap_wait(1)
    ag_e = Gather(r.E, pl.ds(0, ENC), 2)
    ag_e.start()
    w_up.send()
    for g in ag_x:
        g.hop.wait()
        all_of(g.two, g.sems[:2]).wait_send()
    x_both = remote(r.X.at[mine], r.X.at[mine], mate)
    x_both.start()
    w_sq.share()
    w_sq.ready()

    lane = lax.broadcasted_iota(jnp.int32, (1, 128), 1)
    heads = [lane // 64 == 0, lane // 64 == 1]

    def head_of(v, hh):
        return jnp.where(heads[hh], v, jnp.zeros_like(v))

    def own_cols(ref, row, width):
        off = [pl.multiple_of((4 * k + own) * width, 128) for k in range(2)]
        return jnp.concatenate([ref[row : row + 1, pl.ds(o, width)] for o in off], 1)

    def blocks(ref, a, width):
        return ref[:, half(a), :].reshape(4 * SUB, width)

    def shards(ref, rows, cols):
        return ref[rows.start // 128 : rows.stop // 128, :, cols].reshape(rows.stop - rows.start, -1)

    def add_small(row, col, width, value):
        at = slice(0, width) if isinstance(col, int) else pl.ds(pl.multiple_of(col, 128), width)
        ref, row = (r.SB, row) if row < 8 else (r.SM, row - 8)
        ref[row : row + 1, at] += value

    def colsum(v):
        return jnp.sum(v, 0, keepdims=True)

    bias_q = own_cols(r.sb, 0, 128)
    bias_v = own_cols(r.sb, 1, 128)
    for i in range(2):
        lhs = r.X[pl.ds(4 * c + 2 * i, 2)].reshape(256, WIDTH)
        for p in range(3):
            out = dg(lhs, r.WQKV[:, :, p * 256 : (p + 1) * 256].reshape(WIDTH, 256), 1, 0)
            if p == 0:
                out = (out + bias_q) * 0.125
            if p == 2:
                out = out + bias_v
            out = out.astype(BF)
            for k in range(2):
                r.QST[k, p, 2 * i : 2 * i + 2] = out[:, k * 128 : (k + 1) * 128].reshape(2, ROWS, 128)
    qkv_x = remote(r.QST.at[1 - c], r.QKV.at[:, mine], mate)
    qkv_x.start()
    r.QKV[:, mine] = r.QST[c]
    w_cq.relay()
    ag_e.relay()
    w_so.cross()
    qkv_x.wait()

    def keys(p, n):
        return r.QKV[p, 0 : n // ROWS].reshape(n, 128)

    probs = [r.P0, r.P1, r.P2, r.P3]
    for i in range(4):
        n = (i + 1) * 256
        q = r.QKV[0, 2 * i : 2 * i + 2].reshape(256, 128)
        outs = []
        for hh in range(2):
            s = dg(head_of(q, hh), keys(1, n), 1, 1)
            qpos = lax.broadcasted_iota(jnp.int32, (256, n), 0) + i * 256
            kpos = lax.broadcasted_iota(jnp.int32, (256, n), 1)
            s = jnp.where(kpos <= qpos, s, -1e30)
            e = jnp.exp(s - jnp.max(s, 1, keepdims=True))
            p = (e * (1.0 / jnp.sum(e, 1, keepdims=True))).astype(BF)
            probs[i][hh] = p
            outs.append(dg(p, keys(2, n), 1, 0))
        o = jnp.where(heads[0], outs[0], outs[1])
        r.O[i * 256 : (i + 1) * 256] = o
        r.ATF[2 * i : 2 * i + 2] = o.astype(BF).reshape(2, ROWS, 128)
    my_cols = pl.ds(pl.multiple_of(c * 128, 128), 128)
    att_x = remote(r.ATF.at[theirs], r.ATT.at[:, :, my_cols], mate)
    att_x.start()
    r.ATT[:, :, my_cols] = r.ATF[mine]
    w_so.share()
    w_so.ready()
    att_x.wait()

    def partial(a, lhs, w, contract, chunk=512, sums=None):
        for n in range(WIDTH // chunk):
            cols = slice(n * chunk, (n + 1) * chunk)
            out = dg(lhs, w(cols), 1, contract)
            r.PB[:, half(a), cols] = out.astype(BF).reshape(4, SUB, chunk)
        sums = sums or Scatter(r.PB, r.RB, span(a), scatter_pairs[a])
        sums.start()
        return sums

    def norm(i, rows, hidden):
        centre = hidden - jnp.mean(hidden, -1, keepdims=True)
        rstd = lax.rsqrt(jnp.mean(centre * centre, -1, keepdims=True) + EPS)
        xhat = centre * rstd
        return xhat, rstd, xhat * r.gain[i : i + 1, :] + r.shift[i : i + 1, :]

    def norm_back(i, dy, xhat, rstd):
        add_small((5, 9, 10)[i], 0, WIDTH, colsum(dy * xhat))
        add_small((6, 11, 12)[i], 0, WIDTH, colsum(dy))
        d = dy * r.gain[i : i + 1, :]
        mean_d = jnp.mean(d, -1, keepdims=True)
        mean_dx = jnp.mean(d * xhat, -1, keepdims=True)
        return rstd * (d - mean_d - xhat * mean_dx)

    def gathered(buf, a, value, first=None):
        buf[own, half(a)] = value
        g = Gather(buf, span(a), first or way(a), 0, gather_triples[a])
        g.start()
        return g

    def comp1(a):
        return partial(a, blocks(r.ATT, a, 256), lambda cols: r.WSO[:, :, cols].reshape(256, -1), 0)

    def fin1(a, total):
        hidden = r.X[t, half(a)].astype(F32) + total + r.sb[2:3, :]
        xhat, rstd, out = norm(0, half(a), hidden)
        r.XH[0, half(a)] = xhat
        r.RSTD[0, half(a)] = rstd
        r.RES[half(a)] = out
        return gathered(r.F, a, out.astype(BF), 2)

    def encoder_kv():
        w_cq.ready()
        ag_e.wait()
        bias_cv = own_cols(r.cb, 1, 128)
        for k in range(2):
            out = dg(
                r.E[...].reshape(4 * ENC, WIDTH),
                r.WCQ[:, :, 256 + k * 256 : 512 + k * 256].reshape(WIDTH, 256),
                1,
                0,
            )
            if k == 1:
                out = out + bias_cv
            r.KVC[mine, :, k * 256 : (k + 1) * 256] = out.astype(BF).reshape(4, ENC, 256)
        kvc_x.start()

    kvc_x = remote(r.KVC.at[mine], r.KVC.at[mine], mate)

    def enc_keys(part, k):
        return r.KVC[:, :, part * 256 + k * 128 : part * 256 + (k + 1) * 128].reshape(512, 128)

    def comp2(a):
        bias_cq = own_cols(r.cb, 0, 128)
        visible = lax.broadcasted_iota(jnp.int32, (1, 512), 1).astype(F32) < r.LENS[1:2, 0:1]
        q = dg(blocks(r.F, a, WIDTH), r.WCQ[:, :, 0:256].reshape(WIDTH, 256), 1, 0)
        q = ((q + bias_cq) * 0.125).astype(BF)
        r.QC[:, half(a)] = q.reshape(4, SUB, 256)
        for k in range(2):
            outs = []
            for hh in range(2):
                s = dg(head_of(q[:, k * 128 : (k + 1) * 128], hh), enc_keys(0, k), 1, 1)
                s = jnp.where(visible, s, -1e30)
                e = jnp.exp(s - jnp.max(s, 1, keepdims=True))
                p = (e * (1.0 / jnp.sum(e, 1, keepdims=True))).astype(BF)
                r.PC[2 * k + hh, a] = p
                outs.append(dg(p, enc_keys(1, k), 1, 0))
            o = jnp.where(heads[0], outs[0], outs[1])
            r.OC[a, :, k * 128 : (k + 1) * 128] = o
            r.CATT[:, half(a), k * 128 : (k + 1) * 128] = o.astype(BF).reshape(4, SUB, 128)
        return partial(a, blocks(r.CATT, a, 256), lambda cols: r.WCO[:, :, cols].reshape(256, -1), 0)

    def fin2(a, total):
        hidden = r.RES[half(a)] + total + r.cb[2:3, :]
        xhat, rstd, out = norm(1, half(a), hidden)
        r.XH[1, half(a)] = xhat
        r.RSTD[1, half(a)] = rstd
        r.RES2[half(a)] = out
        return gathered(r.S, a, out.astype(BF), 2)

    def comp3(a):
        lhs = blocks(r.S, a, WIDTH)
        for k in range(2):
            cols = slice(k * 512, (k + 1) * 512)
            bias_up = r.fb1[0:1, pl.ds(pl.multiple_of((4 * k + own) * 512, 128), 512)]
            u = dg(lhs, r.WUP[:, :, cols].reshape(WIDTH, 512), 1, 0) + bias_up
            cdf = 0.5 + 0.5 * lax.erf(u * 0.7071067811865476)
            r.ACT[:, half(a), cols] = (u * cdf).astype(BF).reshape(4, SUB, 512)
            slope = cdf + u * (jnp.exp(-0.5 * u * u) * 0.3989422804014327)
            r.DGL[a, :, cols] = slope.astype(BF)
        return partial(a, blocks(r.ACT, a, 1024), lambda cols: r.WDN[:, :, cols].reshape(1024, -1), 0)

    def fin3(a, total):
        hidden = r.RES2[half(a)] + total + r.fb2[0:1, :]
        xhat, rstd, out = norm(2, half(a), hidden)
        r.MXS[half(a)] = out.astype(BF)
        place = lax.broadcasted_iota(jnp.int32, (SUB, 1), 0) + (t * ROWS + a * SUB)
        dy = jnp.where(place.astype(F32) < r.LENS[0:1, 0:1], r.DMX[half(a)].astype(F32), 0.0)
        d = norm_back(2, dy, xhat, rstd)
        r.RES[half(a)] = d
        low = d.astype(BF)
        add_small(13, 0, WIDTH, colsum(low.astype(F32)))
        return gathered(r.DM, a, low)

    def comp4(a):
        lhs = blocks(r.DM, a, WIDTH)
        for k in range(2):
            cols = slice(k * 512, (k + 1) * 512)
            d_act = dg(lhs, r.WDN[k], 1, 1).astype(BF).astype(F32)
            low = (d_act * r.DGL[a, :, cols].astype(F32)).astype(BF)
            r.DUP[:, half(a), cols] = low.reshape(4, SUB, 512)
            at = pl.ds(pl.multiple_of(y * 512, 512), 512)
            r.SM[pl.ds(8 + 2 * k + l, 1), at] += colsum(low.astype(F32))
        return partial(a, blocks(r.DUP, a, 1024), lambda cols: shards(r.WUP, cols, slice(0, 1024)), 1)

    def fin4(a, total):
        d = norm_back(1, r.RES[half(a)] + total, r.XH[1, half(a)], r.RSTD[1, half(a)])
        r.RES2[half(a)] = d
        low = d.astype(BF)
        add_small(8, 0, WIDTH, colsum(low.astype(F32)))
        return gathered(r.DC, a, low)

    def comp5(a):
        d_att = dg(blocks(r.DC, a, WIDTH), r.WCO[...].reshape(256, WIDTH), 1, 1).astype(BF)
        for k in range(2):
            cols = slice(k * 128, (k + 1) * 128)
            d_pair = d_att[:, cols]
            o_pair = r.OC[a, :, cols]
            q_pair = blocks(r.QC, a, 256)[:, cols]
            ds, dk, dv = [], None, None
            for hh in range(2):
                d_head = head_of(d_pair, hh)
                delta = jnp.sum(d_head.astype(F32) * o_pair, 1, keepdims=True)
                p = r.PC[2 * k + hh, a]
                d_scores = (p.astype(F32) * (dg(d_head, enc_keys(1, k), 1, 1) - delta)).astype(BF)
                ds.append(dg(d_scores, enc_keys(0, k), 1, 0))
                new_dk = dg(d_scores, head_of(q_pair, hh), 0, 0)
                new_dv = dg(p, d_head, 0, 0)
                dk = new_dk if dk is None else dk + new_dk
                dv = new_dv if dv is None else dv + new_dv
            dq = (jnp.where(heads[0], ds[0], ds[1]).astype(BF) * 0.125).astype(BF)
            r.DQC[:, half(a), cols] = dq.reshape(4, SUB, 128)
            add_small(3, (4 * k + own) * 128, 128, colsum(dq.astype(F32)))
            dv_cols = slice(256 + k * 128, 384 + k * 128)
            if a == 0:
                r.DKV[:, cols] = dk
                r.DKV[:, dv_cols] = dv
            else:
                r.DKV[:, cols] += dk
                r.DKV[:, dv_cols] += dv
        return partial(a, blocks(r.DQC, a, 256), lambda cols: shards(r.WCQ, cols, slice(0, 256)), 1)

    def fin5(a, total):
        d = norm_back(0, r.RES2[half(a)] + total, r.XH[0, half(a)], r.RSTD[0, half(a)])
        r.RES[half(a)] = d
        low = d.astype(BF)
        add_small(2, 0, WIDTH, colsum(low.astype(F32)))
        return gathered(r.DB, a, low)

    do_sems = pair()

    def comp6(a):
        d_att = dg(blocks(r.DB, a, WIDTH), r.WSO[...].reshape(256, WIDTH), 1, 1).astype(BF)
        mine_d = jnp.where(c == 0, d_att[:, 0:128], d_att[:, 128:256])
        theirs_d = jnp.where(c == 0, d_att[:, 128:256], d_att[:, 0:128])
        r.DATS[:, half(a)] = theirs_d.reshape(4, SUB, 128)
        r.DO[mine, half(a)] = mine_d.reshape(4, SUB, 128)
        remote(r.DATS.at[:, span(a)], r.DO.at[mine, span(a)], mate, do_sems).start()

    class GroupSum:
        def __init__(self, total, land, four):
            self.total, self.land, self.four = total, land, four

        def cores(self):
            self.copy = remote(self.total, self.land, mate)
            self.copy.start()

        def chips(self):
            self.copy.wait()
            at = self.four.at[own]
            at[...] = self.total[...] + self.land[...]
            self.sems = pair()
            start([remote(at, at, peer(j), self.sems) for j in (1, 2, 3)])

        def sum(self):
            all_of(self.four.at[0:3], self.sems).wait()
            f = self.four
            return (f[0] + f[1]) + (f[2] + f[3])

    small = GroupSum(r.SM, r.SMR, r.SM4)
    late = GroupSum(r.SB, r.SBR, r.SB4)
    halves = remote(r.ALL, r.ALLR.at[0], h_peer)
    sides = remote(r.ALL, r.ALLR.at[1], x_peer)

    def sum_halves():
        r.ALL[0:8] = late.sum()
        r.ALL[8:24] = small.sum()
        halves.start()

    def sum_sides():
        halves.wait()
        r.ALL[...] += r.ALLR[0]
        sides.start()

    def sum_end():
        sides.wait()
        r.o_small[...] = r.ALL[...] + r.ALLR[1]

    far_shards, near_shards = pl.ds(4 * (1 - h), 4), pl.ds(4 * h, 4)

    class ColumnGrad:
        def __init__(self, name, out, parts, part=0, pieces=1):
            self.parts, self.out, self.pieces = parts, out, pieces
            for key in ("GS", "GR", "GK", "XS", "XR", "HS", "HR", "TS", "T"):
                setattr(self, key, getattr(r, key + "_" + name, None))
            self.part = part

        def compute(self, left, right, col, width):
            for target, k in ((self.GS, 1 - c), (self.GK, c)):
                rhs = right(k)
                for i in range(4):
                    out = dg(left(slice(i * 256, (i + 1) * 256)), rhs, 0, 0)
                    target[2 * i : 2 * i + 2, :, col : col + width] = out.astype(BF).reshape(2, 128, width)

        def compute_own(self, left, right):
            for i in range(4):
                out = dg(left(slice(i * 256, (i + 1) * 256)), right, 0, 0)
                self.GK[2 * i : 2 * i + 2] = out.astype(BF).reshape(2, 128, -1)

        def s0(self):
            self.core = remote(self.GS, self.GR, mate)
            self.core.start()

        def chip(self, shards, rows):
            if self.GR is None:
                return self.GK[shards, rows].astype(F32)
            return self.GK[shards, rows].astype(F32) + self.GR[shards, rows].astype(F32)

        def s1(self):
            if self.GR is not None:
                self.core.wait()
            self.far()
            self.near()

        def far(self):
            self.hsems, self.xc = pair(), []
            self.XS[0:4] = self.chip(far_shards, other_x).astype(BF)
            for i in range(self.pieces):
                at = slice(i * 4 // self.pieces, (i + 1) * 4 // self.pieces)
                self.xc.append(remote(self.XS.at[at], self.XR.at[at], x_peer))
                self.xc[i].start()

        def near(self):
            self.XS[4:8] = self.chip(near_shards, other_x).astype(BF)
            self.xn = remote(self.XS.at[4:8], self.XR.at[4:8], x_peer)
            self.xn.start()

        def s2(self, i=0):
            self.xc[i].wait()
            k = 4 // self.pieces
            at = slice(i * k, (i + 1) * k)
            total = self.chip(pl.ds(4 * (1 - h) + i * k, k), my_x) + self.XR[at].astype(F32)
            self.HS[at] = total.astype(BF)
            remote(self.HS.at[at], self.HR.at[at], h_peer, self.hsems).start()

        def s3(self):
            self.xn.wait()
            all_of(self.HS, self.hsems).wait()
            total = self.chip(near_shards, my_x) + self.XR[4:8].astype(F32) + self.HR[...].astype(F32)
            self.TS[...] = total.astype(BF)
            self.sems = pair()
            start([remote(self.TS.at[peer_block(j)], self.T.at[t, my_x], peer(j), self.sems) for j in (1, 2, 3)])
            self.T[t, my_x] = self.TS[own]

        def s4(self):
            all_of(self.TS.at[0:3], self.sems).wait()
            part = self.T.at[pl.ds(4 * c, 4), my_x]
            other = self.T.at[pl.ds(4 * c, 4), other_x]
            self.sems = pair()
            self.x2 = remote(part, part, x_peer)
            self.m2 = remote(other, other, mate, self.sems)
            self.x2.start()
            remote(part, part, mate, self.sems).start()

        def s5(self):
            self.x2.wait()
            self.m2.start()

        def s6(self):
            all_of(self.T.at[0:4], self.sems).wait()
            width = self.T.shape[2] // self.parts
            self.sem = new("local")
            for tt in range(8):
                for p in range(self.parts):
                    at = (p + self.part) * WIDTH + tt * width
                    src = self.T.at[tt, :, p * width : (p + 1) * width]
                    local(src, self.out.at[:, at : at + width], self.sem).start()

        def s7(self):
            local(self.T, self.T, self.sem).wait()

    class RowGrad:
        def __init__(self, name, out, pieces=1):
            self.out, self.pieces = out, pieces
            for key in ("GS", "GR", "GK", "XS", "XR", "HS", "HR", "T"):
                setattr(self, key, getattr(r, key + "_" + name))
            self.n = self.GS.shape[0] // 2

        def compute(self, left, right):
            for target, k in ((self.GS, 1 - c), (self.GK, c)):
                lhs = left(k)
                for i in range(2):
                    cols = slice(i * 512, (i + 1) * 512)
                    target[:, cols] = dg(lhs, right(cols), 0, 0).astype(BF)

        def s0(self):
            self.core = remote(self.GS, self.GR, mate)
            self.core.start()

        def rows(self, k):
            return pl.ds(pl.multiple_of(k * self.n, HALF), self.n)

        def piece(self, i):
            return slice(i * self.n // self.pieces, (i + 1) * self.n // self.pieces)

        def s1(self):
            self.core.wait()
            rows = self.rows(1 - x)
            self.XS[...] = (self.GK[rows].astype(F32) + self.GR[rows].astype(F32)).astype(BF)
            self.hsems, self.xc = pair(), []
            for i in range(self.pieces):
                at = self.piece(i)
                self.xc.append(remote(self.XS.at[at], self.XR.at[at], x_peer))
                self.xc[i].start()

        def total(self, i):
            k = self.n // self.pieces
            rows = pl.ds(pl.multiple_of(x * self.n, HALF) + i * k, k)
            return self.GK[rows].astype(F32) + self.GR[rows].astype(F32) + self.XR[self.piece(i)].astype(F32)

        def s2(self, i=0):
            self.xc[i].wait()
            at = self.piece(i)

            @pl.when(jnp.logical_not(stays))
            def _():
                self.HS[at] = self.total(i).astype(BF)
                remote(self.HS.at[at], self.HR.at[at], h_peer, self.hsems).start()

        def s3(self):
            part, other = self.T.at[self.rows(x)], self.T.at[self.rows(1 - x)]
            self.x2 = remote(part, part, x_peer)
            self.sems = pair()
            self.m1 = remote(part, part, mate, self.sems)
            self.m2 = remote(other, other, mate, self.sems)

            @pl.when(jnp.logical_not(stays))
            def _():
                all_of(self.HS, self.hsems).wait_send()

            @pl.when(stays)
            def _():
                all_of(self.HR, self.hsems).wait_recv()
                for i in range(self.pieces):
                    k = self.n // self.pieces
                    rows = pl.ds(pl.multiple_of(x * self.n, HALF) + i * k, k)
                    self.T[rows] = (self.total(i) + self.HR[self.piece(i)].astype(F32)).astype(BF)
                self.x2.start()
                self.m1.start()

        def s4(self):
            pass

        def s5(self):
            @pl.when(stays)
            def _():
                self.x2.wait()
                self.m2.start()

        def s6(self):
            @pl.when(stays)
            def _():
                all_of(self.T, self.sems).wait_send()

            @pl.when(jnp.logical_not(stays))
            def _():
                all_of(self.T, self.sems).wait_recv()

            self.outs = [local(self.T, self.out)]
            start(self.outs)

        def s7(self):
            wait(self.outs)

    g_dn = RowGrad("DN", r.o_dn, 4)
    g_up = ColumnGrad("UP", r.o_up, 1, pieces=2)
    g_co = RowGrad("CO", r.o_co)
    g_cq = ColumnGrad("CQ", r.o_cq, 3, pieces=2)
    g_so = RowGrad("SO", r.o_so)
    g_sq = [ColumnGrad("SQ%d" % p, r.o_sq, 1, p) for p in range(3)]

    def lanes(ref, k, width, base=0):
        return ref[:, :, pl.ds(pl.multiple_of(base + k * width, 128), width)].reshape(-1, width)

    rs_e = RelayScatter(r.PBE, r.VIAE, r.RBE, slice(0, ENC), [pair(), pair()])
    last_pairs = [pair() for _ in range(NSUB)]
    dk_x = remote(r.DKS, r.DKR, mate)

    def encoder_swap():
        their_enc = pl.ds(pl.multiple_of((1 - c) * 256, 256), 256)
        r.DKS[...] = r.DKV[their_enc].astype(BF).reshape(4, ENC, 512)
        dk_x.start()

    def encoder_back():
        dk_x.wait()
        my_enc = pl.ds(pl.multiple_of(c * 256, 256), 256)
        low = (r.DKV[my_enc] + r.DKR[...].reshape(256, 512).astype(F32)).astype(BF)
        r.DKL[...] = low.reshape(4, ENC, 512)
        dv_sum = colsum(low[:, 256:512].astype(F32))
        for k in range(2):
            add_small(4, (4 * k + own) * 128, 128, dv_sum[:, k * 128 : (k + 1) * 128])
        for n in range(2):
            cols = slice(n * 512, (n + 1) * 512)
            out = dg(low, shards(r.WCQ, cols, slice(256, 768)), 1, 1)
            r.PBE[:, :, cols] = out.astype(BF).reshape(4, ENC, 512)
        rs_e.start()

    def encoder_out():
        r.DES[...] = rs_e.finish().astype(BF)
        outs["enc"] = leave(r.DES, r.o_denc)

    def mixed_out():
        outs["mixed"] = leave(r.MXS, r.o_mixed)

    def grad_dn():
        g_dn.compute(lambda k: lanes(r.ACT, k, 512), lambda cols: r.DM[:, :, cols].reshape(512, -1))
        g_dn.s0()

    def grad_up():
        g_up.compute(lambda cols: r.S[:, :, cols].reshape(512, -1), lambda k: lanes(r.DUP, k, 512), 0, 512)
        g_up.s0()

    def grad_co():
        g_co.compute(lambda k: lanes(r.CATT, k, 128), lambda cols: r.DC[:, :, cols].reshape(512, -1))
        g_co.s0()

    def grad_cq():
        g_cq.compute(lambda cols: r.F[:, :, cols].reshape(512, -1), lambda k: lanes(r.DQC, k, 128), 0, 128)
        for p in range(2):
            g_cq.compute(
                lambda cols: r.E[:, :, cols].reshape(256, -1),
                lambda k, p=p: lanes(r.DKL, k, 128, 256 * p),
                128 + 128 * p,
                128,
            )
        g_cq.s0()

    def grad_so():
        g_so.compute(lambda k: lanes(r.ATT, k, 128), lambda cols: r.DB[:, :, cols].reshape(512, -1))
        g_so.s0()

    outs = {}

    beside = {
        1: [w_cq.cross, w_up.relay, w_co.cross],
        2: [w_cq.share, w_dn.send],
        3: [encoder_kv, w_co.share, lambda: swap_start(3), lambda: swap_wait(2), kvc_x.wait, w_co.ready, w_up.cross],
        4: [w_dn.cross],
        5: [w_up.share],
        6: [w_dn.share],
        7: [w_up.ready, w_dn.ready],
        8: [lambda: swap_wait(3), x_both.wait],
        13: [mixed_out],
        15: [grad_dn, grad_up, g_dn.s1],
        16: [g_up.s1, lambda: g_dn.s2(0)],
        17: [lambda: g_dn.s2(1), small.cores],
        18: [lambda: g_dn.s2(2)],
        19: [encoder_swap, grad_co, lambda: g_dn.s2(3)],
        20: [encoder_back, grad_cq, g_co.s1, lambda: g_up.s2(0)],
        21: [small.chips, g_cq.s1, lambda: g_up.s2(1)],
        23: [rs_e.relay, grad_so, g_co.s2, lambda: g_cq.s2(0), lambda: g_cq.s2(1), g_so.s1],
    }

    comps = [comp1, comp2, comp3, comp4, comp5]
    fins = [fin1, fin2, fin3, fin4, fin5]
    rs, ag = {}, {}
    for slot in range(6 * NSUB):
        p, a = divmod(slot, NSUB)
        if p > 0:
            ag[p - 1, a].wait()
        if p < 5:
            rs[p, a] = comps[p](a)
        else:
            comp6(a)
        p, a = divmod(slot - 1, NSUB)
        if 0 <= p < 5:
            ag[p, a] = fins[p](a, rs[p, a].finish())
        p, a = divmod(slot - 2, NSUB)
        if 0 <= p < 5:
            ag[p, a].relay()
        for job in beside.get(slot, ()):
            job()

    all_of(r.DATS, do_sems).wait()
    r.DKVS[...] = jnp.zeros_like(r.DKVS)
    for i in range(4):
        n = (i + 1) * 256
        q = r.QKV[0, 2 * i : 2 * i + 2].reshape(256, 128)
        d_pair = r.DO[2 * i : 2 * i + 2].reshape(256, 128)
        o_pair = r.O[i * 256 : (i + 1) * 256]
        dqs, dk, dv = [], None, None
        for hh in range(2):
            d_head = head_of(d_pair, hh)
            delta = jnp.sum(d_head.astype(F32) * o_pair, 1, keepdims=True)
            p = probs[i][hh]
            d_scores = (p.astype(F32) * (dg(d_head, keys(2, n), 1, 1) - delta)).astype(BF)
            dqs.append(dg(d_scores, keys(1, n), 1, 0))
            new_dk = dg(d_scores, head_of(q, hh), 0, 0)
            new_dv = dg(p, d_head, 0, 0)
            dk = new_dk if dk is None else dk + new_dk
            dv = new_dv if dv is None else dv + new_dv
        dq = (jnp.where(heads[0], dqs[0], dqs[1]).astype(BF) * 0.125).astype(BF)
        r.DJN[0, 2 * i : 2 * i + 2] = dq.reshape(2, ROWS, 128)
        r.SB[0:1, pl.ds(pl.multiple_of(t * 128, 128), 128)] += colsum(dq.astype(F32))
        r.DKVS[0, 0:n] += dk
        r.DKVS[1, 0:n] += dv
    r.DJN[1] = r.DKVS[0].astype(BF).reshape(8, ROWS, 128)
    low = r.DKVS[1].astype(BF)
    r.DJN[2] = low.reshape(8, ROWS, 128)
    r.SB[1:2, pl.ds(pl.multiple_of(t * 128, 128), 128)] = colsum(low.astype(F32))
    dj_sems = pair()
    for p in range(3):
        at = pl.ds(pl.multiple_of(p * 256 + c * 128, 128), 128)
        remote(r.DJN.at[p, theirs], r.DJ.at[:, :, at], mate, dj_sems).start()
        r.DJ[:, :, at] = r.DJN[p, mine]
    late.cores()
    for p in range(3):
        g_sq[p].compute_own(lambda cols: r.X[:, :, cols].reshape(1024, -1), r.DJN[p].reshape(1024, 128))
        g_sq[p].far()
    for p in range(3):
        g_sq[p].near()
    g_so.s2()
    g_up.s3()
    g_dn.s3()
    late.chips()
    all_of(r.DJ.at[:, :, 0:384], dj_sems).wait()
    rs6 = [
        partial(
            a,
            blocks(r.DJ, a, 768),
            lambda cols: shards(r.WQKV, cols, slice(0, 768)),
            1,
            sums=RelayScatter(r.PB, r.VIA, r.RB, span(a), [last_pairs[a], scatter_pairs[a]]),
        )
        for a in range(NSUB)
    ]
    g_sq[0].s2()
    g_sq[1].s2()
    g_sq[2].s2()
    rs6[0].relay()
    g_up.s4()
    rs6[1].relay()
    g_cq.s3()
    rs6[2].relay()
    rs6[3].relay()
    g_co.s3()
    sum_halves()
    g_sq[0].s3()
    g_sq[1].s3()
    g_cq.s4()
    g_sq[2].s3()
    g_so.s3()
    r.DTS[half(0)] = (r.RES[half(0)] + rs6[0].finish()).astype(BF)
    r.DTS[half(1)] = (r.RES[half(1)] + rs6[1].finish()).astype(BF)
    g_sq[0].s4()
    g_sq[1].s4()
    r.DTS[half(2)] = (r.RES[half(2)] + rs6[2].finish()).astype(BF)
    r.DTS[half(3)] = (r.RES[half(3)] + rs6[3].finish()).astype(BF)
    outs["tokens"] = leave(r.DTS, r.o_dtok)
    encoder_out()
    g_sq[2].s4()
    sum_sides()
    g_dn.s5()
    g_up.s5()
    g_co.s5()
    g_so.s5()
    g_dn.s6()
    g_cq.s5()
    g_sq[0].s5()
    g_up.s6()
    g_sq[1].s5()
    g_co.s6()
    g_so.s6()
    g_cq.s6()
    g_sq[2].s5()
    g_sq[0].s6()
    g_sq[1].s6()
    g_sq[2].s6()
    sum_end()

    @pl.when(jnp.logical_not(stays))
    def _():
        for cp in outs.values():
            cp.wait()

    for g in (g_dn, g_up, g_co, g_cq, g_so, *g_sq):
        g.s7()
    assert count["send"] <= N_SEND and count["recv"] <= N_RECV and count["local"] <= N_LOCAL


def on_chip(*args):
    (tokens, encoder, seq_len, enc_len, d_mixed, *rest) = args
    *mats, self_bias, cross_bias, norm_gain, norm_bias, fc1_bias, fc2_bias = rest
    anywhere = pl.BlockSpec(memory_space=pl.ANY)
    vmem = pl.BlockSpec(memory_space=pltpu.VMEM)
    smem = pl.BlockSpec(memory_space=pltpu.SMEM)
    shapes = [
        ((ROWS, WIDTH), BF),
        ((ROWS, WIDTH), BF),
        ((ENC, WIDTH), BF),
        ((128, 3 * WIDTH), BF),
        ((128, WIDTH), BF),
        ((128, 3 * WIDTH), BF),
        ((128, WIDTH), BF),
        ((128, HIDDEN), BF),
        ((512, WIDTH), BF),
        ((24, WIDTH), F32),
    ]
    outs = pl.pallas_call(
        layer_kernel,
        out_shape=[jax.ShapeDtypeStruct(s, d) for s, d in shapes],
        in_specs=[anywhere, anywhere, smem, smem, anywhere] + [anywhere] * 6 + [vmem] * 6,
        out_specs=[vmem] * 3 + [anywhere] * 6 + [vmem],
        scratch_shapes=[pltpu.VMEM(s, d) for s, d in SCRATCH.values()]
        + [
            pltpu.SemaphoreType.DMA((N_SEND,)),
            pltpu.SemaphoreType.DMA((N_RECV,)),
            pltpu.SemaphoreType.DMA((N_LOCAL,)),
        ],
        compiler_params=pltpu.CompilerParams(
            collective_id=0, has_side_effects=True, vmem_limit_bytes=VMEM_BYTES
        ),
        cost_estimate=pl.CostEstimate(
            flops=16 * 10**9, bytes_accessed=16 * 2**20, transcendentals=8 * 2**20
        ),
    )(
        tokens, encoder, seq_len, enc_len, d_mixed, *mats,
        self_bias, cross_bias, norm_gain, norm_bias,
        fc1_bias.reshape(1, -1), fc2_bias.reshape(1, -1),
    )
    steps = 4

    def rows_of(shape):
        return pl.BlockSpec((shape[0] // steps, shape[1]), lambda i: (i, 0))

    def whole(shape):
        return pl.BlockSpec(shape, lambda i: (0, 0))

    wide = [(s, BF if k == 0 else F32) for k, (s, _) in enumerate(shapes[:-1])]
    flat = [((3, WIDTH), F32)] * 4 + [((1, HIDDEN), F32), ((1, WIDTH), F32)]
    *results, fc1_sum, fc2_sum = pl.pallas_call(
        widen_kernel,
        grid=(steps,),
        out_shape=[jax.ShapeDtypeStruct(s, d) for s, d in wide + flat],
        in_specs=[rows_of(s) for s, _ in shapes[:-1]] + [whole(shapes[-1][0])],
        out_specs=[rows_of(s) for s, _ in wide] + [whole(s) for s, _ in flat],
        compiler_params=pltpu.CompilerParams(vmem_limit_bytes=VMEM_BYTES),
    )(*outs)
    return (*results, fc1_sum.reshape(-1), fc2_sum.reshape(-1))


def widen_kernel(*refs):
    n = len(OUT_NAMES)
    small, flat = refs[n - 1], refs[2 * n - 1 :]
    for src, dst in zip(refs[: n - 1], refs[n:]):
        dst[...] = src[...].astype(dst.dtype)
    for k, rows in enumerate(((0, 1, 2), (3, 4, 8), (5, 9, 10), (6, 11, 12))):
        for i, row in enumerate(rows):
            flat[k][i : i + 1, :] = small[row : row + 1, :]
    for k in range(4):
        flat[4][0:1, k * WIDTH : (k + 1) * WIDTH] = small[16 + k : 17 + k, :]
    flat[5][...] = small[13:14, :]


def fits(mesh, tokens, encoder, self_qkv, fc1_weight):
    return (
        (mesh.shape["rep"], mesh.shape["shard"]) == (4, 8)
        and tokens.shape == (32 * ROWS, WIDTH)
        and encoder.shape == (32 * ENC, WIDTH)
        and self_qkv.shape == (WIDTH, 3 * WIDTH)
        and fc1_weight.shape == (WIDTH, HIDDEN)
    )


def solution(mesh):
    def placed(body):
        return jax.shard_map(
            body,
            mesh=mesh,
            in_specs=(
                P(("rep", "shard"), None),
                P(("rep", "shard"), None),
                P("rep"),
                P("rep"),
                P(("rep", "shard"), None),
                P("shard", None),
                P("shard", None),
                P("shard", None),
                P("shard", None),
                P("shard", None),
                P("shard", None),
                P(),
                P(),
                P(),
                P(),
                P(),
                P(),
            ),
            out_specs=(
                P(("rep", "shard"), None),
                P(("rep", "shard"), None),
                P(("rep", "shard"), None),
                P("shard", None),
                P("shard", None),
                P("shard", None),
                P("shard", None),
                P("shard", None),
                P("shard", None),
                P(),
                P(),
                P(),
                P(),
                P(),
                P(),
            ),
            check_vma=False,
        )

    def run(*args):
        fast = fits(mesh, args[0], args[1], args[5], args[9])
        return placed(on_chip if fast else local)(*args)

    return run
```

```python
from functools import partial

import jax
import jax.numpy as jnp
from jax import lax
from jax.experimental import pallas as pl
from jax.experimental.pallas import tpu as pltpu
from jax.sharding import PartitionSpec as P

HEADS = 16
HEAD = 64


def for_sending(array):
    return jax.tree.map(lambda a: a.astype(jnp.bfloat16) if a.dtype == jnp.float32 else a, array)


def layer_norm(hidden, gain_row, shift_row):
    centre = hidden - jnp.mean(hidden, -1, keepdims=True)
    spread = jnp.mean(centre * centre, -1, keepdims=True)
    return centre * lax.rsqrt(spread + 1e-05) * gain_row + shift_row


def exact_gelu(values):
    return jax.nn.gelu(values, approximate=False)


def contract_rows(left, right):
    return lax.dot_general(
        left, right, (((0,), (0,)), ((), ())), preferred_element_type=jnp.float32
    )


def back_dot(grad_rows, weight):
    return lax.dot_general(
        grad_rows, weight, (((1,), (1,)), ((), ())), preferred_element_type=jnp.float32
    )


def causal_mask(query_pos, key_pos):
    return key_pos[None, :] <= query_pos[:, None]


def enc_visible(query_pos, key_pos, enc_limit):
    return jnp.broadcast_to((key_pos < enc_limit)[None, :], (query_pos.shape[0], key_pos.shape[0]))


def only_live(step_fn, live_fn):

    def wrapped(totals, block_in, offset):
        return lax.cond(
            live_fn(block_in, offset), lambda: step_fn(totals, block_in, offset), lambda: totals
        )

    return wrapped


def self_fold(key_pair, step_fn, start_state, store):
    return step_fn(
        start_state,
        jax.tree.map(
            lambda a: lax.all_gather(a, "shard", axis=0, tiled=True), for_sending(key_pair)
        ),
        jnp.int32(0),
    )


def cross_fold(key_pair, step_fn, start_state, store):
    return step_fn(
        start_state,
        jax.tree.map(
            lambda a: lax.all_gather(a, "shard", axis=0, tiled=True), for_sending(key_pair)
        ),
        jnp.int32(0),
    )


def keys_live(query_pos, allowed_fn):

    def live_fn(block_in, offset):
        key_pos = jnp.arange(block_in[0].shape[0], dtype=jnp.int32)
        return jnp.any(allowed_fn(query_pos, key_pos))

    return live_fn


def head_scores(query_heads, query_pos, key_block, allowed_fn):
    key_count = key_block.shape[0]
    key_pos = jnp.arange(key_count, dtype=jnp.int32)
    scores = jnp.einsum(
        "qhd,khd->hqk",
        query_heads,
        key_block.reshape(key_count, HEADS, HEAD),
        preferred_element_type=jnp.float32,
    )
    return (scores, allowed_fn(query_pos, key_pos)[None])


def forward_pass(query_part, query_pos, key_pair, allowed_fn, folder):
    query_count = query_part.shape[0]
    query_heads = query_part.reshape(query_count, HEADS, HEAD)
    live_fn = keys_live(query_pos, allowed_fn)

    def stat_step(totals, block_in, offset):
        highest, mass = totals
        scores, allowed = head_scores(query_heads, query_pos, block_in[0], allowed_fn)
        masked = jnp.where(allowed, scores, -1e30)
        raised = jnp.maximum(highest, jnp.max(masked, -1))
        fresh = jnp.sum(jnp.where(allowed, jnp.exp(masked - raised[:, :, None]), 0.0), -1)
        return (raised, fresh)

    start_state = (
        jnp.full((HEADS, query_count), -1e30, jnp.float32),
        jnp.zeros((HEADS, query_count), jnp.float32),
    )
    highest, mass = folder(key_pair, only_live(stat_step, live_fn), start_state, None)
    log_total = highest + jnp.log(mass)

    def out_step(totals, block_in, offset):
        scores, allowed = head_scores(query_heads, query_pos, block_in[0], allowed_fn)
        weights_low = jnp.where(allowed, jnp.exp(scores - log_total[:, :, None]), 0.0).astype(
            jnp.bfloat16
        )
        value_heads = block_in[1].reshape(block_in[1].shape[0], HEADS, HEAD)
        return jnp.einsum(
            "hqk,khd->qhd", weights_low, value_heads, preferred_element_type=jnp.float32
        )

    summed = folder(
        key_pair,
        only_live(out_step, live_fn),
        jnp.zeros((query_count, HEADS, HEAD), jnp.float32),
        None,
    )
    return (log_total.T, summed)


def query_step(query_part, query_pos, allowed_fn, log_rows, delta_rows, d_out):
    query_count = query_part.shape[0]
    query_heads = query_part.reshape(query_count, HEADS, HEAD)
    grad_heads = d_out.reshape(query_count, HEADS, HEAD)
    log_total = log_rows.T
    correction = delta_rows.T

    def grad_step(totals, block_in, offset):
        key_block, value_block = block_in
        key_count = key_block.shape[0]
        scores, allowed = head_scores(query_heads, query_pos, key_block, allowed_fn)
        probs = jnp.where(allowed, jnp.exp(scores - log_total[:, :, None]), 0.0)
        d_probs = jnp.einsum(
            "qhd,khd->hqk",
            grad_heads,
            value_block.reshape(key_count, HEADS, HEAD),
            preferred_element_type=jnp.float32,
        )
        d_scores = (probs * (d_probs - correction[:, :, None])).astype(jnp.bfloat16)
        return jnp.einsum(
            "hqk,khd->qhd",
            d_scores,
            key_block.reshape(key_count, HEADS, HEAD),
            preferred_element_type=jnp.float32,
        )

    return only_live(grad_step, keys_live(query_pos, allowed_fn))


def query_grad(query_part, query_pos, key_pair, allowed_fn, folder, log_rows, delta_rows, d_out):
    query_count = query_part.shape[0]
    step_fn = query_step(query_part, query_pos, allowed_fn, log_rows, delta_rows, d_out)
    return folder(key_pair, step_fn, jnp.zeros((query_count, HEADS, HEAD), jnp.float32), None)


def key_step(own_keys, own_values, key_pos, allowed_fn, log_all, delta_all):
    key_count = own_keys.shape[0]
    key_heads = own_keys.reshape(key_count, HEADS, HEAD)
    value_heads = own_values.reshape(key_count, HEADS, HEAD)

    def step_fn(totals, block_in, offset):
        query_block, grad_block = block_in
        query_count = query_block.shape[0]
        query_pos = jnp.arange(query_count, dtype=jnp.int32)
        log_part = log_all.T
        delta_part = delta_all.T
        query_heads = query_block.reshape(query_count, HEADS, HEAD)
        grad_heads = grad_block.reshape(query_count, HEADS, HEAD)
        scores = jnp.einsum(
            "qhd,khd->hqk", query_heads, key_heads, preferred_element_type=jnp.float32
        )
        allowed = allowed_fn(query_pos, key_pos)[None]
        probs = jnp.where(allowed, jnp.exp(scores - log_part[:, :, None]), 0.0)
        d_values = jnp.einsum(
            "hqk,qhd->khd",
            probs.astype(jnp.bfloat16),
            grad_heads,
            preferred_element_type=jnp.float32,
        )
        d_probs = jnp.einsum(
            "qhd,khd->hqk", grad_heads, value_heads, preferred_element_type=jnp.float32
        )
        d_scores = (probs * (d_probs - delta_part[:, :, None])).astype(jnp.bfloat16)
        d_keys = jnp.einsum(
            "hqk,qhd->khd", d_scores, query_heads, preferred_element_type=jnp.float32
        )
        return (d_keys, d_values)

    def live_fn(block_in, offset):
        query_pos = jnp.arange(block_in[0].shape[0], dtype=jnp.int32)
        return jnp.any(allowed_fn(query_pos, key_pos))

    return only_live(step_fn, live_fn)


def column_sum(values):
    return jnp.sum(values.astype(jnp.float32), 0)


def local(
    tokens,
    encoder,
    seq_len,
    enc_len,
    d_mixed,
    self_qkv,
    self_out,
    cross_qkv,
    cross_out,
    fc1_weight,
    fc2_weight,
    self_bias,
    cross_bias,
    norm_gain,
    norm_bias,
    fc1_bias,
    fc2_bias,
):
    model_width = tokens.shape[1]
    tok_rows = tokens.shape[0]
    enc_rows = encoder.shape[0]
    device_at = lax.axis_index("shard")
    positions = device_at * tok_rows + jnp.arange(tok_rows, dtype=jnp.int32)
    enc_positions = device_at * enc_rows + jnp.arange(enc_rows, dtype=jnp.int32)
    seq_limit = seq_len[0]
    visible = partial(enc_visible, enc_limit=enc_len[0])
    w_sq, w_so = (
        lax.all_gather(self_qkv, "shard", axis=0, tiled=True),
        lax.all_gather(self_out, "shard", axis=0, tiled=True),
    )
    joined = jnp.dot(tokens, w_sq, preferred_element_type=jnp.float32)
    query_s = ((joined[:, :model_width] + self_bias[0]) * 0.125).astype(jnp.bfloat16)
    key_s = joined[:, model_width : 2 * model_width].astype(jnp.bfloat16)
    value_s = (joined[:, 2 * model_width :] + self_bias[1]).astype(jnp.bfloat16)
    self_lse, self_summed = forward_pass(
        query_s, positions, (key_s, value_s), causal_mask, self_fold
    )
    attended = self_summed.reshape(tok_rows, model_width).astype(jnp.bfloat16)
    branch = jnp.dot(attended, w_so, preferred_element_type=jnp.float32) + self_bias[2]
    first_norm, first_pull = jax.vjp(
        layer_norm, tokens.astype(jnp.float32) + branch, norm_gain[0], norm_bias[0]
    )
    w_cq, w_co = (
        lax.all_gather(cross_qkv, "shard", axis=0, tiled=True),
        lax.all_gather(cross_out, "shard", axis=0, tiled=True),
    )
    first_low = first_norm.astype(jnp.bfloat16)
    query_c = (
        (
            jnp.dot(first_low, w_cq[:, :model_width], preferred_element_type=jnp.float32)
            + cross_bias[0]
        )
        * 0.125
    ).astype(jnp.bfloat16)
    enc_proj = jnp.dot(encoder, w_cq[:, model_width:], preferred_element_type=jnp.float32)
    key_c = enc_proj[:, :model_width].astype(jnp.bfloat16)
    value_c = (enc_proj[:, model_width:] + cross_bias[1]).astype(jnp.bfloat16)
    cross_lse, cross_summed = forward_pass(
        query_c, positions, (key_c, value_c), visible, cross_fold
    )
    cross_att = cross_summed.reshape(tok_rows, model_width).astype(jnp.bfloat16)
    branch_c = jnp.dot(cross_att, w_co, preferred_element_type=jnp.float32) + cross_bias[2]
    second_norm, second_pull = jax.vjp(
        layer_norm, first_norm + branch_c, norm_gain[1], norm_bias[1]
    )
    w_up, w_down = (
        lax.all_gather(fc1_weight, "shard", axis=0, tiled=True),
        lax.all_gather(fc2_weight, "shard", axis=0, tiled=True),
    )
    second_low = second_norm.astype(jnp.bfloat16)
    upward = jnp.dot(second_low, w_up, preferred_element_type=jnp.float32) + fc1_bias
    activated, gelu_pull = jax.vjp(exact_gelu, upward)
    act_low = activated.astype(jnp.bfloat16)
    branch_m = jnp.dot(act_low, w_down, preferred_element_type=jnp.float32) + fc2_bias
    output, third_pull = jax.vjp(layer_norm, second_norm + branch_m, norm_gain[2], norm_bias[2])
    valid = (positions < seq_limit).astype(jnp.float32)[:, None]
    d_third, d_gain3, d_shift3 = third_pull(d_mixed.astype(jnp.float32) * valid)
    d_branch_m = d_third.astype(jnp.bfloat16)
    g_down = contract_rows(act_low, d_branch_m)
    d_act = back_dot(d_branch_m, w_down).astype(jnp.bfloat16)
    (d_up,) = gelu_pull(d_act.astype(jnp.float32))
    d_up_low = d_up.astype(jnp.bfloat16)
    g_up = contract_rows(second_low, d_up_low)
    d_second = d_third + back_dot(d_up_low, w_up)
    d_hidden2, d_gain2, d_shift2 = second_pull(d_second)
    d_branch_c = d_hidden2.astype(jnp.bfloat16)
    g_co = contract_rows(cross_att, d_branch_c)
    d_cross_att = back_dot(d_branch_c, w_co).astype(jnp.bfloat16)
    cross_delta = jnp.einsum(
        "qhd,qhd->qh", d_cross_att.reshape(tok_rows, HEADS, HEAD).astype(jnp.float32), cross_summed
    )
    d_query_c = query_grad(
        query_c,
        positions,
        (key_c, value_c),
        visible,
        cross_fold,
        cross_lse,
        cross_delta,
        d_cross_att,
    )
    d_query_cs = d_query_c.reshape(tok_rows, model_width).astype(jnp.bfloat16) * 0.125
    d_first = d_hidden2 + back_dot(d_query_cs, w_cq[:, :model_width])
    d_hidden1, d_gain1, d_shift1 = first_pull(d_first)
    d_branch = d_hidden1.astype(jnp.bfloat16)
    g_so = contract_rows(attended, d_branch)
    d_attended = back_dot(d_branch, w_so).astype(jnp.bfloat16)
    self_delta = jnp.einsum(
        "qhd,qhd->qh", d_attended.reshape(tok_rows, HEADS, HEAD).astype(jnp.float32), self_summed
    )
    stats = (
        lax.all_gather(self_lse, "shard", axis=0, tiled=True),
        lax.all_gather(self_delta, "shard", axis=0, tiled=True),
        lax.all_gather(cross_lse, "shard", axis=0, tiled=True),
        lax.all_gather(cross_delta, "shard", axis=0, tiled=True),
    )
    tok_zero = jnp.zeros((tok_rows, HEADS, HEAD), jnp.float32)
    query_side = query_step(query_s, positions, causal_mask, self_lse, self_delta, d_attended)
    key_side = key_step(key_s, value_s, positions, causal_mask, stats[0], stats[1])
    offset = jnp.int32(0)
    d_query_part = query_side(
        tok_zero,
        (
            lax.all_gather(key_s, "shard", axis=0, tiled=True),
            lax.all_gather(value_s, "shard", axis=0, tiled=True),
        ),
        offset,
    )
    d_key_part, d_value_part = key_side(
        (tok_zero, tok_zero),
        (
            lax.all_gather(query_s, "shard", axis=0, tiled=True),
            lax.all_gather(d_attended, "shard", axis=0, tiled=True),
        ),
        offset,
    )
    enc_zero = jnp.zeros((enc_rows, HEADS, HEAD), jnp.float32)
    d_key_c, d_value_c = key_step(key_c, value_c, enc_positions, visible, stats[2], stats[3])(
        (enc_zero, enc_zero),
        (
            lax.all_gather(query_c, "shard", axis=0, tiled=True),
            lax.all_gather(d_cross_att, "shard", axis=0, tiled=True),
        ),
        jnp.int32(0),
    )
    d_qs = d_query_part.reshape(tok_rows, model_width).astype(jnp.bfloat16) * 0.125
    d_ks = d_key_part.reshape(tok_rows, model_width).astype(jnp.bfloat16)
    d_vs = d_value_part.reshape(tok_rows, model_width).astype(jnp.bfloat16)
    d_joined = jnp.concatenate([d_qs, d_ks, d_vs], 1)
    g_sq = contract_rows(tokens, d_joined)
    d_tokens = d_hidden1 + back_dot(d_joined, w_sq)
    d_kc = d_key_c.reshape(enc_rows, model_width).astype(jnp.bfloat16)
    d_vc = d_value_c.reshape(enc_rows, model_width).astype(jnp.bfloat16)
    d_enc_proj = jnp.concatenate([d_kc, d_vc], 1)
    g_cq = jnp.concatenate(
        [contract_rows(first_low, d_query_cs), contract_rows(encoder, d_enc_proj)], 1
    )
    d_encoder = back_dot(d_enc_proj, w_cq[:, model_width:])
    d_self_bias = jnp.stack([column_sum(d_qs), column_sum(d_vs), column_sum(d_branch)])
    d_cross_bias = jnp.stack([column_sum(d_query_cs), column_sum(d_vc), column_sum(d_branch_c)])
    d_norm_gain = jnp.stack([d_gain1, d_gain2, d_gain3])
    d_norm_bias = jnp.stack([d_shift1, d_shift2, d_shift3])
    d_fc1_bias = column_sum(d_up_low)
    d_fc2_bias = column_sum(d_branch_m)
    row_grads = (
        lax.psum_scatter(g_sq, "shard", scatter_dimension=0, tiled=True),
        lax.psum_scatter(g_so, "shard", scatter_dimension=0, tiled=True),
        lax.psum_scatter(g_cq, "shard", scatter_dimension=0, tiled=True),
        lax.psum_scatter(g_co, "shard", scatter_dimension=0, tiled=True),
        lax.psum_scatter(g_up, "shard", scatter_dimension=0, tiled=True),
        lax.psum_scatter(g_down, "shard", scatter_dimension=0, tiled=True),
    )
    row_grads = lax.psum(
        (row_grads[0], row_grads[1], row_grads[2], row_grads[3], row_grads[4], row_grads[5]), "rep"
    )
    small_sums = lax.psum(
        (d_self_bias, d_cross_bias, d_norm_gain, d_norm_bias, d_fc1_bias, d_fc2_bias),
        ("rep", "shard"),
    )
    return (
        output.astype(jnp.bfloat16),
        d_tokens,
        d_encoder,
        row_grads[0],
        row_grads[1],
        row_grads[2],
        row_grads[3],
        row_grads[4],
        row_grads[5],
        small_sums[0],
        small_sums[1],
        small_sums[2],
        small_sums[3],
        small_sums[4],
        small_sums[5],
    )


MESH = pl.DeviceIdType.MESH
BF = jnp.bfloat16
F32 = jnp.float32
EPS = 1e-05


def dg(left, right, cl, cr):
    return lax.dot_general(
        left, right, (((cl,), (cr,)), ((), ())), preferred_element_type=F32
    )


class Names:
    pass


WIDTH = 1024
HIDDEN = 4096
ROWS = 128
ENC = 64
HALF = 64
NSUB = 4
SUB = ROWS // NSUB

SCRATCH = {
    "X": ((8, ROWS, WIDTH), BF),
    "E": ((4, ENC, WIDTH), BF),
    "DMX": ((ROWS, WIDTH), BF),
    "LSRC": ((8, 128), F32),
    "LENS": ((8, 128), F32),
    "WQKV": ((8, 128, 768), BF),
    "WSO": ((2, 128, WIDTH), BF),
    "WCQ": ((8, 128, 768), BF),
    "WCO": ((2, 128, WIDTH), BF),
    "WUP": ((8, 128, 1024), BF),
    "WDN": ((2, 512, WIDTH), BF),
    "QST": ((2, 3, 4, ROWS, 128), BF),
    "QKV": ((3, 8, ROWS, 128), BF),
    "P0": ((2, 256, 256), BF),
    "P1": ((2, 256, 512), BF),
    "P2": ((2, 256, 768), BF),
    "P3": ((2, 256, 1024), BF),
    "O": ((1024, 128), F32),
    "ATF": ((8, ROWS, 128), BF),
    "ATT": ((4, ROWS, 256), BF),
    "PB": ((4, ROWS, WIDTH), BF),
    "RB": ((3, ROWS, WIDTH), BF),
    "VIA": ((ROWS, WIDTH), BF),
    "VIAE": ((ENC, WIDTH), BF),
    "PBE": ((4, ENC, WIDTH), BF),
    "RBE": ((3, ENC, WIDTH), BF),
    "F": ((4, ROWS, WIDTH), BF),
    "S": ((4, ROWS, WIDTH), BF),
    "DM": ((4, ROWS, WIDTH), BF),
    "DC": ((4, ROWS, WIDTH), BF),
    "DB": ((4, ROWS, WIDTH), BF),
    "RES": ((ROWS, WIDTH), F32),
    "RES2": ((ROWS, WIDTH), F32),
    "XH": ((2, ROWS, WIDTH), F32),
    "RSTD": ((2, ROWS, 1), F32),
    "QC": ((4, ROWS, 256), BF),
    "KVC": ((8, ENC, 512), BF),
    "PC": ((4, NSUB, 4 * SUB, 512), BF),
    "OC": ((NSUB, 4 * SUB, 256), F32),
    "CATT": ((4, ROWS, 256), BF),
    "ACT": ((4, ROWS, 1024), BF),
    "DGL": ((NSUB, 4 * SUB, 1024), BF),
    "DUP": ((4, ROWS, 1024), BF),
    "DQC": ((4, ROWS, 256), BF),
    "DKV": ((512, 512), F32),
    "DKS": ((4, ENC, 512), BF),
    "DKR": ((4, ENC, 512), BF),
    "DKL": ((4, ENC, 512), BF),
    "DATS": ((4, ROWS, 128), BF),
    "DO": ((8, ROWS, 128), BF),
    "DKVS": ((2, 1024, 128), F32),
    "DJN": ((3, 8, ROWS, 128), BF),
    "DJ": ((4, ROWS, 768), BF),
    "MXS": ((ROWS, WIDTH), BF),
    "DTS": ((ROWS, WIDTH), BF),
    "DES": ((ENC, WIDTH), BF),
    "SM": ((16, WIDTH), F32),
    "SMR": ((16, WIDTH), F32),
    "SM4": ((4, 16, WIDTH), F32),
    "SB": ((8, WIDTH), F32),
    "SBR": ((8, WIDTH), F32),
    "SB4": ((4, 8, WIDTH), F32),
    "ALL": ((24, WIDTH), F32),
    "ALLR": ((2, 24, WIDTH), F32),
}
for _name, _rows in (("SO", 128), ("CO", 128), ("DN", 512)):
    SCRATCH["GS_" + _name] = ((_rows, WIDTH), BF)
    SCRATCH["GR_" + _name] = ((_rows, WIDTH), BF)
    SCRATCH["GK_" + _name] = ((_rows, WIDTH), BF)
    SCRATCH["XS_" + _name] = ((_rows // 2, WIDTH), BF)
    SCRATCH["XR_" + _name] = ((_rows // 2, WIDTH), BF)
    SCRATCH["HS_" + _name] = ((_rows // 2, WIDTH), BF)
    SCRATCH["HR_" + _name] = ((_rows // 2, WIDTH), BF)
    SCRATCH["T_" + _name] = ((_rows, WIDTH), BF)
for _name, _cols in (("SQ0", 128), ("SQ1", 128), ("SQ2", 128), ("CQ", 384), ("UP", 512)):
    if _cols > 128:
        SCRATCH["GS_" + _name] = ((8, 128, _cols), BF)
        SCRATCH["GR_" + _name] = ((8, 128, _cols), BF)
    SCRATCH["GK_" + _name] = ((8, 128, _cols), BF)
    SCRATCH["XS_" + _name] = ((8, HALF, _cols), BF)
    SCRATCH["XR_" + _name] = ((8, HALF, _cols), BF)
    SCRATCH["HS_" + _name] = ((4, HALF, _cols), BF)
    SCRATCH["HR_" + _name] = ((4, HALF, _cols), BF)
    SCRATCH["TS_" + _name] = ((4, HALF, _cols), BF)
    SCRATCH["T_" + _name] = ((8, 128, _cols), BF)

IN_NAMES = (
    "tokens", "encoder", "seq", "enc", "dmix", "w_sq", "w_so", "w_cq", "w_co", "w_up", "w_dn",
    "sb", "cb", "gain", "shift", "fb1", "fb2",
)
OUT_NAMES = (
    "o_mixed", "o_dtok", "o_denc", "o_sq", "o_so", "o_cq", "o_co", "o_up", "o_dn", "o_small",
)
VMEM_BYTES = 64 * 2**20 - 2**19
N_SEND, N_RECV, N_LOCAL = 133, 140, 20


def layer_kernel(*refs):
    n_in, n_out = len(IN_NAMES), len(OUT_NAMES)
    r = Names()
    names = IN_NAMES + OUT_NAMES + tuple(SCRATCH)
    for name, ref in zip(names, refs):
        setattr(r, name, ref)
    send_sem, recv_sem, local_sem = refs[len(names) :]
    count = {"send": 0, "recv": 0, "local": 0}

    def new(kind):
        count[kind] += 1
        return count[kind] - 1

    def pair():
        return new("send"), new("recv")

    rep, shard = lax.axis_index("rep"), lax.axis_index("shard")
    x, c = rep // 2, rep % 2
    z, y = shard // 2, shard % 2
    h, l = z // 2, z % 2
    own = 2 * l + y
    t = 4 * c + own
    s_own = 4 * h + own

    def dev(xx, hh, ll, yy, cc):
        return (xx * 2 + cc, (2 * hh + ll) * 2 + yy)

    mate = dev(x, h, l, y, 1 - c)
    x_peer = dev(1 - x, h, l, y, c)
    h_peer = dev(x, 1 - h, l, y, c)
    swap_peer = dev(x, 1 - h, l, y, 1 - c)

    def peer_lc(j):
        return (l + j // 2) % 2, (y + j % 2) % 2

    def peer(j):
        ll, yy = peer_lc(j)
        return dev(x, h, ll, yy, c)

    def peer_block(j):
        ll, yy = peer_lc(j)
        return 2 * ll + yy

    def remote(src, dst, device, sems=None):
        i, j = sems or pair()
        return pltpu.make_async_remote_copy(
            src_ref=src,
            dst_ref=dst,
            send_sem=send_sem.at[i],
            recv_sem=recv_sem.at[j],
            device_id=device,
            device_id_type=MESH,
        )

    def all_of(ref, sems):
        return remote(ref, ref, mate, sems)

    def local(src, dst, sem=None):
        return pltpu.make_async_copy(src, dst, local_sem.at[new("local") if sem is None else sem])

    barrier = pltpu.get_barrier_semaphore()
    greet = [mate, x_peer, swap_peer]
    for m in range(1, 8):
        greet.append(dev(x, (h + m // 4) % 2, (l + (m // 2) % 2) % 2, (y + m % 2) % 2, c))
    for device in greet:
        pl.semaphore_signal(barrier, inc=1, device_id=device, device_id_type=MESH)
    r.LSRC[0:1, :] = jnp.full((1, 128), r.seq[0].astype(F32))
    r.LSRC[1:2, :] = jnp.full((1, 128), r.enc[0].astype(F32))
    r.SM[...] = jnp.zeros_like(r.SM)
    r.SB[...] = jnp.zeros_like(r.SB)
    pl.semaphore_wait(barrier, len(greet))

    moved = [
        (r.tokens, r.X.at[4 * (1 - c) + own], r.X.at[t]),
        (r.encoder, r.E.at[own], r.E.at[own]),
        (r.LSRC, r.LENS, r.LENS),
        (r.dmix, r.DMX, r.DMX),
    ]
    swaps = [(remote(s, there, swap_peer), local(s, here)) for s, there, here in moved]
    stays = c == h

    def swap_start(i):
        @pl.when(stays)
        def _():
            swaps[i][1].start()

        @pl.when(jnp.logical_not(stays))
        def _():
            swaps[i][0].start()

    def swap_wait(i):
        @pl.when(stays)
        def _():
            swaps[i][1].wait()

        @pl.when(jnp.logical_not(stays))
        def _():
            swaps[i][0].wait()

    my_x = pl.ds(pl.multiple_of(x * HALF, HALF), HALF)
    other_x = pl.ds(pl.multiple_of((1 - x) * HALF, HALF), HALF)
    inner = h != l

    class ColumnWeight:
        def __init__(self, w_hbm, dst, groups, width, full=False):
            self.w, self.dst, self.width, self.full = w_hbm, dst, width, full
            self.groups = [(parts, [pair() for _ in range(6)], new("local")) for parts in groups]

        def at(self, p, shards, rows):
            first = pl.multiple_of(p * 2 * self.width + c * self.width, 128)
            return self.dst.at[shards, rows, pl.ds(first, self.width)]

        def rows(self, m):
            return slice(0, 128) if self.full and m < 4 else my_x

        def bytes(self, parts, blocks, rows):
            return self.dst.at[0:blocks, rows, 0 : len(parts) * self.width]

        def copy(self, p, m, sems, sem):
            hh, ll, yy = (h + m // 4) % 2, (l + (m // 2) % 2) % 2, (y + m % 2) % 2
            col = pl.multiple_of(p * WIDTH + (4 * c + 2 * ll + yy) * self.width, 128)
            src = self.w.at[self.rows(m), pl.ds(col, self.width)]
            at = self.at(p, s_own, self.rows(m))
            if m == 0:
                return local(src, at, sem)
            return remote(src, at, dev(x, hh, ll, yy, c), sems[m // 4])

        def near(self):
            for parts, sems, sem in self.groups:
                for p in parts:
                    start([self.copy(p, m, sems, sem) for m in (1, 2, 3, 0)])

        def far(self):
            for parts, sems, sem in self.groups:
                for p in parts:
                    start([self.copy(p, m, sems, sem) for m in (4, 5)])

            @pl.when(inner)
            def _():
                for parts, sems, sem in self.groups:
                    for p in parts:
                        start([self.copy(p, m, sems, sem) for m in (6, 7)])

        def send(self):
            self.far()
            self.near()

        def relay(self):
            @pl.when(inner)
            def _():
                for parts, sems, sem in self.groups:
                    all_of(self.bytes(parts, 3, self.rows(1)), sems[0]).wait_recv()
                    for p in parts:
                        on = self.at(p, pl.ds(4 * h + 2 * (1 - l), 2), my_x)
                        remote(on, on, h_peer, sems[2]).start()

        def cross(self):
            for parts, sems, sem in self.groups:
                near = all_of(self.bytes(parts, 3, self.rows(1)), sems[0])
                hop = all_of(self.bytes(parts, 2, my_x), sems[2])
                near.wait_send()
                here = self.dst.at[0, self.rows(0), 0 : len(parts) * self.width]
                local(here, here, sem).wait()

                @pl.when(inner)
                def _():
                    all_of(self.bytes(parts, 4, my_x), sems[1]).wait()
                    hop.wait_send()

                @pl.when(jnp.logical_not(inner))
                def _():
                    near.wait_recv()
                    all_of(self.bytes(parts, 2, my_x), sems[1]).wait()
                    hop.wait_recv()

                shards = pl.ds(4 * (1 - h), 4) if self.full else slice(None)
                for p in parts:
                    at = self.at(p, shards, my_x)
                    remote(at, at, x_peer, sems[3]).start()
                for p in parts:
                    at = self.at(p, shards, my_x)
                    remote(at, at, mate, sems[4]).start()
                    if self.full:
                        at = self.at(p, pl.ds(4 * h, 4), slice(None))
                        remote(at, at, mate, sems[4]).start()

        def share(self):
            for parts, sems, sem in self.groups:
                all_of(self.bytes(parts, 4 if self.full else 8, my_x), sems[3]).wait()
                shards = pl.ds(4 * (1 - h), 4) if self.full else slice(None)
                for p in parts:
                    at = self.at(p, shards, other_x)
                    remote(at, at, mate, sems[5]).start()

        def ready(self):
            for parts, sems, sem in self.groups:
                all_of(self.bytes(parts, 6 if self.full else 4, slice(None)), sems[4]).wait()
                all_of(self.bytes(parts, 4 if self.full else 8, my_x), sems[5]).wait()

    class RowWeight:
        def __init__(self, w_hbm, dst, rows):
            self.w, self.dst, self.n = w_hbm, dst, rows // 4

        def rows(self, xx):
            return pl.ds(pl.multiple_of(c * 2 * self.n + xx * self.n, 32), self.n)

        def send(self):
            at = self.rows(x)
            self.first = [local(self.w, self.dst.at[h]), remote(self.w.at[at], self.dst.at[h, at], h_peer)]
            start(self.first)

        def cross(self):
            wait(self.first)
            at = self.dst.at[1 - h, self.rows(x)]
            self.xc, self.m1 = remote(at, at, x_peer), remote(at, at, mate)
            self.xc.start()
            self.m1.start()

        def share(self):
            self.xc.wait()
            at = self.dst.at[1 - h, self.rows(1 - x)]
            self.m2 = remote(at, at, mate)
            self.m2.start()

        def ready(self):
            self.m1.wait()
            self.m2.wait()

    def leave(src, out):
        cp = remote(src, out, swap_peer)

        @pl.when(stays)
        def _():
            out[...] = src[...]

        @pl.when(jnp.logical_not(stays))
        def _():
            cp.start()

        return cp

    def start(copies):
        for cp in copies:
            cp.start()

    def wait(copies):
        for cp in copies:
            cp.wait()

    NBR = (1, 2)

    class Gather:
        def __init__(self, buf, rows, first, base=0, sems=None, apart=False):
            self.first = first - 1
            self.sems = sems or gather_sems()
            send, recv_first, recv_rest = self.sems
            blk = buf.at[base + own, rows]
            self.direct = [
                remote(blk, blk, peer(j), (send, recv_first if j == first else recv_rest)) for j in NBR
            ]
            on = buf.at[base + peer_block(first), rows]
            self.hop = remote(on, on, peer(3 - first), None if apart else (send, recv_rest))
            self.two, self.three = buf.at[0:2, rows], buf.at[0:3, rows]

        def start(self):
            start(self.direct)

        def relay(self):
            self.direct[self.first].wait_recv()
            self.hop.start()

        def wait(self):
            send, recv_first, recv_rest = self.sems
            all_of(self.two, (send, recv_rest)).wait_recv()
            all_of(self.three, (send, recv_rest)).wait_send()

    def gather_sems():
        return new("send"), new("recv"), new("recv")

    class Scatter:
        def __init__(self, buf, land, rows, sems=None):
            self.buf, self.land, self.rows, self.sems = buf, land, rows, sems or pair()
            self.sends = [
                remote(buf.at[peer_block(j), rows], land.at[j - 1, rows], peer(j), self.sems) for j in (3, 1, 2)
            ]

        def start(self):
            start(self.sends)

        def finish(self):
            all_of(self.land.at[:, self.rows], self.sems).wait()
            total = self.buf[own, self.rows].astype(F32)
            for j in range(3):
                total = total + self.land[j, self.rows].astype(F32)
            return total

    class RelayScatter:
        def __init__(self, buf, via, land, rows, sems):
            self.buf, self.via, self.land, self.rows = buf, via, land, rows
            self.second = peer_block(2)
            self.first, self.rest = sems
            self.sends = [
                remote(buf.at[peer_block(3), rows], via.at[rows], peer(1), self.first),
                remote(buf.at[peer_block(1), rows], land.at[0, rows], peer(1), self.rest),
            ]
            self.last = remote(buf.at[self.second, rows], land.at[1, rows], peer(2), self.rest)

        def start(self):
            start(self.sends)

        def relay(self):
            self.sends[0].wait()
            total = self.buf[self.second, self.rows].astype(F32) + self.via[self.rows].astype(F32)
            self.buf[self.second, self.rows] = total.astype(BF)
            self.last.start()

        def finish(self):
            all_of(self.land.at[0:2, self.rows], self.rest).wait()
            return (
                self.buf[own, self.rows].astype(F32)
                + self.land[0, self.rows].astype(F32)
                + self.land[1, self.rows].astype(F32)
            )

    gather_triples = [gather_sems() for _ in range(NSUB)]
    scatter_pairs = [pair() for _ in range(NSUB)]

    def span(a):
        return pl.ds(a * SUB, SUB)

    def half(a):
        return slice(a * SUB, (a + 1) * SUB)

    def way(a):
        return 1 + a % 2

    mine = pl.ds(4 * c, 4)
    theirs = pl.ds(4 * (1 - c), 4)
    w_sq = ColumnWeight(r.w_sq, r.WQKV, [[0], [1], [2]], 128, True)
    w_so = RowWeight(r.w_so, r.WSO, 128)
    w_cq = ColumnWeight(r.w_cq, r.WCQ, [[0, 1, 2]], 128)
    w_co = RowWeight(r.w_co, r.WCO, 128)
    w_up = ColumnWeight(r.w_up, r.WUP, [[0]], 512)
    w_dn = RowWeight(r.w_dn, r.WDN, 512)
    ag_x = [Gather(r.X, pl.ds(k * HALF, HALF), 2, 4 * c, apart=True) for k in range(2)]
    swap_start(0)

    @pl.when(stays)
    def _():
        swaps[0][1].wait()
        for g in ag_x:
            g.direct[0].start()
        w_sq.near()
        for g in ag_x:
            g.direct[0].wait_recv()
        w_sq.far()
        for g in ag_x:
            g.direct[1].start()
        swaps[1][1].start()
        swaps[2][1].start()
        w_sq.relay()
        for g in ag_x:
            g.relay()

    @pl.when(jnp.logical_not(stays))
    def _():
        w_sq.near()
        w_sq.far()
        w_sq.relay()
        swaps[1][0].start()
        swaps[2][0].start()
        swaps[0][0].wait()
        start(ag_x)
        for g in ag_x:
            g.relay()
            g.direct[0].wait_recv()

    w_so.send()
    w_cq.send()
    w_sq.cross()
    w_co.send()
    swap_wait(1)
    ag_e = Gather(r.E, pl.ds(0, ENC), 2)
    ag_e.start()
    w_up.send()
    for g in ag_x:
        g.hop.wait()
        all_of(g.two, g.sems[:2]).wait_send()
    x_both = remote(r.X.at[mine], r.X.at[mine], mate)
    x_both.start()
    w_sq.share()
    w_sq.ready()

    lane = lax.broadcasted_iota(jnp.int32, (1, 128), 1)
    heads = [lane // 64 == 0, lane // 64 == 1]

    def head_of(v, hh):
        return jnp.where(heads[hh], v, jnp.zeros_like(v))

    def own_cols(ref, row, width):
        off = [pl.multiple_of((4 * k + own) * width, 128) for k in range(2)]
        return jnp.concatenate([ref[row : row + 1, pl.ds(o, width)] for o in off], 1)

    def blocks(ref, a, width):
        return ref[:, half(a), :].reshape(4 * SUB, width)

    def shards(ref, rows, cols):
        return ref[rows.start // 128 : rows.stop // 128, :, cols].reshape(rows.stop - rows.start, -1)

    def add_small(row, col, width, value):
        at = slice(0, width) if isinstance(col, int) else pl.ds(pl.multiple_of(col, 128), width)
        ref, row = (r.SB, row) if row < 8 else (r.SM, row - 8)
        ref[row : row + 1, at] += value

    def colsum(v):
        return jnp.sum(v, 0, keepdims=True)

    bias_q = own_cols(r.sb, 0, 128)
    bias_v = own_cols(r.sb, 1, 128)
    for i in range(2):
        lhs = r.X[pl.ds(4 * c + 2 * i, 2)].reshape(256, WIDTH)
        for p in range(3):
            out = dg(lhs, r.WQKV[:, :, p * 256 : (p + 1) * 256].reshape(WIDTH, 256), 1, 0)
            if p == 0:
                out = (out + bias_q) * 0.125
            if p == 2:
                out = out + bias_v
            out = out.astype(BF)
            for k in range(2):
                r.QST[k, p, 2 * i : 2 * i + 2] = out[:, k * 128 : (k + 1) * 128].reshape(2, ROWS, 128)
    qkv_x = remote(r.QST.at[1 - c], r.QKV.at[:, mine], mate)
    qkv_x.start()
    r.QKV[:, mine] = r.QST[c]
    w_cq.relay()
    ag_e.relay()
    w_so.cross()
    qkv_x.wait()

    def keys(p, n):
        return r.QKV[p, 0 : n // ROWS].reshape(n, 128)

    probs = [r.P0, r.P1, r.P2, r.P3]
    for i in range(4):
        n = (i + 1) * 256
        q = r.QKV[0, 2 * i : 2 * i + 2].reshape(256, 128)
        outs = []
        for hh in range(2):
            s = dg(head_of(q, hh), keys(1, n), 1, 1)
            qpos = lax.broadcasted_iota(jnp.int32, (256, n), 0) + i * 256
            kpos = lax.broadcasted_iota(jnp.int32, (256, n), 1)
            s = jnp.where(kpos <= qpos, s, -1e30)
            e = jnp.exp(s - jnp.max(s, 1, keepdims=True))
            p = (e * (1.0 / jnp.sum(e, 1, keepdims=True))).astype(BF)
            probs[i][hh] = p
            outs.append(dg(p, keys(2, n), 1, 0))
        o = jnp.where(heads[0], outs[0], outs[1])
        r.O[i * 256 : (i + 1) * 256] = o
        r.ATF[2 * i : 2 * i + 2] = o.astype(BF).reshape(2, ROWS, 128)
    my_cols = pl.ds(pl.multiple_of(c * 128, 128), 128)
    att_x = remote(r.ATF.at[theirs], r.ATT.at[:, :, my_cols], mate)
    att_x.start()
    r.ATT[:, :, my_cols] = r.ATF[mine]
    w_so.share()
    w_so.ready()
    att_x.wait()

    def partial(a, lhs, w, contract, chunk=512, sums=None):
        for n in range(WIDTH // chunk):
            cols = slice(n * chunk, (n + 1) * chunk)
            out = dg(lhs, w(cols), 1, contract)
            r.PB[:, half(a), cols] = out.astype(BF).reshape(4, SUB, chunk)
        sums = sums or Scatter(r.PB, r.RB, span(a), scatter_pairs[a])
        sums.start()
        return sums

    def norm(i, rows, hidden):
        centre = hidden - jnp.mean(hidden, -1, keepdims=True)
        rstd = lax.rsqrt(jnp.mean(centre * centre, -1, keepdims=True) + EPS)
        xhat = centre * rstd
        return xhat, rstd, xhat * r.gain[i : i + 1, :] + r.shift[i : i + 1, :]

    def norm_back(i, dy, xhat, rstd):
        add_small((5, 9, 10)[i], 0, WIDTH, colsum(dy * xhat))
        add_small((6, 11, 12)[i], 0, WIDTH, colsum(dy))
        d = dy * r.gain[i : i + 1, :]
        mean_d = jnp.mean(d, -1, keepdims=True)
        mean_dx = jnp.mean(d * xhat, -1, keepdims=True)
        return rstd * (d - mean_d - xhat * mean_dx)

    def gathered(buf, a, value, first=None):
        buf[own, half(a)] = value
        g = Gather(buf, span(a), first or way(a), 0, gather_triples[a])
        g.start()
        return g

    def comp1(a):
        return partial(a, blocks(r.ATT, a, 256), lambda cols: r.WSO[:, :, cols].reshape(256, -1), 0)

    def fin1(a, total):
        hidden = r.X[t, half(a)].astype(F32) + total + r.sb[2:3, :]
        xhat, rstd, out = norm(0, half(a), hidden)
        r.XH[0, half(a)] = xhat
        r.RSTD[0, half(a)] = rstd
        r.RES[half(a)] = out
        return gathered(r.F, a, out.astype(BF), 2)

    def encoder_kv():
        w_cq.ready()
        ag_e.wait()
        bias_cv = own_cols(r.cb, 1, 128)
        for k in range(2):
            out = dg(
                r.E[...].reshape(4 * ENC, WIDTH),
                r.WCQ[:, :, 256 + k * 256 : 512 + k * 256].reshape(WIDTH, 256),
                1,
                0,
            )
            if k == 1:
                out = out + bias_cv
            r.KVC[mine, :, k * 256 : (k + 1) * 256] = out.astype(BF).reshape(4, ENC, 256)
        kvc_x.start()

    kvc_x = remote(r.KVC.at[mine], r.KVC.at[mine], mate)

    def enc_keys(part, k):
        return r.KVC[:, :, part * 256 + k * 128 : part * 256 + (k + 1) * 128].reshape(512, 128)

    def comp2(a):
        bias_cq = own_cols(r.cb, 0, 128)
        visible = lax.broadcasted_iota(jnp.int32, (1, 512), 1).astype(F32) < r.LENS[1:2, 0:1]
        q = dg(blocks(r.F, a, WIDTH), r.WCQ[:, :, 0:256].reshape(WIDTH, 256), 1, 0)
        q = ((q + bias_cq) * 0.125).astype(BF)
        r.QC[:, half(a)] = q.reshape(4, SUB, 256)
        for k in range(2):
            outs = []
            for hh in range(2):
                s = dg(head_of(q[:, k * 128 : (k + 1) * 128], hh), enc_keys(0, k), 1, 1)
                s = jnp.where(visible, s, -1e30)
                e = jnp.exp(s - jnp.max(s, 1, keepdims=True))
                p = (e * (1.0 / jnp.sum(e, 1, keepdims=True))).astype(BF)
                r.PC[2 * k + hh, a] = p
                outs.append(dg(p, enc_keys(1, k), 1, 0))
            o = jnp.where(heads[0], outs[0], outs[1])
            r.OC[a, :, k * 128 : (k + 1) * 128] = o
            r.CATT[:, half(a), k * 128 : (k + 1) * 128] = o.astype(BF).reshape(4, SUB, 128)
        return partial(a, blocks(r.CATT, a, 256), lambda cols: r.WCO[:, :, cols].reshape(256, -1), 0)

    def fin2(a, total):
        hidden = r.RES[half(a)] + total + r.cb[2:3, :]
        xhat, rstd, out = norm(1, half(a), hidden)
        r.XH[1, half(a)] = xhat
        r.RSTD[1, half(a)] = rstd
        r.RES2[half(a)] = out
        return gathered(r.S, a, out.astype(BF))

    def comp3(a):
        lhs = blocks(r.S, a, WIDTH)
        for k in range(2):
            cols = slice(k * 512, (k + 1) * 512)
            bias_up = r.fb1[0:1, pl.ds(pl.multiple_of((4 * k + own) * 512, 128), 512)]
            u = dg(lhs, r.WUP[:, :, cols].reshape(WIDTH, 512), 1, 0) + bias_up
            cdf = 0.5 + 0.5 * lax.erf(u * 0.7071067811865476)
            r.ACT[:, half(a), cols] = (u * cdf).astype(BF).reshape(4, SUB, 512)
            slope = cdf + u * (jnp.exp(-0.5 * u * u) * 0.3989422804014327)
            r.DGL[a, :, cols] = slope.astype(BF)
        return partial(a, blocks(r.ACT, a, 1024), lambda cols: r.WDN[:, :, cols].reshape(1024, -1), 0)

    def fin3(a, total):
        hidden = r.RES2[half(a)] + total + r.fb2[0:1, :]
        xhat, rstd, out = norm(2, half(a), hidden)
        r.MXS[half(a)] = out.astype(BF)
        place = lax.broadcasted_iota(jnp.int32, (SUB, 1), 0) + (t * ROWS + a * SUB)
        dy = jnp.where(place.astype(F32) < r.LENS[0:1, 0:1], r.DMX[half(a)].astype(F32), 0.0)
        d = norm_back(2, dy, xhat, rstd)
        r.RES[half(a)] = d
        low = d.astype(BF)
        add_small(13, 0, WIDTH, colsum(low.astype(F32)))
        return gathered(r.DM, a, low)

    def comp4(a):
        lhs = blocks(r.DM, a, WIDTH)
        for k in range(2):
            cols = slice(k * 512, (k + 1) * 512)
            d_act = dg(lhs, r.WDN[k], 1, 1).astype(BF).astype(F32)
            low = (d_act * r.DGL[a, :, cols].astype(F32)).astype(BF)
            r.DUP[:, half(a), cols] = low.reshape(4, SUB, 512)
            at = pl.ds(pl.multiple_of(y * 512, 512), 512)
            r.SM[pl.ds(8 + 2 * k + l, 1), at] += colsum(low.astype(F32))
        return partial(a, blocks(r.DUP, a, 1024), lambda cols: shards(r.WUP, cols, slice(0, 1024)), 1)

    def fin4(a, total):
        d = norm_back(1, r.RES[half(a)] + total, r.XH[1, half(a)], r.RSTD[1, half(a)])
        r.RES2[half(a)] = d
        low = d.astype(BF)
        add_small(8, 0, WIDTH, colsum(low.astype(F32)))
        return gathered(r.DC, a, low)

    def comp5(a):
        d_att = dg(blocks(r.DC, a, WIDTH), r.WCO[...].reshape(256, WIDTH), 1, 1).astype(BF)
        for k in range(2):
            cols = slice(k * 128, (k + 1) * 128)
            d_pair = d_att[:, cols]
            o_pair = r.OC[a, :, cols]
            q_pair = blocks(r.QC, a, 256)[:, cols]
            ds, dk, dv = [], None, None
            for hh in range(2):
                d_head = head_of(d_pair, hh)
                delta = jnp.sum(d_head.astype(F32) * o_pair, 1, keepdims=True)
                p = r.PC[2 * k + hh, a]
                d_scores = (p.astype(F32) * (dg(d_head, enc_keys(1, k), 1, 1) - delta)).astype(BF)
                ds.append(dg(d_scores, enc_keys(0, k), 1, 0))
                new_dk = dg(d_scores, head_of(q_pair, hh), 0, 0)
                new_dv = dg(p, d_head, 0, 0)
                dk = new_dk if dk is None else dk + new_dk
                dv = new_dv if dv is None else dv + new_dv
            dq = (jnp.where(heads[0], ds[0], ds[1]).astype(BF) * 0.125).astype(BF)
            r.DQC[:, half(a), cols] = dq.reshape(4, SUB, 128)
            add_small(3, (4 * k + own) * 128, 128, colsum(dq.astype(F32)))
            dv_cols = slice(256 + k * 128, 384 + k * 128)
            if a == 0:
                r.DKV[:, cols] = dk
                r.DKV[:, dv_cols] = dv
            else:
                r.DKV[:, cols] += dk
                r.DKV[:, dv_cols] += dv
        return partial(a, blocks(r.DQC, a, 256), lambda cols: shards(r.WCQ, cols, slice(0, 256)), 1)

    def fin5(a, total):
        d = norm_back(0, r.RES2[half(a)] + total, r.XH[0, half(a)], r.RSTD[0, half(a)])
        r.RES[half(a)] = d
        low = d.astype(BF)
        add_small(2, 0, WIDTH, colsum(low.astype(F32)))
        return gathered(r.DB, a, low)

    do_sems = pair()

    def comp6(a):
        d_att = dg(blocks(r.DB, a, WIDTH), r.WSO[...].reshape(256, WIDTH), 1, 1).astype(BF)
        mine_d = jnp.where(c == 0, d_att[:, 0:128], d_att[:, 128:256])
        theirs_d = jnp.where(c == 0, d_att[:, 128:256], d_att[:, 0:128])
        r.DATS[:, half(a)] = theirs_d.reshape(4, SUB, 128)
        r.DO[mine, half(a)] = mine_d.reshape(4, SUB, 128)
        remote(r.DATS.at[:, span(a)], r.DO.at[mine, span(a)], mate, do_sems).start()

    class GroupSum:
        def __init__(self, total, land, four):
            self.total, self.land, self.four = total, land, four

        def cores(self):
            self.copy = remote(self.total, self.land, mate)
            self.copy.start()

        def chips(self):
            self.copy.wait()
            at = self.four.at[own]
            at[...] = self.total[...] + self.land[...]
            self.sems = pair()
            start([remote(at, at, peer(j), self.sems) for j in (1, 2, 3)])

        def sum(self):
            all_of(self.four.at[0:3], self.sems).wait()
            f = self.four
            return (f[0] + f[1]) + (f[2] + f[3])

    small = GroupSum(r.SM, r.SMR, r.SM4)
    late = GroupSum(r.SB, r.SBR, r.SB4)
    halves = remote(r.ALL, r.ALLR.at[0], h_peer)
    sides = remote(r.ALL, r.ALLR.at[1], x_peer)

    def sum_halves():
        r.ALL[0:8] = late.sum()
        r.ALL[8:24] = small.sum()
        halves.start()

    def sum_sides():
        halves.wait()
        r.ALL[...] += r.ALLR[0]
        sides.start()

    def sum_end():
        sides.wait()
        r.o_small[...] = r.ALL[...] + r.ALLR[1]

    far_shards, near_shards = pl.ds(4 * (1 - h), 4), pl.ds(4 * h, 4)

    class ColumnGrad:
        def __init__(self, name, out, parts, part=0, pieces=1):
            self.parts, self.out, self.pieces = parts, out, pieces
            for key in ("GS", "GR", "GK", "XS", "XR", "HS", "HR", "TS", "T"):
                setattr(self, key, getattr(r, key + "_" + name, None))
            self.part = part

        def compute(self, left, right, col, width):
            for target, k in ((self.GS, 1 - c), (self.GK, c)):
                rhs = right(k)
                for i in range(4):
                    out = dg(left(slice(i * 256, (i + 1) * 256)), rhs, 0, 0)
                    target[2 * i : 2 * i + 2, :, col : col + width] = out.astype(BF).reshape(2, 128, width)

        def compute_own(self, left, right):
            for i in range(4):
                out = dg(left(slice(i * 256, (i + 1) * 256)), right, 0, 0)
                self.GK[2 * i : 2 * i + 2] = out.astype(BF).reshape(2, 128, -1)

        def s0(self):
            self.core = remote(self.GS, self.GR, mate)
            self.core.start()

        def chip(self, shards, rows):
            if self.GR is None:
                return self.GK[shards, rows].astype(F32)
            return self.GK[shards, rows].astype(F32) + self.GR[shards, rows].astype(F32)

        def s1(self):
            if self.GR is not None:
                self.core.wait()
            self.far()
            self.near()

        def far(self):
            self.hsems, self.xc = pair(), []
            self.XS[0:4] = self.chip(far_shards, other_x).astype(BF)
            for i in range(self.pieces):
                at = slice(i * 4 // self.pieces, (i + 1) * 4 // self.pieces)
                self.xc.append(remote(self.XS.at[at], self.XR.at[at], x_peer))
                self.xc[i].start()

        def near(self):
            self.XS[4:8] = self.chip(near_shards, other_x).astype(BF)
            self.xn = remote(self.XS.at[4:8], self.XR.at[4:8], x_peer)
            self.xn.start()

        def s2(self, i=0):
            self.xc[i].wait()
            k = 4 // self.pieces
            at = slice(i * k, (i + 1) * k)
            total = self.chip(pl.ds(4 * (1 - h) + i * k, k), my_x) + self.XR[at].astype(F32)
            self.HS[at] = total.astype(BF)
            remote(self.HS.at[at], self.HR.at[at], h_peer, self.hsems).start()

        def s3(self):
            self.xn.wait()
            all_of(self.HS, self.hsems).wait()
            total = self.chip(near_shards, my_x) + self.XR[4:8].astype(F32) + self.HR[...].astype(F32)
            self.TS[...] = total.astype(BF)
            self.sems = pair()
            start([remote(self.TS.at[peer_block(j)], self.T.at[t, my_x], peer(j), self.sems) for j in (1, 2, 3)])
            self.T[t, my_x] = self.TS[own]

        def s4(self):
            all_of(self.TS.at[0:3], self.sems).wait()
            part = self.T.at[pl.ds(4 * c, 4), my_x]
            other = self.T.at[pl.ds(4 * c, 4), other_x]
            self.sems = pair()
            self.x2 = remote(part, part, x_peer)
            self.m2 = remote(other, other, mate, self.sems)
            self.x2.start()
            remote(part, part, mate, self.sems).start()

        def s5(self):
            self.x2.wait()
            self.m2.start()

        def s6(self):
            all_of(self.T.at[0:4], self.sems).wait()
            width = self.T.shape[2] // self.parts
            self.sem = new("local")
            for tt in range(8):
                for p in range(self.parts):
                    at = (p + self.part) * WIDTH + tt * width
                    src = self.T.at[tt, :, p * width : (p + 1) * width]
                    local(src, self.out.at[:, at : at + width], self.sem).start()

        def s7(self):
            local(self.T, self.T, self.sem).wait()

    class RowGrad:
        def __init__(self, name, out, pieces=1):
            self.out, self.pieces = out, pieces
            for key in ("GS", "GR", "GK", "XS", "XR", "HS", "HR", "T"):
                setattr(self, key, getattr(r, key + "_" + name))
            self.n = self.GS.shape[0] // 2

        def compute(self, left, right):
            for target, k in ((self.GS, 1 - c), (self.GK, c)):
                lhs = left(k)
                for i in range(2):
                    cols = slice(i * 512, (i + 1) * 512)
                    target[:, cols] = dg(lhs, right(cols), 0, 0).astype(BF)

        def s0(self):
            self.core = remote(self.GS, self.GR, mate)
            self.core.start()

        def rows(self, k):
            return pl.ds(pl.multiple_of(k * self.n, HALF), self.n)

        def piece(self, i):
            return slice(i * self.n // self.pieces, (i + 1) * self.n // self.pieces)

        def s1(self):
            self.core.wait()
            rows = self.rows(1 - x)
            self.XS[...] = (self.GK[rows].astype(F32) + self.GR[rows].astype(F32)).astype(BF)
            self.hsems, self.xc = pair(), []
            for i in range(self.pieces):
                at = self.piece(i)
                self.xc.append(remote(self.XS.at[at], self.XR.at[at], x_peer))
                self.xc[i].start()

        def total(self, i):
            k = self.n // self.pieces
            rows = pl.ds(pl.multiple_of(x * self.n, HALF) + i * k, k)
            return self.GK[rows].astype(F32) + self.GR[rows].astype(F32) + self.XR[self.piece(i)].astype(F32)

        def s2(self, i=0):
            self.xc[i].wait()
            at = self.piece(i)

            @pl.when(jnp.logical_not(stays))
            def _():
                self.HS[at] = self.total(i).astype(BF)
                remote(self.HS.at[at], self.HR.at[at], h_peer, self.hsems).start()

        def s3(self):
            part, other = self.T.at[self.rows(x)], self.T.at[self.rows(1 - x)]
            self.x2 = remote(part, part, x_peer)
            self.sems = pair()
            self.m1 = remote(part, part, mate, self.sems)
            self.m2 = remote(other, other, mate, self.sems)

            @pl.when(jnp.logical_not(stays))
            def _():
                all_of(self.HS, self.hsems).wait_send()

            @pl.when(stays)
            def _():
                all_of(self.HR, self.hsems).wait_recv()
                for i in range(self.pieces):
                    k = self.n // self.pieces
                    rows = pl.ds(pl.multiple_of(x * self.n, HALF) + i * k, k)
                    self.T[rows] = (self.total(i) + self.HR[self.piece(i)].astype(F32)).astype(BF)
                self.x2.start()
                self.m1.start()

        def s4(self):
            pass

        def s5(self):
            @pl.when(stays)
            def _():
                self.x2.wait()
                self.m2.start()

        def s6(self):
            @pl.when(stays)
            def _():
                all_of(self.T, self.sems).wait_send()

            @pl.when(jnp.logical_not(stays))
            def _():
                all_of(self.T, self.sems).wait_recv()

            self.outs = [local(self.T, self.out)]
            start(self.outs)

        def s7(self):
            wait(self.outs)

    g_dn = RowGrad("DN", r.o_dn, 4)
    g_up = ColumnGrad("UP", r.o_up, 1, pieces=2)
    g_co = RowGrad("CO", r.o_co)
    g_cq = ColumnGrad("CQ", r.o_cq, 3, pieces=2)
    g_so = RowGrad("SO", r.o_so)
    g_sq = [ColumnGrad("SQ%d" % p, r.o_sq, 1, p) for p in range(3)]

    def lanes(ref, k, width, base=0):
        return ref[:, :, pl.ds(pl.multiple_of(base + k * width, 128), width)].reshape(-1, width)

    rs_e = RelayScatter(r.PBE, r.VIAE, r.RBE, slice(0, ENC), [pair(), pair()])
    last_pairs = [pair() for _ in range(NSUB)]
    dk_x = remote(r.DKS, r.DKR, mate)

    def encoder_swap():
        their_enc = pl.ds(pl.multiple_of((1 - c) * 256, 256), 256)
        r.DKS[...] = r.DKV[their_enc].astype(BF).reshape(4, ENC, 512)
        dk_x.start()

    def encoder_back():
        dk_x.wait()
        my_enc = pl.ds(pl.multiple_of(c * 256, 256), 256)
        low = (r.DKV[my_enc] + r.DKR[...].reshape(256, 512).astype(F32)).astype(BF)
        r.DKL[...] = low.reshape(4, ENC, 512)
        dv_sum = colsum(low[:, 256:512].astype(F32))
        for k in range(2):
            add_small(4, (4 * k + own) * 128, 128, dv_sum[:, k * 128 : (k + 1) * 128])
        for n in range(2):
            cols = slice(n * 512, (n + 1) * 512)
            out = dg(low, shards(r.WCQ, cols, slice(256, 768)), 1, 1)
            r.PBE[:, :, cols] = out.astype(BF).reshape(4, ENC, 512)
        rs_e.start()

    def encoder_out():
        r.DES[...] = rs_e.finish().astype(BF)
        outs["enc"] = leave(r.DES, r.o_denc)

    def mixed_out():
        outs["mixed"] = leave(r.MXS, r.o_mixed)

    def grad_dn():
        g_dn.compute(lambda k: lanes(r.ACT, k, 512), lambda cols: r.DM[:, :, cols].reshape(512, -1))
        g_dn.s0()

    def grad_up():
        g_up.compute(lambda cols: r.S[:, :, cols].reshape(512, -1), lambda k: lanes(r.DUP, k, 512), 0, 512)
        g_up.s0()

    def grad_co():
        g_co.compute(lambda k: lanes(r.CATT, k, 128), lambda cols: r.DC[:, :, cols].reshape(512, -1))
        g_co.s0()

    def grad_cq():
        g_cq.compute(lambda cols: r.F[:, :, cols].reshape(512, -1), lambda k: lanes(r.DQC, k, 128), 0, 128)
        for p in range(2):
            g_cq.compute(
                lambda cols: r.E[:, :, cols].reshape(256, -1),
                lambda k, p=p: lanes(r.DKL, k, 128, 256 * p),
                128 + 128 * p,
                128,
            )
        g_cq.s0()

    def grad_so():
        g_so.compute(lambda k: lanes(r.ATT, k, 128), lambda cols: r.DB[:, :, cols].reshape(512, -1))
        g_so.s0()

    outs = {}

    beside = {
        1: [w_cq.cross, w_up.relay, w_co.cross],
        2: [w_cq.share, w_dn.send],
        3: [encoder_kv, w_co.share, lambda: swap_start(3), lambda: swap_wait(2), kvc_x.wait, w_co.ready, w_up.cross],
        4: [w_dn.cross],
        5: [w_up.share],
        6: [w_dn.share],
        7: [w_up.ready, w_dn.ready],
        8: [lambda: swap_wait(3), x_both.wait],
        13: [mixed_out],
        15: [grad_dn],
        16: [g_dn.s1, grad_up],
        17: [g_up.s1, lambda: g_dn.s2(0), small.cores],
        18: [lambda: g_dn.s2(1), lambda: g_dn.s2(2)],
        19: [encoder_swap, grad_co, lambda: g_dn.s2(3)],
        20: [encoder_back, grad_cq, g_co.s1, lambda: g_up.s2(0)],
        21: [small.chips, g_cq.s1, lambda: g_up.s2(1)],
        23: [rs_e.relay, grad_so, g_co.s2, lambda: g_cq.s2(0), lambda: g_cq.s2(1), g_so.s1],
    }

    comps = [comp1, comp2, comp3, comp4, comp5]
    fins = [fin1, fin2, fin3, fin4, fin5]
    rs, ag = {}, {}
    for slot in range(6 * NSUB):
        p, a = divmod(slot, NSUB)
        if p > 0:
            ag[p - 1, a].wait()
        if p < 5:
            rs[p, a] = comps[p](a)
        else:
            comp6(a)
        p, a = divmod(slot - 1, NSUB)
        if 0 <= p < 5:
            ag[p, a] = fins[p](a, rs[p, a].finish())
        p, a = divmod(slot - 2, NSUB)
        if 0 <= p < 5:
            ag[p, a].relay()
        for job in beside.get(slot, ()):
            job()

    all_of(r.DATS, do_sems).wait()
    r.DKVS[...] = jnp.zeros_like(r.DKVS)
    for i in range(4):
        n = (i + 1) * 256
        q = r.QKV[0, 2 * i : 2 * i + 2].reshape(256, 128)
        d_pair = r.DO[2 * i : 2 * i + 2].reshape(256, 128)
        o_pair = r.O[i * 256 : (i + 1) * 256]
        dqs, dk, dv = [], None, None
        for hh in range(2):
            d_head = head_of(d_pair, hh)
            delta = jnp.sum(d_head.astype(F32) * o_pair, 1, keepdims=True)
            p = probs[i][hh]
            d_scores = (p.astype(F32) * (dg(d_head, keys(2, n), 1, 1) - delta)).astype(BF)
            dqs.append(dg(d_scores, keys(1, n), 1, 0))
            new_dk = dg(d_scores, head_of(q, hh), 0, 0)
            new_dv = dg(p, d_head, 0, 0)
            dk = new_dk if dk is None else dk + new_dk
            dv = new_dv if dv is None else dv + new_dv
        dq = (jnp.where(heads[0], dqs[0], dqs[1]).astype(BF) * 0.125).astype(BF)
        r.DJN[0, 2 * i : 2 * i + 2] = dq.reshape(2, ROWS, 128)
        r.SB[0:1, pl.ds(pl.multiple_of(t * 128, 128), 128)] += colsum(dq.astype(F32))
        r.DKVS[0, 0:n] += dk
        r.DKVS[1, 0:n] += dv
    r.DJN[1] = r.DKVS[0].astype(BF).reshape(8, ROWS, 128)
    low = r.DKVS[1].astype(BF)
    r.DJN[2] = low.reshape(8, ROWS, 128)
    r.SB[1:2, pl.ds(pl.multiple_of(t * 128, 128), 128)] = colsum(low.astype(F32))
    dj_sems = pair()
    for p in range(3):
        at = pl.ds(pl.multiple_of(p * 256 + c * 128, 128), 128)
        remote(r.DJN.at[p, theirs], r.DJ.at[:, :, at], mate, dj_sems).start()
        r.DJ[:, :, at] = r.DJN[p, mine]
    late.cores()
    for p in range(3):
        g_sq[p].compute_own(lambda cols: r.X[:, :, cols].reshape(1024, -1), r.DJN[p].reshape(1024, 128))
        g_sq[p].far()
    for p in range(3):
        g_sq[p].near()
    g_so.s2()
    g_up.s3()
    g_dn.s3()
    late.chips()
    all_of(r.DJ.at[:, :, 0:384], dj_sems).wait()
    rs6 = [
        partial(
            a,
            blocks(r.DJ, a, 768),
            lambda cols: shards(r.WQKV, cols, slice(0, 768)),
            1,
            sums=RelayScatter(r.PB, r.VIA, r.RB, span(a), [last_pairs[a], scatter_pairs[a]]),
        )
        for a in range(NSUB)
    ]
    g_sq[0].s2()
    g_sq[1].s2()
    g_sq[2].s2()
    rs6[0].relay()
    g_up.s4()
    rs6[1].relay()
    g_cq.s3()
    rs6[2].relay()
    g_sq[0].s3()
    rs6[3].relay()
    g_sq[1].s3()
    g_sq[2].s3()
    g_so.s3()
    g_co.s3()
    sum_halves()
    g_cq.s4()
    r.DTS[half(0)] = (r.RES[half(0)] + rs6[0].finish()).astype(BF)
    r.DTS[half(1)] = (r.RES[half(1)] + rs6[1].finish()).astype(BF)
    r.DTS[half(2)] = (r.RES[half(2)] + rs6[2].finish()).astype(BF)
    r.DTS[half(3)] = (r.RES[half(3)] + rs6[3].finish()).astype(BF)
    outs["tokens"] = leave(r.DTS, r.o_dtok)
    g_sq[0].s4()
    g_sq[1].s4()
    g_sq[2].s4()
    encoder_out()
    g_dn.s5()
    g_up.s5()
    g_co.s5()
    g_so.s5()
    g_dn.s6()
    g_cq.s5()
    sum_sides()
    g_sq[0].s5()
    g_up.s6()
    g_sq[1].s5()
    g_co.s6()
    g_so.s6()
    g_cq.s6()
    g_sq[2].s5()
    g_sq[0].s6()
    g_sq[1].s6()
    g_sq[2].s6()
    sum_end()

    @pl.when(jnp.logical_not(stays))
    def _():
        for cp in outs.values():
            cp.wait()

    for g in (g_dn, g_up, g_co, g_cq, g_so, *g_sq):
        g.s7()
    assert count["send"] <= N_SEND and count["recv"] <= N_RECV and count["local"] <= N_LOCAL


def on_chip(*args):
    (tokens, encoder, seq_len, enc_len, d_mixed, *rest) = args
    *mats, self_bias, cross_bias, norm_gain, norm_bias, fc1_bias, fc2_bias = rest
    anywhere = pl.BlockSpec(memory_space=pl.ANY)
    vmem = pl.BlockSpec(memory_space=pltpu.VMEM)
    smem = pl.BlockSpec(memory_space=pltpu.SMEM)
    shapes = [
        ((ROWS, WIDTH), BF),
        ((ROWS, WIDTH), BF),
        ((ENC, WIDTH), BF),
        ((128, 3 * WIDTH), BF),
        ((128, WIDTH), BF),
        ((128, 3 * WIDTH), BF),
        ((128, WIDTH), BF),
        ((128, HIDDEN), BF),
        ((512, WIDTH), BF),
        ((24, WIDTH), F32),
    ]
    outs = pl.pallas_call(
        layer_kernel,
        out_shape=[jax.ShapeDtypeStruct(s, d) for s, d in shapes],
        in_specs=[anywhere, anywhere, smem, smem, anywhere] + [anywhere] * 6 + [vmem] * 6,
        out_specs=[vmem] * 3 + [anywhere] * 6 + [vmem],
        scratch_shapes=[pltpu.VMEM(s, d) for s, d in SCRATCH.values()]
        + [
            pltpu.SemaphoreType.DMA((N_SEND,)),
            pltpu.SemaphoreType.DMA((N_RECV,)),
            pltpu.SemaphoreType.DMA((N_LOCAL,)),
        ],
        compiler_params=pltpu.CompilerParams(
            collective_id=0, has_side_effects=True, vmem_limit_bytes=VMEM_BYTES
        ),
        cost_estimate=pl.CostEstimate(
            flops=16 * 10**9, bytes_accessed=16 * 2**20, transcendentals=8 * 2**20
        ),
    )(
        tokens, encoder, seq_len, enc_len, d_mixed, *mats,
        self_bias, cross_bias, norm_gain, norm_bias,
        fc1_bias.reshape(1, -1), fc2_bias.reshape(1, -1),
    )
    steps = 4

    def rows_of(shape):
        return pl.BlockSpec((shape[0] // steps, shape[1]), lambda i: (i, 0))

    def whole(shape):
        return pl.BlockSpec(shape, lambda i: (0, 0))

    wide = [(s, BF if k == 0 else F32) for k, (s, _) in enumerate(shapes[:-1])]
    flat = [((3, WIDTH), F32)] * 4 + [((1, HIDDEN), F32), ((1, WIDTH), F32)]
    *results, fc1_sum, fc2_sum = pl.pallas_call(
        widen_kernel,
        grid=(steps,),
        out_shape=[jax.ShapeDtypeStruct(s, d) for s, d in wide + flat],
        in_specs=[rows_of(s) for s, _ in shapes[:-1]] + [whole(shapes[-1][0])],
        out_specs=[rows_of(s) for s, _ in wide] + [whole(s) for s, _ in flat],
        compiler_params=pltpu.CompilerParams(vmem_limit_bytes=VMEM_BYTES),
    )(*outs)
    return (*results, fc1_sum.reshape(-1), fc2_sum.reshape(-1))


def widen_kernel(*refs):
    n = len(OUT_NAMES)
    small, flat = refs[n - 1], refs[2 * n - 1 :]
    for src, dst in zip(refs[: n - 1], refs[n:]):
        dst[...] = src[...].astype(dst.dtype)
    for k, rows in enumerate(((0, 1, 2), (3, 4, 8), (5, 9, 10), (6, 11, 12))):
        for i, row in enumerate(rows):
            flat[k][i : i + 1, :] = small[row : row + 1, :]
    for k in range(4):
        flat[4][0:1, k * WIDTH : (k + 1) * WIDTH] = small[16 + k : 17 + k, :]
    flat[5][...] = small[13:14, :]


def fits(mesh, tokens, encoder, self_qkv, fc1_weight):
    return (
        (mesh.shape["rep"], mesh.shape["shard"]) == (4, 8)
        and tokens.shape == (32 * ROWS, WIDTH)
        and encoder.shape == (32 * ENC, WIDTH)
        and self_qkv.shape == (WIDTH, 3 * WIDTH)
        and fc1_weight.shape == (WIDTH, HIDDEN)
    )


def solution(mesh):
    def placed(body):
        return jax.shard_map(
            body,
            mesh=mesh,
            in_specs=(
                P(("rep", "shard"), None),
                P(("rep", "shard"), None),
                P("rep"),
                P("rep"),
                P(("rep", "shard"), None),
                P("shard", None),
                P("shard", None),
                P("shard", None),
                P("shard", None),
                P("shard", None),
                P("shard", None),
                P(),
                P(),
                P(),
                P(),
                P(),
                P(),
            ),
            out_specs=(
                P(("rep", "shard"), None),
                P(("rep", "shard"), None),
                P(("rep", "shard"), None),
                P("shard", None),
                P("shard", None),
                P("shard", None),
                P("shard", None),
                P("shard", None),
                P("shard", None),
                P(),
                P(),
                P(),
                P(),
                P(),
                P(),
            ),
            check_vma=False,
        )

    def run(*args):
        fast = fits(mesh, args[0], args[1], args[5], args[9])
        return placed(on_chip if fast else local)(*args)

    return run
```

```python
from functools import partial

import jax
import jax.numpy as jnp
from jax import lax
from jax.experimental import pallas as pl
from jax.experimental.pallas import tpu as pltpu
from jax.sharding import PartitionSpec as P

HEADS = 16
HEAD = 64


def for_sending(array):
    return jax.tree.map(lambda a: a.astype(jnp.bfloat16) if a.dtype == jnp.float32 else a, array)


def layer_norm(hidden, gain_row, shift_row):
    centre = hidden - jnp.mean(hidden, -1, keepdims=True)
    spread = jnp.mean(centre * centre, -1, keepdims=True)
    return centre * lax.rsqrt(spread + 1e-05) * gain_row + shift_row


def exact_gelu(values):
    return jax.nn.gelu(values, approximate=False)


def contract_rows(left, right):
    return lax.dot_general(
        left, right, (((0,), (0,)), ((), ())), preferred_element_type=jnp.float32
    )


def back_dot(grad_rows, weight):
    return lax.dot_general(
        grad_rows, weight, (((1,), (1,)), ((), ())), preferred_element_type=jnp.float32
    )


def causal_mask(query_pos, key_pos):
    return key_pos[None, :] <= query_pos[:, None]


def enc_visible(query_pos, key_pos, enc_limit):
    return jnp.broadcast_to((key_pos < enc_limit)[None, :], (query_pos.shape[0], key_pos.shape[0]))


def only_live(step_fn, live_fn):

    def wrapped(totals, block_in, offset):
        return lax.cond(
            live_fn(block_in, offset), lambda: step_fn(totals, block_in, offset), lambda: totals
        )

    return wrapped


def self_fold(key_pair, step_fn, start_state, store):
    return step_fn(
        start_state,
        jax.tree.map(
            lambda a: lax.all_gather(a, "shard", axis=0, tiled=True), for_sending(key_pair)
        ),
        jnp.int32(0),
    )


def cross_fold(key_pair, step_fn, start_state, store):
    return step_fn(
        start_state,
        jax.tree.map(
            lambda a: lax.all_gather(a, "shard", axis=0, tiled=True), for_sending(key_pair)
        ),
        jnp.int32(0),
    )


def keys_live(query_pos, allowed_fn):

    def live_fn(block_in, offset):
        key_pos = jnp.arange(block_in[0].shape[0], dtype=jnp.int32)
        return jnp.any(allowed_fn(query_pos, key_pos))

    return live_fn


def head_scores(query_heads, query_pos, key_block, allowed_fn):
    key_count = key_block.shape[0]
    key_pos = jnp.arange(key_count, dtype=jnp.int32)
    scores = jnp.einsum(
        "qhd,khd->hqk",
        query_heads,
        key_block.reshape(key_count, HEADS, HEAD),
        preferred_element_type=jnp.float32,
    )
    return (scores, allowed_fn(query_pos, key_pos)[None])


def forward_pass(query_part, query_pos, key_pair, allowed_fn, folder):
    query_count = query_part.shape[0]
    query_heads = query_part.reshape(query_count, HEADS, HEAD)
    live_fn = keys_live(query_pos, allowed_fn)

    def stat_step(totals, block_in, offset):
        highest, mass = totals
        scores, allowed = head_scores(query_heads, query_pos, block_in[0], allowed_fn)
        masked = jnp.where(allowed, scores, -1e30)
        raised = jnp.maximum(highest, jnp.max(masked, -1))
        fresh = jnp.sum(jnp.where(allowed, jnp.exp(masked - raised[:, :, None]), 0.0), -1)
        return (raised, fresh)

    start_state = (
        jnp.full((HEADS, query_count), -1e30, jnp.float32),
        jnp.zeros((HEADS, query_count), jnp.float32),
    )
    highest, mass = folder(key_pair, only_live(stat_step, live_fn), start_state, None)
    log_total = highest + jnp.log(mass)

    def out_step(totals, block_in, offset):
        scores, allowed = head_scores(query_heads, query_pos, block_in[0], allowed_fn)
        weights_low = jnp.where(allowed, jnp.exp(scores - log_total[:, :, None]), 0.0).astype(
            jnp.bfloat16
        )
        value_heads = block_in[1].reshape(block_in[1].shape[0], HEADS, HEAD)
        return jnp.einsum(
            "hqk,khd->qhd", weights_low, value_heads, preferred_element_type=jnp.float32
        )

    summed = folder(
        key_pair,
        only_live(out_step, live_fn),
        jnp.zeros((query_count, HEADS, HEAD), jnp.float32),
        None,
    )
    return (log_total.T, summed)


def query_step(query_part, query_pos, allowed_fn, log_rows, delta_rows, d_out):
    query_count = query_part.shape[0]
    query_heads = query_part.reshape(query_count, HEADS, HEAD)
    grad_heads = d_out.reshape(query_count, HEADS, HEAD)
    log_total = log_rows.T
    correction = delta_rows.T

    def grad_step(totals, block_in, offset):
        key_block, value_block = block_in
        key_count = key_block.shape[0]
        scores, allowed = head_scores(query_heads, query_pos, key_block, allowed_fn)
        probs = jnp.where(allowed, jnp.exp(scores - log_total[:, :, None]), 0.0)
        d_probs = jnp.einsum(
            "qhd,khd->hqk",
            grad_heads,
            value_block.reshape(key_count, HEADS, HEAD),
            preferred_element_type=jnp.float32,
        )
        d_scores = (probs * (d_probs - correction[:, :, None])).astype(jnp.bfloat16)
        return jnp.einsum(
            "hqk,khd->qhd",
            d_scores,
            key_block.reshape(key_count, HEADS, HEAD),
            preferred_element_type=jnp.float32,
        )

    return only_live(grad_step, keys_live(query_pos, allowed_fn))


def query_grad(query_part, query_pos, key_pair, allowed_fn, folder, log_rows, delta_rows, d_out):
    query_count = query_part.shape[0]
    step_fn = query_step(query_part, query_pos, allowed_fn, log_rows, delta_rows, d_out)
    return folder(key_pair, step_fn, jnp.zeros((query_count, HEADS, HEAD), jnp.float32), None)


def key_step(own_keys, own_values, key_pos, allowed_fn, log_all, delta_all):
    key_count = own_keys.shape[0]
    key_heads = own_keys.reshape(key_count, HEADS, HEAD)
    value_heads = own_values.reshape(key_count, HEADS, HEAD)

    def step_fn(totals, block_in, offset):
        query_block, grad_block = block_in
        query_count = query_block.shape[0]
        query_pos = jnp.arange(query_count, dtype=jnp.int32)
        log_part = log_all.T
        delta_part = delta_all.T
        query_heads = query_block.reshape(query_count, HEADS, HEAD)
        grad_heads = grad_block.reshape(query_count, HEADS, HEAD)
        scores = jnp.einsum(
            "qhd,khd->hqk", query_heads, key_heads, preferred_element_type=jnp.float32
        )
        allowed = allowed_fn(query_pos, key_pos)[None]
        probs = jnp.where(allowed, jnp.exp(scores - log_part[:, :, None]), 0.0)
        d_values = jnp.einsum(
            "hqk,qhd->khd",
            probs.astype(jnp.bfloat16),
            grad_heads,
            preferred_element_type=jnp.float32,
        )
        d_probs = jnp.einsum(
            "qhd,khd->hqk", grad_heads, value_heads, preferred_element_type=jnp.float32
        )
        d_scores = (probs * (d_probs - delta_part[:, :, None])).astype(jnp.bfloat16)
        d_keys = jnp.einsum(
            "hqk,qhd->khd", d_scores, query_heads, preferred_element_type=jnp.float32
        )
        return (d_keys, d_values)

    def live_fn(block_in, offset):
        query_pos = jnp.arange(block_in[0].shape[0], dtype=jnp.int32)
        return jnp.any(allowed_fn(query_pos, key_pos))

    return only_live(step_fn, live_fn)


def column_sum(values):
    return jnp.sum(values.astype(jnp.float32), 0)


def local(
    tokens,
    encoder,
    seq_len,
    enc_len,
    d_mixed,
    self_qkv,
    self_out,
    cross_qkv,
    cross_out,
    fc1_weight,
    fc2_weight,
    self_bias,
    cross_bias,
    norm_gain,
    norm_bias,
    fc1_bias,
    fc2_bias,
):
    model_width = tokens.shape[1]
    tok_rows = tokens.shape[0]
    enc_rows = encoder.shape[0]
    device_at = lax.axis_index("shard")
    positions = device_at * tok_rows + jnp.arange(tok_rows, dtype=jnp.int32)
    enc_positions = device_at * enc_rows + jnp.arange(enc_rows, dtype=jnp.int32)
    seq_limit = seq_len[0]
    visible = partial(enc_visible, enc_limit=enc_len[0])
    w_sq, w_so = (
        lax.all_gather(self_qkv, "shard", axis=0, tiled=True),
        lax.all_gather(self_out, "shard", axis=0, tiled=True),
    )
    joined = jnp.dot(tokens, w_sq, preferred_element_type=jnp.float32)
    query_s = ((joined[:, :model_width] + self_bias[0]) * 0.125).astype(jnp.bfloat16)
    key_s = joined[:, model_width : 2 * model_width].astype(jnp.bfloat16)
    value_s = (joined[:, 2 * model_width :] + self_bias[1]).astype(jnp.bfloat16)
    self_lse, self_summed = forward_pass(
        query_s, positions, (key_s, value_s), causal_mask, self_fold
    )
    attended = self_summed.reshape(tok_rows, model_width).astype(jnp.bfloat16)
    branch = jnp.dot(attended, w_so, preferred_element_type=jnp.float32) + self_bias[2]
    first_norm, first_pull = jax.vjp(
        layer_norm, tokens.astype(jnp.float32) + branch, norm_gain[0], norm_bias[0]
    )
    w_cq, w_co = (
        lax.all_gather(cross_qkv, "shard", axis=0, tiled=True),
        lax.all_gather(cross_out, "shard", axis=0, tiled=True),
    )
    first_low = first_norm.astype(jnp.bfloat16)
    query_c = (
        (
            jnp.dot(first_low, w_cq[:, :model_width], preferred_element_type=jnp.float32)
            + cross_bias[0]
        )
        * 0.125
    ).astype(jnp.bfloat16)
    enc_proj = jnp.dot(encoder, w_cq[:, model_width:], preferred_element_type=jnp.float32)
    key_c = enc_proj[:, :model_width].astype(jnp.bfloat16)
    value_c = (enc_proj[:, model_width:] + cross_bias[1]).astype(jnp.bfloat16)
    cross_lse, cross_summed = forward_pass(
        query_c, positions, (key_c, value_c), visible, cross_fold
    )
    cross_att = cross_summed.reshape(tok_rows, model_width).astype(jnp.bfloat16)
    branch_c = jnp.dot(cross_att, w_co, preferred_element_type=jnp.float32) + cross_bias[2]
    second_norm, second_pull = jax.vjp(
        layer_norm, first_norm + branch_c, norm_gain[1], norm_bias[1]
    )
    w_up, w_down = (
        lax.all_gather(fc1_weight, "shard", axis=0, tiled=True),
        lax.all_gather(fc2_weight, "shard", axis=0, tiled=True),
    )
    second_low = second_norm.astype(jnp.bfloat16)
    upward = jnp.dot(second_low, w_up, preferred_element_type=jnp.float32) + fc1_bias
    activated, gelu_pull = jax.vjp(exact_gelu, upward)
    act_low = activated.astype(jnp.bfloat16)
    branch_m = jnp.dot(act_low, w_down, preferred_element_type=jnp.float32) + fc2_bias
    output, third_pull = jax.vjp(layer_norm, second_norm + branch_m, norm_gain[2], norm_bias[2])
    valid = (positions < seq_limit).astype(jnp.float32)[:, None]
    d_third, d_gain3, d_shift3 = third_pull(d_mixed.astype(jnp.float32) * valid)
    d_branch_m = d_third.astype(jnp.bfloat16)
    g_down = contract_rows(act_low, d_branch_m)
    d_act = back_dot(d_branch_m, w_down).astype(jnp.bfloat16)
    (d_up,) = gelu_pull(d_act.astype(jnp.float32))
    d_up_low = d_up.astype(jnp.bfloat16)
    g_up = contract_rows(second_low, d_up_low)
    d_second = d_third + back_dot(d_up_low, w_up)
    d_hidden2, d_gain2, d_shift2 = second_pull(d_second)
    d_branch_c = d_hidden2.astype(jnp.bfloat16)
    g_co = contract_rows(cross_att, d_branch_c)
    d_cross_att = back_dot(d_branch_c, w_co).astype(jnp.bfloat16)
    cross_delta = jnp.einsum(
        "qhd,qhd->qh", d_cross_att.reshape(tok_rows, HEADS, HEAD).astype(jnp.float32), cross_summed
    )
    d_query_c = query_grad(
        query_c,
        positions,
        (key_c, value_c),
        visible,
        cross_fold,
        cross_lse,
        cross_delta,
        d_cross_att,
    )
    d_query_cs = d_query_c.reshape(tok_rows, model_width).astype(jnp.bfloat16) * 0.125
    d_first = d_hidden2 + back_dot(d_query_cs, w_cq[:, :model_width])
    d_hidden1, d_gain1, d_shift1 = first_pull(d_first)
    d_branch = d_hidden1.astype(jnp.bfloat16)
    g_so = contract_rows(attended, d_branch)
    d_attended = back_dot(d_branch, w_so).astype(jnp.bfloat16)
    self_delta = jnp.einsum(
        "qhd,qhd->qh", d_attended.reshape(tok_rows, HEADS, HEAD).astype(jnp.float32), self_summed
    )
    stats = (
        lax.all_gather(self_lse, "shard", axis=0, tiled=True),
        lax.all_gather(self_delta, "shard", axis=0, tiled=True),
        lax.all_gather(cross_lse, "shard", axis=0, tiled=True),
        lax.all_gather(cross_delta, "shard", axis=0, tiled=True),
    )
    tok_zero = jnp.zeros((tok_rows, HEADS, HEAD), jnp.float32)
    query_side = query_step(query_s, positions, causal_mask, self_lse, self_delta, d_attended)
    key_side = key_step(key_s, value_s, positions, causal_mask, stats[0], stats[1])
    offset = jnp.int32(0)
    d_query_part = query_side(
        tok_zero,
        (
            lax.all_gather(key_s, "shard", axis=0, tiled=True),
            lax.all_gather(value_s, "shard", axis=0, tiled=True),
        ),
        offset,
    )
    d_key_part, d_value_part = key_side(
        (tok_zero, tok_zero),
        (
            lax.all_gather(query_s, "shard", axis=0, tiled=True),
            lax.all_gather(d_attended, "shard", axis=0, tiled=True),
        ),
        offset,
    )
    enc_zero = jnp.zeros((enc_rows, HEADS, HEAD), jnp.float32)
    d_key_c, d_value_c = key_step(key_c, value_c, enc_positions, visible, stats[2], stats[3])(
        (enc_zero, enc_zero),
        (
            lax.all_gather(query_c, "shard", axis=0, tiled=True),
            lax.all_gather(d_cross_att, "shard", axis=0, tiled=True),
        ),
        jnp.int32(0),
    )
    d_qs = d_query_part.reshape(tok_rows, model_width).astype(jnp.bfloat16) * 0.125
    d_ks = d_key_part.reshape(tok_rows, model_width).astype(jnp.bfloat16)
    d_vs = d_value_part.reshape(tok_rows, model_width).astype(jnp.bfloat16)
    d_joined = jnp.concatenate([d_qs, d_ks, d_vs], 1)
    g_sq = contract_rows(tokens, d_joined)
    d_tokens = d_hidden1 + back_dot(d_joined, w_sq)
    d_kc = d_key_c.reshape(enc_rows, model_width).astype(jnp.bfloat16)
    d_vc = d_value_c.reshape(enc_rows, model_width).astype(jnp.bfloat16)
    d_enc_proj = jnp.concatenate([d_kc, d_vc], 1)
    g_cq = jnp.concatenate(
        [contract_rows(first_low, d_query_cs), contract_rows(encoder, d_enc_proj)], 1
    )
    d_encoder = back_dot(d_enc_proj, w_cq[:, model_width:])
    d_self_bias = jnp.stack([column_sum(d_qs), column_sum(d_vs), column_sum(d_branch)])
    d_cross_bias = jnp.stack([column_sum(d_query_cs), column_sum(d_vc), column_sum(d_branch_c)])
    d_norm_gain = jnp.stack([d_gain1, d_gain2, d_gain3])
    d_norm_bias = jnp.stack([d_shift1, d_shift2, d_shift3])
    d_fc1_bias = column_sum(d_up_low)
    d_fc2_bias = column_sum(d_branch_m)
    row_grads = (
        lax.psum_scatter(g_sq, "shard", scatter_dimension=0, tiled=True),
        lax.psum_scatter(g_so, "shard", scatter_dimension=0, tiled=True),
        lax.psum_scatter(g_cq, "shard", scatter_dimension=0, tiled=True),
        lax.psum_scatter(g_co, "shard", scatter_dimension=0, tiled=True),
        lax.psum_scatter(g_up, "shard", scatter_dimension=0, tiled=True),
        lax.psum_scatter(g_down, "shard", scatter_dimension=0, tiled=True),
    )
    row_grads = lax.psum(
        (row_grads[0], row_grads[1], row_grads[2], row_grads[3], row_grads[4], row_grads[5]), "rep"
    )
    small_sums = lax.psum(
        (d_self_bias, d_cross_bias, d_norm_gain, d_norm_bias, d_fc1_bias, d_fc2_bias),
        ("rep", "shard"),
    )
    return (
        output.astype(jnp.bfloat16),
        d_tokens,
        d_encoder,
        row_grads[0],
        row_grads[1],
        row_grads[2],
        row_grads[3],
        row_grads[4],
        row_grads[5],
        small_sums[0],
        small_sums[1],
        small_sums[2],
        small_sums[3],
        small_sums[4],
        small_sums[5],
    )


MESH = pl.DeviceIdType.MESH
BF = jnp.bfloat16
F32 = jnp.float32
EPS = 1e-05


def dg(left, right, cl, cr):
    return lax.dot_general(
        left, right, (((cl,), (cr,)), ((), ())), preferred_element_type=F32
    )


class Names:
    pass


WIDTH = 1024
HIDDEN = 4096
ROWS = 128
ENC = 64
HALF = 64
NSUB = 4
SUB = ROWS // NSUB

SCRATCH = {
    "X": ((8, ROWS, WIDTH), BF),
    "E": ((4, ENC, WIDTH), BF),
    "DMX": ((ROWS, WIDTH), BF),
    "LSRC": ((8, 128), F32),
    "LENS": ((8, 128), F32),
    "WQKV": ((8, 128, 768), BF),
    "WSO": ((2, 128, WIDTH), BF),
    "WCQ": ((8, 128, 768), BF),
    "WCO": ((2, 128, WIDTH), BF),
    "WUP": ((8, 128, 1024), BF),
    "WDN": ((2, 512, WIDTH), BF),
    "QST": ((2, 3, 4, ROWS, 128), BF),
    "QKV": ((3, 8, ROWS, 128), BF),
    "P0": ((2, 256, 256), BF),
    "P1": ((2, 256, 512), BF),
    "P2": ((2, 256, 768), BF),
    "P3": ((2, 256, 1024), BF),
    "O": ((1024, 128), F32),
    "ATF": ((8, ROWS, 128), BF),
    "ATT": ((4, ROWS, 256), BF),
    "PB": ((4, ROWS, WIDTH), BF),
    "RB": ((3, ROWS, WIDTH), BF),
    "VIA": ((ROWS, WIDTH), BF),
    "VIAE": ((ENC, WIDTH), BF),
    "PBE": ((4, ENC, WIDTH), BF),
    "RBE": ((3, ENC, WIDTH), BF),
    "F": ((4, ROWS, WIDTH), BF),
    "S": ((4, ROWS, WIDTH), BF),
    "DM": ((4, ROWS, WIDTH), BF),
    "DC": ((4, ROWS, WIDTH), BF),
    "DB": ((4, ROWS, WIDTH), BF),
    "RES": ((ROWS, WIDTH), F32),
    "RES2": ((ROWS, WIDTH), F32),
    "XH": ((2, ROWS, WIDTH), F32),
    "RSTD": ((2, ROWS, 1), F32),
    "QC": ((4, ROWS, 256), BF),
    "KVC": ((8, ENC, 512), BF),
    "PC": ((4, NSUB, 4 * SUB, 512), BF),
    "OC": ((NSUB, 4 * SUB, 256), F32),
    "CATT": ((4, ROWS, 256), BF),
    "ACT": ((4, ROWS, 1024), BF),
    "DGL": ((NSUB, 4 * SUB, 1024), BF),
    "DUP": ((4, ROWS, 1024), BF),
    "DQC": ((4, ROWS, 256), BF),
    "DKV": ((512, 512), F32),
    "DKS": ((4, ENC, 512), BF),
    "DKR": ((4, ENC, 512), BF),
    "DKL": ((4, ENC, 512), BF),
    "DATS": ((4, ROWS, 128), BF),
    "DO": ((8, ROWS, 128), BF),
    "DKVS": ((2, 1024, 128), F32),
    "DJN": ((3, 8, ROWS, 128), BF),
    "DJ": ((4, ROWS, 768), BF),
    "MXS": ((ROWS, WIDTH), BF),
    "DTS": ((ROWS, WIDTH), BF),
    "DES": ((ENC, WIDTH), BF),
    "SM": ((16, WIDTH), F32),
    "SMR": ((16, WIDTH), F32),
    "SM4": ((4, 16, WIDTH), F32),
    "SB": ((8, WIDTH), F32),
    "SBR": ((8, WIDTH), F32),
    "SB4": ((4, 8, WIDTH), F32),
    "ALL": ((24, WIDTH), F32),
    "ALLR": ((2, 24, WIDTH), F32),
}
for _name, _rows in (("SO", 128), ("CO", 128), ("DN", 512)):
    SCRATCH["GS_" + _name] = ((_rows, WIDTH), BF)
    SCRATCH["GR_" + _name] = ((_rows, WIDTH), BF)
    SCRATCH["GK_" + _name] = ((_rows, WIDTH), BF)
    SCRATCH["XS_" + _name] = ((_rows // 2, WIDTH), BF)
    SCRATCH["XR_" + _name] = ((_rows // 2, WIDTH), BF)
    SCRATCH["HS_" + _name] = ((_rows // 2, WIDTH), BF)
    SCRATCH["HR_" + _name] = ((_rows // 2, WIDTH), BF)
    SCRATCH["T_" + _name] = ((_rows, WIDTH), BF)
for _name, _cols in (("SQ0", 128), ("SQ1", 128), ("SQ2", 128), ("CQ", 384), ("UP", 512)):
    if _cols > 128:
        SCRATCH["GS_" + _name] = ((8, 128, _cols), BF)
        SCRATCH["GR_" + _name] = ((8, 128, _cols), BF)
    SCRATCH["GK_" + _name] = ((8, 128, _cols), BF)
    SCRATCH["XS_" + _name] = ((8, HALF, _cols), BF)
    SCRATCH["XR_" + _name] = ((8, HALF, _cols), BF)
    SCRATCH["HS_" + _name] = ((4, HALF, _cols), BF)
    SCRATCH["HR_" + _name] = ((4, HALF, _cols), BF)
    SCRATCH["TS_" + _name] = ((4, HALF, _cols), BF)
    SCRATCH["T_" + _name] = ((8, 128, _cols), BF)

IN_NAMES = (
    "tokens", "encoder", "seq", "enc", "dmix", "w_sq", "w_so", "w_cq", "w_co", "w_up", "w_dn",
    "sb", "cb", "gain", "shift", "fb1", "fb2",
)
OUT_NAMES = (
    "o_mixed", "o_dtok", "o_denc", "o_sq", "o_so", "o_cq", "o_co", "o_up", "o_dn", "o_small",
)
VMEM_BYTES = 64 * 2**20 - 2**19
N_SEND, N_RECV, N_LOCAL = 139, 146, 21


def layer_kernel(*refs):
    n_in, n_out = len(IN_NAMES), len(OUT_NAMES)
    r = Names()
    names = IN_NAMES + OUT_NAMES + tuple(SCRATCH)
    for name, ref in zip(names, refs):
        setattr(r, name, ref)
    send_sem, recv_sem, local_sem = refs[len(names) :]
    count = {"send": 0, "recv": 0, "local": 0}

    def new(kind):
        count[kind] += 1
        return count[kind] - 1

    def pair():
        return new("send"), new("recv")

    rep, shard = lax.axis_index("rep"), lax.axis_index("shard")
    x, c = rep // 2, rep % 2
    z, y = shard // 2, shard % 2
    h, l = z // 2, z % 2
    own = 2 * l + y
    t = 4 * c + own
    s_own = 4 * h + own

    def dev(xx, hh, ll, yy, cc):
        return (xx * 2 + cc, (2 * hh + ll) * 2 + yy)

    mate = dev(x, h, l, y, 1 - c)
    x_peer = dev(1 - x, h, l, y, c)
    h_peer = dev(x, 1 - h, l, y, c)
    swap_peer = dev(x, 1 - h, l, y, 1 - c)

    def peer_lc(j):
        return (l + j // 2) % 2, (y + j % 2) % 2

    def peer(j):
        ll, yy = peer_lc(j)
        return dev(x, h, ll, yy, c)

    def peer_block(j):
        ll, yy = peer_lc(j)
        return 2 * ll + yy

    def remote(src, dst, device, sems=None):
        i, j = sems or pair()
        return pltpu.make_async_remote_copy(
            src_ref=src,
            dst_ref=dst,
            send_sem=send_sem.at[i],
            recv_sem=recv_sem.at[j],
            device_id=device,
            device_id_type=MESH,
        )

    def all_of(ref, sems):
        return remote(ref, ref, mate, sems)

    def local(src, dst, sem=None):
        return pltpu.make_async_copy(src, dst, local_sem.at[new("local") if sem is None else sem])

    barrier = pltpu.get_barrier_semaphore()
    greet = [mate, x_peer, swap_peer]
    for m in range(1, 8):
        greet.append(dev(x, (h + m // 4) % 2, (l + (m // 2) % 2) % 2, (y + m % 2) % 2, c))
    for device in greet:
        pl.semaphore_signal(barrier, inc=1, device_id=device, device_id_type=MESH)
    r.LSRC[0:1, :] = jnp.full((1, 128), r.seq[0].astype(F32))
    r.LSRC[1:2, :] = jnp.full((1, 128), r.enc[0].astype(F32))
    r.SM[...] = jnp.zeros_like(r.SM)
    r.SB[...] = jnp.zeros_like(r.SB)
    pl.semaphore_wait(barrier, len(greet))

    moved = [
        (r.tokens, r.X.at[4 * (1 - c) + own], r.X.at[t]),
        (r.encoder, r.E.at[own], r.E.at[own]),
        (r.LSRC, r.LENS, r.LENS),
        (r.dmix, r.DMX, r.DMX),
    ]
    swaps = [(remote(s, there, swap_peer), local(s, here)) for s, there, here in moved]
    stays = c == h

    def swap_start(i):
        @pl.when(stays)
        def _():
            swaps[i][1].start()

        @pl.when(jnp.logical_not(stays))
        def _():
            swaps[i][0].start()

    def swap_wait(i):
        @pl.when(stays)
        def _():
            swaps[i][1].wait()

        @pl.when(jnp.logical_not(stays))
        def _():
            swaps[i][0].wait()

    my_x = pl.ds(pl.multiple_of(x * HALF, HALF), HALF)
    other_x = pl.ds(pl.multiple_of((1 - x) * HALF, HALF), HALF)
    inner = h != l

    class ColumnWeight:
        def __init__(self, w_hbm, dst, groups, width, full=False):
            self.w, self.dst, self.width, self.full = w_hbm, dst, width, full
            self.groups = [(parts, [pair() for _ in range(6)], new("local")) for parts in groups]

        def at(self, p, shards, rows):
            first = pl.multiple_of(p * 2 * self.width + c * self.width, 128)
            return self.dst.at[shards, rows, pl.ds(first, self.width)]

        def rows(self, m):
            return slice(0, 128) if self.full and m < 4 else my_x

        def bytes(self, parts, blocks, rows):
            return self.dst.at[0:blocks, rows, 0 : len(parts) * self.width]

        def copy(self, p, m, sems, sem):
            hh, ll, yy = (h + m // 4) % 2, (l + (m // 2) % 2) % 2, (y + m % 2) % 2
            col = pl.multiple_of(p * WIDTH + (4 * c + 2 * ll + yy) * self.width, 128)
            src = self.w.at[self.rows(m), pl.ds(col, self.width)]
            at = self.at(p, s_own, self.rows(m))
            if m == 0:
                return local(src, at, sem)
            return remote(src, at, dev(x, hh, ll, yy, c), sems[m // 4])

        def near(self):
            for parts, sems, sem in self.groups:
                for p in parts:
                    start([self.copy(p, m, sems, sem) for m in (1, 2, 3, 0)])

        def far(self):
            for parts, sems, sem in self.groups:
                for p in parts:
                    start([self.copy(p, m, sems, sem) for m in (4, 5)])

            @pl.when(inner)
            def _():
                for parts, sems, sem in self.groups:
                    for p in parts:
                        start([self.copy(p, m, sems, sem) for m in (6, 7)])

        def send(self):
            self.far()
            self.near()

        def relay(self):
            @pl.when(inner)
            def _():
                for parts, sems, sem in self.groups:
                    all_of(self.bytes(parts, 3, self.rows(1)), sems[0]).wait_recv()
                    for p in parts:
                        on = self.at(p, pl.ds(4 * h + 2 * (1 - l), 2), my_x)
                        remote(on, on, h_peer, sems[2]).start()

        def cross(self):
            for parts, sems, sem in self.groups:
                near = all_of(self.bytes(parts, 3, self.rows(1)), sems[0])
                hop = all_of(self.bytes(parts, 2, my_x), sems[2])
                near.wait_send()
                here = self.dst.at[0, self.rows(0), 0 : len(parts) * self.width]
                local(here, here, sem).wait()

                @pl.when(inner)
                def _():
                    all_of(self.bytes(parts, 4, my_x), sems[1]).wait()
                    hop.wait_send()

                @pl.when(jnp.logical_not(inner))
                def _():
                    near.wait_recv()
                    all_of(self.bytes(parts, 2, my_x), sems[1]).wait()
                    hop.wait_recv()

                shards = pl.ds(4 * (1 - h), 4) if self.full else slice(None)
                for p in parts:
                    at = self.at(p, shards, my_x)
                    remote(at, at, x_peer, sems[3]).start()
                for p in parts:
                    at = self.at(p, shards, my_x)
                    remote(at, at, mate, sems[4]).start()
                    if self.full:
                        at = self.at(p, pl.ds(4 * h, 4), slice(None))
                        remote(at, at, mate, sems[4]).start()

        def share(self, which=slice(None)):
            for parts, sems, sem in self.groups[which]:
                all_of(self.bytes(parts, 4 if self.full else 8, my_x), sems[3]).wait()
                shards = pl.ds(4 * (1 - h), 4) if self.full else slice(None)
                for p in parts:
                    at = self.at(p, shards, other_x)
                    remote(at, at, mate, sems[5]).start()

        def ready(self, which=slice(None)):
            for parts, sems, sem in self.groups[which]:
                all_of(self.bytes(parts, 6 if self.full else 4, slice(None)), sems[4]).wait()
                all_of(self.bytes(parts, 4 if self.full else 8, my_x), sems[5]).wait()

    class RowWeight:
        def __init__(self, w_hbm, dst, rows):
            self.w, self.dst, self.n = w_hbm, dst, rows // 4

        def rows(self, xx):
            return pl.ds(pl.multiple_of(c * 2 * self.n + xx * self.n, 32), self.n)

        def send(self):
            at = self.rows(x)
            self.first = [local(self.w, self.dst.at[h]), remote(self.w.at[at], self.dst.at[h, at], h_peer)]
            start(self.first)

        def cross(self):
            wait(self.first)
            at = self.dst.at[1 - h, self.rows(x)]
            self.xc, self.m1 = remote(at, at, x_peer), remote(at, at, mate)
            self.xc.start()
            self.m1.start()

        def share(self):
            self.xc.wait()
            at = self.dst.at[1 - h, self.rows(1 - x)]
            self.m2 = remote(at, at, mate)
            self.m2.start()

        def ready(self):
            self.m1.wait()
            self.m2.wait()

    def leave(src, out):
        cp = remote(src, out, swap_peer)

        @pl.when(stays)
        def _():
            out[...] = src[...]

        @pl.when(jnp.logical_not(stays))
        def _():
            cp.start()

        return cp

    def start(copies):
        for cp in copies:
            cp.start()

    def wait(copies):
        for cp in copies:
            cp.wait()

    NBR = (1, 2)

    class Gather:
        def __init__(self, buf, rows, first, base=0, sems=None, apart=False):
            self.first = first - 1
            self.sems = sems or gather_sems()
            send, recv_first, recv_rest = self.sems
            blk = buf.at[base + own, rows]
            self.direct = [
                remote(blk, blk, peer(j), (send, recv_first if j == first else recv_rest)) for j in NBR
            ]
            on = buf.at[base + peer_block(first), rows]
            self.hop = remote(on, on, peer(3 - first), None if apart else (send, recv_rest))
            self.two, self.three = buf.at[0:2, rows], buf.at[0:3, rows]

        def start(self):
            start(self.direct)

        def relay(self):
            self.direct[self.first].wait_recv()
            self.hop.start()

        def wait(self):
            send, recv_first, recv_rest = self.sems
            all_of(self.two, (send, recv_rest)).wait_recv()
            all_of(self.three, (send, recv_rest)).wait_send()

    def gather_sems():
        return new("send"), new("recv"), new("recv")

    class Scatter:
        def __init__(self, buf, land, rows, sems=None):
            self.buf, self.land, self.rows, self.sems = buf, land, rows, sems or pair()
            self.sends = [
                remote(buf.at[peer_block(j), rows], land.at[j - 1, rows], peer(j), self.sems) for j in (3, 1, 2)
            ]

        def start(self):
            start(self.sends)

        def finish(self):
            all_of(self.land.at[:, self.rows], self.sems).wait()
            total = self.buf[own, self.rows].astype(F32)
            for j in range(3):
                total = total + self.land[j, self.rows].astype(F32)
            return total

    class RelayScatter:
        def __init__(self, buf, via, land, rows, sems):
            self.buf, self.via, self.land, self.rows = buf, via, land, rows
            self.second = peer_block(2)
            self.first, self.rest = sems
            self.sends = [
                remote(buf.at[peer_block(3), rows], via.at[rows], peer(1), self.first),
                remote(buf.at[peer_block(1), rows], land.at[0, rows], peer(1), self.rest),
            ]
            self.last = remote(buf.at[self.second, rows], land.at[1, rows], peer(2), self.rest)

        def start(self):
            start(self.sends)

        def relay(self):
            self.sends[0].wait()
            total = self.buf[self.second, self.rows].astype(F32) + self.via[self.rows].astype(F32)
            self.buf[self.second, self.rows] = total.astype(BF)
            self.last.start()

        def finish(self):
            all_of(self.land.at[0:2, self.rows], self.rest).wait()
            return (
                self.buf[own, self.rows].astype(F32)
                + self.land[0, self.rows].astype(F32)
                + self.land[1, self.rows].astype(F32)
            )

    gather_triples = [gather_sems() for _ in range(NSUB)]
    scatter_pairs = [pair() for _ in range(NSUB)]

    def span(a):
        return pl.ds(a * SUB, SUB)

    def half(a):
        return slice(a * SUB, (a + 1) * SUB)

    def way(a):
        return 1 + a % 2

    mine = pl.ds(4 * c, 4)
    theirs = pl.ds(4 * (1 - c), 4)
    w_sq = ColumnWeight(r.w_sq, r.WQKV, [[0], [1], [2]], 128, True)
    w_so = RowWeight(r.w_so, r.WSO, 128)
    w_cq = ColumnWeight(r.w_cq, r.WCQ, [[1, 2], [0]], 128)
    w_co = RowWeight(r.w_co, r.WCO, 128)
    w_up = ColumnWeight(r.w_up, r.WUP, [[0]], 512)
    w_dn = RowWeight(r.w_dn, r.WDN, 512)
    ag_x = [Gather(r.X, pl.ds(k * HALF, HALF), 2, 4 * c, apart=True) for k in range(2)]
    swap_start(0)

    @pl.when(stays)
    def _():
        swaps[0][1].wait()
        for g in ag_x:
            g.direct[0].start()
        w_sq.near()
        for g in ag_x:
            g.direct[0].wait_recv()
        w_sq.far()
        for g in ag_x:
            g.direct[1].start()
        swaps[1][1].start()
        swaps[2][1].start()
        w_sq.relay()
        for g in ag_x:
            g.relay()

    @pl.when(jnp.logical_not(stays))
    def _():
        w_sq.near()
        w_sq.far()
        w_sq.relay()
        swaps[1][0].start()
        swaps[2][0].start()
        swaps[0][0].wait()
        start(ag_x)
        for g in ag_x:
            g.relay()
            g.direct[0].wait_recv()

    w_so.send()
    w_cq.send()
    w_sq.cross()
    w_co.send()
    swap_wait(1)
    ag_e = Gather(r.E, pl.ds(0, ENC), 2)
    ag_e.start()
    w_up.send()
    for g in ag_x:
        g.hop.wait()
        all_of(g.two, g.sems[:2]).wait_send()
    x_both = remote(r.X.at[mine], r.X.at[mine], mate)
    x_both.start()
    w_sq.share()
    w_sq.ready()

    lane = lax.broadcasted_iota(jnp.int32, (1, 128), 1)
    heads = [lane // 64 == 0, lane // 64 == 1]

    def head_of(v, hh):
        return jnp.where(heads[hh], v, jnp.zeros_like(v))

    def own_cols(ref, row, width):
        off = [pl.multiple_of((4 * k + own) * width, 128) for k in range(2)]
        return jnp.concatenate([ref[row : row + 1, pl.ds(o, width)] for o in off], 1)

    def blocks(ref, a, width):
        return ref[:, half(a), :].reshape(4 * SUB, width)

    def shards(ref, rows, cols):
        return ref[rows.start // 128 : rows.stop // 128, :, cols].reshape(rows.stop - rows.start, -1)

    def add_small(row, col, width, value):
        at = slice(0, width) if isinstance(col, int) else pl.ds(pl.multiple_of(col, 128), width)
        ref, row = (r.SB, row) if row < 8 else (r.SM, row - 8)
        ref[row : row + 1, at] += value

    def colsum(v):
        return jnp.sum(v, 0, keepdims=True)

    bias_q = own_cols(r.sb, 0, 128)
    bias_v = own_cols(r.sb, 1, 128)
    for i in range(2):
        lhs = r.X[pl.ds(4 * c + 2 * i, 2)].reshape(256, WIDTH)
        for p in range(3):
            out = dg(lhs, r.WQKV[:, :, p * 256 : (p + 1) * 256].reshape(WIDTH, 256), 1, 0)
            if p == 0:
                out = (out + bias_q) * 0.125
            if p == 2:
                out = out + bias_v
            out = out.astype(BF)
            for k in range(2):
                r.QST[k, p, 2 * i : 2 * i + 2] = out[:, k * 128 : (k + 1) * 128].reshape(2, ROWS, 128)
    qkv_x = remote(r.QST.at[1 - c], r.QKV.at[:, mine], mate)
    qkv_x.start()
    r.QKV[:, mine] = r.QST[c]
    w_cq.relay()
    ag_e.relay()
    w_so.cross()
    qkv_x.wait()

    def keys(p, n):
        return r.QKV[p, 0 : n // ROWS].reshape(n, 128)

    probs = [r.P0, r.P1, r.P2, r.P3]
    for i in range(4):
        n = (i + 1) * 256
        q = r.QKV[0, 2 * i : 2 * i + 2].reshape(256, 128)
        outs = []
        for hh in range(2):
            s = dg(head_of(q, hh), keys(1, n), 1, 1)
            qpos = lax.broadcasted_iota(jnp.int32, (256, n), 0) + i * 256
            kpos = lax.broadcasted_iota(jnp.int32, (256, n), 1)
            s = jnp.where(kpos <= qpos, s, -1e30)
            e = jnp.exp(s - jnp.max(s, 1, keepdims=True))
            p = (e * (1.0 / jnp.sum(e, 1, keepdims=True))).astype(BF)
            probs[i][hh] = p
            outs.append(dg(p, keys(2, n), 1, 0))
        o = jnp.where(heads[0], outs[0], outs[1])
        r.O[i * 256 : (i + 1) * 256] = o
        r.ATF[2 * i : 2 * i + 2] = o.astype(BF).reshape(2, ROWS, 128)
    my_cols = pl.ds(pl.multiple_of(c * 128, 128), 128)
    att_x = remote(r.ATF.at[theirs], r.ATT.at[:, :, my_cols], mate)
    att_x.start()
    r.ATT[:, :, my_cols] = r.ATF[mine]
    w_so.share()
    w_so.ready()
    att_x.wait()

    def partial(a, lhs, w, contract, chunk=512, sums=None):
        for n in range(WIDTH // chunk):
            cols = slice(n * chunk, (n + 1) * chunk)
            out = dg(lhs, w(cols), 1, contract)
            r.PB[:, half(a), cols] = out.astype(BF).reshape(4, SUB, chunk)
        sums = sums or Scatter(r.PB, r.RB, span(a), scatter_pairs[a])
        sums.start()
        return sums

    def norm(i, rows, hidden):
        centre = hidden - jnp.mean(hidden, -1, keepdims=True)
        rstd = lax.rsqrt(jnp.mean(centre * centre, -1, keepdims=True) + EPS)
        xhat = centre * rstd
        return xhat, rstd, xhat * r.gain[i : i + 1, :] + r.shift[i : i + 1, :]

    def norm_back(i, dy, xhat, rstd):
        add_small((5, 9, 10)[i], 0, WIDTH, colsum(dy * xhat))
        add_small((6, 11, 12)[i], 0, WIDTH, colsum(dy))
        d = dy * r.gain[i : i + 1, :]
        mean_d = jnp.mean(d, -1, keepdims=True)
        mean_dx = jnp.mean(d * xhat, -1, keepdims=True)
        return rstd * (d - mean_d - xhat * mean_dx)

    def gathered(buf, a, value, first=None):
        buf[own, half(a)] = value
        g = Gather(buf, span(a), first or way(a), 0, gather_triples[a])
        g.start()
        return g

    def comp1(a):
        return partial(a, blocks(r.ATT, a, 256), lambda cols: r.WSO[:, :, cols].reshape(256, -1), 0)

    def fin1(a, total):
        hidden = r.X[t, half(a)].astype(F32) + total + r.sb[2:3, :]
        xhat, rstd, out = norm(0, half(a), hidden)
        r.XH[0, half(a)] = xhat
        r.RSTD[0, half(a)] = rstd
        r.RES[half(a)] = out
        return gathered(r.F, a, out.astype(BF), 2)

    def encoder_kv():
        w_cq.ready(slice(0, 1))
        ag_e.wait()
        bias_cv = own_cols(r.cb, 1, 128)
        for k in range(2):
            out = dg(
                r.E[...].reshape(4 * ENC, WIDTH),
                r.WCQ[:, :, 256 + k * 256 : 512 + k * 256].reshape(WIDTH, 256),
                1,
                0,
            )
            if k == 1:
                out = out + bias_cv
            r.KVC[mine, :, k * 256 : (k + 1) * 256] = out.astype(BF).reshape(4, ENC, 256)
        kvc_x.start()

    kvc_x = remote(r.KVC.at[mine], r.KVC.at[mine], mate)

    def enc_keys(part, k):
        return r.KVC[:, :, part * 256 + k * 128 : part * 256 + (k + 1) * 128].reshape(512, 128)

    def comp2(a):
        bias_cq = own_cols(r.cb, 0, 128)
        visible = lax.broadcasted_iota(jnp.int32, (1, 512), 1).astype(F32) < r.LENS[1:2, 0:1]
        q = dg(blocks(r.F, a, WIDTH), r.WCQ[:, :, 0:256].reshape(WIDTH, 256), 1, 0)
        q = ((q + bias_cq) * 0.125).astype(BF)
        r.QC[:, half(a)] = q.reshape(4, SUB, 256)
        for k in range(2):
            outs = []
            for hh in range(2):
                s = dg(head_of(q[:, k * 128 : (k + 1) * 128], hh), enc_keys(0, k), 1, 1)
                s = jnp.where(visible, s, -1e30)
                e = jnp.exp(s - jnp.max(s, 1, keepdims=True))
                p = (e * (1.0 / jnp.sum(e, 1, keepdims=True))).astype(BF)
                r.PC[2 * k + hh, a] = p
                outs.append(dg(p, enc_keys(1, k), 1, 0))
            o = jnp.where(heads[0], outs[0], outs[1])
            r.OC[a, :, k * 128 : (k + 1) * 128] = o
            r.CATT[:, half(a), k * 128 : (k + 1) * 128] = o.astype(BF).reshape(4, SUB, 128)
        return partial(a, blocks(r.CATT, a, 256), lambda cols: r.WCO[:, :, cols].reshape(256, -1), 0)

    def fin2(a, total):
        hidden = r.RES[half(a)] + total + r.cb[2:3, :]
        xhat, rstd, out = norm(1, half(a), hidden)
        r.XH[1, half(a)] = xhat
        r.RSTD[1, half(a)] = rstd
        r.RES2[half(a)] = out
        return gathered(r.S, a, out.astype(BF))

    def comp3(a):
        lhs = blocks(r.S, a, WIDTH)
        for k in range(2):
            cols = slice(k * 512, (k + 1) * 512)
            bias_up = r.fb1[0:1, pl.ds(pl.multiple_of((4 * k + own) * 512, 128), 512)]
            u = dg(lhs, r.WUP[:, :, cols].reshape(WIDTH, 512), 1, 0) + bias_up
            cdf = 0.5 + 0.5 * lax.erf(u * 0.7071067811865476)
            r.ACT[:, half(a), cols] = (u * cdf).astype(BF).reshape(4, SUB, 512)
            slope = cdf + u * (jnp.exp(-0.5 * u * u) * 0.3989422804014327)
            r.DGL[a, :, cols] = slope.astype(BF)
        return partial(a, blocks(r.ACT, a, 1024), lambda cols: r.WDN[:, :, cols].reshape(1024, -1), 0)

    def fin3(a, total):
        hidden = r.RES2[half(a)] + total + r.fb2[0:1, :]
        xhat, rstd, out = norm(2, half(a), hidden)
        r.MXS[half(a)] = out.astype(BF)
        place = lax.broadcasted_iota(jnp.int32, (SUB, 1), 0) + (t * ROWS + a * SUB)
        dy = jnp.where(place.astype(F32) < r.LENS[0:1, 0:1], r.DMX[half(a)].astype(F32), 0.0)
        d = norm_back(2, dy, xhat, rstd)
        r.RES[half(a)] = d
        low = d.astype(BF)
        add_small(13, 0, WIDTH, colsum(low.astype(F32)))
        return gathered(r.DM, a, low)

    def comp4(a):
        lhs = blocks(r.DM, a, WIDTH)
        for k in range(2):
            cols = slice(k * 512, (k + 1) * 512)
            d_act = dg(lhs, r.WDN[k], 1, 1).astype(BF).astype(F32)
            low = (d_act * r.DGL[a, :, cols].astype(F32)).astype(BF)
            r.DUP[:, half(a), cols] = low.reshape(4, SUB, 512)
            at = pl.ds(pl.multiple_of(y * 512, 512), 512)
            r.SM[pl.ds(8 + 2 * k + l, 1), at] += colsum(low.astype(F32))
        return partial(a, blocks(r.DUP, a, 1024), lambda cols: shards(r.WUP, cols, slice(0, 1024)), 1)

    def fin4(a, total):
        d = norm_back(1, r.RES[half(a)] + total, r.XH[1, half(a)], r.RSTD[1, half(a)])
        r.RES2[half(a)] = d
        low = d.astype(BF)
        add_small(8, 0, WIDTH, colsum(low.astype(F32)))
        return gathered(r.DC, a, low, 2)

    def comp5(a):
        d_att = dg(blocks(r.DC, a, WIDTH), r.WCO[...].reshape(256, WIDTH), 1, 1).astype(BF)
        for k in range(2):
            cols = slice(k * 128, (k + 1) * 128)
            d_pair = d_att[:, cols]
            o_pair = r.OC[a, :, cols]
            q_pair = blocks(r.QC, a, 256)[:, cols]
            ds, dk, dv = [], None, None
            for hh in range(2):
                d_head = head_of(d_pair, hh)
                delta = jnp.sum(d_head.astype(F32) * o_pair, 1, keepdims=True)
                p = r.PC[2 * k + hh, a]
                d_scores = (p.astype(F32) * (dg(d_head, enc_keys(1, k), 1, 1) - delta)).astype(BF)
                ds.append(dg(d_scores, enc_keys(0, k), 1, 0))
                new_dk = dg(d_scores, head_of(q_pair, hh), 0, 0)
                new_dv = dg(p, d_head, 0, 0)
                dk = new_dk if dk is None else dk + new_dk
                dv = new_dv if dv is None else dv + new_dv
            dq = (jnp.where(heads[0], ds[0], ds[1]).astype(BF) * 0.125).astype(BF)
            r.DQC[:, half(a), cols] = dq.reshape(4, SUB, 128)
            add_small(3, (4 * k + own) * 128, 128, colsum(dq.astype(F32)))
            dv_cols = slice(256 + k * 128, 384 + k * 128)
            if a == 0:
                r.DKV[:, cols] = dk
                r.DKV[:, dv_cols] = dv
            else:
                r.DKV[:, cols] += dk
                r.DKV[:, dv_cols] += dv
        return partial(a, blocks(r.DQC, a, 256), lambda cols: shards(r.WCQ, cols, slice(0, 256)), 1)

    def fin5(a, total):
        d = norm_back(0, r.RES2[half(a)] + total, r.XH[0, half(a)], r.RSTD[0, half(a)])
        r.RES[half(a)] = d
        low = d.astype(BF)
        add_small(2, 0, WIDTH, colsum(low.astype(F32)))
        return gathered(r.DB, a, low, 2)

    do_sems = pair()

    def comp6(a):
        d_att = dg(blocks(r.DB, a, WIDTH), r.WSO[...].reshape(256, WIDTH), 1, 1).astype(BF)
        mine_d = jnp.where(c == 0, d_att[:, 0:128], d_att[:, 128:256])
        theirs_d = jnp.where(c == 0, d_att[:, 128:256], d_att[:, 0:128])
        r.DATS[:, half(a)] = theirs_d.reshape(4, SUB, 128)
        r.DO[mine, half(a)] = mine_d.reshape(4, SUB, 128)
        remote(r.DATS.at[:, span(a)], r.DO.at[mine, span(a)], mate, do_sems).start()

    class GroupSum:
        def __init__(self, total, land, four):
            self.total, self.land, self.four = total, land, four

        def cores(self):
            self.copy = remote(self.total, self.land, mate)
            self.copy.start()

        def chips(self):
            self.copy.wait()
            at = self.four.at[own]
            at[...] = self.total[...] + self.land[...]
            self.sems = pair()
            start([remote(at, at, peer(j), self.sems) for j in (1, 2, 3)])

        def sum(self):
            all_of(self.four.at[0:3], self.sems).wait()
            f = self.four
            return (f[0] + f[1]) + (f[2] + f[3])

    small = GroupSum(r.SM, r.SMR, r.SM4)
    late = GroupSum(r.SB, r.SBR, r.SB4)
    halves = remote(r.ALL, r.ALLR.at[0], h_peer)
    sides = remote(r.ALL, r.ALLR.at[1], x_peer)

    def sum_halves():
        r.ALL[0:8] = late.sum()
        r.ALL[8:24] = small.sum()
        halves.start()

    def sum_sides():
        halves.wait()
        r.ALL[...] += r.ALLR[0]
        sides.start()

    def sum_end():
        sides.wait()
        r.o_small[...] = r.ALL[...] + r.ALLR[1]

    far_shards, near_shards = pl.ds(4 * (1 - h), 4), pl.ds(4 * h, 4)

    class ColumnGrad:
        def __init__(self, name, out, parts, part=0, pieces=1):
            self.parts, self.out, self.pieces = parts, out, pieces
            for key in ("GS", "GR", "GK", "XS", "XR", "HS", "HR", "TS", "T"):
                setattr(self, key, getattr(r, key + "_" + name, None))
            self.part = part

        def compute(self, left, right, col, width):
            for target, k in ((self.GS, 1 - c), (self.GK, c)):
                rhs = right(k)
                for i in range(4):
                    out = dg(left(slice(i * 256, (i + 1) * 256)), rhs, 0, 0)
                    target[2 * i : 2 * i + 2, :, col : col + width] = out.astype(BF).reshape(2, 128, width)

        def compute_own(self, left, right):
            for i in range(4):
                out = dg(left(slice(i * 256, (i + 1) * 256)), right, 0, 0)
                self.GK[2 * i : 2 * i + 2] = out.astype(BF).reshape(2, 128, -1)

        def s0(self):
            self.core = remote(self.GS, self.GR, mate)
            self.core.start()

        def chip(self, shards, rows):
            if self.GR is None:
                return self.GK[shards, rows].astype(F32)
            return self.GK[shards, rows].astype(F32) + self.GR[shards, rows].astype(F32)

        def s1(self):
            if self.GR is not None:
                self.core.wait()
            self.far()
            self.near()

        def far(self):
            self.hsems, self.xc = pair(), []
            self.XS[0:4] = self.chip(far_shards, other_x).astype(BF)
            for i in range(self.pieces):
                at = slice(i * 4 // self.pieces, (i + 1) * 4 // self.pieces)
                self.xc.append(remote(self.XS.at[at], self.XR.at[at], x_peer))
                self.xc[i].start()

        def near(self):
            self.XS[4:8] = self.chip(near_shards, other_x).astype(BF)
            self.xn = remote(self.XS.at[4:8], self.XR.at[4:8], x_peer)
            self.xn.start()

        def s2(self, i=0):
            self.xc[i].wait()
            k = 4 // self.pieces
            at = slice(i * k, (i + 1) * k)
            total = self.chip(pl.ds(4 * (1 - h) + i * k, k), my_x) + self.XR[at].astype(F32)
            self.HS[at] = total.astype(BF)
            remote(self.HS.at[at], self.HR.at[at], h_peer, self.hsems).start()

        def s3(self):
            self.xn.wait()
            all_of(self.HS, self.hsems).wait()
            total = self.chip(near_shards, my_x) + self.XR[4:8].astype(F32) + self.HR[...].astype(F32)
            self.TS[...] = total.astype(BF)
            self.sems = pair()
            start([remote(self.TS.at[peer_block(j)], self.T.at[t, my_x], peer(j), self.sems) for j in (1, 2, 3)])
            self.T[t, my_x] = self.TS[own]

        def s4(self):
            all_of(self.TS.at[0:3], self.sems).wait()
            part = self.T.at[pl.ds(4 * c, 4), my_x]
            other = self.T.at[pl.ds(4 * c, 4), other_x]
            self.sems = pair()
            self.x2 = remote(part, part, x_peer)
            self.m2 = remote(other, other, mate, self.sems)
            self.x2.start()
            remote(part, part, mate, self.sems).start()

        def s5(self):
            self.x2.wait()
            self.m2.start()

        def s6(self):
            all_of(self.T.at[0:4], self.sems).wait()
            width = self.T.shape[2] // self.parts
            self.sem = new("local")
            for tt in range(8):
                for p in range(self.parts):
                    at = (p + self.part) * WIDTH + tt * width
                    src = self.T.at[tt, :, p * width : (p + 1) * width]
                    local(src, self.out.at[:, at : at + width], self.sem).start()

        def s7(self):
            local(self.T, self.T, self.sem).wait()

    class RowGrad:
        def __init__(self, name, out, pieces=1):
            self.out, self.pieces = out, pieces
            for key in ("GS", "GR", "GK", "XS", "XR", "HS", "HR", "T"):
                setattr(self, key, getattr(r, key + "_" + name))
            self.n = self.GS.shape[0] // 2

        def compute(self, left, right):
            for target, k in ((self.GS, 1 - c), (self.GK, c)):
                lhs = left(k)
                for i in range(2):
                    cols = slice(i * 512, (i + 1) * 512)
                    target[:, cols] = dg(lhs, right(cols), 0, 0).astype(BF)

        def s0(self):
            self.core = remote(self.GS, self.GR, mate)
            self.core.start()

        def rows(self, k):
            return pl.ds(pl.multiple_of(k * self.n, HALF), self.n)

        def piece(self, i):
            return slice(i * self.n // self.pieces, (i + 1) * self.n // self.pieces)

        def s1(self):
            self.core.wait()
            rows = self.rows(1 - x)
            self.XS[...] = (self.GK[rows].astype(F32) + self.GR[rows].astype(F32)).astype(BF)
            self.hsems, self.xc = pair(), []
            for i in range(self.pieces):
                at = self.piece(i)
                self.xc.append(remote(self.XS.at[at], self.XR.at[at], x_peer))
                self.xc[i].start()

        def total(self, i):
            k = self.n // self.pieces
            rows = pl.ds(pl.multiple_of(x * self.n, HALF) + i * k, k)
            return self.GK[rows].astype(F32) + self.GR[rows].astype(F32) + self.XR[self.piece(i)].astype(F32)

        def s2(self, i=0):
            self.xc[i].wait()
            at = self.piece(i)

            @pl.when(jnp.logical_not(stays))
            def _():
                self.HS[at] = self.total(i).astype(BF)
                remote(self.HS.at[at], self.HR.at[at], h_peer, self.hsems).start()

        def s3(self):
            part, other = self.T.at[self.rows(x)], self.T.at[self.rows(1 - x)]
            self.x2 = remote(part, part, x_peer)
            self.sems = pair()
            self.m1 = remote(part, part, mate, self.sems)
            self.m2 = remote(other, other, mate, self.sems)

            @pl.when(jnp.logical_not(stays))
            def _():
                all_of(self.HS, self.hsems).wait_send()

            @pl.when(stays)
            def _():
                all_of(self.HR, self.hsems).wait_recv()
                for i in range(self.pieces):
                    k = self.n // self.pieces
                    rows = pl.ds(pl.multiple_of(x * self.n, HALF) + i * k, k)
                    self.T[rows] = (self.total(i) + self.HR[self.piece(i)].astype(F32)).astype(BF)
                self.x2.start()
                self.m1.start()

        def s4(self):
            pass

        def s5(self):
            @pl.when(stays)
            def _():
                self.x2.wait()
                self.m2.start()

        def s6(self):
            @pl.when(stays)
            def _():
                all_of(self.T, self.sems).wait_send()

            @pl.when(jnp.logical_not(stays))
            def _():
                all_of(self.T, self.sems).wait_recv()

            self.outs = [local(self.T, self.out)]
            start(self.outs)

        def s7(self):
            wait(self.outs)

    g_dn = RowGrad("DN", r.o_dn, 4)
    g_up = ColumnGrad("UP", r.o_up, 1, pieces=2)
    g_co = RowGrad("CO", r.o_co)
    g_cq = ColumnGrad("CQ", r.o_cq, 3, pieces=2)
    g_so = RowGrad("SO", r.o_so)
    g_sq = [ColumnGrad("SQ%d" % p, r.o_sq, 1, p) for p in range(3)]

    def lanes(ref, k, width, base=0):
        return ref[:, :, pl.ds(pl.multiple_of(base + k * width, 128), width)].reshape(-1, width)

    rs_e = RelayScatter(r.PBE, r.VIAE, r.RBE, slice(0, ENC), [pair(), pair()])
    last_pairs = [pair() for _ in range(NSUB)]
    dk_x = remote(r.DKS, r.DKR, mate)

    def encoder_swap():
        their_enc = pl.ds(pl.multiple_of((1 - c) * 256, 256), 256)
        r.DKS[...] = r.DKV[their_enc].astype(BF).reshape(4, ENC, 512)
        dk_x.start()

    def encoder_back():
        dk_x.wait()
        my_enc = pl.ds(pl.multiple_of(c * 256, 256), 256)
        low = (r.DKV[my_enc] + r.DKR[...].reshape(256, 512).astype(F32)).astype(BF)
        r.DKL[...] = low.reshape(4, ENC, 512)
        dv_sum = colsum(low[:, 256:512].astype(F32))
        for k in range(2):
            add_small(4, (4 * k + own) * 128, 128, dv_sum[:, k * 128 : (k + 1) * 128])
        for n in range(2):
            cols = slice(n * 512, (n + 1) * 512)
            out = dg(low, shards(r.WCQ, cols, slice(256, 768)), 1, 1)
            r.PBE[:, :, cols] = out.astype(BF).reshape(4, ENC, 512)
        rs_e.start()

    def encoder_out():
        r.DES[...] = rs_e.finish().astype(BF)
        outs["enc"] = leave(r.DES, r.o_denc)

    def mixed_out():
        outs["mixed"] = leave(r.MXS, r.o_mixed)

    def grad_dn():
        g_dn.compute(lambda k: lanes(r.ACT, k, 512), lambda cols: r.DM[:, :, cols].reshape(512, -1))
        g_dn.s0()

    def grad_up():
        g_up.compute(lambda cols: r.S[:, :, cols].reshape(512, -1), lambda k: lanes(r.DUP, k, 512), 0, 512)
        g_up.s0()

    def grad_co():
        g_co.compute(lambda k: lanes(r.CATT, k, 128), lambda cols: r.DC[:, :, cols].reshape(512, -1))
        g_co.s0()

    def grad_cq():
        g_cq.compute(lambda cols: r.F[:, :, cols].reshape(512, -1), lambda k: lanes(r.DQC, k, 128), 0, 128)
        for p in range(2):
            g_cq.compute(
                lambda cols: r.E[:, :, cols].reshape(256, -1),
                lambda k, p=p: lanes(r.DKL, k, 128, 256 * p),
                128 + 128 * p,
                128,
            )
        g_cq.s0()

    def grad_so():
        g_so.compute(lambda k: lanes(r.ATT, k, 128), lambda cols: r.DB[:, :, cols].reshape(512, -1))
        g_so.s0()

    outs = {}

    beside = {
        1: [w_cq.cross, w_up.relay, w_co.cross],
        2: [lambda: w_cq.share(slice(0, 1)), w_dn.send],
        3: [encoder_kv, lambda: w_cq.share(slice(1, 2)), w_co.share, lambda: swap_start(3), lambda: swap_wait(2), kvc_x.wait, w_co.ready, lambda: w_cq.ready(slice(1, 2)), w_up.cross],
        4: [w_dn.cross],
        5: [w_up.share],
        6: [w_dn.share],
        7: [w_up.ready, w_dn.ready],
        8: [lambda: swap_wait(3), x_both.wait],
        13: [mixed_out],
        15: [grad_dn],
        16: [g_dn.s1, grad_up],
        17: [g_up.s1, lambda: g_dn.s2(0), small.cores],
        18: [lambda: g_dn.s2(1), lambda: g_dn.s2(2)],
        19: [encoder_swap, grad_co, lambda: g_dn.s2(3)],
        20: [encoder_back, grad_cq, g_co.s1, lambda: g_up.s2(0)],
        21: [small.chips, g_cq.s1, lambda: g_up.s2(1)],
        23: [rs_e.relay, grad_so, g_co.s2, lambda: g_cq.s2(0), lambda: g_cq.s2(1), g_so.s1],
    }

    comps = [comp1, comp2, comp3, comp4, comp5]
    fins = [fin1, fin2, fin3, fin4, fin5]
    rs, ag = {}, {}
    for slot in range(6 * NSUB):
        p, a = divmod(slot, NSUB)
        if p > 0:
            ag[p - 1, a].wait()
        if p < 5:
            rs[p, a] = comps[p](a)
        else:
            comp6(a)
        p, a = divmod(slot - 1, NSUB)
        if 0 <= p < 5:
            ag[p, a] = fins[p](a, rs[p, a].finish())
        p, a = divmod(slot - 2, NSUB)
        if 0 <= p < 5:
            ag[p, a].relay()
        for job in beside.get(slot, ()):
            job()

    all_of(r.DATS, do_sems).wait()
    r.DKVS[...] = jnp.zeros_like(r.DKVS)
    for i in range(4):
        n = (i + 1) * 256
        q = r.QKV[0, 2 * i : 2 * i + 2].reshape(256, 128)
        d_pair = r.DO[2 * i : 2 * i + 2].reshape(256, 128)
        o_pair = r.O[i * 256 : (i + 1) * 256]
        dqs, dk, dv = [], None, None
        for hh in range(2):
            d_head = head_of(d_pair, hh)
            delta = jnp.sum(d_head.astype(F32) * o_pair, 1, keepdims=True)
            p = probs[i][hh]
            d_scores = (p.astype(F32) * (dg(d_head, keys(2, n), 1, 1) - delta)).astype(BF)
            dqs.append(dg(d_scores, keys(1, n), 1, 0))
            new_dk = dg(d_scores, head_of(q, hh), 0, 0)
            new_dv = dg(p, d_head, 0, 0)
            dk = new_dk if dk is None else dk + new_dk
            dv = new_dv if dv is None else dv + new_dv
        dq = (jnp.where(heads[0], dqs[0], dqs[1]).astype(BF) * 0.125).astype(BF)
        r.DJN[0, 2 * i : 2 * i + 2] = dq.reshape(2, ROWS, 128)
        r.SB[0:1, pl.ds(pl.multiple_of(t * 128, 128), 128)] += colsum(dq.astype(F32))
        r.DKVS[0, 0:n] += dk
        r.DKVS[1, 0:n] += dv
    r.DJN[1] = r.DKVS[0].astype(BF).reshape(8, ROWS, 128)
    low = r.DKVS[1].astype(BF)
    r.DJN[2] = low.reshape(8, ROWS, 128)
    r.SB[1:2, pl.ds(pl.multiple_of(t * 128, 128), 128)] = colsum(low.astype(F32))
    dj_sems = pair()
    for p in range(3):
        at = pl.ds(pl.multiple_of(p * 256 + c * 128, 128), 128)
        remote(r.DJN.at[p, theirs], r.DJ.at[:, :, at], mate, dj_sems).start()
        r.DJ[:, :, at] = r.DJN[p, mine]
    late.cores()
    for p in range(3):
        g_sq[p].compute_own(lambda cols: r.X[:, :, cols].reshape(1024, -1), r.DJN[p].reshape(1024, 128))
        g_sq[p].far()
    for p in range(3):
        g_sq[p].near()
    g_so.s2()
    g_up.s3()
    g_dn.s3()
    late.chips()
    all_of(r.DJ.at[:, :, 0:384], dj_sems).wait()
    rs6 = [
        partial(
            a,
            blocks(r.DJ, a, 768),
            lambda cols: shards(r.WQKV, cols, slice(0, 768)),
            1,
            sums=RelayScatter(r.PB, r.VIA, r.RB, span(a), [last_pairs[a], scatter_pairs[a]]),
        )
        for a in range(NSUB)
    ]
    g_sq[0].s2()
    g_sq[1].s2()
    g_sq[2].s2()
    rs6[0].relay()
    g_up.s4()
    rs6[1].relay()
    g_cq.s3()
    rs6[2].relay()
    g_sq[0].s3()
    rs6[3].relay()
    g_sq[1].s3()
    g_sq[2].s3()
    g_so.s3()
    g_co.s3()
    sum_halves()
    g_cq.s4()
    r.DTS[half(0)] = (r.RES[half(0)] + rs6[0].finish()).astype(BF)
    r.DTS[half(1)] = (r.RES[half(1)] + rs6[1].finish()).astype(BF)
    r.DTS[half(2)] = (r.RES[half(2)] + rs6[2].finish()).astype(BF)
    r.DTS[half(3)] = (r.RES[half(3)] + rs6[3].finish()).astype(BF)
    outs["tokens"] = leave(r.DTS, r.o_dtok)
    g_sq[0].s4()
    g_sq[1].s4()
    g_sq[2].s4()
    encoder_out()
    g_dn.s5()
    g_up.s5()
    g_co.s5()
    g_so.s5()
    g_dn.s6()
    g_cq.s5()
    sum_sides()
    g_sq[0].s5()
    g_up.s6()
    g_sq[1].s5()
    g_co.s6()
    g_so.s6()
    g_cq.s6()
    g_sq[2].s5()
    g_sq[0].s6()
    g_sq[1].s6()
    g_sq[2].s6()
    sum_end()

    @pl.when(jnp.logical_not(stays))
    def _():
        for cp in outs.values():
            cp.wait()

    for g in (g_dn, g_up, g_co, g_cq, g_so, *g_sq):
        g.s7()
    assert count["send"] <= N_SEND and count["recv"] <= N_RECV and count["local"] <= N_LOCAL


def on_chip(*args):
    (tokens, encoder, seq_len, enc_len, d_mixed, *rest) = args
    *mats, self_bias, cross_bias, norm_gain, norm_bias, fc1_bias, fc2_bias = rest
    anywhere = pl.BlockSpec(memory_space=pl.ANY)
    vmem = pl.BlockSpec(memory_space=pltpu.VMEM)
    smem = pl.BlockSpec(memory_space=pltpu.SMEM)
    shapes = [
        ((ROWS, WIDTH), BF),
        ((ROWS, WIDTH), BF),
        ((ENC, WIDTH), BF),
        ((128, 3 * WIDTH), BF),
        ((128, WIDTH), BF),
        ((128, 3 * WIDTH), BF),
        ((128, WIDTH), BF),
        ((128, HIDDEN), BF),
        ((512, WIDTH), BF),
        ((24, WIDTH), F32),
    ]
    outs = pl.pallas_call(
        layer_kernel,
        out_shape=[jax.ShapeDtypeStruct(s, d) for s, d in shapes],
        in_specs=[anywhere, anywhere, smem, smem, anywhere] + [anywhere] * 6 + [vmem] * 6,
        out_specs=[vmem] * 3 + [anywhere] * 6 + [vmem],
        scratch_shapes=[pltpu.VMEM(s, d) for s, d in SCRATCH.values()]
        + [
            pltpu.SemaphoreType.DMA((N_SEND,)),
            pltpu.SemaphoreType.DMA((N_RECV,)),
            pltpu.SemaphoreType.DMA((N_LOCAL,)),
        ],
        compiler_params=pltpu.CompilerParams(
            collective_id=0, has_side_effects=True, vmem_limit_bytes=VMEM_BYTES
        ),
        cost_estimate=pl.CostEstimate(
            flops=16 * 10**9, bytes_accessed=16 * 2**20, transcendentals=8 * 2**20
        ),
    )(
        tokens, encoder, seq_len, enc_len, d_mixed, *mats,
        self_bias, cross_bias, norm_gain, norm_bias,
        fc1_bias.reshape(1, -1), fc2_bias.reshape(1, -1),
    )
    steps = 4

    def rows_of(shape):
        return pl.BlockSpec((shape[0] // steps, shape[1]), lambda i: (i, 0))

    def whole(shape):
        return pl.BlockSpec(shape, lambda i: (0, 0))

    wide = [(s, BF if k == 0 else F32) for k, (s, _) in enumerate(shapes[:-1])]
    flat = [((3, WIDTH), F32)] * 4 + [((1, HIDDEN), F32), ((1, WIDTH), F32)]
    *results, fc1_sum, fc2_sum = pl.pallas_call(
        widen_kernel,
        grid=(steps,),
        out_shape=[jax.ShapeDtypeStruct(s, d) for s, d in wide + flat],
        in_specs=[rows_of(s) for s, _ in shapes[:-1]] + [whole(shapes[-1][0])],
        out_specs=[rows_of(s) for s, _ in wide] + [whole(s) for s, _ in flat],
        compiler_params=pltpu.CompilerParams(vmem_limit_bytes=VMEM_BYTES),
    )(*outs)
    return (*results, fc1_sum.reshape(-1), fc2_sum.reshape(-1))


def widen_kernel(*refs):
    n = len(OUT_NAMES)
    small, flat = refs[n - 1], refs[2 * n - 1 :]
    for src, dst in zip(refs[: n - 1], refs[n:]):
        dst[...] = src[...].astype(dst.dtype)
    for k, rows in enumerate(((0, 1, 2), (3, 4, 8), (5, 9, 10), (6, 11, 12))):
        for i, row in enumerate(rows):
            flat[k][i : i + 1, :] = small[row : row + 1, :]
    for k in range(4):
        flat[4][0:1, k * WIDTH : (k + 1) * WIDTH] = small[16 + k : 17 + k, :]
    flat[5][...] = small[13:14, :]


def fits(mesh, tokens, encoder, self_qkv, fc1_weight):
    return (
        (mesh.shape["rep"], mesh.shape["shard"]) == (4, 8)
        and tokens.shape == (32 * ROWS, WIDTH)
        and encoder.shape == (32 * ENC, WIDTH)
        and self_qkv.shape == (WIDTH, 3 * WIDTH)
        and fc1_weight.shape == (WIDTH, HIDDEN)
    )


def solution(mesh):
    def placed(body):
        return jax.shard_map(
            body,
            mesh=mesh,
            in_specs=(
                P(("rep", "shard"), None),
                P(("rep", "shard"), None),
                P("rep"),
                P("rep"),
                P(("rep", "shard"), None),
                P("shard", None),
                P("shard", None),
                P("shard", None),
                P("shard", None),
                P("shard", None),
                P("shard", None),
                P(),
                P(),
                P(),
                P(),
                P(),
                P(),
            ),
            out_specs=(
                P(("rep", "shard"), None),
                P(("rep", "shard"), None),
                P(("rep", "shard"), None),
                P("shard", None),
                P("shard", None),
                P("shard", None),
                P("shard", None),
                P("shard", None),
                P("shard", None),
                P(),
                P(),
                P(),
                P(),
                P(),
                P(),
            ),
            check_vma=False,
        )

    def run(*args):
        fast = fits(mesh, args[0], args[1], args[5], args[9])
        return placed(on_chip if fast else local)(*args)

    return run
```
